32 devices in a mesh: lat: 16 (over z, y, x), lev: 2 (over core).
Axes of the slice: x: 2, y: 2, z: 4, core: 2. Of those that a mesh axis runs over, the one named last changes fastest.
Arguments:
- fields: bfloat16 [4, 4, 32, 2816], P('lev', None, 'lat'), may hold values from -6 to 6
- rows_first: int32 [32], P('lat'), may hold values from 0 to 28, as said below
- points: int32 [32], replicated, may hold values from 2753 to 2816, as said below
- starts: int32 [32, 4, 2816], P('lat'), may hold values from -60 to 2939, as said below
- weights: bfloat16 [32, 4, 4, 2816], P('lat'), may hold values from -1.5 to 1.5
- thickness: float32 [4], P('lev'), may hold values from 0.05 to 0.4
- legendre: bfloat16 [640, 32, 1281], P('lat'), may hold values from -1 to 1
Outputs:
- spectra: bfloat16 [4, 5, 2, 640, 1281], P('lev', None, None, 'lat')
The draws below stay inside these ranges and needn't reach their ends.
Inputs may be any that keep to these rules, and one draw needn't show every extreme that they name: rows_first[j] is j - 2 or j - 1, moved into 0 to 28 at the ends. Columns of latitude j from points[j] on are padding. For every point k below points[j], starts[j, t, k] - k lies between minus half of 256 and half of 256 minus 4, and both ends are taken.
All inputs are finite; a program needn't handle non-finite values.
Results may differ from the reference program's by a relative error of at most 0.0064.
Values may be sent and summed in bfloat16 or wider, within the bound.
No kernel may reach another device: no remote copies, remote signals or barrier semaphores. Data moves between devices by JAX's collectives and lax.ppermute only.
A program may use at most 64 MiB of HBM per device.

```python
import math
import jax
import jax.numpy as jnp
from jax import lax

M = 1280
NLON = 2816
FIELDS = 4
BLOCK = 256
SPREAD = 63
LEVELS = 4
NLAT = 32
PAIRS = 640
K = 1281


def draw_layout(key):
    lat_index = jnp.arange(NLAT, dtype=jnp.int32)
    offset = jax.random.randint(jax.random.fold_in(key, 101), (NLAT,), -2, 0)
    first_rows = jnp.clip(lat_index + offset, 0, NLAT - 4)
    counts = jax.random.randint(jax.random.fold_in(key, 102), (NLAT,), NLON - SPREAD, NLON + 1)
    picked = jax.random.randint(jax.random.fold_in(key, 103), (2,), 0, NLAT)
    second = (picked[0] + 1 + picked[1] % (NLAT - 1)) % NLAT
    counts = jnp.where(lat_index == picked[0], NLON, counts)
    counts = jnp.where(lat_index == second, NLON - SPREAD, counts)
    return (first_rows.astype(jnp.int32), counts.astype(jnp.int32))


def draw_rows_first(key, part):
    return draw_layout(key)[0]


def draw_points(key, part):
    return draw_layout(key)[1]


def draw_starts(key, part):
    first_rows, counts = draw_layout(key)
    key = jax.random.fold_in(key, 3)
    displace = BLOCK // 2 - SPREAD - 5
    shifts = jax.random.randint(key, (NLAT, 4, NLON), -displace, displace + 1)
    source_counts = counts[first_rows[:, None] + jnp.arange(4, dtype=jnp.int32)[None, :]]
    column = jnp.arange(NLON, dtype=jnp.int32)
    scaled = column[None, None, :] * source_counts[:, :, None] // counts[:, None, None]
    result = scaled + shifts
    result = result.at[0, 0, BLOCK].set(BLOCK - BLOCK // 2)
    result = result.at[1, 0, BLOCK].set(BLOCK + BLOCK // 2 - 4)
    result = result.at[0, 1, 0].set(-displace)
    result = result.at[NLAT - 1, 3, NLON - 1].set(NLON + BLOCK // 2 - 5)
    return result.astype(jnp.int32)


def levels(rng, dims, shards, least, top_value):
    factor_of, own = 1.0, jax.random.fold_in(rng, 6)
    for dim, parts in shards:
        heights = jnp.exp(jax.random.uniform(jax.random.fold_in(own, dim), (parts,), jnp.float32, least / len(shards), top_value / len(shards)))
        factor_of = factor_of * jnp.repeat(heights, dims[dim] // parts).reshape([-1 if axis == dim else 1 for axis in range(len(dims))])
    return factor_of


def normal_values(key, shape, deviation, reach, shards=(), kind=jnp.bfloat16):
    drawn = jax.random.normal(key, shape, jnp.float32) * deviation
    if len(shards) > 0:
        drawn = levels(key, shape, shards, -0.22, 0.18) * drawn
    return jnp.clip(drawn, min=-reach, max=reach).astype(kind)


def setup_inputs(seed: int = 0) -> dict:
    splits = jax.random.split(jax.random.key(seed), 8)
    return {
        "fields": normal_values(splits[0], (LEVELS, FIELDS, NLAT, NLON), 1.0, 6.0, ((0, 2), (2, 16))),
        "rows_first": draw_rows_first(jax.random.fold_in(splits[7], 71), 0),
        "points": draw_points(jax.random.fold_in(splits[7], 71), 0),
        "starts": draw_starts(jax.random.fold_in(splits[7], 71), 0),
        "weights": normal_values(splits[4], (NLAT, 4, 4, NLON), 0.25, 1.5, ((0, 16),)),
        "thickness": jnp.clip(jnp.exp(math.log(0.4) - 2.0794415 * jax.random.uniform(splits[5], (LEVELS,), jnp.float32) ** levels(splits[5], (LEVELS,), ((0, 2),), -0.2, 0.2)), 0.05, 0.4),
        "legendre": normal_values(splits[6], (PAIRS, NLAT, K), NLAT ** -0.5, 1.0, ((0, 16),)),
    }


def fourier_table(point_total):
    half_pairs = M // 2
    column = lax.broadcasted_iota(jnp.int32, (NLON, 2 * half_pairs), 1)
    point_index = lax.broadcasted_iota(jnp.int32, (NLON, 2 * half_pairs), 0)
    pairing = column % half_pairs
    wavenumber = jnp.where(column < half_pairs, pairing, M - 1 - pairing)
    phase_int = wavenumber * point_index % point_total
    angles = phase_int.astype(jnp.float32) * (2.0 * jnp.pi / point_total.astype(jnp.float32))
    scaling = jnp.sqrt(2.0 / point_total.astype(jnp.float32))
    is_live = point_index < point_total
    cosine = jnp.where(is_live, scaling * jnp.cos(angles), 0.0)
    sines = jnp.where(is_live, -scaling * jnp.sin(angles), 0.0)
    return jnp.concatenate([cosine, sines], axis=1).astype(jnp.bfloat16)

def reference(fields, rows_first, points, starts, weights, thickness, legendre):

    def interpolate(latitude):
        summed = jnp.zeros((LEVELS, FIELDS, NLON), jnp.float32)
        for stencil_row in range(4):
            global_row = rows_first[latitude] + stencil_row
            source = lax.dynamic_index_in_dim(fields, global_row, 2, keepdims=False).astype(jnp.float32)
            source_total = points[global_row]
            for offset in range(4):
                column = (starts[latitude, stencil_row] + offset) % source_total
                factor = weights[latitude, stencil_row, offset].astype(jnp.float32)
                summed = summed + factor * jnp.take(source, column, axis=2)
        is_live = jnp.arange(NLON, dtype=jnp.int32) < points[latitude]
        return jnp.where(is_live, summed, 0.0).astype(jnp.bfloat16)
    departed = lax.map(interpolate, jnp.arange(NLAT, dtype=jnp.int32))
    virtual = departed[:, :, 2].astype(jnp.float32) + 0.61 * departed[:, :, 3].astype(jnp.float32)
    layered = thickness[None, :, None] * virtual
    geopotential = jnp.flip(jnp.cumsum(jnp.flip(layered, 1), axis=1), 1).astype(jnp.bfloat16)
    gridded = jnp.concatenate([departed, geopotential[:, :, None]], axis=2)
    row_total = LEVELS * (FIELDS + 1)
    grid_rows = gridded.reshape(NLAT, row_total, NLON)

    def transform(packed):
        row_block, latitude = packed
        table = fourier_table(points[latitude]).astype(jnp.float32)
        return jnp.dot(row_block.astype(jnp.float32), table, preferred_element_type=jnp.float32).astype(jnp.bfloat16)
    coefficients = lax.map(transform, (grid_rows, jnp.arange(NLAT, dtype=jnp.int32)))
    coefficients = coefficients.reshape(NLAT, row_total, 2, 2, PAIRS)
    slot_index = jnp.arange(K, dtype=jnp.int32)

    def degree_sums(pair_index):
        picked = lax.dynamic_index_in_dim(coefficients, pair_index, 4, keepdims=False).astype(jnp.float32)
        table = lax.dynamic_index_in_dim(legendre, pair_index, 0, keepdims=False).astype(jnp.float32)
        first_part = jnp.einsum('lrc,lk->rck', picked[:, :, :, 0], table, precision=lax.Precision.HIGHEST)
        second_part = jnp.einsum('lrc,lk->rck', picked[:, :, :, 1], table, precision=lax.Precision.HIGHEST)
        return jnp.where(slot_index < M - pair_index, first_part, second_part).astype(jnp.bfloat16)
    spectra = lax.map(degree_sums, jnp.arange(PAIRS, dtype=jnp.int32))
    return spectra.reshape(PAIRS, LEVELS, FIELDS + 1, 2, K).transpose(1, 2, 3, 0, 4)
```

```python
import functools

import jax
import jax.numpy as jnp
import numpy as np
from jax import lax
from jax.experimental import pallas as pl
from jax.experimental.pallas import tpu as pltpu
from jax.sharding import PartitionSpec as P

LANES = 128
SUB = 8
HALF = 64
STENCIL = 4
LIMIT = 56 * 1024 * 1024


def turn_parts(product, total, inverse):
    turns = (product - jnp.floor(product * inverse + 0.5) * total) * inverse
    halves = jnp.floor(2.0 * turns + 0.5)
    sign = 1.0 - 2.0 * jnp.abs(halves)
    x = (turns - 0.5 * halves) * np.float32(2.0 * np.pi)
    y = x * x
    sine = -1.0 / 39916800.0
    for term in (1.0 / 362880.0, -1.0 / 5040.0, 1.0 / 120.0, -1.0 / 6.0, 1.0):
        sine = sine * y + np.float32(term)
    cosine = 1.0 / 479001600.0
    for term in (-1.0 / 3628800.0, 1.0 / 40320.0, -1.0 / 720.0, 1.0 / 24.0, -0.5, 1.0):
        cosine = cosine * y + np.float32(term)
    return sign * cosine, sign * (sine * x)


def extend(source, row, total, ext, slot):
    levels, fields, _, lon = source.shape
    blocks = lon // LANES
    for level in range(levels):
        for field in range(fields):
            place = level * fields + field
            line = source[level, field].astype(jnp.float32)
            for block in range(blocks):
                ext[slot, block + 1, place : place + 1, :] = line[
                    row : row + 1, block * LANES : (block + 1) * LANES
                ]
    lane = lax.broadcasted_iota(jnp.int32, (SUB, LANES), 1)
    missing = lon - total
    ahead = lane + missing
    behind = lane - missing
    first = jnp.take_along_axis(ext[slot, 1], ahead & (LANES - 1), axis=1)
    second = jnp.take_along_axis(ext[slot, 2], ahead & (LANES - 1), axis=1)
    last = ext[slot, blocks]
    final = jnp.take_along_axis(last, behind & (LANES - 1), axis=1)
    before = jnp.take_along_axis(ext[slot, blocks - 1], behind & (LANES - 1), axis=1)
    ext[slot, 0] = jnp.where(behind >= 0, final, before)
    ext[slot, blocks] = jnp.where(ahead < LANES, last, first)
    ext[slot, blocks + 1] = jnp.where(ahead < LANES, first, second)


def spread_rows(starts, begins):
    for latitude in range(starts.shape[0]):
        for row in range(STENCIL):
            begins[latitude, row] = starts[latitude, row : row + 1, :]


def gathered(block, latitude, picks, ext, starts, weights):
    offset = pl.multiple_of(block * LANES, LANES)
    total = jnp.zeros((SUB, LANES), jnp.float32)
    for row, slot in picks:
        start = starts[latitude, row, :, pl.ds(offset, LANES)] - (offset - LANES)
        start = jnp.broadcast_to(start, (SUB, LANES))
        factors = weights[latitude, row, :, pl.ds(offset, LANES)].astype(jnp.float32)
        parts = [ext[slot, block + piece] for piece in range(3)]
        for column in range(4):
            place = start + column
            lane = place & (LANES - 1)
            low, middle, high = [jnp.take_along_axis(part, lane, axis=1) for part in parts]
            value = jnp.where(place < LANES, low, jnp.where(place < 2 * LANES, middle, high))
            total = total + factors[column : column + 1] * value
    return total


def near_kernel(
    pair_total, pair_count, rows_first, points, fields, starts, weights,
    partial, table, twiddle, ext, fine, begins,
):
    lat_count = starts.shape[0]
    spread_rows(starts, begins)
    blocks = partial.shape[1]
    columns = table.shape[2] // 2
    first_lat = lax.axis_index("lat") * lat_count
    for latitude in range(lat_count):
        extend(fields, latitude, points[first_lat + latitude], ext, latitude)
    for latitude in range(lat_count):
        mine = first_lat - rows_first[latitude]
        picks = [(mine + row, row) for row in range(lat_count)]

        def one(block, carry, latitude=latitude, picks=picks):
            partial[latitude, block] = gathered(block, latitude, picks, ext, begins, weights)
            return carry

        lax.fori_loop(0, blocks, one, 0)
    for latitude in range(lat_count):
        total = jnp.full((1, 1), points[first_lat + latitude], jnp.int32).astype(jnp.float32)
        inverse = 1.0 / total
        scaling = jnp.sqrt(2.0 * inverse)
        width = min(columns, 512)

        def chunk(index, carry, latitude=latitude, total=total, inverse=inverse, scaling=scaling):
            at = pl.multiple_of(index * width, width)
            numbers = wavenumbers_at(at, width, pair_count, pair_total)
            step = lax.broadcasted_iota(jnp.int32, (blocks, width), 0).astype(jnp.float32)
            cosine, sine = turn_parts(numbers * step * float(LANES), total, inverse)
            twiddle[latitude, :, pl.ds(at, width)] = scaling * cosine
            twiddle[latitude, :, pl.ds(columns + at, width)] = scaling * sine
            step = lax.broadcasted_iota(jnp.int32, (16, width), 0).astype(jnp.float32)
            low_cos, low_sin = turn_parts(numbers * step, total, inverse)
            step = lax.broadcasted_iota(jnp.int32, (SUB, width), 0).astype(jnp.float32)
            high_cos, high_sin = turn_parts(numbers * step * 16.0, total, inverse)
            fine[0] = high_cos
            fine[1] = high_sin
            for high in range(SUB):
                this_cos = fine[0, high : high + 1, :]
                this_sin = fine[1, high : high + 1, :]
                rows = pl.ds(16 * high, 16)
                table[latitude, rows, pl.ds(at, width)] = (
                    this_cos * low_cos - this_sin * low_sin
                ).astype(jnp.bfloat16)
                table[latitude, rows, pl.ds(columns + at, width)] = (
                    this_cos * low_sin + this_sin * low_cos
                ).astype(jnp.bfloat16)
            return carry

        lax.fori_loop(0, columns // width, chunk, 0)


def wavenumbers_at(at, width, pair_count, pair_total):
    column = lax.broadcasted_iota(jnp.int32, (1, width), 1) + at
    lane = column & (LANES - 1)
    second = lane >= HALF
    inner = jnp.where(second, lane - HALF, lane)
    pair = (column >> 7) * pair_count + inner
    number = jnp.where(second, 2 * pair_total - 1 - pair, pair)
    return jnp.where(inner < pair_count, number, 0).astype(jnp.float32)


def far_kernel(
    rows_first, points, below, above, starts, weights, partial, table, twiddle,
    out, ext, grid, begins,
):
    lat_count = starts.shape[0]
    spread_rows(starts, begins)
    blocks = partial.shape[1]
    columns = table.shape[2] // 2
    first_lat = lax.axis_index("lat") * lat_count
    lat_total = points.shape[0]
    for row in range(lat_count):
        under = jnp.maximum(first_lat - lat_count + row, 0)
        over = jnp.minimum(first_lat + lat_count + row, lat_total - 1)
        extend(below, row, points[under], ext, row)
        extend(above, row, points[over], ext, lat_count + row)
    lane = lax.broadcasted_iota(jnp.int32, (SUB, LANES), 1)
    for latitude in range(lat_count):
        mine = first_lat - rows_first[latitude]
        one_row = jnp.where(mine >= 1, 0, 2)
        two_row = jnp.where(mine <= 1, 3, 1)
        picks = []
        for row in (one_row, two_row):
            picks.append((row, jnp.where(row < mine, row - mine + 2, row - mine)))

        def one(block, carry, latitude=latitude, picks=picks):
            value = partial[latitude, block] + gathered(
                block, latitude, picks, ext, begins, weights
            )
            live = lane + block * LANES < points[first_lat + latitude]
            grid[block] = jnp.where(live, value, 0.0)
            return carry

        lax.fori_loop(0, blocks, one, 0)
        rows = grid[...].reshape(blocks * SUB, LANES).astype(jnp.bfloat16)
        width = 2 * LANES

        def chunk(index, carry, latitude=latitude, rows=rows):
            at = pl.multiple_of(index * width, width)
            real = jnp.dot(
                rows, table[latitude, :, pl.ds(at, width)], preferred_element_type=jnp.float32
            ).reshape(blocks, SUB, width)
            imag = jnp.dot(
                rows,
                table[latitude, :, pl.ds(columns + at, width)],
                preferred_element_type=jnp.float32,
            ).reshape(blocks, SUB, width)
            cosine = jnp.zeros((SUB, width), jnp.float32)
            sine = jnp.zeros((SUB, width), jnp.float32)
            for block in range(blocks):
                turn_cos = twiddle[latitude, block : block + 1, pl.ds(at, width)]
                turn_sin = twiddle[latitude, block : block + 1, pl.ds(columns + at, width)]
                cosine = cosine + (real[block] * turn_cos - imag[block] * turn_sin)
                sine = sine - (real[block] * turn_sin + imag[block] * turn_cos)
            both = jnp.concatenate([cosine, sine], axis=0).astype(jnp.bfloat16)
            for piece in range(width // LANES):
                out[index * (width // LANES) + piece, 2 * SUB * latitude : 2 * SUB * (latitude + 1), :] = (
                    both[:, piece * LANES : (piece + 1) * LANES]
                )
            return carry

        lax.fori_loop(0, columns // width, chunk, 0)


def legendre_kernel(
    level_count, field_count, thickness, received, totals, legendre, out, wide, left,
):
    owners, packed_rows, _ = received.shape
    lat_total = wide.shape[0] // (2 * SUB)
    pair_count = legendre.shape[0]
    tile = legendre.shape[2]
    groups = [(at, min(SUB, pair_count - at)) for at in range(0, pair_count, SUB)]
    out_rows = level_count * (field_count + 1) * 2
    step = pl.program_id(0)

    @pl.when(step == 0)
    def build():
        wide[...] = received[...].astype(jnp.float32).reshape(wide.shape)
        level_place = lax.axis_index("lev")
        lines = {}
        for part in range(2):
            running = jnp.zeros((lat_total, LANES), jnp.float32)
            for other in range(1, totals.shape[0]):
                running = running + jnp.where(other > level_place, totals[other, part], 0.0)
            for level in reversed(range(level_count)):
                for field in range(field_count):
                    place = part * SUB + level * field_count + field
                    lines[level, field, part] = wide[pl.ds(place, lat_total, stride=2 * SUB), :]
                running = running + thickness[level] * (
                    lines[level, 2, part] + 0.61 * lines[level, 3, part]
                )
                lines[level, field_count, part] = running
        depth = SUB * lat_total
        spread = (
            lax.broadcasted_iota(jnp.int32, (lat_total, depth), 0)
            == lax.broadcasted_iota(jnp.int32, (lat_total, depth), 1) % lat_total
        ).astype(jnp.bfloat16)
        keep = (
            lax.broadcasted_iota(jnp.int32, (SUB, depth), 0)
            == lax.broadcasted_iota(jnp.int32, (SUB, depth), 1) // lat_total
        )
        order = [
            (level, field, part)
            for level in range(level_count)
            for field in range(field_count + 1)
            for part in range(2)
        ]
        for place in range(0, out_rows, 2):
            couple = [
                lax.dot_general(
                    lines[key].astype(jnp.bfloat16),
                    spread,
                    (((0,), (0,)), ((), ())),
                    preferred_element_type=jnp.float32,
                )
                for key in order[place : place + 2]
            ]
            for member in range(2):
                for group, (at, _) in enumerate(groups):
                    begin = member * HALF + at
                    pieces = [jnp.where(keep, one[begin : begin + SUB], 0.0) for one in couple]
                    into = (member * out_rows + place) * SUB
                    left[group, into : into + 2 * SUB, :] = jnp.concatenate(
                        pieces, axis=0
                    ).astype(jnp.bfloat16)

    first_pair = lax.axis_index("lat") * pair_count
    pair_total = pair_count * owners
    parts = []
    for group, (at, size) in enumerate(groups):
        depth = size * lat_total
        values = legendre[at : at + size].reshape(depth, tile)
        sums = jnp.dot(left[group, :, :depth], values, preferred_element_type=jnp.float32)
        sums = sums.reshape(2, out_rows, SUB, tile)
        slot = lax.broadcasted_iota(jnp.int32, (SUB, tile), 1) + step * tile
        pair = lax.broadcasted_iota(jnp.int32, (SUB, tile), 0) + (first_pair + at)
        first = slot + pair < 2 * pair_total
        chosen = jnp.where(first, sums[0], sums[1])
        parts.append(chosen[:, :size])
    out[...] = jnp.concatenate(parts, axis=1).astype(jnp.bfloat16).reshape(out.shape)


def local(fields, rows_first, points, starts, weights, thickness, legendre):
    level_count, field_count, lat_count, lon_count = fields.shape
    pair_count, lat_total, degrees = legendre.shape
    owners = lax.axis_size("lat")
    level_owners = lax.axis_size("lev")
    blocks = lon_count // LANES
    columns = owners * LANES
    up = [(i, i + 1) for i in range(owners - 1)]
    below = lax.ppermute(fields, "lat", up)
    above = lax.ppermute(fields, "lat", [(j, i) for i, j in up])

    scalar = pl.BlockSpec(memory_space=pltpu.SMEM)
    vector = pl.BlockSpec(memory_space=pltpu.VMEM)
    params = pltpu.CompilerParams(vmem_limit_bytes=LIMIT)
    partial, table, twiddle = pl.pallas_call(
        functools.partial(near_kernel, pair_count * owners, pair_count),
        out_shape=(
            jax.ShapeDtypeStruct((lat_count, blocks, SUB, LANES), jnp.float32),
            jax.ShapeDtypeStruct((lat_count, LANES, 2 * columns), jnp.bfloat16),
            jax.ShapeDtypeStruct((lat_count, blocks, 2 * columns), jnp.float32),
        ),
        in_specs=[scalar, scalar, vector, vector, vector],
        out_specs=(vector, vector, vector),
        scratch_shapes=[
            pltpu.VMEM((lat_count, blocks + 2, SUB, LANES), jnp.float32),
            pltpu.VMEM((2, SUB, min(columns, 512)), jnp.float32),
            pltpu.VMEM((lat_count, STENCIL, 1, lon_count), jnp.int32),
        ],
        compiler_params=params,
        cost_estimate=pl.CostEstimate(flops=10_000_000, bytes_accessed=4_000_000, transcendentals=0),
        name="near_rows",
    )(rows_first, points, fields, starts, weights)

    coefficients = pl.pallas_call(
        far_kernel,
        out_shape=jax.ShapeDtypeStruct((owners, 2 * SUB * lat_count, LANES), jnp.bfloat16),
        in_specs=[scalar, scalar] + [vector] * 7,
        out_specs=vector,
        scratch_shapes=[
            pltpu.VMEM((2 * lat_count, blocks + 2, SUB, LANES), jnp.float32),
            pltpu.VMEM((blocks, SUB, LANES), jnp.float32),
            pltpu.VMEM((lat_count, STENCIL, 1, lon_count), jnp.int32),
        ],
        compiler_params=params,
        name="far_rows",
    )(rows_first, points, below, above, starts, weights, partial, table, twiddle)

    received = lax.all_to_all(coefficients, "lat", split_axis=0, concat_axis=0, tiled=True)
    by_level = received.reshape(lat_total, 2, level_count, field_count, LANES).astype(jnp.float32)
    virtual = by_level[:, :, :, 2] + 0.61 * by_level[:, :, :, 3]
    total = jnp.sum(thickness[None, None, :, None] * virtual, axis=2).transpose(1, 0, 2)
    totals = lax.all_gather(total, "lev")

    tile = 256
    out_rows = level_count * (field_count + 1) * 2
    steps = (degrees + tile - 1) // tile
    group_count = (pair_count + SUB - 1) // SUB
    return pl.pallas_call(
        functools.partial(legendre_kernel, level_count, field_count),
        grid=(steps,),
        out_shape=jax.ShapeDtypeStruct(
            (level_count, field_count + 1, 2, pair_count, degrees), jnp.bfloat16
        ),
        in_specs=[
            scalar,
            pl.BlockSpec(received.shape, lambda i: (0, 0, 0)),
            pl.BlockSpec(totals.shape, lambda i: (0, 0, 0, 0)),
            pl.BlockSpec((pair_count, lat_total, tile), lambda i: (0, 0, i)),
        ],
        out_specs=pl.BlockSpec(
            (level_count, field_count + 1, 2, pair_count, tile), lambda i: (0, 0, 0, 0, i)
        ),
        scratch_shapes=[
            pltpu.VMEM((lat_total * 2 * SUB, LANES), jnp.float32),
            pltpu.VMEM((group_count, 2 * out_rows * SUB, SUB * lat_total), jnp.bfloat16),
        ],
        compiler_params=params,
        name="degree_sums",
    )(thickness, received, totals, legendre)


def solution(mesh):
    placed = (
        P("lev", None, "lat", None),
        P("lat"),
        P(),
        P("lat", None, None),
        P("lat", None, None, None),
        P("lev"),
        P("lat", None, None),
    )
    return jax.shard_map(
        local,
        mesh=mesh,
        in_specs=placed,
        out_specs=P("lev", None, None, "lat", None),
        check_vma=False,
    )
```

```python
import functools

import jax
import jax.numpy as jnp
import numpy as np
from jax import lax
from jax.experimental import pallas as pl
from jax.experimental.pallas import tpu as pltpu
from jax.sharding import PartitionSpec as P

LANES = 128
SUB = 8
HALF = 64
STENCIL = 4
LIMIT = 56 * 1024 * 1024


def lane_gather(values, lanes):
    return jnp.take_along_axis(values, lanes, axis=1, mode="promise_in_bounds")


def turn_parts(product, total, inverse):
    turns = (product - jnp.floor(product * inverse + 0.5) * total) * inverse
    halves = jnp.floor(2.0 * turns + 0.5)
    sign = 1.0 - 2.0 * jnp.abs(halves)
    x = (turns - 0.5 * halves) * np.float32(2.0 * np.pi)
    y = x * x
    sine = -1.0 / 39916800.0
    for term in (1.0 / 362880.0, -1.0 / 5040.0, 1.0 / 120.0, -1.0 / 6.0, 1.0):
        sine = sine * y + np.float32(term)
    cosine = 1.0 / 479001600.0
    for term in (-1.0 / 3628800.0, 1.0 / 40320.0, -1.0 / 720.0, 1.0 / 24.0, -0.5, 1.0):
        cosine = cosine * y + np.float32(term)
    return sign * cosine, sign * (sine * x)


def extend(source, row, total, ext, slot):
    levels, fields, _, lon = source.shape
    blocks = lon // LANES
    for level in range(levels):
        for field in range(fields):
            place = level * fields + field
            line = source[level, field].astype(jnp.float32)
            for block in range(blocks):
                ext[slot, block + 1, place : place + 1, :] = line[
                    row : row + 1, block * LANES : (block + 1) * LANES
                ]
    lane = lax.broadcasted_iota(jnp.int32, (SUB, LANES), 1)
    missing = lon - total
    ahead = lane + missing
    behind = lane - missing
    first = lane_gather(ext[slot, 1], ahead & (LANES - 1))
    second = lane_gather(ext[slot, 2], ahead & (LANES - 1))
    last = ext[slot, blocks]
    final = lane_gather(last, behind & (LANES - 1))
    before = lane_gather(ext[slot, blocks - 1], behind & (LANES - 1))
    ext[slot, 0] = jnp.where(behind >= 0, final, before)
    ext[slot, blocks] = jnp.where(ahead < LANES, last, first)
    ext[slot, blocks + 1] = jnp.where(ahead < LANES, first, second)


def spread_rows(starts, begins):
    for latitude in range(starts.shape[0]):
        for row in range(STENCIL):
            begins[latitude, row] = starts[latitude, row : row + 1, :]


def gathered(block, latitude, picks, ext, starts, weights):
    offset = pl.multiple_of(block * LANES, LANES)
    total = jnp.zeros((SUB, LANES), jnp.float32)
    for row, slot in picks:
        start = starts[latitude, row, :, pl.ds(offset, LANES)] - (offset - LANES)
        start = jnp.broadcast_to(start, (SUB, LANES))
        factors = weights[latitude, row, :, pl.ds(offset, LANES)].astype(jnp.float32)
        parts = [ext[slot, block + piece] for piece in range(3)]
        for column in range(4):
            place = start + column
            lane = place & (LANES - 1)
            low, middle, high = [lane_gather(part, lane) for part in parts]
            value = jnp.where(place < LANES, low, jnp.where(place < 2 * LANES, middle, high))
            total = total + factors[column : column + 1] * value
    return total


def near_kernel(
    pair_total, pair_count, rows_first, points, fields, starts, weights,
    partial, table, twiddle, ext, fine, begins,
):
    lat_count = starts.shape[0]
    spread_rows(starts, begins)
    blocks = partial.shape[1]
    columns = table.shape[2] // 2
    first_lat = lax.axis_index("lat") * lat_count
    for latitude in range(lat_count):
        extend(fields, latitude, points[first_lat + latitude], ext, latitude)
    for latitude in range(lat_count):
        mine = first_lat - rows_first[latitude]
        picks = [(mine + row, row) for row in range(lat_count)]

        def one(block, carry, latitude=latitude, picks=picks):
            partial[latitude, block] = gathered(block, latitude, picks, ext, begins, weights)
            return carry

        lax.fori_loop(0, blocks, one, 0, unroll=11)
    for latitude in range(lat_count):
        total = jnp.full((1, 1), points[first_lat + latitude], jnp.int32).astype(jnp.float32)
        inverse = 1.0 / total
        scaling = jnp.sqrt(2.0 * inverse)
        width = min(columns, 512)

        def chunk(index, carry, latitude=latitude, total=total, inverse=inverse, scaling=scaling):
            at = pl.multiple_of(index * width, width)
            numbers = wavenumbers_at(at, width, pair_count, pair_total)
            step = lax.broadcasted_iota(jnp.int32, (blocks, width), 0).astype(jnp.float32)
            cosine, sine = turn_parts(numbers * step * float(LANES), total, inverse)
            twiddle[latitude, :, pl.ds(at, width)] = scaling * cosine
            twiddle[latitude, :, pl.ds(columns + at, width)] = scaling * sine
            step = lax.broadcasted_iota(jnp.int32, (16, width), 0).astype(jnp.float32)
            low_cos, low_sin = turn_parts(numbers * step, total, inverse)
            step = lax.broadcasted_iota(jnp.int32, (SUB, width), 0).astype(jnp.float32)
            high_cos, high_sin = turn_parts(numbers * step * 16.0, total, inverse)
            fine[0] = high_cos
            fine[1] = high_sin
            for high in range(SUB):
                this_cos = fine[0, high : high + 1, :]
                this_sin = fine[1, high : high + 1, :]
                rows = pl.ds(16 * high, 16)
                table[latitude, rows, pl.ds(at, width)] = (
                    this_cos * low_cos - this_sin * low_sin
                ).astype(jnp.bfloat16)
                table[latitude, rows, pl.ds(columns + at, width)] = (
                    this_cos * low_sin + this_sin * low_cos
                ).astype(jnp.bfloat16)
            return carry

        lax.fori_loop(0, columns // width, chunk, 0)


def wavenumbers_at(at, width, pair_count, pair_total):
    column = lax.broadcasted_iota(jnp.int32, (1, width), 1) + at
    lane = column & (LANES - 1)
    second = lane >= HALF
    inner = jnp.where(second, lane - HALF, lane)
    pair = (column >> 7) * pair_count + inner
    number = jnp.where(second, 2 * pair_total - 1 - pair, pair)
    return jnp.where(inner < pair_count, number, 0).astype(jnp.float32)


def far_kernel(
    rows_first, points, below, above, starts, weights, partial, table, twiddle,
    out, ext, grid, begins,
):
    lat_count = starts.shape[0]
    spread_rows(starts, begins)
    blocks = partial.shape[1]
    columns = table.shape[2] // 2
    first_lat = lax.axis_index("lat") * lat_count
    lat_total = points.shape[0]
    for row in range(lat_count):
        under = jnp.maximum(first_lat - lat_count + row, 0)
        over = jnp.minimum(first_lat + lat_count + row, lat_total - 1)
        extend(below, row, points[under], ext, row)
        extend(above, row, points[over], ext, lat_count + row)
    lane = lax.broadcasted_iota(jnp.int32, (SUB, LANES), 1)
    for latitude in range(lat_count):
        mine = first_lat - rows_first[latitude]
        one_row = jnp.where(mine >= 1, 0, 2)
        two_row = jnp.where(mine <= 1, 3, 1)
        picks = []
        for row in (one_row, two_row):
            picks.append((row, jnp.where(row < mine, row - mine + 2, row - mine)))

        def one(block, carry, latitude=latitude, picks=picks):
            value = partial[latitude, block] + gathered(
                block, latitude, picks, ext, begins, weights
            )
            live = lane + block * LANES < points[first_lat + latitude]
            grid[block] = jnp.where(live, value, 0.0)
            return carry

        lax.fori_loop(0, blocks, one, 0, unroll=11)
        rows = grid[...].reshape(blocks * SUB, LANES).astype(jnp.bfloat16)
        width = 2 * LANES

        def chunk(index, carry, latitude=latitude, rows=rows):
            at = pl.multiple_of(index * width, width)
            real = jnp.dot(
                rows, table[latitude, :, pl.ds(at, width)], preferred_element_type=jnp.float32
            ).reshape(blocks, SUB, width)
            imag = jnp.dot(
                rows,
                table[latitude, :, pl.ds(columns + at, width)],
                preferred_element_type=jnp.float32,
            ).reshape(blocks, SUB, width)
            cosine = jnp.zeros((SUB, width), jnp.float32)
            sine = jnp.zeros((SUB, width), jnp.float32)
            for block in range(blocks):
                turn_cos = twiddle[latitude, block : block + 1, pl.ds(at, width)]
                turn_sin = twiddle[latitude, block : block + 1, pl.ds(columns + at, width)]
                cosine = cosine + (real[block] * turn_cos - imag[block] * turn_sin)
                sine = sine - (real[block] * turn_sin + imag[block] * turn_cos)
            both = jnp.concatenate([cosine, sine], axis=0).astype(jnp.bfloat16)
            for piece in range(width // LANES):
                out[index * (width // LANES) + piece, 2 * SUB * latitude : 2 * SUB * (latitude + 1), :] = (
                    both[:, piece * LANES : (piece + 1) * LANES]
                )
            return carry

        lax.fori_loop(0, columns // width, chunk, 0)


def legendre_kernel(
    level_count, field_count, thickness, received, totals, legendre, out, wide, left,
):
    owners, packed_rows, _ = received.shape
    lat_total = wide.shape[0] // (2 * SUB)
    pair_count = legendre.shape[0]
    tile = legendre.shape[2]
    groups = [(at, min(SUB, pair_count - at)) for at in range(0, pair_count, SUB)]
    out_rows = level_count * (field_count + 1) * 2
    step = pl.program_id(0)

    @pl.when(step == 0)
    def build():
        wide[...] = received[...].astype(jnp.float32).reshape(wide.shape)
        level_place = lax.axis_index("lev")
        lines = {}
        for part in range(2):
            running = jnp.zeros((lat_total, LANES), jnp.float32)
            for other in range(1, totals.shape[0]):
                running = running + jnp.where(other > level_place, totals[other, part], 0.0)
            for level in reversed(range(level_count)):
                for field in range(field_count):
                    place = part * SUB + level * field_count + field
                    lines[level, field, part] = wide[pl.ds(place, lat_total, stride=2 * SUB), :]
                running = running + thickness[level] * (
                    lines[level, 2, part] + 0.61 * lines[level, 3, part]
                )
                lines[level, field_count, part] = running
        depth = SUB * lat_total
        spread = (
            lax.broadcasted_iota(jnp.int32, (lat_total, depth), 0)
            == lax.broadcasted_iota(jnp.int32, (lat_total, depth), 1) % lat_total
        ).astype(jnp.bfloat16)
        keep = (
            lax.broadcasted_iota(jnp.int32, (SUB, depth), 0)
            == lax.broadcasted_iota(jnp.int32, (SUB, depth), 1) // lat_total
        )
        order = [
            (level, field, part)
            for level in range(level_count)
            for field in range(field_count + 1)
            for part in range(2)
        ]
        for place in range(0, out_rows, 2):
            couple = [
                lax.dot_general(
                    lines[key].astype(jnp.bfloat16),
                    spread,
                    (((0,), (0,)), ((), ())),
                    preferred_element_type=jnp.float32,
                )
                for key in order[place : place + 2]
            ]
            for member in range(2):
                for group, (at, _) in enumerate(groups):
                    begin = member * HALF + at
                    pieces = [jnp.where(keep, one[begin : begin + SUB], 0.0) for one in couple]
                    into = (member * out_rows + place) * SUB
                    left[group, into : into + 2 * SUB, :] = jnp.concatenate(
                        pieces, axis=0
                    ).astype(jnp.bfloat16)

    first_pair = lax.axis_index("lat") * pair_count
    pair_total = pair_count * owners
    parts = []
    for group, (at, size) in enumerate(groups):
        depth = size * lat_total
        values = legendre[at : at + size].reshape(depth, tile)
        sums = jnp.dot(left[group, :, :depth], values, preferred_element_type=jnp.float32)
        sums = sums.reshape(2, out_rows, SUB, tile)
        slot = lax.broadcasted_iota(jnp.int32, (SUB, tile), 1) + step * tile
        pair = lax.broadcasted_iota(jnp.int32, (SUB, tile), 0) + (first_pair + at)
        first = slot + pair < 2 * pair_total
        chosen = jnp.where(first, sums[0], sums[1])
        parts.append(chosen[:, :size])
    out[...] = jnp.concatenate(parts, axis=1).astype(jnp.bfloat16).reshape(out.shape)


def local(fields, rows_first, points, starts, weights, thickness, legendre):
    level_count, field_count, lat_count, lon_count = fields.shape
    pair_count, lat_total, degrees = legendre.shape
    owners = lax.axis_size("lat")
    level_owners = lax.axis_size("lev")
    blocks = lon_count // LANES
    columns = owners * LANES
    up = [(i, i + 1) for i in range(owners - 1)]
    below = lax.ppermute(fields, "lat", up)
    above = lax.ppermute(fields, "lat", [(j, i) for i, j in up])

    scalar = pl.BlockSpec(memory_space=pltpu.SMEM)
    vector = pl.BlockSpec(memory_space=pltpu.VMEM)
    params = pltpu.CompilerParams(vmem_limit_bytes=LIMIT)
    partial, table, twiddle = pl.pallas_call(
        functools.partial(near_kernel, pair_count * owners, pair_count),
        out_shape=(
            jax.ShapeDtypeStruct((lat_count, blocks, SUB, LANES), jnp.float32),
            jax.ShapeDtypeStruct((lat_count, LANES, 2 * columns), jnp.bfloat16),
            jax.ShapeDtypeStruct((lat_count, blocks, 2 * columns), jnp.float32),
        ),
        in_specs=[scalar, scalar, vector, vector, vector],
        out_specs=(vector, vector, vector),
        scratch_shapes=[
            pltpu.VMEM((lat_count, blocks + 2, SUB, LANES), jnp.float32),
            pltpu.VMEM((2, SUB, min(columns, 512)), jnp.float32),
            pltpu.VMEM((lat_count, STENCIL, 1, lon_count), jnp.int32),
        ],
        compiler_params=params,
        cost_estimate=pl.CostEstimate(flops=10_000_000, bytes_accessed=4_000_000, transcendentals=0),
        name="near_rows",
    )(rows_first, points, fields, starts, weights)

    coefficients = pl.pallas_call(
        far_kernel,
        out_shape=jax.ShapeDtypeStruct((owners, 2 * SUB * lat_count, LANES), jnp.bfloat16),
        in_specs=[scalar, scalar] + [vector] * 7,
        out_specs=vector,
        scratch_shapes=[
            pltpu.VMEM((2 * lat_count, blocks + 2, SUB, LANES), jnp.float32),
            pltpu.VMEM((blocks, SUB, LANES), jnp.float32),
            pltpu.VMEM((lat_count, STENCIL, 1, lon_count), jnp.int32),
        ],
        compiler_params=params,
        name="far_rows",
    )(rows_first, points, below, above, starts, weights, partial, table, twiddle)

    received = lax.all_to_all(coefficients, "lat", split_axis=0, concat_axis=0, tiled=True)
    by_level = received.reshape(lat_total, 2, level_count, field_count, LANES).astype(jnp.float32)
    virtual = by_level[:, :, :, 2] + 0.61 * by_level[:, :, :, 3]
    total = jnp.sum(thickness[None, None, :, None] * virtual, axis=2).transpose(1, 0, 2)
    totals = lax.all_gather(total, "lev")

    tile = 256
    out_rows = level_count * (field_count + 1) * 2
    steps = (degrees + tile - 1) // tile
    group_count = (pair_count + SUB - 1) // SUB
    return pl.pallas_call(
        functools.partial(legendre_kernel, level_count, field_count),
        grid=(steps,),
        out_shape=jax.ShapeDtypeStruct(
            (level_count, field_count + 1, 2, pair_count, degrees), jnp.bfloat16
        ),
        in_specs=[
            scalar,
            pl.BlockSpec(received.shape, lambda i: (0, 0, 0)),
            pl.BlockSpec(totals.shape, lambda i: (0, 0, 0, 0)),
            pl.BlockSpec((pair_count, lat_total, tile), lambda i: (0, 0, i)),
        ],
        out_specs=pl.BlockSpec(
            (level_count, field_count + 1, 2, pair_count, tile), lambda i: (0, 0, 0, 0, i)
        ),
        scratch_shapes=[
            pltpu.VMEM((lat_total * 2 * SUB, LANES), jnp.float32),
            pltpu.VMEM((group_count, 2 * out_rows * SUB, SUB * lat_total), jnp.bfloat16),
        ],
        compiler_params=params,
        name="degree_sums",
    )(thickness, received, totals, legendre)


def solution(mesh):
    placed = (
        P("lev", None, "lat", None),
        P("lat"),
        P(),
        P("lat", None, None),
        P("lat", None, None, None),
        P("lev"),
        P("lat", None, None),
    )
    return jax.shard_map(
        local,
        mesh=mesh,
        in_specs=placed,
        out_specs=P("lev", None, None, "lat", None),
        check_vma=False,
    )
```

```python
import functools

import jax
import jax.numpy as jnp
import numpy as np
from jax import lax
from jax.experimental import pallas as pl
from jax.experimental.pallas import tpu as pltpu
from jax.sharding import PartitionSpec as P

LANES = 128
SUB = 8
STENCIL = 4
LIMIT = 24 * 1024 * 1024


def lane_gather(values, lanes):
    return jnp.take_along_axis(values, lanes, axis=1, mode="promise_in_bounds")


def turn_parts(product, total, inverse):
    turns = (product - jnp.floor(product * inverse + 0.5) * total) * inverse
    halves = jnp.floor(2.0 * turns + 0.5)
    sign = 1.0 - 2.0 * jnp.abs(halves)
    x = (turns - 0.5 * halves) * np.float32(2.0 * np.pi)
    y = x * x
    sine = -1.0 / 39916800.0
    for term in (1.0 / 362880.0, -1.0 / 5040.0, 1.0 / 120.0, -1.0 / 6.0, 1.0):
        sine = sine * y + np.float32(term)
    cosine = 1.0 / 479001600.0
    for term in (-1.0 / 3628800.0, 1.0 / 40320.0, -1.0 / 720.0, 1.0 / 24.0, -0.5, 1.0):
        cosine = cosine * y + np.float32(term)
    return sign * cosine, sign * (sine * x)


def wavenumbers(at, width, pair_count, pair_total):
    column = lax.broadcasted_iota(jnp.int32, (1, width), 1) + at
    owner = column // (2 * pair_count)
    inner = column - owner * (2 * pair_count)
    second = inner >= pair_count
    pair = owner * pair_count + jnp.where(second, inner - pair_count, inner)
    return jnp.where(second, 2 * pair_total - 1 - pair, pair).astype(jnp.float32)


def extend(lines, row, rows_each, missing, ext, slot):
    blocks = ext.shape[1] - 2
    for block in range(blocks):
        ext[slot, block + 1] = lines[
            pl.ds(block * rows_each + row, SUB, stride=blocks * rows_each), :
        ]
    lane = lax.broadcasted_iota(jnp.int32, (SUB, LANES), 1)
    ahead = lane + missing
    behind = lane - missing
    first = lane_gather(ext[slot, 1], ahead & (LANES - 1))
    second = lane_gather(ext[slot, 2], ahead & (LANES - 1))
    last = ext[slot, blocks]
    final = lane_gather(last, behind & (LANES - 1))
    before = lane_gather(ext[slot, blocks - 1], behind & (LANES - 1))
    ext[slot, 0] = jnp.where(behind >= 0, final, before)
    ext[slot, blocks] = jnp.where(ahead < LANES, last, first)
    ext[slot, blocks + 1] = jnp.where(ahead < LANES, first, second)


def spread_rows(starts, begins):
    lat_count, _, blocks = begins.shape[:3]
    for latitude in range(lat_count):
        for block in range(blocks):
            for row in range(STENCIL):
                lanes = slice(block * LANES, (block + 1) * LANES)
                begins[latitude, row, block] = (
                    starts[latitude, row : row + 1, lanes] - (block - 1) * LANES
                )


def spread_lines(source, lines):
    first, second, rows, lon = source.shape
    at = 0
    for one in range(first):
        for two in range(second):
            values = source[one, two].astype(jnp.float32)
            for block in range(lon // LANES):
                lines[at : at + rows, :] = values[:, block * LANES : (block + 1) * LANES]
                at += rows


def gathered(couple, latitude, picks, ext, begins, factors):
    totals = [jnp.zeros((SUB, LANES), jnp.float32) for _ in range(2)]
    couples = begins.shape[2] // 2
    for row, slot in picks:
        at = ((latitude * STENCIL + row) * couples + couple) * SUB
        scale = factors[pl.ds(pl.multiple_of(at, SUB), SUB), :]
        parts = [ext[slot, 2 * couple + piece] for piece in range(4)]
        for side in range(2):
            start = jnp.broadcast_to(begins[latitude, row, 2 * couple + side], (SUB, LANES))
            for column in range(4):
                place = start + column
                lane = place & (LANES - 1)
                low, middle, high = [
                    lane_gather(part, lane) for part in parts[side : side + 3]
                ]
                value = jnp.where(place < LANES, low, jnp.where(place < 2 * LANES, middle, high))
                line = STENCIL * side + column
                totals[side] = totals[side] + scale[line : line + 1] * value
    return totals


def near_kernel(
    pair_total, pair_count, rows_first, points, fields, starts, weights,
    partial, table, twiddle, lines, ext, fine, begins, factors,
):
    lat_count, couples = partial.shape[:2]
    lon = 2 * couples * LANES
    columns = table.shape[2] // 2
    first_lat = lax.axis_index("lat") * lat_count
    spread_rows(starts, begins)
    spread_lines(weights, factors)
    spread_lines(fields, lines)
    for latitude in range(lat_count):
        extend(lines, latitude, lat_count, lon - points[first_lat + latitude], ext, latitude)
    for latitude in range(lat_count):
        mine = first_lat - rows_first[latitude]
        picks = [(mine + row, row) for row in range(lat_count)]
        for couple in range(couples):
            totals = gathered(couple, latitude, picks, ext, begins, factors)
            for side in range(2):
                partial[latitude, couple, :, side * LANES : (side + 1) * LANES] = totals[side]
    width = 256
    for latitude in range(lat_count):
        total = jnp.full((1, 1), points[first_lat + latitude], jnp.int32).astype(jnp.float32)
        inverse = 1.0 / total
        scaling = jnp.sqrt(2.0 * inverse)

        def chunk(index, carry, latitude=latitude, total=total, inverse=inverse, scaling=scaling):
            at = pl.multiple_of(index * width, width)
            numbers = wavenumbers(at, width, pair_count, pair_total)
            step = lax.broadcasted_iota(jnp.int32, (couples, width), 0).astype(jnp.float32)
            cosine, sine = turn_parts(numbers * step * float(2 * LANES), total, inverse)
            twiddle[latitude, :, pl.ds(at, width)] = scaling * cosine
            twiddle[latitude, :, pl.ds(columns + at, width)] = scaling * sine
            step = lax.broadcasted_iota(jnp.int32, (16, width), 0).astype(jnp.float32)
            low_cos, low_sin = turn_parts(numbers * step, total, inverse)
            high_cos, high_sin = turn_parts(numbers * step * 16.0, total, inverse)
            fine[0] = high_cos
            fine[1] = high_sin
            for high in range(16):
                this_cos = fine[0, high : high + 1, :]
                this_sin = fine[1, high : high + 1, :]
                rows = pl.ds(16 * high, 16)
                table[latitude, rows, pl.ds(at, width)] = (
                    this_cos * low_cos - this_sin * low_sin
                ).astype(jnp.bfloat16)
                table[latitude, rows, pl.ds(columns + at, width)] = (
                    this_cos * low_sin + this_sin * low_cos
                ).astype(jnp.bfloat16)
            return carry

        lax.fori_loop(0, columns // width, chunk, 0)


def far_kernel(
    rows_first, points, below, above, starts, weights, partial, table, twiddle,
    out, lines, ext, grid, begins, factors, waves,
):
    lat_count, couples = partial.shape[:2]
    lon = 2 * couples * LANES
    columns = table.shape[2] // 2
    owners = out.shape[0]
    first_lat = lax.axis_index("lat") * lat_count
    lat_total = points.shape[0]
    spread_rows(starts, begins)
    spread_lines(weights, factors)
    for side, source in enumerate((below, above)):
        spread_lines(source, lines.at[side])
        for row in range(lat_count):
            if side == 0:
                place = jnp.maximum(first_lat - lat_count + row, 0)
            else:
                place = jnp.minimum(first_lat + lat_count + row, lat_total - 1)
            extend(
                lines.at[side], row, lat_count, lon - points[place], ext, side * lat_count + row
            )
    lane = lax.broadcasted_iota(jnp.int32, (SUB, LANES), 1)
    width = 256
    for latitude in range(lat_count):
        mine = first_lat - rows_first[latitude]
        one_row = jnp.where(mine >= 1, 0, 2)
        two_row = jnp.where(mine <= 1, 3, 1)
        picks = []
        for row in (one_row, two_row):
            picks.append((row, jnp.where(row < mine, row - mine + lat_count, row - mine)))
        for couple in range(couples):
            totals = gathered(couple, latitude, picks, ext, begins, factors)
            for side in range(2):
                lanes = pl.ds(side * LANES, LANES)
                live = lane + (2 * couple + side) * LANES < points[first_lat + latitude]
                value = partial[latitude, couple, :, lanes] + totals[side]
                grid[couple, :, lanes] = jnp.where(live, value, 0.0)
        rows = grid[...].reshape(couples * SUB, 2 * LANES).astype(jnp.bfloat16)
        for at in range(0, columns, width):
            real = jnp.dot(
                rows, table[latitude, :, at : at + width], preferred_element_type=jnp.float32
            )
            imag = jnp.dot(
                rows,
                table[latitude, :, columns + at : columns + at + width],
                preferred_element_type=jnp.float32,
            )
            cosine = jnp.zeros((SUB, width), jnp.float32)
            sine = jnp.zeros((SUB, width), jnp.float32)
            for couple in range(couples):
                turn_cos = twiddle[latitude, couple : couple + 1, at : at + width]
                turn_sin = twiddle[latitude, couple : couple + 1, columns + at : columns + at + width]
                here = slice(couple * SUB, (couple + 1) * SUB)
                cosine = cosine + (real[here] * turn_cos - imag[here] * turn_sin)
                sine = sine - (real[here] * turn_sin + imag[here] * turn_cos)
            waves[0:SUB, at : at + width] = cosine
            waves[SUB : 2 * SUB, at : at + width] = sine
        waves[:, columns:] = jnp.zeros((2 * SUB, waves.shape[1] - columns), jnp.float32)
        used = columns // owners
        for owner in range(owners):
            out[owner, 2 * SUB * latitude : 2 * SUB * (latitude + 1), :] = waves[
                :, owner * used : owner * used + LANES
            ].astype(jnp.bfloat16)


def legendre_kernel(
    level_count, field_count, thickness, received, totals, legendre, out, wide, left, planes, sent,
):
    owners = received.shape[0]
    lat_total = wide.shape[0] // (2 * SUB)
    pair_count, _, degrees = legendre.shape
    pair_total = pair_count * owners
    groups = [(at, min(SUB, pair_count - at)) for at in range(0, pair_count, SUB)]
    keys = [(field, part) for field in range(field_count + 1) for part in range(2)]
    half = len(keys) * SUB
    level_place = lax.axis_index("lev")
    first_pair = lax.axis_index("lat") * pair_count
    wide[...] = received[...].astype(jnp.float32).reshape(wide.shape)
    lines = {}
    for part in range(2):
        running = jnp.zeros((lat_total, LANES), jnp.float32)
        for other in range(1, totals.shape[0]):
            running = running + jnp.where(other > level_place, totals[other, part], 0.0)
        for level in reversed(range(level_count)):
            for field in range(field_count):
                place = part * SUB + level * field_count + field
                lines[level, field, part] = wide[pl.ds(place, lat_total, stride=2 * SUB), :]
            running = running + thickness[level] * (
                lines[level, 2, part] + 0.61 * lines[level, 3, part]
            )
            lines[level, field_count, part] = running
    depth = SUB * lat_total
    spread = (
        lax.broadcasted_iota(jnp.int32, (lat_total, depth), 0)
        == lax.broadcasted_iota(jnp.int32, (lat_total, depth), 1) % lat_total
    ).astype(jnp.bfloat16)
    keep = (
        lax.broadcasted_iota(jnp.int32, (SUB, depth), 0)
        == lax.broadcasted_iota(jnp.int32, (SUB, depth), 1) // lat_total
    )
    copies = []
    for level in range(level_count):
        for place in range(0, len(keys), 2):
            couple = [
                lax.dot_general(
                    lines[(level,) + key].astype(jnp.bfloat16),
                    spread,
                    (((0,), (0,)), ((), ())),
                    preferred_element_type=jnp.float32,
                )
                for key in keys[place : place + 2]
            ]
            for member in range(2):
                for group, (at, _) in enumerate(groups):
                    begin = member * pair_count + at
                    pieces = [jnp.where(keep, one[begin : begin + SUB], 0.0) for one in couple]
                    into = member * half + place * SUB
                    left[level, group, into : into + 2 * SUB, :] = jnp.concatenate(
                        pieces, axis=0
                    ).astype(jnp.bfloat16)
        for start in range(0, degrees, 256):
            stop = min(start + 256, degrees)
            low = 0 if start < 2 * pair_total else half
            high = 2 * half if stop > pair_total + 1 else half
            parts = []
            for group, (at, size) in enumerate(groups):
                values = legendre[at : at + size, :, start:stop].reshape(
                    size * lat_total, stop - start
                )
                sums = jnp.dot(
                    left[level, group, low:high, : size * lat_total],
                    values,
                    preferred_element_type=jnp.float32,
                ).reshape((high - low) // SUB, SUB, stop - start)
                if high - low > half:
                    shape = (SUB, stop - start)
                    slot = lax.broadcasted_iota(jnp.int32, shape, 1) + start
                    pair = lax.broadcasted_iota(jnp.int32, shape, 0) + (first_pair + at)
                    sums = jnp.where(
                        slot + pair < 2 * pair_total, sums[: len(keys)], sums[len(keys) :]
                    )
                parts.append(sums[:, :size])
            planes[level, :, :, :, start:stop] = (
                jnp.concatenate(parts, axis=1)
                .astype(jnp.bfloat16)
                .reshape(field_count + 1, 2, pair_count, stop - start)
            )
        copies.append(pltpu.make_async_copy(planes.at[level], out.at[level], sent.at[level]))
        copies[-1].start()
    for copy in copies:
        copy.wait()


def local(fields, rows_first, points, starts, weights, thickness, legendre):
    level_count, field_count, lat_count, lon_count = fields.shape
    pair_count, lat_total, degrees = legendre.shape
    owners = lax.axis_size("lat")
    couples = lon_count // (2 * LANES)
    blocks = 2 * couples
    columns = 2 * owners * pair_count
    up = [(i, i + 1) for i in range(owners - 1)]
    below = lax.ppermute(fields, "lat", up)
    above = lax.ppermute(fields, "lat", [(j, i) for i, j in up])

    scalar = pl.BlockSpec(memory_space=pltpu.SMEM)
    vector = pl.BlockSpec(memory_space=pltpu.VMEM)
    params = pltpu.CompilerParams(vmem_limit_bytes=LIMIT)
    shared = [
        pltpu.VMEM((lat_count, STENCIL, blocks, 1, LANES), jnp.int32),
        pltpu.VMEM((weights.size // LANES, LANES), jnp.float32),
    ]
    partial, table, twiddle = pl.pallas_call(
        functools.partial(near_kernel, pair_count * owners, pair_count),
        out_shape=(
            jax.ShapeDtypeStruct((lat_count, couples, SUB, 2 * LANES), jnp.float32),
            jax.ShapeDtypeStruct((lat_count, 2 * LANES, 2 * columns), jnp.bfloat16),
            jax.ShapeDtypeStruct((lat_count, couples, 2 * columns), jnp.float32),
        ),
        in_specs=[scalar, scalar, vector, vector, vector],
        out_specs=(vector, vector, vector),
        scratch_shapes=[
            pltpu.VMEM((fields.size // LANES, LANES), jnp.float32),
            pltpu.VMEM((lat_count, blocks + 2, SUB, LANES), jnp.float32),
            pltpu.VMEM((2, 16, 256), jnp.float32),
        ]
        + shared,
        compiler_params=params,
        cost_estimate=pl.CostEstimate(flops=10_000_000, bytes_accessed=4_000_000, transcendentals=0),
        name="near_rows",
    )(rows_first, points, fields, starts, weights)

    coefficients = pl.pallas_call(
        far_kernel,
        out_shape=jax.ShapeDtypeStruct((owners, 2 * SUB * lat_count, LANES), jnp.bfloat16),
        in_specs=[scalar, scalar] + [vector] * 7,
        out_specs=vector,
        scratch_shapes=[
            pltpu.VMEM((2, fields.size // LANES, LANES), jnp.float32),
            pltpu.VMEM((2 * lat_count, blocks + 2, SUB, LANES), jnp.float32),
            pltpu.VMEM((couples, SUB, 2 * LANES), jnp.float32),
        ]
        + shared
        + [pltpu.VMEM((2 * SUB, columns + LANES), jnp.float32)],
        compiler_params=params,
        name="far_rows",
    )(rows_first, points, below, above, starts, weights, partial, table, twiddle)

    received = lax.all_to_all(coefficients, "lat", split_axis=0, concat_axis=0, tiled=True)
    by_level = received.reshape(lat_total, 2, level_count, field_count, LANES).astype(jnp.float32)
    virtual = by_level[:, :, :, 2] + 0.61 * by_level[:, :, :, 3]
    total = jnp.sum(thickness[None, None, :, None] * virtual, axis=2).transpose(1, 0, 2)
    totals = lax.all_gather(total, "lev")

    out_shape = (level_count, field_count + 1, 2, pair_count, degrees)
    half = (field_count + 1) * 2 * SUB
    group_count = (pair_count + SUB - 1) // SUB
    return pl.pallas_call(
        functools.partial(legendre_kernel, level_count, field_count),
        out_shape=jax.ShapeDtypeStruct(out_shape, jnp.bfloat16),
        in_specs=[scalar, vector, vector, vector],
        out_specs=pl.BlockSpec(memory_space=pl.ANY),
        scratch_shapes=[
            pltpu.VMEM((lat_total * 2 * SUB, LANES), jnp.float32),
            pltpu.VMEM((level_count, group_count, 2 * half, SUB * lat_total), jnp.bfloat16),
            pltpu.VMEM(out_shape, jnp.bfloat16),
            pltpu.SemaphoreType.DMA((level_count,)),
        ],
        compiler_params=params,
        name="degree_sums",
    )(thickness, received, totals, legendre)


def solution(mesh):
    placed = (
        P("lev", None, "lat", None),
        P("lat"),
        P(),
        P("lat", None, None),
        P("lat", None, None, None),
        P("lev"),
        P("lat", None, None),
    )
    return jax.shard_map(
        local,
        mesh=mesh,
        in_specs=placed,
        out_specs=P("lev", None, None, "lat", None),
        check_vma=False,
    )
```

```python
import functools

import jax
import jax.numpy as jnp
import numpy as np
from jax import lax
from jax.experimental import pallas as pl
from jax.experimental.pallas import tpu as pltpu
from jax.sharding import PartitionSpec as P

LANES = 128
SUB = 8
STENCIL = 4
LIMIT = 24 * 1024 * 1024


def lane_gather(values, lanes):
    return jnp.take_along_axis(values, lanes, axis=1, mode="promise_in_bounds")


def turn_parts(product, total, inverse):
    turns = (product - jnp.floor(product * inverse + 0.5) * total) * inverse
    halves = jnp.floor(2.0 * turns + 0.5)
    sign = 1.0 - 2.0 * jnp.abs(halves)
    x = (turns - 0.5 * halves) * np.float32(2.0 * np.pi)
    y = x * x
    sine = -1.0 / 39916800.0
    for term in (1.0 / 362880.0, -1.0 / 5040.0, 1.0 / 120.0, -1.0 / 6.0, 1.0):
        sine = sine * y + np.float32(term)
    cosine = 1.0 / 479001600.0
    for term in (-1.0 / 3628800.0, 1.0 / 40320.0, -1.0 / 720.0, 1.0 / 24.0, -0.5, 1.0):
        cosine = cosine * y + np.float32(term)
    return sign * cosine, sign * (sine * x)


def wavenumbers(at, width, pair_count, pair_total):
    column = lax.broadcasted_iota(jnp.int32, (1, width), 1) + at
    owner = column // (2 * pair_count)
    inner = column - owner * (2 * pair_count)
    second = inner >= pair_count
    pair = owner * pair_count + jnp.where(second, inner - pair_count, inner)
    return jnp.where(second, 2 * pair_total - 1 - pair, pair).astype(jnp.float32)


def extend(lines, row, rows_each, missing, ext, slot):
    blocks = ext.shape[1] - 2
    for block in range(blocks):
        ext[slot, block + 1] = lines[
            pl.ds(block * rows_each + row, SUB, stride=blocks * rows_each), :
        ]
    lane = lax.broadcasted_iota(jnp.int32, (SUB, LANES), 1)
    ahead = lane + missing
    behind = lane - missing
    first = lane_gather(ext[slot, 1], ahead & (LANES - 1))
    second = lane_gather(ext[slot, 2], ahead & (LANES - 1))
    last = ext[slot, blocks]
    final = lane_gather(last, behind & (LANES - 1))
    before = lane_gather(ext[slot, blocks - 1], behind & (LANES - 1))
    ext[slot, 0] = jnp.where(behind >= 0, final, before)
    ext[slot, blocks] = jnp.where(ahead < LANES, last, first)
    ext[slot, blocks + 1] = jnp.where(ahead < LANES, first, second)


def spread_rows(starts, begins):
    lat_count, _, blocks = begins.shape[:3]
    for latitude in range(lat_count):
        for block in range(blocks):
            for row in range(STENCIL):
                lanes = slice(block * LANES, (block + 1) * LANES)
                begins[latitude, row, block] = (
                    starts[latitude, row : row + 1, lanes] - (block - 1) * LANES
                )


def spread_lines(source, lines):
    first, second, rows, lon = source.shape
    at = 0
    for one in range(first):
        for two in range(second):
            values = source[one, two].astype(jnp.float32)
            for block in range(lon // LANES):
                lines[at : at + rows, :] = values[:, block * LANES : (block + 1) * LANES]
                at += rows


def gathered(couple, latitude, picks, ext, begins, factors):
    totals = [jnp.zeros((SUB, LANES), jnp.float32) for _ in range(2)]
    couples = begins.shape[2] // 2
    for row, slot in picks:
        at = ((latitude * STENCIL + row) * couples + couple) * SUB
        scale = factors[pl.ds(pl.multiple_of(at, SUB), SUB), :]
        parts = [ext[slot, 2 * couple + piece] for piece in range(4)]
        for side in range(2):
            start = jnp.broadcast_to(begins[latitude, row, 2 * couple + side], (SUB, LANES))
            for column in range(4):
                place = start + column
                lane = place & (LANES - 1)
                low, middle, high = [
                    lane_gather(part, lane) for part in parts[side : side + 3]
                ]
                value = jnp.where(place < LANES, low, jnp.where(place < 2 * LANES, middle, high))
                line = STENCIL * side + column
                totals[side] = totals[side] + scale[line : line + 1] * value
    return totals


def near_kernel(
    pair_total, pair_count, rows_first_far, points_far, fields_far, starts_far, weights_far,
    partial, table, twiddle, begins, factors,
    rows_first, points, fields, starts, weights, lines, ext, fine, arrived,
):
    lat_count, couples = partial.shape[:2]
    lon = 2 * couples * LANES
    columns = table.shape[2] // 2
    first_lat = lax.axis_index("lat") * lat_count
    fetches = [
        pltpu.make_async_copy(source, target, arrived.at[place])
        for place, (source, target) in enumerate(
            (
                (points_far, points),
                (rows_first_far, rows_first),
                (starts_far, starts),
                (weights_far, weights),
                (fields_far, fields),
            )
        )
    ]
    for fetch in fetches:
        fetch.start()
    fetches[0].wait()
    width = 256
    for latitude in range(lat_count):
        total = jnp.full((1, 1), points[first_lat + latitude], jnp.int32).astype(jnp.float32)
        inverse = 1.0 / total
        scaling = jnp.sqrt(2.0 * inverse)

        def chunk(index, carry, latitude=latitude, total=total, inverse=inverse, scaling=scaling):
            at = pl.multiple_of(index * width, width)
            numbers = wavenumbers(at, width, pair_count, pair_total)
            step = lax.broadcasted_iota(jnp.int32, (couples, width), 0).astype(jnp.float32)
            cosine, sine = turn_parts(numbers * step * float(2 * LANES), total, inverse)
            twiddle[latitude, :, pl.ds(at, width)] = scaling * cosine
            twiddle[latitude, :, pl.ds(columns + at, width)] = scaling * sine
            step = lax.broadcasted_iota(jnp.int32, (16, width), 0).astype(jnp.float32)
            low_cos, low_sin = turn_parts(numbers * step, total, inverse)
            high_cos, high_sin = turn_parts(numbers * step * 16.0, total, inverse)
            fine[0] = high_cos
            fine[1] = high_sin
            for high in range(16):
                this_cos = fine[0, high : high + 1, :]
                this_sin = fine[1, high : high + 1, :]
                rows = pl.ds(16 * high, 16)
                table[latitude, rows, pl.ds(at, width)] = (
                    this_cos * low_cos - this_sin * low_sin
                ).astype(jnp.bfloat16)
                table[latitude, rows, pl.ds(columns + at, width)] = (
                    this_cos * low_sin + this_sin * low_cos
                ).astype(jnp.bfloat16)
            return carry

        lax.fori_loop(0, columns // width, chunk, 0)
    for fetch in fetches[1:]:
        fetch.wait()
    spread_rows(starts, begins)
    spread_lines(weights, factors)
    spread_lines(fields, lines)
    for latitude in range(lat_count):
        extend(lines, latitude, lat_count, lon - points[first_lat + latitude], ext, latitude)
    for latitude in range(lat_count):
        mine = first_lat - rows_first[latitude]
        picks = [(mine + row, row) for row in range(lat_count)]
        for couple in range(couples):
            totals = gathered(couple, latitude, picks, ext, begins, factors)
            for side in range(2):
                partial[latitude, couple, :, side * LANES : (side + 1) * LANES] = totals[side]


def far_kernel(
    rows_first_far, points_far, below, above, begins, factors, partial, table, twiddle,
    out, rows_first, points, lines, ext, grid, waves, arrived,
):
    fetches = [
        pltpu.make_async_copy(points_far, points, arrived.at[0]),
        pltpu.make_async_copy(rows_first_far, rows_first, arrived.at[1]),
    ]
    for fetch in fetches:
        fetch.start()
    lat_count, couples = partial.shape[:2]
    lon = 2 * couples * LANES
    columns = table.shape[2] // 2
    owners = out.shape[0]
    first_lat = lax.axis_index("lat") * lat_count
    lat_total = points.shape[0]
    for side, source in enumerate((below, above)):
        spread_lines(source, lines.at[side])
    for fetch in fetches:
        fetch.wait()
    for side in range(2):
        for row in range(lat_count):
            if side == 0:
                place = jnp.maximum(first_lat - lat_count + row, 0)
            else:
                place = jnp.minimum(first_lat + lat_count + row, lat_total - 1)
            extend(
                lines.at[side], row, lat_count, lon - points[place], ext, side * lat_count + row
            )
    lane = lax.broadcasted_iota(jnp.int32, (SUB, LANES), 1)
    width = 256
    for latitude in range(lat_count):
        mine = first_lat - rows_first[latitude]
        one_row = jnp.where(mine >= 1, 0, 2)
        two_row = jnp.where(mine <= 1, 3, 1)
        picks = []
        for row in (one_row, two_row):
            picks.append((row, jnp.where(row < mine, row - mine + lat_count, row - mine)))
        for couple in range(couples):
            totals = gathered(couple, latitude, picks, ext, begins, factors)
            for side in range(2):
                lanes = pl.ds(side * LANES, LANES)
                live = lane + (2 * couple + side) * LANES < points[first_lat + latitude]
                value = partial[latitude, couple, :, lanes] + totals[side]
                grid[couple, :, lanes] = jnp.where(live, value, 0.0)
        rows = grid[...].reshape(couples * SUB, 2 * LANES).astype(jnp.bfloat16)
        for at in range(0, columns, width):
            real = jnp.dot(
                rows, table[latitude, :, at : at + width], preferred_element_type=jnp.float32
            )
            imag = jnp.dot(
                rows,
                table[latitude, :, columns + at : columns + at + width],
                preferred_element_type=jnp.float32,
            )
            cosine = jnp.zeros((SUB, width), jnp.float32)
            sine = jnp.zeros((SUB, width), jnp.float32)
            for couple in range(couples):
                turn_cos = twiddle[latitude, couple : couple + 1, at : at + width]
                turn_sin = twiddle[latitude, couple : couple + 1, columns + at : columns + at + width]
                here = slice(couple * SUB, (couple + 1) * SUB)
                cosine = cosine + (real[here] * turn_cos - imag[here] * turn_sin)
                sine = sine - (real[here] * turn_sin + imag[here] * turn_cos)
            waves[0:SUB, at : at + width] = cosine
            waves[SUB : 2 * SUB, at : at + width] = sine
        waves[:, columns:] = jnp.zeros((2 * SUB, waves.shape[1] - columns), jnp.float32)
        used = columns // owners
        for owner in range(owners):
            out[owner, 2 * SUB * latitude : 2 * SUB * (latitude + 1), :] = waves[
                :, owner * used : owner * used + LANES
            ].astype(jnp.bfloat16)


def legendre_kernel(
    level_count, field_count, thickness, received, totals, legendre, out, wide, left, planes, sent,
):
    owners = received.shape[0]
    lat_total = wide.shape[0] // (2 * SUB)
    pair_count, _, degrees = legendre.shape
    pair_total = pair_count * owners
    groups = [(at, min(SUB, pair_count - at)) for at in range(0, pair_count, SUB)]
    keys = [(field, part) for field in range(field_count + 1) for part in range(2)]
    half = len(keys) * SUB
    level_place = lax.axis_index("lev")
    first_pair = lax.axis_index("lat") * pair_count
    wide[...] = received[...].astype(jnp.float32).reshape(wide.shape)
    lines = {}
    for part in range(2):
        running = jnp.zeros((lat_total, LANES), jnp.float32)
        for other in range(1, totals.shape[0]):
            running = running + jnp.where(other > level_place, totals[other, part], 0.0)
        for level in reversed(range(level_count)):
            for field in range(field_count):
                place = part * SUB + level * field_count + field
                lines[level, field, part] = wide[pl.ds(place, lat_total, stride=2 * SUB), :]
            running = running + thickness[level] * (
                lines[level, 2, part] + 0.61 * lines[level, 3, part]
            )
            lines[level, field_count, part] = running
    depth = SUB * lat_total
    spread = (
        lax.broadcasted_iota(jnp.int32, (lat_total, depth), 0)
        == lax.broadcasted_iota(jnp.int32, (lat_total, depth), 1) % lat_total
    ).astype(jnp.bfloat16)
    keep = (
        lax.broadcasted_iota(jnp.int32, (SUB, depth), 0)
        == lax.broadcasted_iota(jnp.int32, (SUB, depth), 1) // lat_total
    )
    copies = []
    for level in range(level_count):
        for place in range(0, len(keys), 2):
            couple = [
                lax.dot_general(
                    lines[(level,) + key].astype(jnp.bfloat16),
                    spread,
                    (((0,), (0,)), ((), ())),
                    preferred_element_type=jnp.float32,
                )
                for key in keys[place : place + 2]
            ]
            for member in range(2):
                for group, (at, _) in enumerate(groups):
                    begin = member * pair_count + at
                    pieces = [jnp.where(keep, one[begin : begin + SUB], 0.0) for one in couple]
                    into = member * half + place * SUB
                    left[level, group, into : into + 2 * SUB, :] = jnp.concatenate(
                        pieces, axis=0
                    ).astype(jnp.bfloat16)
        for start in range(0, degrees, 256):
            stop = min(start + 256, degrees)
            low = 0 if start < 2 * pair_total else half
            high = 2 * half if stop > pair_total + 1 else half
            parts = []
            for group, (at, size) in enumerate(groups):
                values = legendre[at : at + size, :, start:stop].reshape(
                    size * lat_total, stop - start
                )
                sums = jnp.dot(
                    left[level, group, low:high, : size * lat_total],
                    values,
                    preferred_element_type=jnp.float32,
                ).reshape((high - low) // SUB, SUB, stop - start)
                if high - low > half:
                    shape = (SUB, stop - start)
                    slot = lax.broadcasted_iota(jnp.int32, shape, 1) + start
                    pair = lax.broadcasted_iota(jnp.int32, shape, 0) + (first_pair + at)
                    sums = jnp.where(
                        slot + pair < 2 * pair_total, sums[: len(keys)], sums[len(keys) :]
                    )
                parts.append(sums[:, :size])
            planes[level, :, :, :, start:stop] = (
                jnp.concatenate(parts, axis=1)
                .astype(jnp.bfloat16)
                .reshape(field_count + 1, 2, pair_count, stop - start)
            )
        copies.append(pltpu.make_async_copy(planes.at[level], out.at[level], sent.at[level]))
        copies[-1].start()
    for copy in copies:
        copy.wait()


def held(value):
    return pltpu.with_memory_space_constraint(value, pltpu.HBM)


def local(fields, rows_first, points, starts, weights, thickness, legendre):
    level_count, field_count, lat_count, lon_count = fields.shape
    pair_count, lat_total, degrees = legendre.shape
    owners = lax.axis_size("lat")
    couples = lon_count // (2 * LANES)
    blocks = 2 * couples
    columns = 2 * owners * pair_count
    up = [(i, i + 1) for i in range(owners - 1)]
    below = lax.ppermute(fields, "lat", up)
    above = lax.ppermute(fields, "lat", [(j, i) for i, j in up])

    scalar = pl.BlockSpec(memory_space=pltpu.SMEM)
    vector = pl.BlockSpec(memory_space=pltpu.VMEM)
    params = pltpu.CompilerParams(vmem_limit_bytes=LIMIT)
    remote = pl.BlockSpec(memory_space=pltpu.HBM)
    scalars = [
        pltpu.SMEM(rows_first.shape, jnp.int32),
        pltpu.SMEM(points.shape, jnp.int32),
    ]
    partial, table, twiddle, begins, factors = pl.pallas_call(
        functools.partial(near_kernel, pair_count * owners, pair_count),
        out_shape=(
            jax.ShapeDtypeStruct((lat_count, couples, SUB, 2 * LANES), jnp.float32),
            jax.ShapeDtypeStruct((lat_count, 2 * LANES, 2 * columns), jnp.bfloat16),
            jax.ShapeDtypeStruct((lat_count, couples, 2 * columns), jnp.float32),
            jax.ShapeDtypeStruct((lat_count, STENCIL, blocks, 1, LANES), jnp.int32),
            jax.ShapeDtypeStruct((weights.size // LANES, LANES), jnp.float32),
        ),
        in_specs=[remote] * 5,
        out_specs=(vector,) * 5,
        scratch_shapes=scalars
        + [
            pltpu.VMEM(fields.shape, fields.dtype),
            pltpu.VMEM(starts.shape, starts.dtype),
            pltpu.VMEM(weights.shape, weights.dtype),
            pltpu.VMEM((fields.size // LANES, LANES), jnp.float32),
            pltpu.VMEM((lat_count, blocks + 2, SUB, LANES), jnp.float32),
            pltpu.VMEM((2, 16, 256), jnp.float32),
            pltpu.SemaphoreType.DMA((5,)),
        ],
        compiler_params=params,
        cost_estimate=pl.CostEstimate(flops=10_000_000, bytes_accessed=4_000_000, transcendentals=0),
        name="near_rows",
    )(*(held(value) for value in (rows_first, points, fields, starts, weights)))

    coefficients = pl.pallas_call(
        far_kernel,
        out_shape=jax.ShapeDtypeStruct((owners, 2 * SUB * lat_count, LANES), jnp.bfloat16),
        in_specs=[remote] * 2 + [vector] * 7,
        out_specs=vector,
        scratch_shapes=scalars
        + [
            pltpu.VMEM((2, fields.size // LANES, LANES), jnp.float32),
            pltpu.VMEM((2 * lat_count, blocks + 2, SUB, LANES), jnp.float32),
            pltpu.VMEM((couples, SUB, 2 * LANES), jnp.float32),
            pltpu.VMEM((2 * SUB, columns + LANES), jnp.float32),
            pltpu.SemaphoreType.DMA((2,)),
        ],
        compiler_params=params,
        name="far_rows",
    )(held(rows_first), held(points), below, above, begins, factors, partial, table, twiddle)

    received = lax.all_to_all(coefficients, "lat", split_axis=0, concat_axis=0, tiled=True)
    by_level = received.reshape(lat_total, 2, level_count, field_count, LANES).astype(jnp.float32)
    virtual = by_level[:, :, :, 2] + 0.61 * by_level[:, :, :, 3]
    total = jnp.sum(thickness[None, None, :, None] * virtual, axis=2).transpose(1, 0, 2)
    totals = lax.all_gather(total, "lev")

    out_shape = (level_count, field_count + 1, 2, pair_count, degrees)
    half = (field_count + 1) * 2 * SUB
    group_count = (pair_count + SUB - 1) // SUB
    return pl.pallas_call(
        functools.partial(legendre_kernel, level_count, field_count),
        out_shape=jax.ShapeDtypeStruct(out_shape, jnp.bfloat16),
        in_specs=[scalar, vector, vector, vector],
        out_specs=pl.BlockSpec(memory_space=pl.ANY),
        scratch_shapes=[
            pltpu.VMEM((lat_total * 2 * SUB, LANES), jnp.float32),
            pltpu.VMEM((level_count, group_count, 2 * half, SUB * lat_total), jnp.bfloat16),
            pltpu.VMEM(out_shape, jnp.bfloat16),
            pltpu.SemaphoreType.DMA((level_count,)),
        ],
        compiler_params=params,
        name="degree_sums",
    )(thickness, received, totals, legendre)


def solution(mesh):
    placed = (
        P("lev", None, "lat", None),
        P("lat"),
        P(),
        P("lat", None, None),
        P("lat", None, None, None),
        P("lev"),
        P("lat", None, None),
    )
    return jax.shard_map(
        local,
        mesh=mesh,
        in_specs=placed,
        out_specs=P("lev", None, None, "lat", None),
        check_vma=False,
    )
```

```python
import functools

import jax
import jax.numpy as jnp
import numpy as np
from jax import lax
from jax.experimental import pallas as pl
from jax.experimental.pallas import tpu as pltpu
from jax.sharding import PartitionSpec as P

LANES = 128
SUB = 8
STENCIL = 4
LIMIT = 24 * 1024 * 1024


def lane_gather(values, lanes):
    return jnp.take_along_axis(values, lanes, axis=1, mode="promise_in_bounds")


def turn_parts(product, total, inverse):
    turns = (product - jnp.floor(product * inverse + 0.5) * total) * inverse
    halves = jnp.floor(2.0 * turns + 0.5)
    sign = 1.0 - 2.0 * jnp.abs(halves)
    x = (turns - 0.5 * halves) * np.float32(2.0 * np.pi)
    y = x * x
    sine = -1.0 / 39916800.0
    for term in (1.0 / 362880.0, -1.0 / 5040.0, 1.0 / 120.0, -1.0 / 6.0, 1.0):
        sine = sine * y + np.float32(term)
    cosine = 1.0 / 479001600.0
    for term in (-1.0 / 3628800.0, 1.0 / 40320.0, -1.0 / 720.0, 1.0 / 24.0, -0.5, 1.0):
        cosine = cosine * y + np.float32(term)
    return sign * cosine, sign * (sine * x)


def wavenumbers(at, width, pair_count, pair_total):
    column = lax.broadcasted_iota(jnp.int32, (1, width), 1) + at
    owner = column // (2 * pair_count)
    inner = column - owner * (2 * pair_count)
    second = inner >= pair_count
    pair = owner * pair_count + jnp.where(second, inner - pair_count, inner)
    return jnp.where(second, 2 * pair_total - 1 - pair, pair).astype(jnp.float32)


def extend(lines, row, rows_each, missing, ext, slot):
    blocks = ext.shape[1] - 2
    for block in range(blocks):
        ext[slot, block + 1] = lines[
            pl.ds(block * rows_each + row, SUB, stride=blocks * rows_each), :
        ]
    lane = lax.broadcasted_iota(jnp.int32, (SUB, LANES), 1)
    ahead = lane + missing
    behind = lane - missing
    first = lane_gather(ext[slot, 1], ahead & (LANES - 1))
    second = lane_gather(ext[slot, 2], ahead & (LANES - 1))
    last = ext[slot, blocks]
    final = lane_gather(last, behind & (LANES - 1))
    before = lane_gather(ext[slot, blocks - 1], behind & (LANES - 1))
    ext[slot, 0] = jnp.where(behind >= 0, final, before)
    ext[slot, blocks] = jnp.where(ahead < LANES, last, first)
    ext[slot, blocks + 1] = jnp.where(ahead < LANES, first, second)


def spread_rows(starts, begins):
    lat_count, _, blocks = begins.shape[:3]
    for latitude in range(lat_count):
        for block in range(blocks):
            for row in range(STENCIL):
                lanes = slice(block * LANES, (block + 1) * LANES)
                begins[latitude, row, block] = (
                    starts[latitude, row : row + 1, lanes] - (block - 1) * LANES
                )


def spread_lines(source, lines):
    first, second, rows, lon = source.shape
    at = 0
    for one in range(first):
        for two in range(second):
            values = source[one, two].astype(jnp.float32)
            for block in range(lon // LANES):
                lines[at : at + rows, :] = values[:, block * LANES : (block + 1) * LANES]
                at += rows


def gathered(couple, latitude, picks, ext, begins, factors):
    totals = [jnp.zeros((SUB, LANES), jnp.float32) for _ in range(2)]
    couples = begins.shape[2] // 2
    for row, slot in picks:
        at = ((latitude * STENCIL + row) * couples + couple) * SUB
        scale = factors[pl.ds(pl.multiple_of(at, SUB), SUB), :]
        parts = [ext[slot, 2 * couple + piece] for piece in range(4)]
        for side in range(2):
            start = jnp.broadcast_to(begins[latitude, row, 2 * couple + side], (SUB, LANES))
            for column in range(4):
                place = start + column
                lane = place & (LANES - 1)
                low, middle, high = [
                    lane_gather(part, lane) for part in parts[side : side + 3]
                ]
                value = jnp.where(place < LANES, low, jnp.where(place < 2 * LANES, middle, high))
                line = STENCIL * side + column
                totals[side] = totals[side] + scale[line : line + 1] * value
    return totals


def near_kernel(
    pair_total, pair_count, rows_first_far, points_far, fields_far, starts_far, weights_far,
    partial, table, twiddle, begins, factors,
    rows_first, points, fields, starts, weights, lines, ext, fine, arrived,
):
    lat_count, couples = partial.shape[:2]
    lon = 2 * couples * LANES
    columns = table.shape[2] // 2
    first_lat = lax.axis_index("lat") * lat_count
    fetches = [
        pltpu.make_async_copy(source, target, arrived.at[place])
        for place, (source, target) in enumerate(
            (
                (points_far, points),
                (rows_first_far, rows_first),
                (starts_far, starts),
                (weights_far, weights),
                (fields_far, fields),
            )
        )
    ]
    for fetch in fetches:
        fetch.start()
    fetches[0].wait()
    width = 256
    for latitude in range(lat_count):
        total = jnp.full((1, 1), points[first_lat + latitude], jnp.int32).astype(jnp.float32)
        inverse = 1.0 / total
        scaling = jnp.sqrt(2.0 * inverse)

        def chunk(index, carry, latitude=latitude, total=total, inverse=inverse, scaling=scaling):
            at = pl.multiple_of(index * width, width)
            numbers = wavenumbers(at, width, pair_count, pair_total)
            step = lax.broadcasted_iota(jnp.int32, (couples, width), 0).astype(jnp.float32)
            cosine, sine = turn_parts(numbers * step * float(2 * LANES), total, inverse)
            twiddle[latitude, :, pl.ds(at, width)] = scaling * cosine
            twiddle[latitude, :, pl.ds(columns + at, width)] = scaling * sine
            step = lax.broadcasted_iota(jnp.int32, (16, width), 0).astype(jnp.float32)
            low_cos, low_sin = turn_parts(numbers * step, total, inverse)
            high_cos, high_sin = turn_parts(numbers * step * 16.0, total, inverse)
            fine[0] = high_cos
            fine[1] = high_sin
            for high in range(16):
                this_cos = fine[0, high : high + 1, :]
                this_sin = fine[1, high : high + 1, :]
                rows = pl.ds(16 * high, 16)
                table[latitude, rows, pl.ds(at, width)] = (
                    this_cos * low_cos - this_sin * low_sin
                ).astype(jnp.bfloat16)
                table[latitude, rows, pl.ds(columns + at, width)] = (
                    this_cos * low_sin + this_sin * low_cos
                ).astype(jnp.bfloat16)
            return carry

        lax.fori_loop(0, columns // width, chunk, 0)
    for fetch in fetches[1:]:
        fetch.wait()
    spread_rows(starts, begins)
    spread_lines(weights, factors)
    spread_lines(fields, lines)
    for latitude in range(lat_count):
        extend(lines, latitude, lat_count, lon - points[first_lat + latitude], ext, latitude)
    for latitude in range(lat_count):
        mine = first_lat - rows_first[latitude]
        picks = [(mine + row, row) for row in range(lat_count)]
        for couple in range(couples):
            totals = gathered(couple, latitude, picks, ext, begins, factors)
            for side in range(2):
                partial[latitude, couple, :, side * LANES : (side + 1) * LANES] = totals[side]


def far_kernel(
    rows_first_far, points_far, near_side, far_side, begins, factors, partial, table, twiddle,
    out, rows_first, points, lines, ext, grid, waves, arrived,
):
    fetches = [
        pltpu.make_async_copy(points_far, points, arrived.at[0]),
        pltpu.make_async_copy(rows_first_far, rows_first, arrived.at[1]),
    ]
    for fetch in fetches:
        fetch.start()
    lat_count, couples = partial.shape[:2]
    lon = 2 * couples * LANES
    columns = table.shape[2] // 2
    owners = out.shape[0]
    first_lat = lax.axis_index("lat") * lat_count
    lat_total = points.shape[0]
    toward = 1 - lax.axis_index("lat") % 2
    spread_lines(near_side, lines.at[toward])
    spread_lines(far_side, lines.at[1 - toward])
    for fetch in fetches:
        fetch.wait()
    for side in range(2):
        for row in range(lat_count):
            if side == 0:
                place = jnp.maximum(first_lat - lat_count + row, 0)
            else:
                place = jnp.minimum(first_lat + lat_count + row, lat_total - 1)
            extend(
                lines.at[side], row, lat_count, lon - points[place], ext, side * lat_count + row
            )
    lane = lax.broadcasted_iota(jnp.int32, (SUB, LANES), 1)
    width = 256
    for latitude in range(lat_count):
        mine = first_lat - rows_first[latitude]
        one_row = jnp.where(mine >= 1, 0, 2)
        two_row = jnp.where(mine <= 1, 3, 1)
        picks = []
        for row in (one_row, two_row):
            picks.append((row, jnp.where(row < mine, row - mine + lat_count, row - mine)))
        for couple in range(couples):
            totals = gathered(couple, latitude, picks, ext, begins, factors)
            for side in range(2):
                lanes = pl.ds(side * LANES, LANES)
                live = lane + (2 * couple + side) * LANES < points[first_lat + latitude]
                value = partial[latitude, couple, :, lanes] + totals[side]
                grid[couple, :, lanes] = jnp.where(live, value, 0.0)
        rows = grid[...].reshape(couples * SUB, 2 * LANES).astype(jnp.bfloat16)
        for at in range(0, columns, width):
            real = jnp.dot(
                rows, table[latitude, :, at : at + width], preferred_element_type=jnp.float32
            )
            imag = jnp.dot(
                rows,
                table[latitude, :, columns + at : columns + at + width],
                preferred_element_type=jnp.float32,
            )
            cosine = jnp.zeros((SUB, width), jnp.float32)
            sine = jnp.zeros((SUB, width), jnp.float32)
            for couple in range(couples):
                turn_cos = twiddle[latitude, couple : couple + 1, at : at + width]
                turn_sin = twiddle[latitude, couple : couple + 1, columns + at : columns + at + width]
                here = slice(couple * SUB, (couple + 1) * SUB)
                cosine = cosine + (real[here] * turn_cos - imag[here] * turn_sin)
                sine = sine - (real[here] * turn_sin + imag[here] * turn_cos)
            waves[0:SUB, at : at + width] = cosine
            waves[SUB : 2 * SUB, at : at + width] = sine
        waves[:, columns:] = jnp.zeros((2 * SUB, waves.shape[1] - columns), jnp.float32)
        used = columns // owners
        for owner in range(owners):
            out[owner, 2 * SUB * latitude : 2 * SUB * (latitude + 1), :] = waves[
                :, owner * used : owner * used + LANES
            ].astype(jnp.bfloat16)


def legendre_kernel(
    level_count, field_count, thickness, received, totals, legendre, out, wide, left, planes, sent,
):
    owners = received.shape[0]
    lat_total = wide.shape[0] // (2 * SUB)
    pair_count, _, degrees = legendre.shape
    pair_total = pair_count * owners
    groups = [(at, min(SUB, pair_count - at)) for at in range(0, pair_count, SUB)]
    keys = [(field, part) for field in range(field_count + 1) for part in range(2)]
    half = len(keys) * SUB
    level_place = lax.axis_index("lev")
    first_pair = lax.axis_index("lat") * pair_count
    wide[...] = received[...].astype(jnp.float32).reshape(wide.shape)
    lines = {}
    for part in range(2):
        running = jnp.zeros((lat_total, LANES), jnp.float32)
        for other in range(1, totals.shape[0]):
            running = running + jnp.where(other > level_place, totals[other, part], 0.0)
        for level in reversed(range(level_count)):
            for field in range(field_count):
                place = part * SUB + level * field_count + field
                lines[level, field, part] = wide[pl.ds(place, lat_total, stride=2 * SUB), :]
            running = running + thickness[level] * (
                lines[level, 2, part] + 0.61 * lines[level, 3, part]
            )
            lines[level, field_count, part] = running
    depth = SUB * lat_total
    spread = (
        lax.broadcasted_iota(jnp.int32, (lat_total, depth), 0)
        == lax.broadcasted_iota(jnp.int32, (lat_total, depth), 1) % lat_total
    ).astype(jnp.bfloat16)
    keep = (
        lax.broadcasted_iota(jnp.int32, (SUB, depth), 0)
        == lax.broadcasted_iota(jnp.int32, (SUB, depth), 1) // lat_total
    )
    copies = []
    for level in range(level_count):
        for place in range(0, len(keys), 2):
            couple = [
                lax.dot_general(
                    lines[(level,) + key].astype(jnp.bfloat16),
                    spread,
                    (((0,), (0,)), ((), ())),
                    preferred_element_type=jnp.float32,
                )
                for key in keys[place : place + 2]
            ]
            for member in range(2):
                for group, (at, _) in enumerate(groups):
                    begin = member * pair_count + at
                    pieces = [jnp.where(keep, one[begin : begin + SUB], 0.0) for one in couple]
                    into = member * half + place * SUB
                    left[level, group, into : into + 2 * SUB, :] = jnp.concatenate(
                        pieces, axis=0
                    ).astype(jnp.bfloat16)
        for start in range(0, degrees, 256):
            stop = min(start + 256, degrees)
            low = 0 if start < 2 * pair_total else half
            high = 2 * half if stop > pair_total + 1 else half
            parts = []
            for group, (at, size) in enumerate(groups):
                values = legendre[at : at + size, :, start:stop].reshape(
                    size * lat_total, stop - start
                )
                sums = jnp.dot(
                    left[level, group, low:high, : size * lat_total],
                    values,
                    preferred_element_type=jnp.float32,
                ).reshape((high - low) // SUB, SUB, stop - start)
                if high - low > half:
                    shape = (SUB, stop - start)
                    slot = lax.broadcasted_iota(jnp.int32, shape, 1) + start
                    pair = lax.broadcasted_iota(jnp.int32, shape, 0) + (first_pair + at)
                    sums = jnp.where(
                        slot + pair < 2 * pair_total, sums[: len(keys)], sums[len(keys) :]
                    )
                parts.append(sums[:, :size])
            planes[level, :, :, :, start:stop] = (
                jnp.concatenate(parts, axis=1)
                .astype(jnp.bfloat16)
                .reshape(field_count + 1, 2, pair_count, stop - start)
            )
        copies.append(pltpu.make_async_copy(planes.at[level], out.at[level], sent.at[level]))
        copies[-1].start()
    for copy in copies:
        copy.wait()


def held(value):
    return pltpu.with_memory_space_constraint(value, pltpu.HBM)


def local(fields, rows_first, points, starts, weights, thickness, legendre):
    level_count, field_count, lat_count, lon_count = fields.shape
    pair_count, lat_total, degrees = legendre.shape
    owners = lax.axis_size("lat")
    couples = lon_count // (2 * LANES)
    blocks = 2 * couples
    columns = 2 * owners * pair_count
    sides = []
    for first in range(2):
        edges = [(i, i + 1) for i in range(first, owners - 1, 2)]
        sides.append(lax.ppermute(fields, "lat", edges + [(j, i) for i, j in edges]))

    scalar = pl.BlockSpec(memory_space=pltpu.SMEM)
    vector = pl.BlockSpec(memory_space=pltpu.VMEM)
    params = pltpu.CompilerParams(vmem_limit_bytes=LIMIT)
    remote = pl.BlockSpec(memory_space=pltpu.HBM)
    scalars = [
        pltpu.SMEM(rows_first.shape, jnp.int32),
        pltpu.SMEM(points.shape, jnp.int32),
    ]
    partial, table, twiddle, begins, factors = pl.pallas_call(
        functools.partial(near_kernel, pair_count * owners, pair_count),
        out_shape=(
            jax.ShapeDtypeStruct((lat_count, couples, SUB, 2 * LANES), jnp.float32),
            jax.ShapeDtypeStruct((lat_count, 2 * LANES, 2 * columns), jnp.bfloat16),
            jax.ShapeDtypeStruct((lat_count, couples, 2 * columns), jnp.float32),
            jax.ShapeDtypeStruct((lat_count, STENCIL, blocks, 1, LANES), jnp.int32),
            jax.ShapeDtypeStruct((weights.size // LANES, LANES), jnp.float32),
        ),
        in_specs=[remote] * 5,
        out_specs=(vector,) * 5,
        scratch_shapes=scalars
        + [
            pltpu.VMEM(fields.shape, fields.dtype),
            pltpu.VMEM(starts.shape, starts.dtype),
            pltpu.VMEM(weights.shape, weights.dtype),
            pltpu.VMEM((fields.size // LANES, LANES), jnp.float32),
            pltpu.VMEM((lat_count, blocks + 2, SUB, LANES), jnp.float32),
            pltpu.VMEM((2, 16, 256), jnp.float32),
            pltpu.SemaphoreType.DMA((5,)),
        ],
        compiler_params=params,
        cost_estimate=pl.CostEstimate(flops=10_000_000, bytes_accessed=4_000_000, transcendentals=0),
        name="near_rows",
    )(*(held(value) for value in (rows_first, points, fields, starts, weights)))

    coefficients = pl.pallas_call(
        far_kernel,
        out_shape=jax.ShapeDtypeStruct((owners, 2 * SUB * lat_count, LANES), jnp.bfloat16),
        in_specs=[remote] * 2 + [vector] * 7,
        out_specs=vector,
        scratch_shapes=scalars
        + [
            pltpu.VMEM((2, fields.size // LANES, LANES), jnp.float32),
            pltpu.VMEM((2 * lat_count, blocks + 2, SUB, LANES), jnp.float32),
            pltpu.VMEM((couples, SUB, 2 * LANES), jnp.float32),
            pltpu.VMEM((2 * SUB, columns + LANES), jnp.float32),
            pltpu.SemaphoreType.DMA((2,)),
        ],
        compiler_params=params,
        name="far_rows",
    )(held(rows_first), held(points), *sides, begins, factors, partial, table, twiddle)

    received = lax.all_to_all(coefficients, "lat", split_axis=0, concat_axis=0, tiled=True)
    by_level = received.reshape(lat_total, 2, level_count, field_count, LANES).astype(jnp.float32)
    virtual = by_level[:, :, :, 2] + 0.61 * by_level[:, :, :, 3]
    total = jnp.sum(thickness[None, None, :, None] * virtual, axis=2).transpose(1, 0, 2)
    totals = lax.all_gather(total, "lev")

    out_shape = (level_count, field_count + 1, 2, pair_count, degrees)
    half = (field_count + 1) * 2 * SUB
    group_count = (pair_count + SUB - 1) // SUB
    return pl.pallas_call(
        functools.partial(legendre_kernel, level_count, field_count),
        out_shape=jax.ShapeDtypeStruct(out_shape, jnp.bfloat16),
        in_specs=[scalar, vector, vector, vector],
        out_specs=pl.BlockSpec(memory_space=pl.ANY),
        scratch_shapes=[
            pltpu.VMEM((lat_total * 2 * SUB, LANES), jnp.float32),
            pltpu.VMEM((level_count, group_count, 2 * half, SUB * lat_total), jnp.bfloat16),
            pltpu.VMEM(out_shape, jnp.bfloat16),
            pltpu.SemaphoreType.DMA((level_count,)),
        ],
        compiler_params=params,
        name="degree_sums",
    )(thickness, received, totals, legendre)


def solution(mesh):
    placed = (
        P("lev", None, "lat", None),
        P("lat"),
        P(),
        P("lat", None, None),
        P("lat", None, None, None),
        P("lev"),
        P("lat", None, None),
    )
    return jax.shard_map(
        local,
        mesh=mesh,
        in_specs=placed,
        out_specs=P("lev", None, None, "lat", None),
        check_vma=False,
    )
```

```python
import functools

import jax
import jax.numpy as jnp
import numpy as np
from jax import lax
from jax.experimental import pallas as pl
from jax.experimental.pallas import tpu as pltpu
from jax.sharding import PartitionSpec as P

LANES = 128
SUB = 8
STENCIL = 4
LIMIT = 24 * 1024 * 1024


def lane_gather(values, lanes):
    return jnp.take_along_axis(values, lanes, axis=1, mode="promise_in_bounds")


def turn_parts(product, total, inverse):
    turns = (product - jnp.floor(product * inverse + 0.5) * total) * inverse
    halves = jnp.floor(2.0 * turns + 0.5)
    sign = 1.0 - 2.0 * jnp.abs(halves)
    x = (turns - 0.5 * halves) * np.float32(2.0 * np.pi)
    y = x * x
    sine = -1.0 / 39916800.0
    for term in (1.0 / 362880.0, -1.0 / 5040.0, 1.0 / 120.0, -1.0 / 6.0, 1.0):
        sine = sine * y + np.float32(term)
    cosine = 1.0 / 479001600.0
    for term in (-1.0 / 3628800.0, 1.0 / 40320.0, -1.0 / 720.0, 1.0 / 24.0, -0.5, 1.0):
        cosine = cosine * y + np.float32(term)
    return sign * cosine, sign * (sine * x)


def wavenumbers(at, width, pair_count, pair_total):
    column = lax.broadcasted_iota(jnp.int32, (1, width), 1) + at
    owner = column // (2 * pair_count)
    inner = column - owner * (2 * pair_count)
    second = inner >= pair_count
    pair = owner * pair_count + jnp.where(second, inner - pair_count, inner)
    return jnp.where(second, 2 * pair_total - 1 - pair, pair).astype(jnp.float32)


def extend(lines, row, rows_each, missing, ext, slot):
    blocks = ext.shape[1] - 2
    for block in range(blocks):
        ext[slot, block + 1] = lines[
            pl.ds(block * rows_each + row, SUB, stride=blocks * rows_each), :
        ]
    lane = lax.broadcasted_iota(jnp.int32, (SUB, LANES), 1)
    ahead = lane + missing
    behind = lane - missing
    first = lane_gather(ext[slot, 1], ahead & (LANES - 1))
    second = lane_gather(ext[slot, 2], ahead & (LANES - 1))
    last = ext[slot, blocks]
    final = lane_gather(last, behind & (LANES - 1))
    before = lane_gather(ext[slot, blocks - 1], behind & (LANES - 1))
    ext[slot, 0] = jnp.where(behind >= 0, final, before)
    ext[slot, blocks] = jnp.where(ahead < LANES, last, first)
    ext[slot, blocks + 1] = jnp.where(ahead < LANES, first, second)


def spread_rows(starts, begins):
    lat_count, _, blocks = begins.shape[:3]
    for latitude in range(lat_count):
        for block in range(blocks):
            for row in range(STENCIL):
                lanes = slice(block * LANES, (block + 1) * LANES)
                begins[latitude, row, block] = (
                    starts[latitude, row : row + 1, lanes] - (block - 1) * LANES
                )


def spread_lines(source, lines):
    first, second, rows, lon = source.shape
    at = 0
    for one in range(first):
        for two in range(second):
            values = source[one, two].astype(jnp.float32)
            for block in range(lon // LANES):
                lines[at : at + rows, :] = values[:, block * LANES : (block + 1) * LANES]
                at += rows


def gathered(couple, latitude, picks, ext, begins, factors):
    totals = [jnp.zeros((SUB, LANES), jnp.float32) for _ in range(2)]
    couples = begins.shape[2] // 2
    for row, slot in picks:
        at = ((latitude * STENCIL + row) * couples + couple) * SUB
        scale = factors[pl.ds(pl.multiple_of(at, SUB), SUB), :]
        parts = [ext[slot, 2 * couple + piece] for piece in range(4)]
        for side in range(2):
            start = jnp.broadcast_to(begins[latitude, row, 2 * couple + side], (SUB, LANES))
            for column in range(4):
                place = start + column
                lane = place & (LANES - 1)
                low, middle, high = [
                    lane_gather(part, lane) for part in parts[side : side + 3]
                ]
                value = jnp.where(place < LANES, low, jnp.where(place < 2 * LANES, middle, high))
                line = STENCIL * side + column
                totals[side] = totals[side] + scale[line : line + 1] * value
    return totals


def near_kernel(
    pair_total, pair_count, rows_first_far, points_far, fields_far, starts_far, weights_far,
    partial, table, twiddle, begins, factors,
    rows_first, points, fields, starts, weights, lines, ext, fine, arrived,
):
    lat_count, couples = partial.shape[:2]
    lon = 2 * couples * LANES
    columns = table.shape[2] // 2
    first_lat = lax.axis_index("lat") * lat_count
    fetches = [
        pltpu.make_async_copy(source, target, arrived.at[place])
        for place, (source, target) in enumerate(
            (
                (points_far, points),
                (rows_first_far, rows_first),
                (starts_far, starts),
                (weights_far, weights),
                (fields_far, fields),
            )
        )
    ]
    for fetch in fetches:
        fetch.start()
    fetches[0].wait()
    width = 256
    for latitude in range(lat_count):
        total = jnp.full((1, 1), points[first_lat + latitude], jnp.int32).astype(jnp.float32)
        inverse = 1.0 / total
        scaling = jnp.sqrt(2.0 * inverse)

        def chunk(index, carry, latitude=latitude, total=total, inverse=inverse, scaling=scaling):
            at = pl.multiple_of(index * width, width)
            numbers = wavenumbers(at, width, pair_count, pair_total)
            step = lax.broadcasted_iota(jnp.int32, (couples, width), 0).astype(jnp.float32)
            cosine, sine = turn_parts(numbers * step * float(2 * LANES), total, inverse)
            twiddle[latitude, :, pl.ds(at, width)] = scaling * cosine
            twiddle[latitude, :, pl.ds(columns + at, width)] = scaling * sine
            step = lax.broadcasted_iota(jnp.int32, (16, width), 0).astype(jnp.float32)
            low_cos, low_sin = turn_parts(numbers * step, total, inverse)
            high_cos, high_sin = turn_parts(numbers * step * 16.0, total, inverse)
            fine[0] = high_cos
            fine[1] = high_sin
            for high in range(16):
                this_cos = fine[0, high : high + 1, :]
                this_sin = fine[1, high : high + 1, :]
                rows = pl.ds(16 * high, 16)
                table[latitude, rows, pl.ds(at, width)] = (
                    this_cos * low_cos - this_sin * low_sin
                ).astype(jnp.bfloat16)
                table[latitude, rows, pl.ds(columns + at, width)] = (
                    this_cos * low_sin + this_sin * low_cos
                ).astype(jnp.bfloat16)
            return carry

        lax.fori_loop(0, columns // width, chunk, 0)
    for fetch in fetches[1:]:
        fetch.wait()
    spread_rows(starts, begins)
    spread_lines(weights, factors)
    spread_lines(fields, lines)
    for latitude in range(lat_count):
        extend(lines, latitude, lat_count, lon - points[first_lat + latitude], ext, latitude)
    for latitude in range(lat_count):
        mine = first_lat - rows_first[latitude]
        picks = [(mine + row, row) for row in range(lat_count)]
        for couple in range(couples):
            totals = gathered(couple, latitude, picks, ext, begins, factors)
            for side in range(2):
                partial[latitude, couple, :, side * LANES : (side + 1) * LANES] = totals[side]


def far_kernel(
    rows_first_far, points_far, near_side, far_side, begins, factors, partial, table, twiddle,
    out, rows_first, points, lines, ext, grid, waves, arrived,
):
    fetches = [
        pltpu.make_async_copy(points_far, points, arrived.at[0]),
        pltpu.make_async_copy(rows_first_far, rows_first, arrived.at[1]),
    ]
    for fetch in fetches:
        fetch.start()
    lat_count, couples = partial.shape[:2]
    lon = 2 * couples * LANES
    columns = table.shape[2] // 2
    owners = out.shape[0]
    first_lat = lax.axis_index("lat") * lat_count
    lat_total = points.shape[0]
    toward = 1 - lax.axis_index("lat") % 2
    spread_lines(near_side, lines.at[toward])
    spread_lines(far_side, lines.at[1 - toward])
    for fetch in fetches:
        fetch.wait()
    for side in range(2):
        for row in range(lat_count):
            if side == 0:
                place = jnp.maximum(first_lat - lat_count + row, 0)
            else:
                place = jnp.minimum(first_lat + lat_count + row, lat_total - 1)
            extend(
                lines.at[side], row, lat_count, lon - points[place], ext, side * lat_count + row
            )
    lane = lax.broadcasted_iota(jnp.int32, (SUB, LANES), 1)
    width = 256
    for latitude in range(lat_count):
        mine = first_lat - rows_first[latitude]
        one_row = jnp.where(mine >= 1, 0, 2)
        two_row = jnp.where(mine <= 1, 3, 1)
        picks = []
        for row in (one_row, two_row):
            picks.append((row, jnp.where(row < mine, row - mine + lat_count, row - mine)))
        for couple in range(couples):
            totals = gathered(couple, latitude, picks, ext, begins, factors)
            for side in range(2):
                lanes = pl.ds(side * LANES, LANES)
                live = lane + (2 * couple + side) * LANES < points[first_lat + latitude]
                value = partial[latitude, couple, :, lanes] + totals[side]
                grid[couple, :, lanes] = jnp.where(live, value, 0.0)
        rows = grid[...].reshape(couples * SUB, 2 * LANES).astype(jnp.bfloat16)
        for at in range(0, columns, width):
            real = jnp.dot(
                rows, table[latitude, :, at : at + width], preferred_element_type=jnp.float32
            )
            imag = jnp.dot(
                rows,
                table[latitude, :, columns + at : columns + at + width],
                preferred_element_type=jnp.float32,
            )
            cosine = jnp.zeros((SUB, width), jnp.float32)
            sine = jnp.zeros((SUB, width), jnp.float32)
            for couple in range(couples):
                turn_cos = twiddle[latitude, couple : couple + 1, at : at + width]
                turn_sin = twiddle[latitude, couple : couple + 1, columns + at : columns + at + width]
                here = slice(couple * SUB, (couple + 1) * SUB)
                cosine = cosine + (real[here] * turn_cos - imag[here] * turn_sin)
                sine = sine - (real[here] * turn_sin + imag[here] * turn_cos)
            waves[0:SUB, at : at + width] = cosine
            waves[SUB : 2 * SUB, at : at + width] = sine
        waves[:, columns:] = jnp.zeros((2 * SUB, waves.shape[1] - columns), jnp.float32)
        used = columns // owners
        for owner in range(owners):
            out[owner, 2 * SUB * latitude : 2 * SUB * (latitude + 1), :] = waves[
                :, owner * used : owner * used + LANES
            ].astype(jnp.bfloat16)


def legendre_kernel(
    level_count, field_count, thickness, received, totals, legendre, out, wide, left, planes, sent,
):
    owners = received.shape[0]
    lat_total = wide.shape[0] // (2 * SUB)
    pair_count, _, degrees = legendre.shape
    pair_total = pair_count * owners
    groups = [(at, min(SUB, pair_count - at)) for at in range(0, pair_count, SUB)]
    keys = [(field, part) for field in range(field_count + 1) for part in range(2)]
    half = len(keys) * SUB
    level_place = lax.axis_index("lev")
    first_pair = lax.axis_index("lat") * pair_count
    wide[...] = received[...].astype(jnp.float32).reshape(wide.shape)
    lines = {}
    for part in range(2):
        running = jnp.zeros((lat_total, LANES), jnp.float32)
        for other in range(1, totals.shape[0]):
            running = running + jnp.where(other > level_place, totals[other, part], 0.0)
        for level in reversed(range(level_count)):
            for field in range(field_count):
                place = part * SUB + level * field_count + field
                lines[level, field, part] = wide[pl.ds(place, lat_total, stride=2 * SUB), :]
            running = running + thickness[level] * (
                lines[level, 2, part] + 0.61 * lines[level, 3, part]
            )
            lines[level, field_count, part] = running
    depth = SUB * lat_total
    outer, inner = split_of(owners)
    lat_count = lat_total // owners
    row = lax.broadcasted_iota(jnp.int32, (lat_total, depth), 0)
    sender = row // lat_count
    latitude = (sender % outer * inner + sender // outer) * lat_count + row % lat_count
    spread = (
        latitude == lax.broadcasted_iota(jnp.int32, (lat_total, depth), 1) % lat_total
    ).astype(jnp.bfloat16)
    keep = (
        lax.broadcasted_iota(jnp.int32, (SUB, depth), 0)
        == lax.broadcasted_iota(jnp.int32, (SUB, depth), 1) // lat_total
    )
    copies = []
    for level in range(level_count):
        for place in range(0, len(keys), 2):
            couple = [
                lax.dot_general(
                    lines[(level,) + key].astype(jnp.bfloat16),
                    spread,
                    (((0,), (0,)), ((), ())),
                    preferred_element_type=jnp.float32,
                )
                for key in keys[place : place + 2]
            ]
            for member in range(2):
                for group, (at, _) in enumerate(groups):
                    begin = member * pair_count + at
                    pieces = [jnp.where(keep, one[begin : begin + SUB], 0.0) for one in couple]
                    into = member * half + place * SUB
                    left[level, group, into : into + 2 * SUB, :] = jnp.concatenate(
                        pieces, axis=0
                    ).astype(jnp.bfloat16)
        for start in range(0, degrees, 256):
            stop = min(start + 256, degrees)
            low = 0 if start < 2 * pair_total else half
            high = 2 * half if stop > pair_total + 1 else half
            parts = []
            for group, (at, size) in enumerate(groups):
                values = legendre[at : at + size, :, start:stop].reshape(
                    size * lat_total, stop - start
                )
                sums = jnp.dot(
                    left[level, group, low:high, : size * lat_total],
                    values,
                    preferred_element_type=jnp.float32,
                ).reshape((high - low) // SUB, SUB, stop - start)
                if high - low > half:
                    shape = (SUB, stop - start)
                    slot = lax.broadcasted_iota(jnp.int32, shape, 1) + start
                    pair = lax.broadcasted_iota(jnp.int32, shape, 0) + (first_pair + at)
                    sums = jnp.where(
                        slot + pair < 2 * pair_total, sums[: len(keys)], sums[len(keys) :]
                    )
                parts.append(sums[:, :size])
            planes[level, :, :, :, start:stop] = (
                jnp.concatenate(parts, axis=1)
                .astype(jnp.bfloat16)
                .reshape(field_count + 1, 2, pair_count, stop - start)
            )
        copies.append(pltpu.make_async_copy(planes.at[level], out.at[level], sent.at[level]))
        copies[-1].start()
    for copy in copies:
        copy.wait()


def split_of(owners):
    inner = 1
    while inner * inner < owners:
        inner *= 2
    return owners // inner, inner


def exchanged(parts, owners):
    outer, inner = split_of(owners)
    across = [[high * inner + low for high in range(outer)] for low in range(inner)]
    within = [[high * inner + low for low in range(inner)] for high in range(outer)]
    shape = parts.shape
    parts = parts.reshape(outer, inner, *shape[1:])
    parts = lax.all_to_all(parts, "lat", 0, 0, axis_index_groups=across, tiled=True)
    parts = jnp.swapaxes(parts, 0, 1)
    parts = lax.all_to_all(parts, "lat", 0, 0, axis_index_groups=within, tiled=True)
    return parts.reshape(shape)


def held(value):
    return pltpu.with_memory_space_constraint(value, pltpu.HBM)


def local(fields, rows_first, points, starts, weights, thickness, legendre):
    level_count, field_count, lat_count, lon_count = fields.shape
    pair_count, lat_total, degrees = legendre.shape
    owners = lax.axis_size("lat")
    couples = lon_count // (2 * LANES)
    blocks = 2 * couples
    columns = 2 * owners * pair_count
    sides = []
    for first in range(2):
        edges = [(i, i + 1) for i in range(first, owners - 1, 2)]
        sides.append(lax.ppermute(fields, "lat", edges + [(j, i) for i, j in edges]))

    scalar = pl.BlockSpec(memory_space=pltpu.SMEM)
    vector = pl.BlockSpec(memory_space=pltpu.VMEM)
    params = pltpu.CompilerParams(vmem_limit_bytes=LIMIT)
    remote = pl.BlockSpec(memory_space=pltpu.HBM)
    scalars = [
        pltpu.SMEM(rows_first.shape, jnp.int32),
        pltpu.SMEM(points.shape, jnp.int32),
    ]
    partial, table, twiddle, begins, factors = pl.pallas_call(
        functools.partial(near_kernel, pair_count * owners, pair_count),
        out_shape=(
            jax.ShapeDtypeStruct((lat_count, couples, SUB, 2 * LANES), jnp.float32),
            jax.ShapeDtypeStruct((lat_count, 2 * LANES, 2 * columns), jnp.bfloat16),
            jax.ShapeDtypeStruct((lat_count, couples, 2 * columns), jnp.float32),
            jax.ShapeDtypeStruct((lat_count, STENCIL, blocks, 1, LANES), jnp.int32),
            jax.ShapeDtypeStruct((weights.size // LANES, LANES), jnp.float32),
        ),
        in_specs=[remote] * 5,
        out_specs=(vector,) * 5,
        scratch_shapes=scalars
        + [
            pltpu.VMEM(fields.shape, fields.dtype),
            pltpu.VMEM(starts.shape, starts.dtype),
            pltpu.VMEM(weights.shape, weights.dtype),
            pltpu.VMEM((fields.size // LANES, LANES), jnp.float32),
            pltpu.VMEM((lat_count, blocks + 2, SUB, LANES), jnp.float32),
            pltpu.VMEM((2, 16, 256), jnp.float32),
            pltpu.SemaphoreType.DMA((5,)),
        ],
        compiler_params=params,
        cost_estimate=pl.CostEstimate(flops=10_000_000, bytes_accessed=4_000_000, transcendentals=0),
        name="near_rows",
    )(*(held(value) for value in (rows_first, points, fields, starts, weights)))

    coefficients = pl.pallas_call(
        far_kernel,
        out_shape=jax.ShapeDtypeStruct((owners, 2 * SUB * lat_count, LANES), jnp.bfloat16),
        in_specs=[remote] * 2 + [vector] * 7,
        out_specs=vector,
        scratch_shapes=scalars
        + [
            pltpu.VMEM((2, fields.size // LANES, LANES), jnp.float32),
            pltpu.VMEM((2 * lat_count, blocks + 2, SUB, LANES), jnp.float32),
            pltpu.VMEM((couples, SUB, 2 * LANES), jnp.float32),
            pltpu.VMEM((2 * SUB, columns + LANES), jnp.float32),
            pltpu.SemaphoreType.DMA((2,)),
        ],
        compiler_params=params,
        name="far_rows",
    )(held(rows_first), held(points), *sides, begins, factors, partial, table, twiddle)

    received = exchanged(coefficients, owners)
    by_level = received.reshape(lat_total, 2, level_count, field_count, LANES).astype(jnp.float32)
    virtual = by_level[:, :, :, 2] + 0.61 * by_level[:, :, :, 3]
    total = jnp.sum(thickness[None, None, :, None] * virtual, axis=2).transpose(1, 0, 2)
    totals = lax.all_gather(total, "lev")

    out_shape = (level_count, field_count + 1, 2, pair_count, degrees)
    half = (field_count + 1) * 2 * SUB
    group_count = (pair_count + SUB - 1) // SUB
    return pl.pallas_call(
        functools.partial(legendre_kernel, level_count, field_count),
        out_shape=jax.ShapeDtypeStruct(out_shape, jnp.bfloat16),
        in_specs=[scalar, vector, vector, vector],
        out_specs=pl.BlockSpec(memory_space=pl.ANY),
        scratch_shapes=[
            pltpu.VMEM((lat_total * 2 * SUB, LANES), jnp.float32),
            pltpu.VMEM((level_count, group_count, 2 * half, SUB * lat_total), jnp.bfloat16),
            pltpu.VMEM(out_shape, jnp.bfloat16),
            pltpu.SemaphoreType.DMA((level_count,)),
        ],
        compiler_params=params,
        name="degree_sums",
    )(thickness, received, totals, legendre)


def solution(mesh):
    placed = (
        P("lev", None, "lat", None),
        P("lat"),
        P(),
        P("lat", None, None),
        P("lat", None, None, None),
        P("lev"),
        P("lat", None, None),
    )
    return jax.shard_map(
        local,
        mesh=mesh,
        in_specs=placed,
        out_specs=P("lev", None, None, "lat", None),
        check_vma=False,
    )
```

```python
import functools

import jax
import jax.numpy as jnp
import numpy as np
from jax import lax
from jax.experimental import pallas as pl
from jax.experimental.pallas import tpu as pltpu
from jax.sharding import PartitionSpec as P

LANES = 128
SUB = 8
HALF = 64
STENCIL = 4
LIMIT = 24 * 1024 * 1024


def lane_gather(values, lanes):
    return jnp.take_along_axis(values, lanes, axis=1, mode="promise_in_bounds")


SINE = (-70.99342854244645, 81.34076844400118, -41.337142359536955, 6.283164044230117)
COSINE = (
    56.2423804697887, -85.2403304160897, 64.93459063550272, -19.739171434929204, 0.9999999534680867,
)


def polynomial(terms, square):
    value = np.float32(terms[0])
    for term in terms[1:]:
        value = value * square + np.float32(term)
    return value


def turn_parts(product, total, inverse):
    turns = (product - jnp.floor(product * inverse + 0.5) * total) * inverse
    halves = jnp.floor(2.0 * turns + 0.5)
    sign = 1.0 - 2.0 * jnp.abs(halves)
    part = turns - 0.5 * halves
    square = part * part
    return sign * polynomial(COSINE, square), (sign * part) * polynomial(SINE, square)


def wavenumbers(at, width, pair_count, pair_total):
    column = lax.broadcasted_iota(jnp.int32, (1, width), 1).astype(jnp.float32) + float(at)
    owner = jnp.floor((column + 0.5) * (1.0 / (2 * pair_count)))
    inner = column - owner * (2.0 * pair_count)
    second = inner >= pair_count
    pair = owner * pair_count + jnp.where(second, inner - pair_count, inner)
    return jnp.where(second, 2.0 * pair_total - 1.0 - pair, pair)


def multiplied(one, two):
    return one[0] * two[0] - one[1] * two[1], one[0] * two[1] + one[1] * two[0]


def row_of(pair, row):
    return tuple(part[row : row + 1] for part in pair)


def extend(lines, row, rows_each, missing, ext, slot):
    blocks = ext.shape[1] - 2
    for block in range(blocks):
        ext[slot, block + 1] = lines[
            pl.ds(block * rows_each + row, SUB, stride=blocks * rows_each), :
        ]
    lane = lax.broadcasted_iota(jnp.int32, (SUB, LANES), 1)
    ahead = lane + missing
    behind = lane - missing
    first = lane_gather(ext[slot, 1], ahead & (LANES - 1))
    second = lane_gather(ext[slot, 2], ahead & (LANES - 1))
    last = ext[slot, blocks]
    final = lane_gather(last, behind & (LANES - 1))
    before = lane_gather(ext[slot, blocks - 1], behind & (LANES - 1))
    ext[slot, 0] = jnp.where(behind >= 0, final, before)
    ext[slot, blocks] = jnp.where(ahead < LANES, last, first)
    ext[slot, blocks + 1] = jnp.where(ahead < LANES, first, second)


def spread_rows(starts, begins):
    lat_count, _, blocks = begins.shape[:3]
    for latitude in range(lat_count):
        for block in range(blocks):
            for row in range(STENCIL):
                lanes = slice(block * LANES, (block + 1) * LANES)
                begins[latitude, row, block] = (
                    starts[latitude, row : row + 1, lanes] - (block - 1) * LANES
                )


def spread_lines(source, lines):
    first, second, rows, lon = source.shape
    at = 0
    for one in range(first):
        for two in range(second):
            values = source[one, two].astype(jnp.float32)
            for block in range(lon // LANES):
                lines[at : at + rows, :] = values[:, block * LANES : (block + 1) * LANES]
                at += rows


def gathered(couple, latitude, picks, ext, begins, factors):
    totals = [jnp.zeros((SUB, LANES), jnp.float32) for _ in range(2)]
    couples = begins.shape[2] // 2
    for row, slot in picks:
        at = ((latitude * STENCIL + row) * couples + couple) * SUB
        scale = factors[pl.ds(pl.multiple_of(at, SUB), SUB), :]
        parts = [ext[slot, 2 * couple + piece] for piece in range(4)]
        for side in range(2):
            start = jnp.broadcast_to(begins[latitude, row, 2 * couple + side], (SUB, LANES))
            for column in range(4):
                place = start + column
                lane = place & (LANES - 1)
                low, middle, high = [
                    lane_gather(part, lane) for part in parts[side : side + 3]
                ]
                value = jnp.where(place < LANES, low, jnp.where(place < 2 * LANES, middle, high))
                line = STENCIL * side + column
                totals[side] = totals[side] + scale[line : line + 1] * value
    return totals


def near_kernel(
    pair_total, pair_count, rows_first_far, points_far, fields_far, starts_far, weights_far,
    partial, table, twiddle, begins, factors,
    rows_first, points, fields, starts, weights, lines, ext, arrived,
):
    lat_count, couples = partial.shape[:2]
    lon = 2 * couples * LANES
    columns = table.shape[2] // 2
    first_lat = lax.axis_index("lat") * lat_count
    fetches = [
        pltpu.make_async_copy(source, target, arrived.at[place])
        for place, (source, target) in enumerate(
            (
                (points_far, points),
                (rows_first_far, rows_first),
                (starts_far, starts),
                (weights_far, weights),
                (fields_far, fields),
            )
        )
    ]
    for fetch in fetches:
        fetch.start()
    fetches[0].wait()
    width = 256
    scales = []
    for latitude in range(lat_count):
        total = jnp.full((1, 1), points[first_lat + latitude], jnp.int32).astype(jnp.float32)
        inverse = 1.0 / total
        scales.append((total, inverse, jnp.sqrt(2.0 * inverse)))
    few = lax.broadcasted_iota(jnp.int32, (SUB, width), 0).astype(jnp.float32)
    many = lax.broadcasted_iota(jnp.int32, (couples + 3, width), 0)
    many = jnp.where(many < couples, many * (2 * LANES), (many - (couples - 1)) * HALF)
    many = many.astype(jnp.float32)
    for at in range(0, columns, width):
        numbers = wavenumbers(at, width, pair_count, pair_total)
        for latitude, (total, inverse, scaling) in enumerate(scales):
            ones = turn_parts(numbers * few, total, inverse)
            eights = turn_parts(numbers * (few * float(SUB)), total, inverse)
            large = turn_parts(numbers * many, total, inverse)
            here = slice(at, at + width)
            there = slice(columns + at, columns + at + width)
            twiddle[latitude, :, here] = scaling * large[0][:couples]
            twiddle[latitude, :, there] = scaling * large[1][:couples]
            products = [ones] + [multiplied(row_of(eights, row), ones) for row in range(1, SUB)]
            block = tuple(jnp.concatenate(parts, axis=0) for parts in zip(*products))
            for quarter in range(4):
                turned = block
                if quarter > 0:
                    turned = multiplied(row_of(large, couples + quarter - 1), block)
                rows = slice(HALF * quarter, HALF * (quarter + 1))
                table[latitude, rows, here] = turned[0].astype(jnp.bfloat16)
                table[latitude, rows, there] = turned[1].astype(jnp.bfloat16)
    for fetch in fetches[1:]:
        fetch.wait()
    spread_rows(starts, begins)
    spread_lines(weights, factors)
    spread_lines(fields, lines)
    for latitude in range(lat_count):
        extend(lines, latitude, lat_count, lon - points[first_lat + latitude], ext, latitude)
    for latitude in range(lat_count):
        mine = first_lat - rows_first[latitude]
        picks = [(mine + row, row) for row in range(lat_count)]
        for couple in range(couples):
            totals = gathered(couple, latitude, picks, ext, begins, factors)
            for side in range(2):
                partial[latitude, couple, :, side * LANES : (side + 1) * LANES] = totals[side]


def far_kernel(
    rows_first_far, points_far, near_side, far_side, begins, factors, partial, table, twiddle,
    out, rows_first, points, lines, ext, grid, waves, arrived,
):
    fetches = [
        pltpu.make_async_copy(points_far, points, arrived.at[0]),
        pltpu.make_async_copy(rows_first_far, rows_first, arrived.at[1]),
    ]
    for fetch in fetches:
        fetch.start()
    lat_count, couples = partial.shape[:2]
    lon = 2 * couples * LANES
    columns = table.shape[2] // 2
    owners = out.shape[0]
    first_lat = lax.axis_index("lat") * lat_count
    lat_total = points.shape[0]
    toward = 1 - lax.axis_index("lat") % 2
    spread_lines(near_side, lines.at[toward])
    spread_lines(far_side, lines.at[1 - toward])
    for fetch in fetches:
        fetch.wait()
    for side in range(2):
        for row in range(lat_count):
            if side == 0:
                place = jnp.maximum(first_lat - lat_count + row, 0)
            else:
                place = jnp.minimum(first_lat + lat_count + row, lat_total - 1)
            extend(
                lines.at[side], row, lat_count, lon - points[place], ext, side * lat_count + row
            )
    lane = lax.broadcasted_iota(jnp.int32, (SUB, LANES), 1)
    width = 256
    for latitude in range(lat_count):
        mine = first_lat - rows_first[latitude]
        one_row = jnp.where(mine >= 1, 0, 2)
        two_row = jnp.where(mine <= 1, 3, 1)
        picks = []
        for row in (one_row, two_row):
            picks.append((row, jnp.where(row < mine, row - mine + lat_count, row - mine)))
        for couple in range(couples):
            totals = gathered(couple, latitude, picks, ext, begins, factors)
            for side in range(2):
                lanes = pl.ds(side * LANES, LANES)
                live = lane + (2 * couple + side) * LANES < points[first_lat + latitude]
                value = partial[latitude, couple, :, lanes] + totals[side]
                grid[latitude, couple, :, lanes] = jnp.where(live, value, 0.0)
    for latitude in range(lat_count):
        rows = grid[latitude].reshape(couples * SUB, 2 * LANES).astype(jnp.bfloat16)
        for at in range(0, columns, width):
            real = jnp.dot(
                rows, table[latitude, :, at : at + width], preferred_element_type=jnp.float32
            )
            imag = jnp.dot(
                rows,
                table[latitude, :, columns + at : columns + at + width],
                preferred_element_type=jnp.float32,
            )
            cosine = jnp.zeros((SUB, width), jnp.float32)
            sine = jnp.zeros((SUB, width), jnp.float32)
            for couple in range(couples):
                turn_cos = twiddle[latitude, couple : couple + 1, at : at + width]
                turn_sin = twiddle[latitude, couple : couple + 1, columns + at : columns + at + width]
                here = slice(couple * SUB, (couple + 1) * SUB)
                cosine = cosine + (real[here] * turn_cos - imag[here] * turn_sin)
                sine = sine - (real[here] * turn_sin + imag[here] * turn_cos)
            waves[latitude, 0:SUB, at : at + width] = cosine
            waves[latitude, SUB : 2 * SUB, at : at + width] = sine
        waves[latitude, :, columns:] = jnp.zeros((2 * SUB, waves.shape[2] - columns), jnp.float32)
        used = columns // owners
        for owner in range(owners):
            out[owner, 2 * SUB * latitude : 2 * SUB * (latitude + 1), :] = waves[
                latitude, :, owner * used : owner * used + LANES
            ].astype(jnp.bfloat16)


def legendre_kernel(
    level_count, field_count, thickness, received, totals, legendre, out, wide, left, planes, sent,
):
    owners = received.shape[0]
    lat_total = wide.shape[0] // (2 * SUB)
    pair_count, _, degrees = legendre.shape
    pair_total = pair_count * owners
    groups = [(at, min(SUB, pair_count - at)) for at in range(0, pair_count, SUB)]
    keys = [(field, part) for field in range(field_count + 1) for part in range(2)]
    level_place = lax.axis_index("lev")
    first_pair = lax.axis_index("lat") * pair_count
    wide[...] = received[...].astype(jnp.float32).reshape(wide.shape)
    lines = {}
    for part in range(2):
        running = jnp.zeros((lat_total, LANES), jnp.float32)
        for other in range(1, totals.shape[0]):
            running = running + jnp.where(other > level_place, totals[other, part], 0.0)
        for level in reversed(range(level_count)):
            for field in range(field_count):
                place = part * SUB + level * field_count + field
                lines[level, field, part] = wide[pl.ds(place, lat_total, stride=2 * SUB), :]
            running = running + thickness[level] * (
                lines[level, 2, part] + 0.61 * lines[level, 3, part]
            )
            lines[level, field_count, part] = running
    depth = SUB * lat_total
    spread = (
        lax.broadcasted_iota(jnp.int32, (lat_total, depth), 0)
        == lax.broadcasted_iota(jnp.int32, (lat_total, depth), 1) % lat_total
    ).astype(jnp.bfloat16)
    keep = (
        lax.broadcasted_iota(jnp.int32, (SUB, depth), 0)
        == lax.broadcasted_iota(jnp.int32, (SUB, depth), 1) // lat_total
    )
    keys = [(level,) + key for level in range(level_count) for key in keys]
    half = len(keys) * SUB
    for place in range(0, len(keys), 2):
        couple = [
            lax.dot_general(
                lines[key].astype(jnp.bfloat16),
                spread,
                (((0,), (0,)), ((), ())),
                preferred_element_type=jnp.float32,
            )
            for key in keys[place : place + 2]
        ]
        for member in range(2):
            for group, (at, _) in enumerate(groups):
                begin = member * pair_count + at
                pieces = [jnp.where(keep, one[begin : begin + SUB], 0.0) for one in couple]
                into = member * half + place * SUB
                left[group, into : into + 2 * SUB, :] = jnp.concatenate(pieces, axis=0).astype(
                    jnp.bfloat16
                )
    copies = []
    for start in range(0, degrees, 256):
        stop = min(start + 256, degrees)
        low = 0 if start < 2 * pair_total else half
        high = 2 * half if stop > pair_total + 1 else half
        parts = []
        for group, (at, size) in enumerate(groups):
            values = legendre[at : at + size, :, start:stop].reshape(size * lat_total, stop - start)
            sums = jnp.dot(
                left[group, low:high, : size * lat_total],
                values,
                preferred_element_type=jnp.float32,
            ).reshape((high - low) // SUB, SUB, stop - start)
            if high - low > half:
                shape = (SUB, stop - start)
                slot = lax.broadcasted_iota(jnp.int32, shape, 1) + start
                pair = lax.broadcasted_iota(jnp.int32, shape, 0) + (first_pair + at)
                sums = jnp.where(
                    slot + pair < 2 * pair_total, sums[: len(keys)], sums[len(keys) :]
                )
            parts.append(sums[:, :size])
        planes[:, :, :, :, start:stop] = (
            jnp.concatenate(parts, axis=1).astype(jnp.bfloat16).reshape(planes.shape[:4] + (stop - start,))
        )
        here = pl.ds(start, stop - start)
        copies.append(
            pltpu.make_async_copy(
                planes.at[:, :, :, :, here], out.at[:, :, :, :, here], sent.at[len(copies)]
            )
        )
        copies[-1].start()
    for copy in copies:
        copy.wait()


def held(value):
    return pltpu.with_memory_space_constraint(value, pltpu.HBM)


def local(fields, rows_first, points, starts, weights, thickness, legendre):
    level_count, field_count, lat_count, lon_count = fields.shape
    pair_count, lat_total, degrees = legendre.shape
    owners = lax.axis_size("lat")
    couples = lon_count // (2 * LANES)
    blocks = 2 * couples
    columns = 2 * owners * pair_count
    sides = []
    for first in range(2):
        edges = [(i, i + 1) for i in range(first, owners - 1, 2)]
        sides.append(lax.ppermute(fields, "lat", edges + [(j, i) for i, j in edges]))

    scalar = pl.BlockSpec(memory_space=pltpu.SMEM)
    vector = pl.BlockSpec(memory_space=pltpu.VMEM)
    params = pltpu.CompilerParams(vmem_limit_bytes=LIMIT)
    remote = pl.BlockSpec(memory_space=pltpu.HBM)
    scalars = [
        pltpu.SMEM(rows_first.shape, jnp.int32),
        pltpu.SMEM(points.shape, jnp.int32),
    ]
    partial, table, twiddle, begins, factors = pl.pallas_call(
        functools.partial(near_kernel, pair_count * owners, pair_count),
        out_shape=(
            jax.ShapeDtypeStruct((lat_count, couples, SUB, 2 * LANES), jnp.float32),
            jax.ShapeDtypeStruct((lat_count, 2 * LANES, 2 * columns), jnp.bfloat16),
            jax.ShapeDtypeStruct((lat_count, couples, 2 * columns), jnp.float32),
            jax.ShapeDtypeStruct((lat_count, STENCIL, blocks, 1, LANES), jnp.int32),
            jax.ShapeDtypeStruct((weights.size // LANES, LANES), jnp.float32),
        ),
        in_specs=[remote] * 5,
        out_specs=(vector,) * 5,
        scratch_shapes=scalars
        + [
            pltpu.VMEM(fields.shape, fields.dtype),
            pltpu.VMEM(starts.shape, starts.dtype),
            pltpu.VMEM(weights.shape, weights.dtype),
            pltpu.VMEM((fields.size // LANES, LANES), jnp.float32),
            pltpu.VMEM((lat_count, blocks + 2, SUB, LANES), jnp.float32),
            pltpu.SemaphoreType.DMA((5,)),
        ],
        compiler_params=params,
        cost_estimate=pl.CostEstimate(flops=10_000_000, bytes_accessed=4_000_000, transcendentals=0),
        name="near_rows",
    )(*(held(value) for value in (rows_first, points, fields, starts, weights)))

    coefficients = pl.pallas_call(
        far_kernel,
        out_shape=jax.ShapeDtypeStruct((owners, 2 * SUB * lat_count, LANES), jnp.bfloat16),
        in_specs=[remote] * 2 + [vector] * 7,
        out_specs=vector,
        scratch_shapes=scalars
        + [
            pltpu.VMEM((2, fields.size // LANES, LANES), jnp.float32),
            pltpu.VMEM((2 * lat_count, blocks + 2, SUB, LANES), jnp.float32),
            pltpu.VMEM((lat_count, couples, SUB, 2 * LANES), jnp.float32),
            pltpu.VMEM((lat_count, 2 * SUB, columns + LANES), jnp.float32),
            pltpu.SemaphoreType.DMA((2,)),
        ],
        compiler_params=params,
        name="far_rows",
    )(held(rows_first), held(points), *sides, begins, factors, partial, table, twiddle)

    received = lax.all_to_all(coefficients, "lat", split_axis=0, concat_axis=0, tiled=True)
    by_level = received.reshape(lat_total, 2, level_count, field_count, LANES).astype(jnp.float32)
    virtual = by_level[:, :, :, 2] + 0.61 * by_level[:, :, :, 3]
    total = jnp.sum(thickness[None, None, :, None] * virtual, axis=2).transpose(1, 0, 2)
    totals = lax.all_gather(total, "lev")

    out_shape = (level_count, field_count + 1, 2, pair_count, degrees)
    half = level_count * (field_count + 1) * 2 * SUB
    group_count = (pair_count + SUB - 1) // SUB
    return pl.pallas_call(
        functools.partial(legendre_kernel, level_count, field_count),
        out_shape=jax.ShapeDtypeStruct(out_shape, jnp.bfloat16),
        in_specs=[scalar, vector, vector, vector],
        out_specs=pl.BlockSpec(memory_space=pl.ANY),
        scratch_shapes=[
            pltpu.VMEM((lat_total * 2 * SUB, LANES), jnp.float32),
            pltpu.VMEM((group_count, 2 * half, SUB * lat_total), jnp.bfloat16),
            pltpu.VMEM(out_shape, jnp.bfloat16),
            pltpu.SemaphoreType.DMA(((degrees + 255) // 256,)),
        ],
        compiler_params=params,
        name="degree_sums",
    )(thickness, received, totals, legendre)


def solution(mesh):
    placed = (
        P("lev", None, "lat", None),
        P("lat"),
        P(),
        P("lat", None, None),
        P("lat", None, None, None),
        P("lev"),
        P("lat", None, None),
    )
    return jax.shard_map(
        local,
        mesh=mesh,
        in_specs=placed,
        out_specs=P("lev", None, None, "lat", None),
        check_vma=False,
    )
```

```python
import functools

import jax
import jax.numpy as jnp
import numpy as np
from jax import lax
from jax.experimental import pallas as pl
from jax.experimental.pallas import tpu as pltpu
from jax.sharding import PartitionSpec as P

LANES = 128
SUB = 8
HALF = 64
STENCIL = 4
LIMIT = 24 * 1024 * 1024


def lane_gather(values, lanes):
    return jnp.take_along_axis(values, lanes, axis=1, mode="promise_in_bounds")


SINE = (-70.99342854244645, 81.34076844400118, -41.337142359536955, 6.283164044230117)
COSINE = (
    56.2423804697887, -85.2403304160897, 64.93459063550272, -19.739171434929204, 0.9999999534680867,
)


def polynomial(terms, square):
    value = np.float32(terms[0])
    for term in terms[1:]:
        value = value * square + np.float32(term)
    return value


def turn_parts(product, total, inverse):
    turns = (product - jnp.floor(product * inverse + 0.5) * total) * inverse
    halves = jnp.floor(2.0 * turns + 0.5)
    sign = 1.0 - 2.0 * jnp.abs(halves)
    part = turns - 0.5 * halves
    square = part * part
    return sign * polynomial(COSINE, square), (sign * part) * polynomial(SINE, square)


def wavenumbers(at, width, pair_count, pair_total):
    column = lax.broadcasted_iota(jnp.int32, (1, width), 1).astype(jnp.float32) + float(at)
    owner = jnp.floor((column + 0.5) * (1.0 / (2 * pair_count)))
    inner = column - owner * (2.0 * pair_count)
    second = inner >= pair_count
    pair = owner * pair_count + jnp.where(second, inner - pair_count, inner)
    return jnp.where(second, 2.0 * pair_total - 1.0 - pair, pair)


def multiplied(one, two):
    return one[0] * two[0] - one[1] * two[1], one[0] * two[1] + one[1] * two[0]


def row_of(pair, row):
    return tuple(part[row : row + 1] for part in pair)


def extend(lines, row, rows_each, missing, ext, slot):
    blocks = ext.shape[1] - 2
    for block in range(blocks):
        ext[slot, block + 1] = lines[
            pl.ds(block * rows_each + row, SUB, stride=blocks * rows_each), :
        ]
    lane = lax.broadcasted_iota(jnp.int32, (SUB, LANES), 1)
    ahead = lane + missing
    behind = lane - missing
    first = lane_gather(ext[slot, 1], ahead & (LANES - 1))
    second = lane_gather(ext[slot, 2], ahead & (LANES - 1))
    last = ext[slot, blocks]
    final = lane_gather(last, behind & (LANES - 1))
    before = lane_gather(ext[slot, blocks - 1], behind & (LANES - 1))
    ext[slot, 0] = jnp.where(behind >= 0, final, before)
    ext[slot, blocks] = jnp.where(ahead < LANES, last, first)
    ext[slot, blocks + 1] = jnp.where(ahead < LANES, first, second)


def spread_rows(starts, begins):
    lat_count, _, blocks = begins.shape[:3]
    for latitude in range(lat_count):
        for block in range(blocks):
            for row in range(STENCIL):
                lanes = slice(block * LANES, (block + 1) * LANES)
                begins[latitude, row, block] = (
                    starts[latitude, row : row + 1, lanes] - (block - 1) * LANES
                )


def spread_lines(source, lines):
    first, second, rows, lon = source.shape
    at = 0
    for one in range(first):
        for two in range(second):
            values = source[one, two].astype(jnp.float32)
            for block in range(lon // LANES):
                lines[at : at + rows, :] = values[:, block * LANES : (block + 1) * LANES]
                at += rows


def gathered(couple, latitude, picks, ext, begins, factors):
    totals = [jnp.zeros((SUB, LANES), jnp.float32) for _ in range(2)]
    couples = begins.shape[2] // 2
    for row, slot in picks:
        at = ((latitude * STENCIL + row) * couples + couple) * SUB
        scale = factors[pl.ds(pl.multiple_of(at, SUB), SUB), :]
        parts = [ext[slot, 2 * couple + piece] for piece in range(4)]
        for side in range(2):
            start = jnp.broadcast_to(begins[latitude, row, 2 * couple + side], (SUB, LANES))
            for column in range(4):
                place = start + column
                lane = place & (LANES - 1)
                low, middle, high = [
                    lane_gather(part, lane) for part in parts[side : side + 3]
                ]
                value = jnp.where(place < LANES, low, jnp.where(place < 2 * LANES, middle, high))
                line = STENCIL * side + column
                totals[side] = totals[side] + scale[line : line + 1] * value
    return totals


def near_kernel(
    pair_total, pair_count, rows_first_far, points_far, fields_far, starts_far, weights_far,
    partial, table, twiddle, begins, factors,
    rows_first, points, fields, starts, weights, lines, ext, arrived,
):
    lat_count, couples = partial.shape[:2]
    lon = 2 * couples * LANES
    columns = table.shape[2] // 2
    first_lat = lax.axis_index("lat") * lat_count
    fetches = [
        pltpu.make_async_copy(source, target, arrived.at[place])
        for place, (source, target) in enumerate(
            (
                (points_far, points),
                (rows_first_far, rows_first),
                (starts_far, starts),
                (weights_far, weights),
                (fields_far, fields),
            )
        )
    ]
    for fetch in fetches:
        fetch.start()
    fetches[0].wait()
    width = 256
    scales = []
    for latitude in range(lat_count):
        total = jnp.full((1, 1), points[first_lat + latitude], jnp.int32).astype(jnp.float32)
        inverse = 1.0 / total
        scales.append((total, inverse, jnp.sqrt(2.0 * inverse)))
    few = lax.broadcasted_iota(jnp.int32, (SUB, width), 0).astype(jnp.float32)
    many = lax.broadcasted_iota(jnp.int32, (couples + 3, width), 0)
    many = jnp.where(many < couples, many * (2 * LANES), (many - (couples - 1)) * HALF)
    many = many.astype(jnp.float32)
    for at in range(0, columns, width):
        numbers = wavenumbers(at, width, pair_count, pair_total)
        for latitude, (total, inverse, scaling) in enumerate(scales):
            ones = turn_parts(numbers * few, total, inverse)
            eights = turn_parts(numbers * (few * float(SUB)), total, inverse)
            large = turn_parts(numbers * many, total, inverse)
            here = slice(at, at + width)
            there = slice(columns + at, columns + at + width)
            twiddle[latitude, :, here] = scaling * large[0][:couples]
            twiddle[latitude, :, there] = scaling * large[1][:couples]
            products = [ones] + [multiplied(row_of(eights, row), ones) for row in range(1, SUB)]
            block = tuple(jnp.concatenate(parts, axis=0) for parts in zip(*products))
            for quarter in range(4):
                turned = block
                if quarter > 0:
                    turned = multiplied(row_of(large, couples + quarter - 1), block)
                rows = slice(HALF * quarter, HALF * (quarter + 1))
                table[latitude, rows, here] = turned[0].astype(jnp.bfloat16)
                table[latitude, rows, there] = turned[1].astype(jnp.bfloat16)
    for fetch in fetches[1:]:
        fetch.wait()
    spread_rows(starts, begins)
    spread_lines(weights, factors)
    spread_lines(fields, lines)
    for latitude in range(lat_count):
        extend(lines, latitude, lat_count, lon - points[first_lat + latitude], ext, latitude)
    for latitude in range(lat_count):
        mine = first_lat - rows_first[latitude]
        picks = [(mine + row, row) for row in range(lat_count)]
        for couple in range(couples):
            totals = gathered(couple, latitude, picks, ext, begins, factors)
            for side in range(2):
                partial[latitude, couple, :, side * LANES : (side + 1) * LANES] = totals[side]


def far_kernel(
    rows_first_far, points_far, first_side, second_side, begins, factors, partial, table, twiddle,
    out, rows_first, points, lines, ext, grid, waves, arrived,
):
    fetches = [
        pltpu.make_async_copy(points_far, points, arrived.at[0]),
        pltpu.make_async_copy(rows_first_far, rows_first, arrived.at[1]),
    ]
    for fetch in fetches:
        fetch.start()
    lat_count, couples = partial.shape[:2]
    lon = 2 * couples * LANES
    columns = table.shape[2] // 2
    owners = out.shape[0]
    first_lat = lax.axis_index("lat") * lat_count
    lat_total = points.shape[0]
    toward = lax.axis_index("lat") % 2
    spread_lines(first_side, lines.at[toward])
    spread_lines(second_side, lines.at[1 - toward])
    for fetch in fetches:
        fetch.wait()
    for side in range(2):
        for row in range(lat_count):
            if side == 0:
                place = jnp.maximum(first_lat - lat_count + row, 0)
            else:
                place = jnp.minimum(first_lat + lat_count + row, lat_total - 1)
            extend(
                lines.at[side], row, lat_count, lon - points[place], ext, side * lat_count + row
            )
    lane = lax.broadcasted_iota(jnp.int32, (SUB, LANES), 1)
    width = 256
    for latitude in range(lat_count):
        mine = first_lat - rows_first[latitude]
        one_row = jnp.where(mine >= 1, 0, 2)
        two_row = jnp.where(mine <= 1, 3, 1)
        picks = []
        for row in (one_row, two_row):
            picks.append((row, jnp.where(row < mine, row - mine + lat_count, row - mine)))
        for couple in range(couples):
            totals = gathered(couple, latitude, picks, ext, begins, factors)
            for side in range(2):
                lanes = pl.ds(side * LANES, LANES)
                live = lane + (2 * couple + side) * LANES < points[first_lat + latitude]
                value = partial[latitude, couple, :, lanes] + totals[side]
                grid[latitude, couple, :, lanes] = jnp.where(live, value, 0.0)
    for latitude in range(lat_count):
        rows = grid[latitude].reshape(couples * SUB, 2 * LANES).astype(jnp.bfloat16)
        for at in range(0, columns, width):
            real = jnp.dot(
                rows, table[latitude, :, at : at + width], preferred_element_type=jnp.float32
            )
            imag = jnp.dot(
                rows,
                table[latitude, :, columns + at : columns + at + width],
                preferred_element_type=jnp.float32,
            )
            cosine = jnp.zeros((SUB, width), jnp.float32)
            sine = jnp.zeros((SUB, width), jnp.float32)
            for couple in range(couples):
                turn_cos = twiddle[latitude, couple : couple + 1, at : at + width]
                turn_sin = twiddle[latitude, couple : couple + 1, columns + at : columns + at + width]
                here = slice(couple * SUB, (couple + 1) * SUB)
                cosine = cosine + (real[here] * turn_cos - imag[here] * turn_sin)
                sine = sine - (real[here] * turn_sin + imag[here] * turn_cos)
            waves[latitude, 0:SUB, at : at + width] = cosine
            waves[latitude, SUB : 2 * SUB, at : at + width] = sine
        waves[latitude, :, columns:] = jnp.zeros((2 * SUB, waves.shape[2] - columns), jnp.float32)
        used = columns // owners
        for owner in range(owners):
            out[owner, 2 * SUB * latitude : 2 * SUB * (latitude + 1), :] = waves[
                latitude, :, owner * used : owner * used + LANES
            ].astype(jnp.bfloat16)


def legendre_kernel(
    level_count, field_count, thickness, received, totals, legendre, out, wide, left, planes, sent,
):
    owners = received.shape[0]
    lat_total = wide.shape[0] // (2 * SUB)
    pair_count, _, degrees = legendre.shape
    pair_total = pair_count * owners
    groups = [(at, min(SUB, pair_count - at)) for at in range(0, pair_count, SUB)]
    keys = [(field, part) for field in range(field_count + 1) for part in range(2)]
    level_place = lax.axis_index("lev")
    first_pair = lax.axis_index("lat") * pair_count
    wide[...] = received[...].astype(jnp.float32).reshape(wide.shape)
    lines = {}
    for part in range(2):
        running = jnp.zeros((lat_total, LANES), jnp.float32)
        for other in range(1, totals.shape[0]):
            running = running + jnp.where(other > level_place, totals[other, part], 0.0)
        for level in reversed(range(level_count)):
            for field in range(field_count):
                place = part * SUB + level * field_count + field
                lines[level, field, part] = wide[pl.ds(place, lat_total, stride=2 * SUB), :]
            running = running + thickness[level] * (
                lines[level, 2, part] + 0.61 * lines[level, 3, part]
            )
            lines[level, field_count, part] = running
    depth = SUB * lat_total
    spread = (
        lax.broadcasted_iota(jnp.int32, (lat_total, depth), 0)
        == lax.broadcasted_iota(jnp.int32, (lat_total, depth), 1) % lat_total
    ).astype(jnp.bfloat16)
    keep = (
        lax.broadcasted_iota(jnp.int32, (SUB, depth), 0)
        == lax.broadcasted_iota(jnp.int32, (SUB, depth), 1) // lat_total
    )
    keys = [(level,) + key for level in range(level_count) for key in keys]
    half = len(keys) * SUB
    for place in range(0, len(keys), 2):
        couple = [
            lax.dot_general(
                lines[key].astype(jnp.bfloat16),
                spread,
                (((0,), (0,)), ((), ())),
                preferred_element_type=jnp.float32,
            )
            for key in keys[place : place + 2]
        ]
        for member in range(2):
            for group, (at, _) in enumerate(groups):
                begin = member * pair_count + at
                pieces = [jnp.where(keep, one[begin : begin + SUB], 0.0) for one in couple]
                into = member * half + place * SUB
                left[group, into : into + 2 * SUB, :] = jnp.concatenate(pieces, axis=0).astype(
                    jnp.bfloat16
                )
    copies = []
    for start in range(0, degrees, 256):
        stop = min(start + 256, degrees)
        low = 0 if start < 2 * pair_total else half
        high = 2 * half if stop > pair_total + 1 else half
        parts = []
        for group, (at, size) in enumerate(groups):
            values = legendre[at : at + size, :, start:stop].reshape(size * lat_total, stop - start)
            sums = jnp.dot(
                left[group, low:high, : size * lat_total],
                values,
                preferred_element_type=jnp.float32,
            ).reshape((high - low) // SUB, SUB, stop - start)
            if high - low > half:
                shape = (SUB, stop - start)
                slot = lax.broadcasted_iota(jnp.int32, shape, 1) + start
                pair = lax.broadcasted_iota(jnp.int32, shape, 0) + (first_pair + at)
                sums = jnp.where(
                    slot + pair < 2 * pair_total, sums[: len(keys)], sums[len(keys) :]
                )
            parts.append(sums[:, :size])
        planes[:, :, :, :, start:stop] = (
            jnp.concatenate(parts, axis=1).astype(jnp.bfloat16).reshape(planes.shape[:4] + (stop - start,))
        )
        here = pl.ds(start, stop - start)
        copies.append(
            pltpu.make_async_copy(
                planes.at[:, :, :, :, here], out.at[:, :, :, :, here], sent.at[len(copies)]
            )
        )
        copies[-1].start()
    for copy in copies:
        copy.wait()


def held(value):
    return pltpu.with_memory_space_constraint(value, pltpu.HBM)


def local(fields, rows_first, points, starts, weights, thickness, legendre):
    level_count, field_count, lat_count, lon_count = fields.shape
    pair_count, lat_total, degrees = legendre.shape
    owners = lax.axis_size("lat")
    couples = lon_count // (2 * LANES)
    blocks = 2 * couples
    columns = 2 * owners * pair_count
    sides = []
    for first in (1, 0):
        edges = [(i, i + 1) for i in range(first, owners - 1, 2)]
        sides.append(lax.ppermute(fields, "lat", edges + [(j, i) for i, j in edges]))

    scalar = pl.BlockSpec(memory_space=pltpu.SMEM)
    vector = pl.BlockSpec(memory_space=pltpu.VMEM)
    params = pltpu.CompilerParams(vmem_limit_bytes=LIMIT)
    remote = pl.BlockSpec(memory_space=pltpu.HBM)
    scalars = [
        pltpu.SMEM(rows_first.shape, jnp.int32),
        pltpu.SMEM(points.shape, jnp.int32),
    ]
    partial, table, twiddle, begins, factors = pl.pallas_call(
        functools.partial(near_kernel, pair_count * owners, pair_count),
        out_shape=(
            jax.ShapeDtypeStruct((lat_count, couples, SUB, 2 * LANES), jnp.float32),
            jax.ShapeDtypeStruct((lat_count, 2 * LANES, 2 * columns), jnp.bfloat16),
            jax.ShapeDtypeStruct((lat_count, couples, 2 * columns), jnp.float32),
            jax.ShapeDtypeStruct((lat_count, STENCIL, blocks, 1, LANES), jnp.int32),
            jax.ShapeDtypeStruct((weights.size // LANES, LANES), jnp.float32),
        ),
        in_specs=[remote] * 5,
        out_specs=(vector,) * 5,
        scratch_shapes=scalars
        + [
            pltpu.VMEM(fields.shape, fields.dtype),
            pltpu.VMEM(starts.shape, starts.dtype),
            pltpu.VMEM(weights.shape, weights.dtype),
            pltpu.VMEM((fields.size // LANES, LANES), jnp.float32),
            pltpu.VMEM((lat_count, blocks + 2, SUB, LANES), jnp.float32),
            pltpu.SemaphoreType.DMA((5,)),
        ],
        compiler_params=params,
        cost_estimate=pl.CostEstimate(flops=10_000_000, bytes_accessed=4_000_000, transcendentals=0),
        name="near_rows",
    )(*(held(value) for value in (rows_first, points, fields, starts, weights)))

    coefficients = pl.pallas_call(
        far_kernel,
        out_shape=jax.ShapeDtypeStruct((owners, 2 * SUB * lat_count, LANES), jnp.bfloat16),
        in_specs=[remote] * 2 + [vector] * 7,
        out_specs=vector,
        scratch_shapes=scalars
        + [
            pltpu.VMEM((2, fields.size // LANES, LANES), jnp.float32),
            pltpu.VMEM((2 * lat_count, blocks + 2, SUB, LANES), jnp.float32),
            pltpu.VMEM((lat_count, couples, SUB, 2 * LANES), jnp.float32),
            pltpu.VMEM((lat_count, 2 * SUB, columns + LANES), jnp.float32),
            pltpu.SemaphoreType.DMA((2,)),
        ],
        compiler_params=params,
        name="far_rows",
    )(held(rows_first), held(points), *sides, begins, factors, partial, table, twiddle)

    received = lax.all_to_all(coefficients, "lat", split_axis=0, concat_axis=0, tiled=True)
    by_level = received.reshape(lat_total, 2, level_count, field_count, LANES).astype(jnp.float32)
    virtual = by_level[:, :, :, 2] + 0.61 * by_level[:, :, :, 3]
    total = jnp.sum(thickness[None, None, :, None] * virtual, axis=2).transpose(1, 0, 2)
    totals = lax.all_gather(total, "lev")

    out_shape = (level_count, field_count + 1, 2, pair_count, degrees)
    half = level_count * (field_count + 1) * 2 * SUB
    group_count = (pair_count + SUB - 1) // SUB
    return pl.pallas_call(
        functools.partial(legendre_kernel, level_count, field_count),
        out_shape=jax.ShapeDtypeStruct(out_shape, jnp.bfloat16),
        in_specs=[scalar, vector, vector, vector],
        out_specs=pl.BlockSpec(memory_space=pl.ANY),
        scratch_shapes=[
            pltpu.VMEM((lat_total * 2 * SUB, LANES), jnp.float32),
            pltpu.VMEM((group_count, 2 * half, SUB * lat_total), jnp.bfloat16),
            pltpu.VMEM(out_shape, jnp.bfloat16),
            pltpu.SemaphoreType.DMA(((degrees + 255) // 256,)),
        ],
        compiler_params=params,
        name="degree_sums",
    )(thickness, received, totals, legendre)


def solution(mesh):
    placed = (
        P("lev", None, "lat", None),
        P("lat"),
        P(),
        P("lat", None, None),
        P("lat", None, None, None),
        P("lev"),
        P("lat", None, None),
    )
    return jax.shard_map(
        local,
        mesh=mesh,
        in_specs=placed,
        out_specs=P("lev", None, None, "lat", None),
        check_vma=False,
    )
```

```python
import functools

import jax
import jax.numpy as jnp
import numpy as np
from jax import lax
from jax.experimental import pallas as pl
from jax.experimental.pallas import tpu as pltpu
from jax.sharding import PartitionSpec as P

LANES = 128
SUB = 8
HALF = 64
STENCIL = 4
LIMIT = 24 * 1024 * 1024


def lane_gather(values, lanes):
    return jnp.take_along_axis(values, lanes, axis=1, mode="promise_in_bounds")


SINE = (-70.99342854244645, 81.34076844400118, -41.337142359536955, 6.283164044230117)
COSINE = (
    56.2423804697887, -85.2403304160897, 64.93459063550272, -19.739171434929204, 0.9999999534680867,
)


def polynomial(terms, square):
    value = np.float32(terms[0])
    for term in terms[1:]:
        value = value * square + np.float32(term)
    return value


def turn_parts(product, total, inverse):
    turns = (product - jnp.floor(product * inverse + 0.5) * total) * inverse
    halves = jnp.floor(2.0 * turns + 0.5)
    sign = 1.0 - 2.0 * jnp.abs(halves)
    part = turns - 0.5 * halves
    square = part * part
    return sign * polynomial(COSINE, square), (sign * part) * polynomial(SINE, square)


def wavenumbers(at, width, pair_count, pair_total):
    column = lax.broadcasted_iota(jnp.int32, (1, width), 1).astype(jnp.float32) + float(at)
    owner = jnp.floor((column + 0.5) * (1.0 / (2 * pair_count)))
    inner = column - owner * (2.0 * pair_count)
    second = inner >= pair_count
    pair = owner * pair_count + jnp.where(second, inner - pair_count, inner)
    return jnp.where(second, 2.0 * pair_total - 1.0 - pair, pair)


def multiplied(one, two):
    return one[0] * two[0] - one[1] * two[1], one[0] * two[1] + one[1] * two[0]


def row_of(pair, row):
    return tuple(part[row : row + 1] for part in pair)


def extend(lines, row, rows_each, missing, ext, slot):
    blocks = ext.shape[1] - 2
    for block in range(blocks):
        ext[slot, block + 1] = lines[
            pl.ds(block * rows_each + row, SUB, stride=blocks * rows_each), :
        ]
    lane = lax.broadcasted_iota(jnp.int32, (SUB, LANES), 1)
    ahead = lane + missing
    behind = lane - missing
    first = lane_gather(ext[slot, 1], ahead & (LANES - 1))
    second = lane_gather(ext[slot, 2], ahead & (LANES - 1))
    last = ext[slot, blocks]
    final = lane_gather(last, behind & (LANES - 1))
    before = lane_gather(ext[slot, blocks - 1], behind & (LANES - 1))
    ext[slot, 0] = jnp.where(behind >= 0, final, before)
    ext[slot, blocks] = jnp.where(ahead < LANES, last, first)
    ext[slot, blocks + 1] = jnp.where(ahead < LANES, first, second)


def spread_rows(starts, begins):
    lat_count, _, blocks = begins.shape[:3]
    for latitude in range(lat_count):
        for block in range(blocks):
            for row in range(STENCIL):
                lanes = slice(block * LANES, (block + 1) * LANES)
                begins[latitude, row, block] = (
                    starts[latitude, row : row + 1, lanes] - (block - 1) * LANES
                )


def spread_lines(source, lines):
    first, second, rows, lon = source.shape
    at = 0
    for one in range(first):
        for two in range(second):
            values = source[one, two].astype(jnp.float32)
            for block in range(lon // LANES):
                lines[at : at + rows, :] = values[:, block * LANES : (block + 1) * LANES]
                at += rows


def gathered(couple, latitude, picks, ext, begins, factors):
    totals = [jnp.zeros((SUB, LANES), jnp.float32) for _ in range(2)]
    couples = begins.shape[2] // 2
    for row, slot in picks:
        at = ((latitude * STENCIL + row) * couples + couple) * SUB
        scale = factors[pl.ds(pl.multiple_of(at, SUB), SUB), :]
        parts = [ext[slot, 2 * couple + piece] for piece in range(4)]
        for side in range(2):
            start = jnp.broadcast_to(begins[latitude, row, 2 * couple + side], (SUB, LANES))
            for column in range(4):
                place = start + column
                lane = place & (LANES - 1)
                low, middle, high = [
                    lane_gather(part, lane) for part in parts[side : side + 3]
                ]
                value = jnp.where(place < LANES, low, jnp.where(place < 2 * LANES, middle, high))
                line = STENCIL * side + column
                totals[side] = totals[side] + scale[line : line + 1] * value
    return totals


def near_kernel(
    pair_total, pair_count, rows_first_far, points_far, fields_far, starts_far, weights_far,
    partial, table, twiddle, begins, factors,
    rows_first, points, fields, starts, weights, lines, ext, arrived,
):
    lat_count, couples = partial.shape[:2]
    lon = 2 * couples * LANES
    columns = table.shape[2] // 2
    first_lat = lax.axis_index("lat") * lat_count
    fetches = [
        pltpu.make_async_copy(source, target, arrived.at[place])
        for place, (source, target) in enumerate(
            (
                (points_far, points),
                (rows_first_far, rows_first),
                (starts_far, starts),
                (weights_far, weights),
                (fields_far, fields),
            )
        )
    ]
    for fetch in fetches:
        fetch.start()
    fetches[0].wait()
    width = 256
    scales = []
    for latitude in range(lat_count):
        total = jnp.full((1, 1), points[first_lat + latitude], jnp.int32).astype(jnp.float32)
        inverse = 1.0 / total
        scales.append((total, inverse, jnp.sqrt(2.0 * inverse)))
    few = lax.broadcasted_iota(jnp.int32, (SUB, width), 0).astype(jnp.float32)
    many = lax.broadcasted_iota(jnp.int32, (couples + 3, width), 0)
    many = jnp.where(many < couples, many * (2 * LANES), (many - (couples - 1)) * HALF)
    many = many.astype(jnp.float32)
    for at in range(0, columns, width):
        numbers = wavenumbers(at, width, pair_count, pair_total)
        for latitude, (total, inverse, scaling) in enumerate(scales):
            ones = turn_parts(numbers * few, total, inverse)
            eights = turn_parts(numbers * (few * float(SUB)), total, inverse)
            large = turn_parts(numbers * many, total, inverse)
            here = slice(at, at + width)
            there = slice(columns + at, columns + at + width)
            twiddle[latitude, :, here] = scaling * large[0][:couples]
            twiddle[latitude, :, there] = scaling * large[1][:couples]
            products = [ones] + [multiplied(row_of(eights, row), ones) for row in range(1, SUB)]
            block = tuple(jnp.concatenate(parts, axis=0) for parts in zip(*products))
            for quarter in range(4):
                turned = block
                if quarter > 0:
                    turned = multiplied(row_of(large, couples + quarter - 1), block)
                rows = slice(HALF * quarter, HALF * (quarter + 1))
                table[latitude, rows, here] = turned[0].astype(jnp.bfloat16)
                table[latitude, rows, there] = turned[1].astype(jnp.bfloat16)
    for fetch in fetches[1:]:
        fetch.wait()
    spread_rows(starts, begins)
    spread_lines(weights, factors)
    spread_lines(fields, lines)
    for latitude in range(lat_count):
        extend(lines, latitude, lat_count, lon - points[first_lat + latitude], ext, latitude)
    for latitude in range(lat_count):
        mine = first_lat - rows_first[latitude]
        picks = [(mine + row, row) for row in range(lat_count)]
        for couple in range(couples):
            totals = gathered(couple, latitude, picks, ext, begins, factors)
            for side in range(2):
                partial[latitude, couple, :, side * LANES : (side + 1) * LANES] = totals[side]


def far_kernel(
    rows_first_far, points_far, near_side, far_side, begins, factors, partial, table, twiddle,
    out, rows_first, points, lines, ext, grid, waves, arrived,
):
    fetches = [
        pltpu.make_async_copy(points_far, points, arrived.at[0]),
        pltpu.make_async_copy(rows_first_far, rows_first, arrived.at[1]),
    ]
    for fetch in fetches:
        fetch.start()
    lat_count, couples = partial.shape[:2]
    lon = 2 * couples * LANES
    columns = table.shape[2] // 2
    owners = out.shape[0]
    first_lat = lax.axis_index("lat") * lat_count
    lat_total = points.shape[0]
    toward = 1 - lax.axis_index("lat") % 2
    spread_lines(near_side.at[toward], lines.at[toward])
    spread_lines(far_side.at[1 - toward], lines.at[1 - toward])
    for fetch in fetches:
        fetch.wait()
    for side in range(2):
        for row in range(lat_count):
            if side == 0:
                place = jnp.maximum(first_lat - lat_count + row, 0)
            else:
                place = jnp.minimum(first_lat + lat_count + row, lat_total - 1)
            extend(
                lines.at[side], row, lat_count, lon - points[place], ext, side * lat_count + row
            )
    lane = lax.broadcasted_iota(jnp.int32, (SUB, LANES), 1)
    width = 256
    for latitude in range(lat_count):
        mine = first_lat - rows_first[latitude]
        one_row = jnp.where(mine >= 1, 0, 2)
        two_row = jnp.where(mine <= 1, 3, 1)
        picks = []
        for row in (one_row, two_row):
            picks.append((row, jnp.where(row < mine, row - mine + lat_count, row - mine)))
        for couple in range(couples):
            totals = gathered(couple, latitude, picks, ext, begins, factors)
            for side in range(2):
                lanes = pl.ds(side * LANES, LANES)
                live = lane + (2 * couple + side) * LANES < points[first_lat + latitude]
                value = partial[latitude, couple, :, lanes] + totals[side]
                grid[latitude, couple, :, lanes] = jnp.where(live, value, 0.0)
    for latitude in range(lat_count):
        rows = grid[latitude].reshape(couples * SUB, 2 * LANES).astype(jnp.bfloat16)
        for at in range(0, columns, width):
            real = jnp.dot(
                rows, table[latitude, :, at : at + width], preferred_element_type=jnp.float32
            )
            imag = jnp.dot(
                rows,
                table[latitude, :, columns + at : columns + at + width],
                preferred_element_type=jnp.float32,
            )
            cosine = jnp.zeros((SUB, width), jnp.float32)
            sine = jnp.zeros((SUB, width), jnp.float32)
            for couple in range(couples):
                turn_cos = twiddle[latitude, couple : couple + 1, at : at + width]
                turn_sin = twiddle[latitude, couple : couple + 1, columns + at : columns + at + width]
                here = slice(couple * SUB, (couple + 1) * SUB)
                cosine = cosine + (real[here] * turn_cos - imag[here] * turn_sin)
                sine = sine - (real[here] * turn_sin + imag[here] * turn_cos)
            waves[latitude, 0:SUB, at : at + width] = cosine
            waves[latitude, SUB : 2 * SUB, at : at + width] = sine
        waves[latitude, :, columns:] = jnp.zeros((2 * SUB, waves.shape[2] - columns), jnp.float32)
        used = columns // owners
        for owner in range(owners):
            out[owner, 2 * SUB * latitude : 2 * SUB * (latitude + 1), :] = waves[
                latitude, :, owner * used : owner * used + LANES
            ].astype(jnp.bfloat16)


def legendre_kernel(
    level_count, field_count, thickness, received, totals, legendre, out, wide, left, planes, sent,
):
    owners = received.shape[0]
    lat_total = wide.shape[0] // (2 * SUB)
    pair_count, _, degrees = legendre.shape
    pair_total = pair_count * owners
    groups = [(at, min(SUB, pair_count - at)) for at in range(0, pair_count, SUB)]
    keys = [(field, part) for field in range(field_count + 1) for part in range(2)]
    level_place = lax.axis_index("lev")
    first_pair = lax.axis_index("lat") * pair_count
    wide[...] = received[...].astype(jnp.float32).reshape(wide.shape)
    lines = {}
    for part in range(2):
        running = jnp.zeros((lat_total, LANES), jnp.float32)
        for other in range(1, totals.shape[0]):
            running = running + jnp.where(other > level_place, totals[other, part], 0.0)
        for level in reversed(range(level_count)):
            for field in range(field_count):
                place = part * SUB + level * field_count + field
                lines[level, field, part] = wide[pl.ds(place, lat_total, stride=2 * SUB), :]
            running = running + thickness[level] * (
                lines[level, 2, part] + 0.61 * lines[level, 3, part]
            )
            lines[level, field_count, part] = running
    depth = SUB * lat_total
    spread = (
        lax.broadcasted_iota(jnp.int32, (lat_total, depth), 0)
        == lax.broadcasted_iota(jnp.int32, (lat_total, depth), 1) % lat_total
    ).astype(jnp.bfloat16)
    keep = (
        lax.broadcasted_iota(jnp.int32, (SUB, depth), 0)
        == lax.broadcasted_iota(jnp.int32, (SUB, depth), 1) // lat_total
    )
    keys = [(level,) + key for level in range(level_count) for key in keys]
    half = len(keys) * SUB
    for place in range(0, len(keys), 2):
        couple = [
            lax.dot_general(
                lines[key].astype(jnp.bfloat16),
                spread,
                (((0,), (0,)), ((), ())),
                preferred_element_type=jnp.float32,
            )
            for key in keys[place : place + 2]
        ]
        for member in range(2):
            for group, (at, _) in enumerate(groups):
                begin = member * pair_count + at
                pieces = [jnp.where(keep, one[begin : begin + SUB], 0.0) for one in couple]
                into = member * half + place * SUB
                left[group, into : into + 2 * SUB, :] = jnp.concatenate(pieces, axis=0).astype(
                    jnp.bfloat16
                )
    copies = []
    for start in range(0, degrees, 256):
        stop = min(start + 256, degrees)
        low = 0 if start < 2 * pair_total else half
        high = 2 * half if stop > pair_total + 1 else half
        parts = []
        for group, (at, size) in enumerate(groups):
            values = legendre[at : at + size, :, start:stop].reshape(size * lat_total, stop - start)
            sums = jnp.dot(
                left[group, low:high, : size * lat_total],
                values,
                preferred_element_type=jnp.float32,
            ).reshape((high - low) // SUB, SUB, stop - start)
            if high - low > half:
                shape = (SUB, stop - start)
                slot = lax.broadcasted_iota(jnp.int32, shape, 1) + start
                pair = lax.broadcasted_iota(jnp.int32, shape, 0) + (first_pair + at)
                sums = jnp.where(
                    slot + pair < 2 * pair_total, sums[: len(keys)], sums[len(keys) :]
                )
            parts.append(sums[:, :size])
        planes[:, :, :, :, start:stop] = (
            jnp.concatenate(parts, axis=1).astype(jnp.bfloat16).reshape(planes.shape[:4] + (stop - start,))
        )
        here = pl.ds(start, stop - start)
        copies.append(
            pltpu.make_async_copy(
                planes.at[:, :, :, :, here], out.at[:, :, :, :, here], sent.at[len(copies)]
            )
        )
        copies[-1].start()
    for copy in copies:
        copy.wait()


def held(value):
    return pltpu.with_memory_space_constraint(value, pltpu.HBM)


def local(fields, rows_first, points, starts, weights, thickness, legendre):
    level_count, field_count, lat_count, lon_count = fields.shape
    pair_count, lat_total, degrees = legendre.shape
    owners = lax.axis_size("lat")
    couples = lon_count // (2 * LANES)
    blocks = 2 * couples
    columns = 2 * owners * pair_count
    sides = []
    for first in range(2):
        pairs = [[i, (i + 1) % owners] for i in range(first, owners, 2)]
        sides.append(lax.all_gather(fields, "lat", axis_index_groups=pairs))

    scalar = pl.BlockSpec(memory_space=pltpu.SMEM)
    vector = pl.BlockSpec(memory_space=pltpu.VMEM)
    params = pltpu.CompilerParams(vmem_limit_bytes=LIMIT)
    remote = pl.BlockSpec(memory_space=pltpu.HBM)
    scalars = [
        pltpu.SMEM(rows_first.shape, jnp.int32),
        pltpu.SMEM(points.shape, jnp.int32),
    ]
    partial, table, twiddle, begins, factors = pl.pallas_call(
        functools.partial(near_kernel, pair_count * owners, pair_count),
        out_shape=(
            jax.ShapeDtypeStruct((lat_count, couples, SUB, 2 * LANES), jnp.float32),
            jax.ShapeDtypeStruct((lat_count, 2 * LANES, 2 * columns), jnp.bfloat16),
            jax.ShapeDtypeStruct((lat_count, couples, 2 * columns), jnp.float32),
            jax.ShapeDtypeStruct((lat_count, STENCIL, blocks, 1, LANES), jnp.int32),
            jax.ShapeDtypeStruct((weights.size // LANES, LANES), jnp.float32),
        ),
        in_specs=[remote] * 5,
        out_specs=(vector,) * 5,
        scratch_shapes=scalars
        + [
            pltpu.VMEM(fields.shape, fields.dtype),
            pltpu.VMEM(starts.shape, starts.dtype),
            pltpu.VMEM(weights.shape, weights.dtype),
            pltpu.VMEM((fields.size // LANES, LANES), jnp.float32),
            pltpu.VMEM((lat_count, blocks + 2, SUB, LANES), jnp.float32),
            pltpu.SemaphoreType.DMA((5,)),
        ],
        compiler_params=params,
        cost_estimate=pl.CostEstimate(flops=10_000_000, bytes_accessed=4_000_000, transcendentals=0),
        name="near_rows",
    )(*(held(value) for value in (rows_first, points, fields, starts, weights)))

    coefficients = pl.pallas_call(
        far_kernel,
        out_shape=jax.ShapeDtypeStruct((owners, 2 * SUB * lat_count, LANES), jnp.bfloat16),
        in_specs=[remote] * 2 + [vector] * 7,
        out_specs=vector,
        scratch_shapes=scalars
        + [
            pltpu.VMEM((2, fields.size // LANES, LANES), jnp.float32),
            pltpu.VMEM((2 * lat_count, blocks + 2, SUB, LANES), jnp.float32),
            pltpu.VMEM((lat_count, couples, SUB, 2 * LANES), jnp.float32),
            pltpu.VMEM((lat_count, 2 * SUB, columns + LANES), jnp.float32),
            pltpu.SemaphoreType.DMA((2,)),
        ],
        compiler_params=params,
        name="far_rows",
    )(held(rows_first), held(points), *sides, begins, factors, partial, table, twiddle)

    received = lax.all_to_all(coefficients, "lat", split_axis=0, concat_axis=0, tiled=True)
    by_level = received.reshape(lat_total, 2, level_count, field_count, LANES).astype(jnp.float32)
    virtual = by_level[:, :, :, 2] + 0.61 * by_level[:, :, :, 3]
    total = jnp.sum(thickness[None, None, :, None] * virtual, axis=2).transpose(1, 0, 2)
    totals = lax.all_gather(total, "lev")

    out_shape = (level_count, field_count + 1, 2, pair_count, degrees)
    half = level_count * (field_count + 1) * 2 * SUB
    group_count = (pair_count + SUB - 1) // SUB
    return pl.pallas_call(
        functools.partial(legendre_kernel, level_count, field_count),
        out_shape=jax.ShapeDtypeStruct(out_shape, jnp.bfloat16),
        in_specs=[scalar, vector, vector, vector],
        out_specs=pl.BlockSpec(memory_space=pl.ANY),
        scratch_shapes=[
            pltpu.VMEM((lat_total * 2 * SUB, LANES), jnp.float32),
            pltpu.VMEM((group_count, 2 * half, SUB * lat_total), jnp.bfloat16),
            pltpu.VMEM(out_shape, jnp.bfloat16),
            pltpu.SemaphoreType.DMA(((degrees + 255) // 256,)),
        ],
        compiler_params=params,
        name="degree_sums",
    )(thickness, received, totals, legendre)


def solution(mesh):
    placed = (
        P("lev", None, "lat", None),
        P("lat"),
        P(),
        P("lat", None, None),
        P("lat", None, None, None),
        P("lev"),
        P("lat", None, None),
    )
    return jax.shard_map(
        local,
        mesh=mesh,
        in_specs=placed,
        out_specs=P("lev", None, None, "lat", None),
        check_vma=False,
    )
```

```python
import functools

import jax
import jax.numpy as jnp
import numpy as np
from jax import lax
from jax.experimental import pallas as pl
from jax.experimental.pallas import tpu as pltpu
from jax.sharding import PartitionSpec as P

LANES = 128
SUB = 8
HALF = 64
STENCIL = 4
LIMIT = 24 * 1024 * 1024


def lane_gather(values, lanes):
    return jnp.take_along_axis(values, lanes, axis=1, mode="promise_in_bounds")


SINE = (-70.99342854244645, 81.34076844400118, -41.337142359536955, 6.283164044230117)
COSINE = (
    56.2423804697887, -85.2403304160897, 64.93459063550272, -19.739171434929204, 0.9999999534680867,
)


def polynomial(terms, square):
    value = np.float32(terms[0])
    for term in terms[1:]:
        value = value * square + np.float32(term)
    return value


def turn_parts(product, total, inverse):
    turns = (product - jnp.floor(product * inverse + 0.5) * total) * inverse
    halves = jnp.floor(2.0 * turns + 0.5)
    sign = 1.0 - 2.0 * jnp.abs(halves)
    part = turns - 0.5 * halves
    square = part * part
    return sign * polynomial(COSINE, square), (sign * part) * polynomial(SINE, square)


def wavenumbers(at, width, pair_count, pair_total):
    column = lax.broadcasted_iota(jnp.int32, (1, width), 1).astype(jnp.float32) + float(at)
    owner = jnp.floor((column + 0.5) * (1.0 / (2 * pair_count)))
    inner = column - owner * (2.0 * pair_count)
    second = inner >= pair_count
    pair = owner * pair_count + jnp.where(second, inner - pair_count, inner)
    return jnp.where(second, 2.0 * pair_total - 1.0 - pair, pair)


def multiplied(one, two):
    return one[0] * two[0] - one[1] * two[1], one[0] * two[1] + one[1] * two[0]


def row_of(pair, row):
    return tuple(part[row : row + 1] for part in pair)


def extend(lines, row, rows_each, missing, ext, slot):
    blocks = ext.shape[1] - 2
    for block in range(blocks):
        ext[slot, block + 1] = lines[
            pl.ds(block * rows_each + row, SUB, stride=blocks * rows_each), :
        ]
    lane = lax.broadcasted_iota(jnp.int32, (SUB, LANES), 1)
    ahead = lane + missing
    behind = lane - missing
    first = lane_gather(ext[slot, 1], ahead & (LANES - 1))
    second = lane_gather(ext[slot, 2], ahead & (LANES - 1))
    last = ext[slot, blocks]
    final = lane_gather(last, behind & (LANES - 1))
    before = lane_gather(ext[slot, blocks - 1], behind & (LANES - 1))
    ext[slot, 0] = jnp.where(behind >= 0, final, before)
    ext[slot, blocks] = jnp.where(ahead < LANES, last, first)
    ext[slot, blocks + 1] = jnp.where(ahead < LANES, first, second)


def spread_rows(starts, begins):
    lat_count, _, blocks = begins.shape[:3]
    for latitude in range(lat_count):
        for block in range(blocks):
            for row in range(STENCIL):
                lanes = slice(block * LANES, (block + 1) * LANES)
                begins[latitude, row, block] = (
                    starts[latitude, row : row + 1, lanes] - (block - 1) * LANES
                )


def spread_lines(source, lines):
    first, second, rows, lon = source.shape
    at = 0
    for one in range(first):
        for two in range(second):
            values = source[one, two].astype(jnp.float32)
            for block in range(lon // LANES):
                lines[at : at + rows, :] = values[:, block * LANES : (block + 1) * LANES]
                at += rows


def gathered(totals, starts, scale, parts):
    for side in range(2):
        start = jnp.broadcast_to(starts[side], (SUB, LANES))
        for column in range(4):
            place = start + column
            lane = place & (LANES - 1)
            low, middle, high = [lane_gather(part, lane) for part in parts[side : side + 3]]
            value = jnp.where(place < LANES, low, jnp.where(place < 2 * LANES, middle, high))
            line = STENCIL * side + column
            totals[side] = totals[side] + scale[line : line + 1] * value
    return totals


def near_kernel(
    pair_total, pair_count, rows_first_far, points_far, fields_far, starts_far, weights_far,
    partial, table, twiddle, begins, factors, facts,
    rows_first, points, fields, starts, weights, lines, ext, arrived,
):
    lat_count, couples = partial.shape[:2]
    lon = 2 * couples * LANES
    columns = table.shape[2] // 2
    first_lat = lax.axis_index("lat") * lat_count
    fetches = [
        pltpu.make_async_copy(source, target, arrived.at[place])
        for place, (source, target) in enumerate(
            (
                (points_far, points),
                (rows_first_far, rows_first),
                (starts_far, starts),
                (weights_far, weights),
                (fields_far, fields),
            )
        )
    ]
    for fetch in fetches:
        fetch.start()
    fetches[0].wait()
    width = 256
    scales = []
    for latitude in range(lat_count):
        total = jnp.full((1, 1), points[first_lat + latitude], jnp.int32).astype(jnp.float32)
        inverse = 1.0 / total
        scales.append((total, inverse, jnp.sqrt(2.0 * inverse)))
    few = lax.broadcasted_iota(jnp.int32, (SUB, width), 0).astype(jnp.float32)
    many = lax.broadcasted_iota(jnp.int32, (couples + 3, width), 0)
    many = jnp.where(many < couples, many * (2 * LANES), (many - (couples - 1)) * HALF)
    many = many.astype(jnp.float32)
    for at in range(0, columns, width):
        numbers = wavenumbers(at, width, pair_count, pair_total)
        for latitude, (total, inverse, scaling) in enumerate(scales):
            ones = turn_parts(numbers * few, total, inverse)
            eights = turn_parts(numbers * (few * float(SUB)), total, inverse)
            large = turn_parts(numbers * many, total, inverse)
            here = slice(at, at + width)
            there = slice(columns + at, columns + at + width)
            twiddle[latitude, :, here] = scaling * large[0][:couples]
            twiddle[latitude, :, there] = scaling * large[1][:couples]
            products = [ones] + [multiplied(row_of(eights, row), ones) for row in range(1, SUB)]
            block = tuple(jnp.concatenate(parts, axis=0) for parts in zip(*products))
            for quarter in range(4):
                turned = block
                if quarter > 0:
                    turned = multiplied(row_of(large, couples + quarter - 1), block)
                rows = slice(HALF * quarter, HALF * (quarter + 1))
                table[latitude, rows, here] = turned[0].astype(jnp.bfloat16)
                table[latitude, rows, there] = turned[1].astype(jnp.bfloat16)
    for fetch in fetches[1:]:
        fetch.wait()
    known = [first_lat - rows_first[latitude] for latitude in range(lat_count)]
    known += [points[first_lat + latitude] for latitude in range(lat_count)]
    for place in range(-lat_count, 2 * lat_count):
        if place < 0 or place >= lat_count:
            place = jnp.clip(first_lat + place, 0, points.shape[0] - 1)
            known.append(lon - points[place])
    facts[...] = jnp.concatenate([jnp.full((1, LANES), one, jnp.int32) for one in known], axis=0)
    spread_rows(starts, begins)
    spread_lines(weights, factors)
    spread_lines(fields, lines)
    for latitude in range(lat_count):
        extend(lines, latitude, lat_count, lon - points[first_lat + latitude], ext, latitude)
    for latitude in range(lat_count):
        mine = first_lat - rows_first[latitude]
        for couple in range(couples):
            totals = [jnp.zeros((SUB, LANES), jnp.float32) for _ in range(2)]
            for slot in range(lat_count):
                row = mine + slot
                at = ((latitude * STENCIL + row) * couples + couple) * SUB
                totals = gathered(
                    totals,
                    [begins[latitude, row, 2 * couple + side] for side in range(2)],
                    factors[pl.ds(pl.multiple_of(at, SUB), SUB), :],
                    [ext[slot, 2 * couple + piece] for piece in range(4)],
                )
            for side in range(2):
                partial[latitude, couple, :, side * LANES : (side + 1) * LANES] = totals[side]


def far_kernel(
    near_side, far_side, begins, factors, facts, partial, table, twiddle,
    out, lines, ext, grid, waves,
):
    lat_count, couples = partial.shape[:2]
    columns = table.shape[2] // 2
    owners = out.shape[0]
    toward = 1 - lax.axis_index("lat") % 2
    spread_lines(near_side, lines.at[toward])
    spread_lines(far_side, lines.at[1 - toward])
    fact = [jnp.broadcast_to(facts[row : row + 1], (SUB, LANES)) for row in range(4 * lat_count)]
    for slot in range(2 * lat_count):
        side, row = divmod(slot, lat_count)
        extend(lines.at[side], row, lat_count, fact[2 * lat_count + slot], ext, slot)
    lane = lax.broadcasted_iota(jnp.int32, (SUB, LANES), 1)
    width = 256
    choices = (((2, 0, 0), (2, 1, 0)), ((3, 3, 1), (3, 2, 1)))
    for latitude in range(lat_count):
        at_zero = fact[latitude] == 0
        at_one = fact[latitude] == 1

        def pick(values):
            return jnp.where(at_zero, values[0], jnp.where(at_one, values[1], values[2]))

        def pick_line(values):
            return jnp.where(
                at_zero[:1], values[0], jnp.where(at_one[:1], values[1], values[2])
            )

        for couple in range(couples):
            sides = [pl.ds(side * LANES, LANES) for side in range(2)]
            totals = [partial[latitude, couple, :, lanes] for lanes in sides]
            for rows, slots in choices:
                scales = [
                    factors[pl.ds(((latitude * STENCIL + row) * couples + couple) * SUB, SUB), :]
                    for row in rows
                ]
                starts = [
                    pick_line([begins[latitude, row, 2 * couple + side] for row in rows])
                    for side in range(2)
                ]
                parts = [
                    pick([ext[slot, 2 * couple + piece] for slot in slots]) for piece in range(4)
                ]
                totals = gathered(totals, starts, pick(scales), parts)
            for side in range(2):
                live = lane + (2 * couple + side) * LANES < fact[lat_count + latitude]
                grid[latitude, couple, :, sides[side]] = jnp.where(live, totals[side], 0.0)
    for latitude in range(lat_count):
        rows = grid[latitude].reshape(couples * SUB, 2 * LANES).astype(jnp.bfloat16)
        for at in range(0, columns, width):
            real = jnp.dot(
                rows, table[latitude, :, at : at + width], preferred_element_type=jnp.float32
            )
            imag = jnp.dot(
                rows,
                table[latitude, :, columns + at : columns + at + width],
                preferred_element_type=jnp.float32,
            )
            cosine = jnp.zeros((SUB, width), jnp.float32)
            sine = jnp.zeros((SUB, width), jnp.float32)
            for couple in range(couples):
                turn_cos = twiddle[latitude, couple : couple + 1, at : at + width]
                turn_sin = twiddle[latitude, couple : couple + 1, columns + at : columns + at + width]
                here = slice(couple * SUB, (couple + 1) * SUB)
                cosine = cosine + (real[here] * turn_cos - imag[here] * turn_sin)
                sine = sine - (real[here] * turn_sin + imag[here] * turn_cos)
            waves[latitude, 0:SUB, at : at + width] = cosine
            waves[latitude, SUB : 2 * SUB, at : at + width] = sine
        waves[latitude, :, columns:] = jnp.zeros((2 * SUB, waves.shape[2] - columns), jnp.float32)
        used = columns // owners
        for owner in range(owners):
            out[owner, 2 * SUB * latitude : 2 * SUB * (latitude + 1), :] = waves[
                latitude, :, owner * used : owner * used + LANES
            ].astype(jnp.bfloat16)


def legendre_kernel(
    level_owners, level_count, field_count, thickness, received, totals, legendre, out, wide, left, planes, sent,
):
    owners = received.shape[0]
    lat_total = wide.shape[0] // (2 * SUB)
    pair_count, _, degrees = legendre.shape
    pair_total = pair_count * owners
    groups = [(at, min(SUB, pair_count - at)) for at in range(0, pair_count, SUB)]
    keys = [(field, part) for field in range(field_count + 1) for part in range(2)]
    level_place = lax.axis_index("lev")
    first_pair = lax.axis_index("lat") * pair_count
    wide[...] = received[...].astype(jnp.float32).reshape(wide.shape)
    lines = {}
    for part in range(2):
        running = jnp.zeros((lat_total, LANES), jnp.float32)
        for place in range(totals.shape[0]):
            other = 1 - level_place if level_owners == 2 else place
            running = running + jnp.where(other > level_place, totals[place, part], 0.0)
        for level in reversed(range(level_count)):
            for field in range(field_count):
                place = part * SUB + level * field_count + field
                lines[level, field, part] = wide[pl.ds(place, lat_total, stride=2 * SUB), :]
            running = running + thickness[level] * (
                lines[level, 2, part] + 0.61 * lines[level, 3, part]
            )
            lines[level, field_count, part] = running
    depth = SUB * lat_total
    spread = (
        lax.broadcasted_iota(jnp.int32, (lat_total, depth), 0)
        == lax.broadcasted_iota(jnp.int32, (lat_total, depth), 1) % lat_total
    ).astype(jnp.bfloat16)
    keep = (
        lax.broadcasted_iota(jnp.int32, (SUB, depth), 0)
        == lax.broadcasted_iota(jnp.int32, (SUB, depth), 1) // lat_total
    )
    keys = [(level,) + key for level in range(level_count) for key in keys]
    half = len(keys) * SUB
    for place in range(0, len(keys), 2):
        couple = [
            lax.dot_general(
                lines[key].astype(jnp.bfloat16),
                spread,
                (((0,), (0,)), ((), ())),
                preferred_element_type=jnp.float32,
            )
            for key in keys[place : place + 2]
        ]
        for member in range(2):
            for group, (at, _) in enumerate(groups):
                begin = member * pair_count + at
                pieces = [jnp.where(keep, one[begin : begin + SUB], 0.0) for one in couple]
                into = member * half + place * SUB
                left[group, into : into + 2 * SUB, :] = jnp.concatenate(pieces, axis=0).astype(
                    jnp.bfloat16
                )
    copies = []
    for start in range(0, degrees, 256):
        stop = min(start + 256, degrees)
        low = 0 if start < 2 * pair_total else half
        high = 2 * half if stop > pair_total + 1 else half
        parts = []
        for group, (at, size) in enumerate(groups):
            values = legendre[at : at + size, :, start:stop].reshape(size * lat_total, stop - start)
            sums = jnp.dot(
                left[group, low:high, : size * lat_total],
                values,
                preferred_element_type=jnp.float32,
            ).reshape((high - low) // SUB, SUB, stop - start)
            if high - low > half:
                shape = (SUB, stop - start)
                slot = lax.broadcasted_iota(jnp.int32, shape, 1) + start
                pair = lax.broadcasted_iota(jnp.int32, shape, 0) + (first_pair + at)
                sums = jnp.where(
                    slot + pair < 2 * pair_total, sums[: len(keys)], sums[len(keys) :]
                )
            parts.append(sums[:, :size])
        planes[:, :, :, :, start:stop] = (
            jnp.concatenate(parts, axis=1).astype(jnp.bfloat16).reshape(planes.shape[:4] + (stop - start,))
        )
        here = pl.ds(start, stop - start)
        copies.append(
            pltpu.make_async_copy(
                planes.at[:, :, :, :, here], out.at[:, :, :, :, here], sent.at[len(copies)]
            )
        )
        copies[-1].start()
    for copy in copies:
        copy.wait()


def held(value):
    return pltpu.with_memory_space_constraint(value, pltpu.HBM)


def local(fields, rows_first, points, starts, weights, thickness, legendre):
    level_count, field_count, lat_count, lon_count = fields.shape
    pair_count, lat_total, degrees = legendre.shape
    owners = lax.axis_size("lat")
    couples = lon_count // (2 * LANES)
    blocks = 2 * couples
    columns = 2 * owners * pair_count
    sides = []
    for first in range(2):
        edges = [(i, i + 1) for i in range(first, owners - 1, 2)]
        sides.append(lax.ppermute(fields, "lat", edges + [(j, i) for i, j in edges]))

    scalar = pl.BlockSpec(memory_space=pltpu.SMEM)
    vector = pl.BlockSpec(memory_space=pltpu.VMEM)
    params = pltpu.CompilerParams(vmem_limit_bytes=LIMIT)
    remote = pl.BlockSpec(memory_space=pltpu.HBM)
    partial, table, twiddle, begins, factors, facts = pl.pallas_call(
        functools.partial(near_kernel, pair_count * owners, pair_count),
        out_shape=(
            jax.ShapeDtypeStruct((lat_count, couples, SUB, 2 * LANES), jnp.float32),
            jax.ShapeDtypeStruct((lat_count, 2 * LANES, 2 * columns), jnp.bfloat16),
            jax.ShapeDtypeStruct((lat_count, couples, 2 * columns), jnp.float32),
            jax.ShapeDtypeStruct((lat_count, STENCIL, blocks, 1, LANES), jnp.int32),
            jax.ShapeDtypeStruct((weights.size // LANES, LANES), jnp.float32),
            jax.ShapeDtypeStruct((4 * lat_count, LANES), jnp.int32),
        ),
        in_specs=[remote] * 5,
        out_specs=(vector,) * 6,
        scratch_shapes=[
            pltpu.SMEM(rows_first.shape, jnp.int32),
            pltpu.SMEM(points.shape, jnp.int32),
            pltpu.VMEM(fields.shape, fields.dtype),
            pltpu.VMEM(starts.shape, starts.dtype),
            pltpu.VMEM(weights.shape, weights.dtype),
            pltpu.VMEM((fields.size // LANES, LANES), jnp.float32),
            pltpu.VMEM((lat_count, blocks + 2, SUB, LANES), jnp.float32),
            pltpu.SemaphoreType.DMA((5,)),
        ],
        compiler_params=params,
        cost_estimate=pl.CostEstimate(flops=10_000_000, bytes_accessed=4_000_000, transcendentals=0),
        name="near_rows",
    )(*(held(value) for value in (rows_first, points, fields, starts, weights)))

    coefficients = pl.pallas_call(
        far_kernel,
        out_shape=jax.ShapeDtypeStruct((owners, 2 * SUB * lat_count, LANES), jnp.bfloat16),
        in_specs=[vector] * 8,
        out_specs=vector,
        scratch_shapes=[
            pltpu.VMEM((2, fields.size // LANES, LANES), jnp.float32),
            pltpu.VMEM((2 * lat_count, blocks + 2, SUB, LANES), jnp.float32),
            pltpu.VMEM((lat_count, couples, SUB, 2 * LANES), jnp.float32),
            pltpu.VMEM((lat_count, 2 * SUB, columns + LANES), jnp.float32),
        ],
        compiler_params=params,
        name="far_rows",
    )(*sides, begins, factors, facts, partial, table, twiddle)

    received = lax.all_to_all(coefficients, "lat", split_axis=0, concat_axis=0, tiled=True)
    by_level = received.reshape(lat_total, 2, level_count, field_count, LANES).astype(jnp.float32)
    virtual = by_level[:, :, :, 2] + 0.61 * by_level[:, :, :, 3]
    total = jnp.sum(thickness[None, None, :, None] * virtual, axis=2).transpose(1, 0, 2)
    level_owners = lax.axis_size("lev")
    if level_owners == 2:
        totals = lax.ppermute(total, "lev", [(0, 1), (1, 0)])[None]
    else:
        totals = lax.all_gather(total, "lev")

    out_shape = (level_count, field_count + 1, 2, pair_count, degrees)
    half = level_count * (field_count + 1) * 2 * SUB
    group_count = (pair_count + SUB - 1) // SUB
    return pl.pallas_call(
        functools.partial(legendre_kernel, level_owners, level_count, field_count),
        out_shape=jax.ShapeDtypeStruct(out_shape, jnp.bfloat16),
        in_specs=[scalar, vector, vector, vector],
        out_specs=pl.BlockSpec(memory_space=pl.ANY),
        scratch_shapes=[
            pltpu.VMEM((lat_total * 2 * SUB, LANES), jnp.float32),
            pltpu.VMEM((group_count, 2 * half, SUB * lat_total), jnp.bfloat16),
            pltpu.VMEM(out_shape, jnp.bfloat16),
            pltpu.SemaphoreType.DMA(((degrees + 255) // 256,)),
        ],
        compiler_params=params,
        name="degree_sums",
    )(thickness, received, totals, legendre)


def solution(mesh):
    placed = (
        P("lev", None, "lat", None),
        P("lat"),
        P(),
        P("lat", None, None),
        P("lat", None, None, None),
        P("lev"),
        P("lat", None, None),
    )
    return jax.shard_map(
        local,
        mesh=mesh,
        in_specs=placed,
        out_specs=P("lev", None, None, "lat", None),
        check_vma=False,
    )
```

```python
import functools

import jax
import jax.numpy as jnp
import numpy as np
from jax import lax
from jax.experimental import pallas as pl
from jax.experimental.pallas import tpu as pltpu
from jax.sharding import PartitionSpec as P

LANES = 128
SUB = 8
HALF = 64
STENCIL = 4
LIMIT = 24 * 1024 * 1024


def lane_gather(values, lanes):
    return jnp.take_along_axis(values, lanes, axis=1, mode="promise_in_bounds")


SINE = (-70.99342854244645, 81.34076844400118, -41.337142359536955, 6.283164044230117)
COSINE = (
    56.2423804697887, -85.2403304160897, 64.93459063550272, -19.739171434929204, 0.9999999534680867,
)


def polynomial(terms, square):
    value = np.float32(terms[0])
    for term in terms[1:]:
        value = value * square + np.float32(term)
    return value


def turn_parts(product, total, inverse):
    turns = (product - jnp.floor(product * inverse + 0.5) * total) * inverse
    halves = jnp.floor(2.0 * turns + 0.5)
    sign = 1.0 - 2.0 * jnp.abs(halves)
    part = turns - 0.5 * halves
    square = part * part
    return sign * polynomial(COSINE, square), (sign * part) * polynomial(SINE, square)


def wavenumbers(at, width, pair_count, pair_total):
    column = lax.broadcasted_iota(jnp.int32, (1, width), 1).astype(jnp.float32) + float(at)
    owner = jnp.floor((column + 0.5) * (1.0 / (2 * pair_count)))
    inner = column - owner * (2.0 * pair_count)
    second = inner >= pair_count
    pair = owner * pair_count + jnp.where(second, inner - pair_count, inner)
    return jnp.where(second, 2.0 * pair_total - 1.0 - pair, pair)


def multiplied(one, two):
    return one[0] * two[0] - one[1] * two[1], one[0] * two[1] + one[1] * two[0]


def row_of(pair, row):
    return tuple(part[row : row + 1] for part in pair)


def extend(lines, row, rows_each, missing, ext, slot):
    blocks = ext.shape[1] - 2
    for block in range(blocks):
        ext[slot, block + 1] = lines[
            pl.ds(block * rows_each + row, SUB, stride=blocks * rows_each), :
        ]
    lane = lax.broadcasted_iota(jnp.int32, (SUB, LANES), 1)
    ahead = lane + missing
    behind = lane - missing
    first = lane_gather(ext[slot, 1], ahead & (LANES - 1))
    second = lane_gather(ext[slot, 2], ahead & (LANES - 1))
    last = ext[slot, blocks]
    final = lane_gather(last, behind & (LANES - 1))
    before = lane_gather(ext[slot, blocks - 1], behind & (LANES - 1))
    ext[slot, 0] = jnp.where(behind >= 0, final, before)
    ext[slot, blocks] = jnp.where(ahead < LANES, last, first)
    ext[slot, blocks + 1] = jnp.where(ahead < LANES, first, second)


def spread_rows(starts, begins):
    lat_count, _, blocks = begins.shape[:3]
    for latitude in range(lat_count):
        for block in range(blocks):
            for row in range(STENCIL):
                lanes = slice(block * LANES, (block + 1) * LANES)
                begins[latitude, row, block] = (
                    starts[latitude, row : row + 1, lanes] - (block - 1) * LANES
                )


def spread_lines(source, lines):
    first, second, rows, lon = source.shape
    at = 0
    for one in range(first):
        for two in range(second):
            values = source[one, two].astype(jnp.float32)
            for block in range(lon // LANES):
                lines[at : at + rows, :] = values[:, block * LANES : (block + 1) * LANES]
                at += rows


def gathered(totals, starts, scale, parts):
    for side in range(2):
        start = jnp.broadcast_to(starts[side], (SUB, LANES))
        for column in range(4):
            place = start + column
            lane = place & (LANES - 1)
            low, middle, high = [lane_gather(part, lane) for part in parts[side : side + 3]]
            value = jnp.where(place < LANES, low, jnp.where(place < 2 * LANES, middle, high))
            line = STENCIL * side + column
            totals[side] = totals[side] + scale[line : line + 1] * value
    return totals


def near_kernel(
    pair_total, pair_count, rows_first_far, points_far, fields_far, starts_far, weights_far, side,
    partial, table, twiddle, begins, factors, facts, beside,
    rows_first, points, fields, starts, weights, lines, side_lines, ext, arrived,
):
    lat_count, couples = partial.shape[:2]
    lon = 2 * couples * LANES
    columns = table.shape[2] // 2
    first_lat = lax.axis_index("lat") * lat_count
    fetches = [
        pltpu.make_async_copy(source, target, arrived.at[place])
        for place, (source, target) in enumerate(
            (
                (points_far, points),
                (rows_first_far, rows_first),
                (starts_far, starts),
                (weights_far, weights),
                (fields_far, fields),
            )
        )
    ]
    for fetch in fetches:
        fetch.start()
    spread_lines(side, side_lines)
    for fetch in fetches[:2]:
        fetch.wait()
    known = [first_lat - rows_first[latitude] for latitude in range(lat_count)]
    known += [points[first_lat + latitude] for latitude in range(lat_count)]
    for place in range(-lat_count, 2 * lat_count):
        if place < 0 or place >= lat_count:
            place = jnp.clip(first_lat + place, 0, points.shape[0] - 1)
            known.append(lon - points[place])
    facts[...] = jnp.concatenate([jnp.full((1, LANES), one, jnp.int32) for one in known], axis=0)
    upper = lax.axis_index("lat") % 2 == 0
    for row in range(lat_count):
        missing = jnp.where(upper, known[3 * lat_count + row], known[2 * lat_count + row])
        extend(side_lines, row, lat_count, missing, beside, row)
    width = 256
    scales = []
    for latitude in range(lat_count):
        total = jnp.full((1, 1), points[first_lat + latitude], jnp.int32).astype(jnp.float32)
        inverse = 1.0 / total
        scales.append((total, inverse, jnp.sqrt(2.0 * inverse)))
    few = lax.broadcasted_iota(jnp.int32, (SUB, width), 0).astype(jnp.float32)
    many = lax.broadcasted_iota(jnp.int32, (couples + 3, width), 0)
    many = jnp.where(many < couples, many * (2 * LANES), (many - (couples - 1)) * HALF)
    many = many.astype(jnp.float32)
    for at in range(0, columns, width):
        numbers = wavenumbers(at, width, pair_count, pair_total)
        for latitude, (total, inverse, scaling) in enumerate(scales):
            ones = turn_parts(numbers * few, total, inverse)
            eights = turn_parts(numbers * (few * float(SUB)), total, inverse)
            large = turn_parts(numbers * many, total, inverse)
            here = slice(at, at + width)
            there = slice(columns + at, columns + at + width)
            twiddle[latitude, :, here] = scaling * large[0][:couples]
            twiddle[latitude, :, there] = scaling * large[1][:couples]
            products = [ones] + [multiplied(row_of(eights, row), ones) for row in range(1, SUB)]
            block = tuple(jnp.concatenate(parts, axis=0) for parts in zip(*products))
            for quarter in range(4):
                turned = block
                if quarter > 0:
                    turned = multiplied(row_of(large, couples + quarter - 1), block)
                rows = slice(HALF * quarter, HALF * (quarter + 1))
                table[latitude, rows, here] = turned[0].astype(jnp.bfloat16)
                table[latitude, rows, there] = turned[1].astype(jnp.bfloat16)
    for fetch in fetches[2:]:
        fetch.wait()
    spread_rows(starts, begins)
    spread_lines(weights, factors)
    spread_lines(fields, lines)
    for latitude in range(lat_count):
        extend(lines, latitude, lat_count, lon - points[first_lat + latitude], ext, latitude)
    for latitude in range(lat_count):
        mine = first_lat - rows_first[latitude]
        for couple in range(couples):
            totals = [jnp.zeros((SUB, LANES), jnp.float32) for _ in range(2)]
            for slot in range(lat_count):
                row = mine + slot
                at = ((latitude * STENCIL + row) * couples + couple) * SUB
                totals = gathered(
                    totals,
                    [begins[latitude, row, 2 * couple + side] for side in range(2)],
                    factors[pl.ds(pl.multiple_of(at, SUB), SUB), :],
                    [ext[slot, 2 * couple + piece] for piece in range(4)],
                )
            for side in range(2):
                partial[latitude, couple, :, side * LANES : (side + 1) * LANES] = totals[side]


def far_kernel(
    beside, far_side, begins, factors, facts, partial, table, twiddle,
    out, lines, ext, grid, waves, packed,
):
    lat_count, couples = partial.shape[:2]
    columns = table.shape[2] // 2
    owners = out.shape[0]
    fact = [jnp.broadcast_to(facts[row : row + 1], (SUB, LANES)) for row in range(4 * lat_count)]
    toward = 1 - lax.axis_index("lat") % 2
    ext[pl.ds(toward * lat_count, lat_count)] = beside[...]
    spread_lines(far_side, lines)
    for row in range(lat_count):
        missing = jnp.where(toward == 1, fact[2 * lat_count + row], fact[3 * lat_count + row])
        extend(lines, row, lat_count, missing, ext, (1 - toward) * lat_count + row)
    lane = lax.broadcasted_iota(jnp.int32, (SUB, LANES), 1)
    width = 256
    choices = (((2, 0, 0), (2, 1, 0)), ((3, 3, 1), (3, 2, 1)))
    for latitude in range(lat_count):
        at_zero = fact[latitude] == 0
        at_one = fact[latitude] == 1

        def pick(values):
            return jnp.where(at_zero, values[0], jnp.where(at_one, values[1], values[2]))

        def pick_line(values):
            return jnp.where(
                at_zero[:1], values[0], jnp.where(at_one[:1], values[1], values[2])
            )

        for couple in range(couples):
            sides = [pl.ds(side * LANES, LANES) for side in range(2)]
            totals = [partial[latitude, couple, :, lanes] for lanes in sides]
            for rows, slots in choices:
                scales = [
                    factors[pl.ds(((latitude * STENCIL + row) * couples + couple) * SUB, SUB), :]
                    for row in rows
                ]
                starts = [
                    pick_line([begins[latitude, row, 2 * couple + side] for row in rows])
                    for side in range(2)
                ]
                parts = [
                    pick([ext[slot, 2 * couple + piece] for slot in slots]) for piece in range(4)
                ]
                totals = gathered(totals, starts, pick(scales), parts)
            for side in range(2):
                live = lane + (2 * couple + side) * LANES < fact[lat_count + latitude]
                grid[latitude, couple, :, sides[side]] = jnp.where(live, totals[side], 0.0)
    for latitude in range(lat_count):
        rows = grid[latitude].reshape(couples * SUB, 2 * LANES).astype(jnp.bfloat16)
        for at in range(0, columns, width):
            real = jnp.dot(
                rows, table[latitude, :, at : at + width], preferred_element_type=jnp.float32
            )
            imag = jnp.dot(
                rows,
                table[latitude, :, columns + at : columns + at + width],
                preferred_element_type=jnp.float32,
            )
            cosine = jnp.zeros((SUB, width), jnp.float32)
            sine = jnp.zeros((SUB, width), jnp.float32)
            for couple in range(couples):
                turn_cos = twiddle[latitude, couple : couple + 1, at : at + width]
                turn_sin = twiddle[latitude, couple : couple + 1, columns + at : columns + at + width]
                here = slice(couple * SUB, (couple + 1) * SUB)
                cosine = cosine + (real[here] * turn_cos - imag[here] * turn_sin)
                sine = sine - (real[here] * turn_sin + imag[here] * turn_cos)
            waves[latitude, 0:SUB, at : at + width] = cosine
            waves[latitude, SUB : 2 * SUB, at : at + width] = sine
    used = columns // owners
    for owner in range(owners):
        for latitude in range(lat_count):
            for part in range(2):
                place = (2 * latitude + part) * used
                packed[owner, :, place : place + used] = waves[
                    latitude, part * SUB : (part + 1) * SUB, owner * used : (owner + 1) * used
                ]
        rest = packed.shape[2] - 2 * lat_count * used
        if rest > 0:
            packed[owner, :, packed.shape[2] - rest :] = jnp.zeros((SUB, rest), jnp.float32)
        out[owner] = packed[owner].astype(jnp.bfloat16)


def legendre_kernel(
    level_owners, level_count, field_count, thickness, received, totals, legendre, out, wide, left, planes, sent,
):
    owners = received.shape[0]
    pair_count, lat_total, degrees = legendre.shape
    lat_count = lat_total // owners
    used = 2 * pair_count
    pair_total = pair_count * owners
    groups = [(at, min(SUB, pair_count - at)) for at in range(0, pair_count, SUB)]
    reach = pair_count + len(groups) * SUB
    keys = [(field, part) for field in range(field_count + 1) for part in range(2)]
    level_place = lax.axis_index("lev")
    first_pair = lax.axis_index("lat") * pair_count
    lane_blocks = wide.shape[0]
    for block in range(lane_blocks):
        values = received[:, :, block * LANES : (block + 1) * LANES].astype(jnp.float32)
        wide[block] = values.reshape(wide.shape[1:])


    def unpacked(values, part):
        places = [(2 * latitude + part) * used for latitude in range(lat_count)]
        return jnp.concatenate([values[:, place : place + reach] for place in places], axis=0)

    lines = {}
    for part in range(2):
        running = jnp.zeros((lat_total, reach), jnp.float32)
        for place in range(totals.shape[0]):
            other = 1 - level_place if level_owners == 2 else place
            running = running + jnp.where(other > level_place, unpacked(totals[place], part), 0.0)
        for level in reversed(range(level_count)):
            for field in range(field_count):
                rows = pl.ds(level * field_count + field, owners, stride=SUB)
                values = [wide[block, rows, :] for block in range(lane_blocks)]
                lines[level, field, part] = unpacked(jnp.concatenate(values, axis=1), part)
            running = running + thickness[level] * (
                lines[level, 2, part] + 0.61 * lines[level, 3, part]
            )
            lines[level, field_count, part] = running
    depth = SUB * lat_total
    row = lax.broadcasted_iota(jnp.int32, (lat_total, depth), 0)
    latitude = row % owners * lat_count + row // owners
    spread = (
        latitude == lax.broadcasted_iota(jnp.int32, (lat_total, depth), 1) % lat_total
    ).astype(jnp.bfloat16)
    keep = (
        lax.broadcasted_iota(jnp.int32, (SUB, depth), 0)
        == lax.broadcasted_iota(jnp.int32, (SUB, depth), 1) // lat_total
    )
    keys = [(level,) + key for level in range(level_count) for key in keys]
    half = len(keys) * SUB
    for place in range(0, len(keys), 2):
        couple = [
            lax.dot_general(
                lines[key].astype(jnp.bfloat16),
                spread,
                (((0,), (0,)), ((), ())),
                preferred_element_type=jnp.float32,
            )
            for key in keys[place : place + 2]
        ]
        for member in range(2):
            for group, (at, _) in enumerate(groups):
                begin = member * pair_count + at
                pieces = [jnp.where(keep, one[begin : begin + SUB], 0.0) for one in couple]
                into = member * half + place * SUB
                left[group, into : into + 2 * SUB, :] = jnp.concatenate(pieces, axis=0).astype(
                    jnp.bfloat16
                )
    copies = []
    for start in range(0, degrees, 256):
        stop = min(start + 256, degrees)
        low = 0 if start < 2 * pair_total else half
        high = 2 * half if stop > pair_total + 1 else half
        parts = []
        for group, (at, size) in enumerate(groups):
            values = legendre[at : at + size, :, start:stop].reshape(size * lat_total, stop - start)
            sums = jnp.dot(
                left[group, low:high, : size * lat_total],
                values,
                preferred_element_type=jnp.float32,
            ).reshape((high - low) // SUB, SUB, stop - start)
            if high - low > half:
                shape = (SUB, stop - start)
                slot = lax.broadcasted_iota(jnp.int32, shape, 1) + start
                pair = lax.broadcasted_iota(jnp.int32, shape, 0) + (first_pair + at)
                sums = jnp.where(
                    slot + pair < 2 * pair_total, sums[: len(keys)], sums[len(keys) :]
                )
            parts.append(sums[:, :size])
        planes[:, :, :, :, start:stop] = (
            jnp.concatenate(parts, axis=1).astype(jnp.bfloat16).reshape(planes.shape[:4] + (stop - start,))
        )
        here = pl.ds(start, stop - start)
        copies.append(
            pltpu.make_async_copy(
                planes.at[:, :, :, :, here], out.at[:, :, :, :, here], sent.at[len(copies)]
            )
        )
        copies[-1].start()
    for copy in copies:
        copy.wait()


def held(value):
    return pltpu.with_memory_space_constraint(value, pltpu.HBM)


def local(fields, rows_first, points, starts, weights, thickness, legendre):
    level_count, field_count, lat_count, lon_count = fields.shape
    pair_count, lat_total, degrees = legendre.shape
    owners = lax.axis_size("lat")
    couples = lon_count // (2 * LANES)
    blocks = 2 * couples
    columns = 2 * owners * pair_count
    packed_lanes = -(-2 * lat_count * 2 * pair_count // LANES) * LANES
    sides = []
    for first in range(2):
        edges = [(i, i + 1) for i in range(first, owners - 1, 2)]
        sides.append(lax.ppermute(fields, "lat", edges + [(j, i) for i, j in edges]))

    scalar = pl.BlockSpec(memory_space=pltpu.SMEM)
    vector = pl.BlockSpec(memory_space=pltpu.VMEM)
    params = pltpu.CompilerParams(vmem_limit_bytes=LIMIT)
    remote = pl.BlockSpec(memory_space=pltpu.HBM)
    partial, table, twiddle, begins, factors, facts, beside = pl.pallas_call(
        functools.partial(near_kernel, pair_count * owners, pair_count),
        out_shape=(
            jax.ShapeDtypeStruct((lat_count, couples, SUB, 2 * LANES), jnp.float32),
            jax.ShapeDtypeStruct((lat_count, 2 * LANES, 2 * columns), jnp.bfloat16),
            jax.ShapeDtypeStruct((lat_count, couples, 2 * columns), jnp.float32),
            jax.ShapeDtypeStruct((lat_count, STENCIL, blocks, 1, LANES), jnp.int32),
            jax.ShapeDtypeStruct((weights.size // LANES, LANES), jnp.float32),
            jax.ShapeDtypeStruct((4 * lat_count, LANES), jnp.int32),
            jax.ShapeDtypeStruct((lat_count, blocks + 2, SUB, LANES), jnp.float32),
        ),
        in_specs=[remote] * 5 + [vector],
        out_specs=(vector,) * 7,
        scratch_shapes=[
            pltpu.SMEM(rows_first.shape, jnp.int32),
            pltpu.SMEM(points.shape, jnp.int32),
            pltpu.VMEM(fields.shape, fields.dtype),
            pltpu.VMEM(starts.shape, starts.dtype),
            pltpu.VMEM(weights.shape, weights.dtype),
            pltpu.VMEM((fields.size // LANES, LANES), jnp.float32),
            pltpu.VMEM((fields.size // LANES, LANES), jnp.float32),
            pltpu.VMEM((lat_count, blocks + 2, SUB, LANES), jnp.float32),
            pltpu.SemaphoreType.DMA((5,)),
        ],
        compiler_params=params,
        cost_estimate=pl.CostEstimate(flops=10_000_000, bytes_accessed=4_000_000, transcendentals=0),
        name="near_rows",
    )(*(held(value) for value in (rows_first, points, fields, starts, weights)), sides[0])

    coefficients = pl.pallas_call(
        far_kernel,
        out_shape=jax.ShapeDtypeStruct((owners, SUB, packed_lanes), jnp.bfloat16),
        in_specs=[vector] * 8,
        out_specs=vector,
        scratch_shapes=[
            pltpu.VMEM((fields.size // LANES, LANES), jnp.float32),
            pltpu.VMEM((2 * lat_count, blocks + 2, SUB, LANES), jnp.float32),
            pltpu.VMEM((lat_count, couples, SUB, 2 * LANES), jnp.float32),
            pltpu.VMEM((lat_count, 2 * SUB, columns), jnp.float32),
            pltpu.VMEM((owners, SUB, packed_lanes), jnp.float32),
        ],
        compiler_params=params,
        name="far_rows",
    )(beside, sides[1], begins, factors, facts, partial, table, twiddle)

    received = lax.all_to_all(coefficients, "lat", split_axis=0, concat_axis=0, tiled=True)
    by_level = received.reshape(owners, level_count, field_count, packed_lanes).astype(jnp.float32)
    virtual = by_level[:, :, 2] + 0.61 * by_level[:, :, 3]
    total = jnp.sum(thickness[None, :, None] * virtual, axis=1)
    level_owners = lax.axis_size("lev")
    if level_owners == 2:
        totals = lax.ppermute(total, "lev", [(0, 1), (1, 0)])[None]
    else:
        totals = lax.all_gather(total, "lev")

    out_shape = (level_count, field_count + 1, 2, pair_count, degrees)
    half = level_count * (field_count + 1) * 2 * SUB
    group_count = (pair_count + SUB - 1) // SUB
    return pl.pallas_call(
        functools.partial(legendre_kernel, level_owners, level_count, field_count),
        out_shape=jax.ShapeDtypeStruct(out_shape, jnp.bfloat16),
        in_specs=[scalar, vector, vector, vector],
        out_specs=pl.BlockSpec(memory_space=pl.ANY),
        scratch_shapes=[
            pltpu.VMEM((packed_lanes // LANES, owners * SUB, LANES), jnp.float32),
            pltpu.VMEM((group_count, 2 * half, SUB * lat_total), jnp.bfloat16),
            pltpu.VMEM(out_shape, jnp.bfloat16),
            pltpu.SemaphoreType.DMA(((degrees + 255) // 256,)),
        ],
        compiler_params=params,
        name="degree_sums",
    )(thickness, received, totals, legendre)


def solution(mesh):
    placed = (
        P("lev", None, "lat", None),
        P("lat"),
        P(),
        P("lat", None, None),
        P("lat", None, None, None),
        P("lev"),
        P("lat", None, None),
    )
    return jax.shard_map(
        local,
        mesh=mesh,
        in_specs=placed,
        out_specs=P("lev", None, None, "lat", None),
        check_vma=False,
    )
```

```python
import functools

import jax
import jax.numpy as jnp
import numpy as np
from jax import lax
from jax.experimental import pallas as pl
from jax.experimental.pallas import tpu as pltpu
from jax.sharding import PartitionSpec as P

LANES = 128
SUB = 8
HALF = 64
STENCIL = 4
LIMIT = 24 * 1024 * 1024


def lane_gather(values, lanes):
    return jnp.take_along_axis(values, lanes, axis=1, mode="promise_in_bounds")


SINE = (-70.99342854244645, 81.34076844400118, -41.337142359536955, 6.283164044230117)
COSINE = (
    56.2423804697887, -85.2403304160897, 64.93459063550272, -19.739171434929204, 0.9999999534680867,
)


def polynomial(terms, square):
    value = np.float32(terms[0])
    for term in terms[1:]:
        value = value * square + np.float32(term)
    return value


def turn_parts(product, total, inverse):
    turns = (product - jnp.floor(product * inverse + 0.5) * total) * inverse
    halves = jnp.floor(2.0 * turns + 0.5)
    sign = 1.0 - 2.0 * jnp.abs(halves)
    part = turns - 0.5 * halves
    square = part * part
    return sign * polynomial(COSINE, square), (sign * part) * polynomial(SINE, square)


def wavenumbers(at, width, pair_count, pair_total):
    column = lax.broadcasted_iota(jnp.int32, (1, width), 1).astype(jnp.float32) + float(at)
    owner = jnp.floor((column + 0.5) * (1.0 / (2 * pair_count)))
    inner = column - owner * (2.0 * pair_count)
    second = inner >= pair_count
    pair = owner * pair_count + jnp.where(second, inner - pair_count, inner)
    return jnp.where(second, 2.0 * pair_total - 1.0 - pair, pair)


def multiplied(one, two):
    return one[0] * two[0] - one[1] * two[1], one[0] * two[1] + one[1] * two[0]


def row_of(pair, row):
    return tuple(part[row : row + 1] for part in pair)


def extend(lines, row, rows_each, missing, ext, slot):
    blocks = ext.shape[1] - 2
    for block in range(blocks):
        ext[slot, block + 1] = lines[
            pl.ds(block * rows_each + row, SUB, stride=blocks * rows_each), :
        ]
    lane = lax.broadcasted_iota(jnp.int32, (SUB, LANES), 1)
    ahead = lane + missing
    behind = lane - missing
    first = lane_gather(ext[slot, 1], ahead & (LANES - 1))
    second = lane_gather(ext[slot, 2], ahead & (LANES - 1))
    last = ext[slot, blocks]
    final = lane_gather(last, behind & (LANES - 1))
    before = lane_gather(ext[slot, blocks - 1], behind & (LANES - 1))
    ext[slot, 0] = jnp.where(behind >= 0, final, before)
    ext[slot, blocks] = jnp.where(ahead < LANES, last, first)
    ext[slot, blocks + 1] = jnp.where(ahead < LANES, first, second)


def spread_rows(starts, begins):
    lat_count, _, blocks = begins.shape[:3]
    for latitude in range(lat_count):
        for block in range(blocks):
            for row in range(STENCIL):
                lanes = slice(block * LANES, (block + 1) * LANES)
                begins[latitude, row, block] = (
                    starts[latitude, row : row + 1, lanes] - (block - 1) * LANES
                )


def spread_lines(source, lines):
    first, second, rows, lon = source.shape
    at = 0
    for one in range(first):
        for two in range(second):
            values = source[one, two].astype(jnp.float32)
            for block in range(lon // LANES):
                lines[at : at + rows, :] = values[:, block * LANES : (block + 1) * LANES]
                at += rows


def gathered(totals, starts, scale, parts):
    for side in range(2):
        start = jnp.broadcast_to(starts[side], (SUB, LANES))
        for column in range(4):
            place = start + column
            lane = place & (LANES - 1)
            low, middle, high = [lane_gather(part, lane) for part in parts[side : side + 3]]
            value = jnp.where(place < LANES, low, jnp.where(place < 2 * LANES, middle, high))
            line = STENCIL * side + column
            totals[side] = totals[side] + scale[line : line + 1] * value
    return totals


def near_kernel(
    pair_total, pair_count, rows_first_far, points_far, fields_far, starts_far, weights_far, side,
    partial, table, twiddle, begins, factors, facts, beside,
    rows_first, points, fields, starts, weights, lines, side_lines, ext, arrived,
):
    lat_count, couples = partial.shape[:2]
    lon = 2 * couples * LANES
    columns = table.shape[2] // 2
    first_lat = lax.axis_index("lat") * lat_count
    fetches = [
        pltpu.make_async_copy(source, target, arrived.at[place])
        for place, (source, target) in enumerate(
            (
                (points_far, points),
                (rows_first_far, rows_first),
                (starts_far, starts),
                (weights_far, weights),
                (fields_far, fields),
            )
        )
    ]
    for fetch in fetches:
        fetch.start()
    spread_lines(side, side_lines)
    for fetch in fetches[:2]:
        fetch.wait()
    known = [first_lat - rows_first[latitude] for latitude in range(lat_count)]
    known += [points[first_lat + latitude] for latitude in range(lat_count)]
    for place in range(-lat_count, 2 * lat_count):
        if place < 0 or place >= lat_count:
            place = jnp.clip(first_lat + place, 0, points.shape[0] - 1)
            known.append(lon - points[place])
    facts[...] = jnp.concatenate([jnp.full((1, LANES), one, jnp.int32) for one in known], axis=0)
    upper = lax.axis_index("lat") % 2 == 0
    for row in range(lat_count):
        missing = jnp.where(upper, known[3 * lat_count + row], known[2 * lat_count + row])
        extend(side_lines, row, lat_count, missing, beside, row)
    width = 256
    scales = []
    for latitude in range(lat_count):
        total = jnp.full((1, 1), points[first_lat + latitude], jnp.int32).astype(jnp.float32)
        inverse = 1.0 / total
        scales.append((total, inverse, jnp.sqrt(2.0 * inverse)))
    few = lax.broadcasted_iota(jnp.int32, (SUB, width), 0).astype(jnp.float32)
    many = lax.broadcasted_iota(jnp.int32, (couples + 3, width), 0)
    many = jnp.where(many < couples, many * (2 * LANES), (many - (couples - 1)) * HALF)
    many = many.astype(jnp.float32)
    for at in range(0, columns, width):
        numbers = wavenumbers(at, width, pair_count, pair_total)
        for latitude, (total, inverse, scaling) in enumerate(scales):
            ones = turn_parts(numbers * few, total, inverse)
            eights = turn_parts(numbers * (few * float(SUB)), total, inverse)
            large = turn_parts(numbers * many, total, inverse)
            here = slice(at, at + width)
            there = slice(columns + at, columns + at + width)
            twiddle[latitude, :, here] = scaling * large[0][:couples]
            twiddle[latitude, :, there] = scaling * large[1][:couples]
            products = [ones] + [multiplied(row_of(eights, row), ones) for row in range(1, SUB)]
            block = tuple(jnp.concatenate(parts, axis=0) for parts in zip(*products))
            for quarter in range(4):
                turned = block
                if quarter > 0:
                    turned = multiplied(row_of(large, couples + quarter - 1), block)
                rows = slice(HALF * quarter, HALF * (quarter + 1))
                table[latitude, rows, here] = turned[0].astype(jnp.bfloat16)
                table[latitude, rows, there] = turned[1].astype(jnp.bfloat16)
    for fetch in fetches[2:]:
        fetch.wait()
    spread_rows(starts, begins)
    spread_lines(weights, factors)
    spread_lines(fields, lines)
    for latitude in range(lat_count):
        extend(lines, latitude, lat_count, lon - points[first_lat + latitude], ext, latitude)
    for latitude in range(lat_count):
        mine = first_lat - rows_first[latitude]
        for couple in range(couples):
            totals = [jnp.zeros((SUB, LANES), jnp.float32) for _ in range(2)]
            for slot in range(lat_count):
                row = mine + slot
                at = ((latitude * STENCIL + row) * couples + couple) * SUB
                totals = gathered(
                    totals,
                    [begins[latitude, row, 2 * couple + side] for side in range(2)],
                    factors[pl.ds(pl.multiple_of(at, SUB), SUB), :],
                    [ext[slot, 2 * couple + piece] for piece in range(4)],
                )
            for side in range(2):
                partial[latitude, couple, :, side * LANES : (side + 1) * LANES] = totals[side]


def far_kernel(
    beside, far_side, begins, factors, facts, partial, table, twiddle,
    out, lines, ext, grid, waves,
):
    lat_count, couples = partial.shape[:2]
    columns = table.shape[2] // 2
    owners = out.shape[0]
    fact = [jnp.broadcast_to(facts[row : row + 1], (SUB, LANES)) for row in range(4 * lat_count)]
    toward = 1 - lax.axis_index("lat") % 2
    ext[pl.ds(toward * lat_count, lat_count)] = beside[...]
    spread_lines(far_side, lines)
    for row in range(lat_count):
        missing = jnp.where(toward == 1, fact[2 * lat_count + row], fact[3 * lat_count + row])
        extend(lines, row, lat_count, missing, ext, (1 - toward) * lat_count + row)
    lane = lax.broadcasted_iota(jnp.int32, (SUB, LANES), 1)
    width = 256
    choices = (((2, 0, 0), (2, 1, 0)), ((3, 3, 1), (3, 2, 1)))
    for latitude in range(lat_count):
        at_zero = fact[latitude] == 0
        at_one = fact[latitude] == 1

        def pick(values):
            return jnp.where(at_zero, values[0], jnp.where(at_one, values[1], values[2]))

        def pick_line(values):
            return jnp.where(
                at_zero[:1], values[0], jnp.where(at_one[:1], values[1], values[2])
            )

        for couple in range(couples):
            sides = [pl.ds(side * LANES, LANES) for side in range(2)]
            totals = [partial[latitude, couple, :, lanes] for lanes in sides]
            for rows, slots in choices:
                scales = [
                    factors[pl.ds(((latitude * STENCIL + row) * couples + couple) * SUB, SUB), :]
                    for row in rows
                ]
                starts = [
                    pick_line([begins[latitude, row, 2 * couple + side] for row in rows])
                    for side in range(2)
                ]
                parts = [
                    pick([ext[slot, 2 * couple + piece] for slot in slots]) for piece in range(4)
                ]
                totals = gathered(totals, starts, pick(scales), parts)
            for side in range(2):
                live = lane + (2 * couple + side) * LANES < fact[lat_count + latitude]
                grid[latitude, couple, :, sides[side]] = jnp.where(live, totals[side], 0.0)
    for latitude in range(lat_count):
        rows = grid[latitude].reshape(couples * SUB, 2 * LANES).astype(jnp.bfloat16)
        for at in range(0, columns, width):
            real = jnp.dot(
                rows, table[latitude, :, at : at + width], preferred_element_type=jnp.float32
            )
            imag = jnp.dot(
                rows,
                table[latitude, :, columns + at : columns + at + width],
                preferred_element_type=jnp.float32,
            )
            cosine = jnp.zeros((SUB, width), jnp.float32)
            sine = jnp.zeros((SUB, width), jnp.float32)
            for couple in range(couples):
                turn_cos = twiddle[latitude, couple : couple + 1, at : at + width]
                turn_sin = twiddle[latitude, couple : couple + 1, columns + at : columns + at + width]
                here = slice(couple * SUB, (couple + 1) * SUB)
                cosine = cosine + (real[here] * turn_cos - imag[here] * turn_sin)
                sine = sine - (real[here] * turn_sin + imag[here] * turn_cos)
            waves[latitude, 0:SUB, at : at + width] = cosine
            waves[latitude, SUB : 2 * SUB, at : at + width] = sine
        waves[latitude, :, columns:] = jnp.zeros((2 * SUB, waves.shape[2] - columns), jnp.float32)
        used = columns // owners
        for owner in range(owners):
            out[owner, 2 * SUB * latitude : 2 * SUB * (latitude + 1), :] = waves[
                latitude, :, owner * used : owner * used + LANES
            ].astype(jnp.bfloat16)


def row_keys(level_count, field_count):
    return [
        (level, field, part)
        for level in range(level_count)
        for field in range(field_count + 1)
        for part in range(2)
    ]


def place_rows(lines, keys, pair_count, left):
    lat_total = next(iter(lines.values())).shape[0]
    depth = SUB * lat_total
    half = len(keys) * SUB
    spread = (
        lax.broadcasted_iota(jnp.int32, (lat_total, depth), 0)
        == lax.broadcasted_iota(jnp.int32, (lat_total, depth), 1) % lat_total
    ).astype(jnp.bfloat16)
    keep = (
        lax.broadcasted_iota(jnp.int32, (SUB, depth), 0)
        == lax.broadcasted_iota(jnp.int32, (SUB, depth), 1) // lat_total
    )
    for place in range(0, len(keys), 2):
        if keys[place] not in lines:
            continue
        couple = [
            lax.dot_general(
                lines[key].astype(jnp.bfloat16),
                spread,
                (((0,), (0,)), ((), ())),
                preferred_element_type=jnp.float32,
            )
            for key in keys[place : place + 2]
        ]
        for member in range(2):
            for group in range(left.shape[0]):
                begin = member * pair_count + group * SUB
                pieces = [jnp.where(keep, one[begin : begin + SUB], 0.0) for one in couple]
                into = member * half + place * SUB
                left[group, into : into + 2 * SUB, :] = jnp.concatenate(pieces, axis=0).astype(
                    jnp.bfloat16
                )


def received_rows(received, wide, keys, field_count):
    wide[...] = received[...].astype(jnp.float32).reshape(wide.shape)
    lat_total = wide.shape[0] // (2 * SUB)
    return {
        (level, field, part): wide[
            pl.ds(part * SUB + level * field_count + field, lat_total, stride=2 * SUB), :
        ]
        for level, field, part in keys
    }


def left_kernel(level_count, field_count, pair_count, received, left, wide):
    keys = row_keys(level_count, field_count)
    wanted = [key for key in keys if key[1] < field_count]
    place_rows(received_rows(received, wide, wanted, field_count), keys, pair_count, left)


def legendre_kernel(
    level_owners, level_count, field_count, thickness, received, totals, legendre, left_given,
    out, left, wide, planes, sent,
):
    owners = received.shape[0]
    pair_count, lat_total, degrees = legendre.shape
    pair_total = pair_count * owners
    groups = [(at, min(SUB, pair_count - at)) for at in range(0, pair_count, SUB)]
    keys = row_keys(level_count, field_count)
    half = len(keys) * SUB
    level_place = lax.axis_index("lev")
    first_pair = lax.axis_index("lat") * pair_count
    wanted = [(level, field, part) for level in range(level_count) for field in (2, 3) for part in range(2)]
    lines = received_rows(received, wide, wanted, field_count)
    sums = {}
    for part in range(2):
        running = jnp.zeros((lat_total, LANES), jnp.float32)
        for place in range(totals.shape[0]):
            other = 1 - level_place if level_owners == 2 else place
            total = totals[place, pl.ds(part, lat_total, stride=2), :]
            running = running + jnp.where(other > level_place, total, 0.0)
        for level in reversed(range(level_count)):
            running = running + thickness[level] * (
                lines[level, 2, part] + 0.61 * lines[level, 3, part]
            )
            sums[level, field_count, part] = running
    place_rows(sums, keys, pair_count, left)
    copies = []
    for start in range(0, degrees, 256):
        stop = min(start + 256, degrees)
        low = 0 if start < 2 * pair_total else half
        high = 2 * half if stop > pair_total + 1 else half
        parts = []
        for group, (at, size) in enumerate(groups):
            values = legendre[at : at + size, :, start:stop].reshape(size * lat_total, stop - start)
            sums = jnp.dot(
                left[group, low:high, : size * lat_total],
                values,
                preferred_element_type=jnp.float32,
            ).reshape((high - low) // SUB, SUB, stop - start)
            if high - low > half:
                shape = (SUB, stop - start)
                slot = lax.broadcasted_iota(jnp.int32, shape, 1) + start
                pair = lax.broadcasted_iota(jnp.int32, shape, 0) + (first_pair + at)
                sums = jnp.where(
                    slot + pair < 2 * pair_total, sums[: len(keys)], sums[len(keys) :]
                )
            parts.append(sums[:, :size])
        planes[:, :, :, :, start:stop] = (
            jnp.concatenate(parts, axis=1).astype(jnp.bfloat16).reshape(planes.shape[:4] + (stop - start,))
        )
        here = pl.ds(start, stop - start)
        copies.append(
            pltpu.make_async_copy(
                planes.at[:, :, :, :, here], out.at[:, :, :, :, here], sent.at[len(copies)]
            )
        )
        copies[-1].start()
    for copy in copies:
        copy.wait()


def held(value):
    return pltpu.with_memory_space_constraint(value, pltpu.HBM)


def local(fields, rows_first, points, starts, weights, thickness, legendre):
    level_count, field_count, lat_count, lon_count = fields.shape
    pair_count, lat_total, degrees = legendre.shape
    owners = lax.axis_size("lat")
    couples = lon_count // (2 * LANES)
    blocks = 2 * couples
    columns = 2 * owners * pair_count
    sides = []
    for first in range(2):
        edges = [(i, i + 1) for i in range(first, owners - 1, 2)]
        sides.append(lax.ppermute(fields, "lat", edges + [(j, i) for i, j in edges]))

    scalar = pl.BlockSpec(memory_space=pltpu.SMEM)
    vector = pl.BlockSpec(memory_space=pltpu.VMEM)
    params = pltpu.CompilerParams(vmem_limit_bytes=LIMIT)
    remote = pl.BlockSpec(memory_space=pltpu.HBM)
    partial, table, twiddle, begins, factors, facts, beside = pl.pallas_call(
        functools.partial(near_kernel, pair_count * owners, pair_count),
        out_shape=(
            jax.ShapeDtypeStruct((lat_count, couples, SUB, 2 * LANES), jnp.float32),
            jax.ShapeDtypeStruct((lat_count, 2 * LANES, 2 * columns), jnp.bfloat16),
            jax.ShapeDtypeStruct((lat_count, couples, 2 * columns), jnp.float32),
            jax.ShapeDtypeStruct((lat_count, STENCIL, blocks, 1, LANES), jnp.int32),
            jax.ShapeDtypeStruct((weights.size // LANES, LANES), jnp.float32),
            jax.ShapeDtypeStruct((4 * lat_count, LANES), jnp.int32),
            jax.ShapeDtypeStruct((lat_count, blocks + 2, SUB, LANES), jnp.float32),
        ),
        in_specs=[remote] * 5 + [vector],
        out_specs=(vector,) * 7,
        scratch_shapes=[
            pltpu.SMEM(rows_first.shape, jnp.int32),
            pltpu.SMEM(points.shape, jnp.int32),
            pltpu.VMEM(fields.shape, fields.dtype),
            pltpu.VMEM(starts.shape, starts.dtype),
            pltpu.VMEM(weights.shape, weights.dtype),
            pltpu.VMEM((fields.size // LANES, LANES), jnp.float32),
            pltpu.VMEM((fields.size // LANES, LANES), jnp.float32),
            pltpu.VMEM((lat_count, blocks + 2, SUB, LANES), jnp.float32),
            pltpu.SemaphoreType.DMA((5,)),
        ],
        compiler_params=params,
        cost_estimate=pl.CostEstimate(flops=10_000_000, bytes_accessed=4_000_000, transcendentals=0),
        name="near_rows",
    )(*(held(value) for value in (rows_first, points, fields, starts, weights)), sides[0])

    coefficients = pl.pallas_call(
        far_kernel,
        out_shape=jax.ShapeDtypeStruct((owners, 2 * SUB * lat_count, LANES), jnp.bfloat16),
        in_specs=[vector] * 8,
        out_specs=vector,
        scratch_shapes=[
            pltpu.VMEM((fields.size // LANES, LANES), jnp.float32),
            pltpu.VMEM((2 * lat_count, blocks + 2, SUB, LANES), jnp.float32),
            pltpu.VMEM((lat_count, couples, SUB, 2 * LANES), jnp.float32),
            pltpu.VMEM((lat_count, 2 * SUB, columns + LANES), jnp.float32),
        ],
        compiler_params=params,
        name="far_rows",
    )(beside, sides[1], begins, factors, facts, partial, table, twiddle)

    received = lax.all_to_all(coefficients, "lat", split_axis=0, concat_axis=0, tiled=True)
    share = thickness[:, None] * jnp.asarray([0.0] * (field_count - 2) + [1.0, 0.61], jnp.float32)
    by_row = received.reshape(2 * lat_total, SUB, LANES).astype(jnp.float32)
    total = jnp.sum(by_row * share.reshape(1, SUB, 1), axis=1)
    level_owners = lax.axis_size("lev")
    if level_owners == 2:
        totals = lax.ppermute(total, "lev", [(0, 1), (1, 0)])[None]
    else:
        totals = lax.all_gather(total, "lev")

    out_shape = (level_count, field_count + 1, 2, pair_count, degrees)
    half = level_count * (field_count + 1) * 2 * SUB
    group_count = (pair_count + SUB - 1) // SUB
    left_shape = jax.ShapeDtypeStruct((group_count, 2 * half, SUB * lat_total), jnp.bfloat16)
    wide = pltpu.VMEM((lat_total * 2 * SUB, LANES), jnp.float32)
    left = pl.pallas_call(
        functools.partial(left_kernel, level_count, field_count, pair_count),
        out_shape=left_shape,
        in_specs=[vector],
        out_specs=vector,
        scratch_shapes=[wide],
        compiler_params=params,
        cost_estimate=pl.CostEstimate(flops=50_000_000, bytes_accessed=2_000_000, transcendentals=0),
        name="left_rows",
    )(received)
    return pl.pallas_call(
        functools.partial(legendre_kernel, level_owners, level_count, field_count),
        out_shape=(jax.ShapeDtypeStruct(out_shape, jnp.bfloat16), left_shape),
        in_specs=[scalar, vector, vector, vector, vector],
        out_specs=(pl.BlockSpec(memory_space=pl.ANY), vector),
        input_output_aliases={4: 1},
        scratch_shapes=[
            wide,
            pltpu.VMEM(out_shape, jnp.bfloat16),
            pltpu.SemaphoreType.DMA(((degrees + 255) // 256,)),
        ],
        compiler_params=params,
        name="degree_sums",
    )(thickness, received, totals, legendre, left)[0]


def solution(mesh):
    placed = (
        P("lev", None, "lat", None),
        P("lat"),
        P(),
        P("lat", None, None),
        P("lat", None, None, None),
        P("lev"),
        P("lat", None, None),
    )
    return jax.shard_map(
        local,
        mesh=mesh,
        in_specs=placed,
        out_specs=P("lev", None, None, "lat", None),
        check_vma=False,
    )
```

```python
import functools

import jax
import jax.numpy as jnp
import numpy as np
from jax import lax
from jax.experimental import pallas as pl
from jax.experimental.pallas import tpu as pltpu
from jax.sharding import PartitionSpec as P

LANES = 128
SUB = 8
HALF = 64
STENCIL = 4
LIMIT = 24 * 1024 * 1024


def lane_gather(values, lanes):
    return jnp.take_along_axis(values, lanes, axis=1, mode="promise_in_bounds")


SINE = (-70.99342854244645, 81.34076844400118, -41.337142359536955, 6.283164044230117)
COSINE = (
    56.2423804697887, -85.2403304160897, 64.93459063550272, -19.739171434929204, 0.9999999534680867,
)


def polynomial(terms, square):
    value = np.float32(terms[0])
    for term in terms[1:]:
        value = value * square + np.float32(term)
    return value


def turn_parts(product, total, inverse):
    turns = (product - jnp.floor(product * inverse + 0.5) * total) * inverse
    halves = jnp.floor(2.0 * turns + 0.5)
    sign = 1.0 - 2.0 * jnp.abs(halves)
    part = turns - 0.5 * halves
    square = part * part
    return sign * polynomial(COSINE, square), (sign * part) * polynomial(SINE, square)


def wavenumbers(at, width, pair_count, pair_total):
    column = lax.broadcasted_iota(jnp.int32, (1, width), 1).astype(jnp.float32) + float(at)
    owner = jnp.floor((column + 0.5) * (1.0 / (2 * pair_count)))
    inner = column - owner * (2.0 * pair_count)
    second = inner >= pair_count
    pair = owner * pair_count + jnp.where(second, inner - pair_count, inner)
    return jnp.where(second, 2.0 * pair_total - 1.0 - pair, pair)


def multiplied(one, two):
    return one[0] * two[0] - one[1] * two[1], one[0] * two[1] + one[1] * two[0]


def row_of(pair, row):
    return tuple(part[row : row + 1] for part in pair)


def extend(lines, row, rows_each, missing, ext, slot):
    blocks = ext.shape[1] - 2
    for block in range(blocks):
        ext[slot, block + 1] = lines[
            pl.ds(block * rows_each + row, SUB, stride=blocks * rows_each), :
        ]
    lane = lax.broadcasted_iota(jnp.int32, (SUB, LANES), 1)
    ahead = lane + missing
    behind = lane - missing
    first = lane_gather(ext[slot, 1], ahead & (LANES - 1))
    second = lane_gather(ext[slot, 2], ahead & (LANES - 1))
    last = ext[slot, blocks]
    final = lane_gather(last, behind & (LANES - 1))
    before = lane_gather(ext[slot, blocks - 1], behind & (LANES - 1))
    ext[slot, 0] = jnp.where(behind >= 0, final, before)
    ext[slot, blocks] = jnp.where(ahead < LANES, last, first)
    ext[slot, blocks + 1] = jnp.where(ahead < LANES, first, second)


def spread_rows(starts, begins):
    lat_count, _, blocks = begins.shape[:3]
    for latitude in range(lat_count):
        for block in range(blocks):
            for row in range(STENCIL):
                lanes = slice(block * LANES, (block + 1) * LANES)
                begins[latitude, row, block] = (
                    starts[latitude, row : row + 1, lanes] - (block - 1) * LANES
                )


def spread_lines(source, lines):
    first, second, rows, lon = source.shape
    at = 0
    for one in range(first):
        for two in range(second):
            values = source[one, two].astype(jnp.float32)
            for block in range(lon // LANES):
                lines[at : at + rows, :] = values[:, block * LANES : (block + 1) * LANES]
                at += rows


def gathered(totals, starts, scale, parts):
    for side in range(2):
        start = jnp.broadcast_to(starts[side], (SUB, LANES))
        for column in range(4):
            place = start + column
            lane = place & (LANES - 1)
            low, middle, high = [lane_gather(part, lane) for part in parts[side : side + 3]]
            value = jnp.where(place < LANES, low, jnp.where(place < 2 * LANES, middle, high))
            line = STENCIL * side + column
            totals[side] = totals[side] + scale[line : line + 1] * value
    return totals


def near_kernel(
    pair_total, pair_count, rows_first_far, points_far, fields_far, starts_far, weights_far, side,
    partial, table, twiddle, begins, factors, facts, beside,
    rows_first, points, fields, starts, weights, lines, side_lines, ext, arrived,
):
    lat_count, couples = partial.shape[:2]
    lon = 2 * couples * LANES
    columns = table.shape[2] // 2
    first_lat = lax.axis_index("lat") * lat_count
    fetches = [
        pltpu.make_async_copy(source, target, arrived.at[place])
        for place, (source, target) in enumerate(
            (
                (points_far, points),
                (rows_first_far, rows_first),
                (starts_far, starts),
                (weights_far, weights),
                (fields_far, fields),
            )
        )
    ]
    for fetch in fetches:
        fetch.start()
    spread_lines(side, side_lines)
    for fetch in fetches[:2]:
        fetch.wait()
    known = [first_lat - rows_first[latitude] for latitude in range(lat_count)]
    known += [points[first_lat + latitude] for latitude in range(lat_count)]
    for place in range(-lat_count, 2 * lat_count):
        if place < 0 or place >= lat_count:
            place = jnp.clip(first_lat + place, 0, points.shape[0] - 1)
            known.append(lon - points[place])
    facts[...] = jnp.concatenate([jnp.full((1, LANES), one, jnp.int32) for one in known], axis=0)
    upper = lax.axis_index("lat") % 2 == 0
    for row in range(lat_count):
        missing = jnp.where(upper, known[3 * lat_count + row], known[2 * lat_count + row])
        extend(side_lines, row, lat_count, missing, beside, row)
    width = 256
    scales = []
    for latitude in range(lat_count):
        total = jnp.full((1, 1), points[first_lat + latitude], jnp.int32).astype(jnp.float32)
        inverse = 1.0 / total
        scales.append((total, inverse, jnp.sqrt(2.0 * inverse)))
    few = lax.broadcasted_iota(jnp.int32, (SUB, width), 0).astype(jnp.float32)
    many = lax.broadcasted_iota(jnp.int32, (couples + 3, width), 0)
    many = jnp.where(many < couples, many * (2 * LANES), (many - (couples - 1)) * HALF)
    many = many.astype(jnp.float32)
    for at in range(0, columns, width):
        numbers = wavenumbers(at, width, pair_count, pair_total)
        for latitude, (total, inverse, scaling) in enumerate(scales):
            ones = turn_parts(numbers * few, total, inverse)
            eights = turn_parts(numbers * (few * float(SUB)), total, inverse)
            large = turn_parts(numbers * many, total, inverse)
            here = slice(at, at + width)
            there = slice(columns + at, columns + at + width)
            twiddle[latitude, :, here] = scaling * large[0][:couples]
            twiddle[latitude, :, there] = scaling * large[1][:couples]
            products = [ones] + [multiplied(row_of(eights, row), ones) for row in range(1, SUB)]
            block = tuple(jnp.concatenate(parts, axis=0) for parts in zip(*products))
            for quarter in range(4):
                turned = block
                if quarter > 0:
                    turned = multiplied(row_of(large, couples + quarter - 1), block)
                rows = slice(HALF * quarter, HALF * (quarter + 1))
                table[latitude, rows, here] = turned[0].astype(jnp.bfloat16)
                table[latitude, rows, there] = turned[1].astype(jnp.bfloat16)
    for fetch in fetches[2:]:
        fetch.wait()
    spread_rows(starts, begins)
    spread_lines(weights, factors)
    spread_lines(fields, lines)
    for latitude in range(lat_count):
        extend(lines, latitude, lat_count, lon - points[first_lat + latitude], ext, latitude)
    for latitude in range(lat_count):
        mine = first_lat - rows_first[latitude]
        for couple in range(couples):
            totals = [jnp.zeros((SUB, LANES), jnp.float32) for _ in range(2)]
            for slot in range(lat_count):
                row = mine + slot
                at = ((latitude * STENCIL + row) * couples + couple) * SUB
                totals = gathered(
                    totals,
                    [begins[latitude, row, 2 * couple + side] for side in range(2)],
                    factors[pl.ds(pl.multiple_of(at, SUB), SUB), :],
                    [ext[slot, 2 * couple + piece] for piece in range(4)],
                )
            for side in range(2):
                partial[latitude, couple, :, side * LANES : (side + 1) * LANES] = totals[side]


def far_kernel(
    beside, far_side, begins, factors, facts, partial, table, twiddle,
    out, lines, ext, grid, waves,
):
    lat_count, couples = partial.shape[:2]
    columns = table.shape[2] // 2
    owners = out.shape[0]
    fact = [jnp.broadcast_to(facts[row : row + 1], (SUB, LANES)) for row in range(4 * lat_count)]
    toward = 1 - lax.axis_index("lat") % 2
    ext[pl.ds(toward * lat_count, lat_count)] = beside[...]
    spread_lines(far_side, lines)
    for row in range(lat_count):
        missing = jnp.where(toward == 1, fact[2 * lat_count + row], fact[3 * lat_count + row])
        extend(lines, row, lat_count, missing, ext, (1 - toward) * lat_count + row)
    lane = lax.broadcasted_iota(jnp.int32, (SUB, LANES), 1)
    width = 256
    choices = (((2, 0, 0), (2, 1, 0)), ((3, 3, 1), (3, 2, 1)))
    for latitude in range(lat_count):
        at_zero = fact[latitude] == 0
        at_one = fact[latitude] == 1

        def pick(values):
            return jnp.where(at_zero, values[0], jnp.where(at_one, values[1], values[2]))

        def pick_line(values):
            return jnp.where(
                at_zero[:1], values[0], jnp.where(at_one[:1], values[1], values[2])
            )

        for couple in range(couples):
            sides = [pl.ds(side * LANES, LANES) for side in range(2)]
            totals = [partial[latitude, couple, :, lanes] for lanes in sides]
            for rows, slots in choices:
                scales = [
                    factors[pl.ds(((latitude * STENCIL + row) * couples + couple) * SUB, SUB), :]
                    for row in rows
                ]
                starts = [
                    pick_line([begins[latitude, row, 2 * couple + side] for row in rows])
                    for side in range(2)
                ]
                parts = [
                    pick([ext[slot, 2 * couple + piece] for slot in slots]) for piece in range(4)
                ]
                totals = gathered(totals, starts, pick(scales), parts)
            for side in range(2):
                live = lane + (2 * couple + side) * LANES < fact[lat_count + latitude]
                grid[latitude, couple, :, sides[side]] = jnp.where(live, totals[side], 0.0)
    for latitude in range(lat_count):
        rows = grid[latitude].reshape(couples * SUB, 2 * LANES).astype(jnp.bfloat16)
        for at in range(0, columns, width):
            real = jnp.dot(
                rows, table[latitude, :, at : at + width], preferred_element_type=jnp.float32
            )
            imag = jnp.dot(
                rows,
                table[latitude, :, columns + at : columns + at + width],
                preferred_element_type=jnp.float32,
            )
            cosine = jnp.zeros((SUB, width), jnp.float32)
            sine = jnp.zeros((SUB, width), jnp.float32)
            for couple in range(couples):
                turn_cos = twiddle[latitude, couple : couple + 1, at : at + width]
                turn_sin = twiddle[latitude, couple : couple + 1, columns + at : columns + at + width]
                here = slice(couple * SUB, (couple + 1) * SUB)
                cosine = cosine + (real[here] * turn_cos - imag[here] * turn_sin)
                sine = sine - (real[here] * turn_sin + imag[here] * turn_cos)
            waves[latitude, 0:SUB, at : at + width] = cosine
            waves[latitude, SUB : 2 * SUB, at : at + width] = sine
        waves[latitude, :, columns:] = jnp.zeros((2 * SUB, waves.shape[2] - columns), jnp.float32)
        used = columns // owners
        for owner in range(owners):
            out[owner, 2 * SUB * latitude : 2 * SUB * (latitude + 1), :] = waves[
                latitude, :, owner * used : owner * used + LANES
            ].astype(jnp.bfloat16)


def row_keys(level_count, field_count):
    return [
        (level, field, part)
        for level in range(level_count)
        for field in range(field_count + 1)
        for part in range(2)
    ]


def place_rows(lines, keys, pair_count, left):
    lat_total = next(iter(lines.values())).shape[0]
    depth = SUB * lat_total
    half = len(keys) * SUB
    spread = (
        lax.broadcasted_iota(jnp.int32, (lat_total, depth), 0)
        == lax.broadcasted_iota(jnp.int32, (lat_total, depth), 1) % lat_total
    ).astype(jnp.bfloat16)
    keep = (
        lax.broadcasted_iota(jnp.int32, (SUB, depth), 0)
        == lax.broadcasted_iota(jnp.int32, (SUB, depth), 1) // lat_total
    )
    for place in range(0, len(keys), 2):
        if keys[place] not in lines:
            continue
        couple = [
            lax.dot_general(
                lines[key].astype(jnp.bfloat16),
                spread,
                (((0,), (0,)), ((), ())),
                preferred_element_type=jnp.float32,
            )
            for key in keys[place : place + 2]
        ]
        for member in range(2):
            for group in range(left.shape[0]):
                begin = member * pair_count + group * SUB
                pieces = [jnp.where(keep, one[begin : begin + SUB], 0.0) for one in couple]
                into = member * half + place * SUB
                left[group, into : into + 2 * SUB, :] = jnp.concatenate(pieces, axis=0).astype(
                    jnp.bfloat16
                )


def received_rows(received, wide, keys, field_count):
    wide[...] = received[...].astype(jnp.float32).reshape(wide.shape)
    lat_total = wide.shape[0] // (2 * SUB)
    return {
        (level, field, part): wide[
            pl.ds(part * SUB + level * field_count + field, lat_total, stride=2 * SUB), :
        ]
        for level, field, part in keys
    }


def left_kernel(level_count, field_count, pair_count, received, left, wide):
    keys = row_keys(level_count, field_count)
    wanted = [key for key in keys if key[1] < field_count]
    place_rows(received_rows(received, wide, wanted, field_count), keys, pair_count, left)


def legendre_kernel(
    level_owners, level_count, field_count, thickness, received, totals, legendre, left_given,
    out, left, wide, planes, sent,
):
    owners = received.shape[0]
    pair_count, lat_total, degrees = legendre.shape
    pair_total = pair_count * owners
    groups = [(at, min(SUB, pair_count - at)) for at in range(0, pair_count, SUB)]
    keys = row_keys(level_count, field_count)
    half = len(keys) * SUB
    level_place = lax.axis_index("lev")
    first_pair = lax.axis_index("lat") * pair_count
    wanted = [(level, field, part) for level in range(level_count) for field in (2, 3) for part in range(2)]
    lines = received_rows(received, wide, wanted, field_count)
    sums = {}
    for part in range(2):
        running = jnp.zeros((lat_total, LANES), jnp.float32)
        for place in range(totals.shape[0]):
            other = 1 - level_place if level_owners == 2 else place
            running = running + jnp.where(other > level_place, totals[place, part], 0.0)
        for level in reversed(range(level_count)):
            running = running + thickness[level] * (
                lines[level, 2, part] + 0.61 * lines[level, 3, part]
            )
            sums[level, field_count, part] = running
    place_rows(sums, keys, pair_count, left)
    copies = []
    for start in range(0, degrees, 256):
        stop = min(start + 256, degrees)
        low = 0 if start < 2 * pair_total else half
        high = 2 * half if stop > pair_total + 1 else half
        parts = []
        for group, (at, size) in enumerate(groups):
            values = legendre[at : at + size, :, start:stop].reshape(size * lat_total, stop - start)
            sums = jnp.dot(
                left[group, low:high, : size * lat_total],
                values,
                preferred_element_type=jnp.float32,
            ).reshape((high - low) // SUB, SUB, stop - start)
            if high - low > half:
                shape = (SUB, stop - start)
                slot = lax.broadcasted_iota(jnp.int32, shape, 1) + start
                pair = lax.broadcasted_iota(jnp.int32, shape, 0) + (first_pair + at)
                sums = jnp.where(
                    slot + pair < 2 * pair_total, sums[: len(keys)], sums[len(keys) :]
                )
            parts.append(sums[:, :size])
        planes[:, :, :, :, start:stop] = (
            jnp.concatenate(parts, axis=1).astype(jnp.bfloat16).reshape(planes.shape[:4] + (stop - start,))
        )
        here = pl.ds(start, stop - start)
        copies.append(
            pltpu.make_async_copy(
                planes.at[:, :, :, :, here], out.at[:, :, :, :, here], sent.at[len(copies)]
            )
        )
        copies[-1].start()
    for copy in copies:
        copy.wait()


def held(value):
    return pltpu.with_memory_space_constraint(value, pltpu.HBM)


def local(fields, rows_first, points, starts, weights, thickness, legendre):
    level_count, field_count, lat_count, lon_count = fields.shape
    pair_count, lat_total, degrees = legendre.shape
    owners = lax.axis_size("lat")
    couples = lon_count // (2 * LANES)
    blocks = 2 * couples
    columns = 2 * owners * pair_count
    sides = []
    for first in range(2):
        edges = [(i, i + 1) for i in range(first, owners - 1, 2)]
        sides.append(lax.ppermute(fields, "lat", edges + [(j, i) for i, j in edges]))

    scalar = pl.BlockSpec(memory_space=pltpu.SMEM)
    vector = pl.BlockSpec(memory_space=pltpu.VMEM)
    params = pltpu.CompilerParams(vmem_limit_bytes=LIMIT)
    remote = pl.BlockSpec(memory_space=pltpu.HBM)
    partial, table, twiddle, begins, factors, facts, beside = pl.pallas_call(
        functools.partial(near_kernel, pair_count * owners, pair_count),
        out_shape=(
            jax.ShapeDtypeStruct((lat_count, couples, SUB, 2 * LANES), jnp.float32),
            jax.ShapeDtypeStruct((lat_count, 2 * LANES, 2 * columns), jnp.bfloat16),
            jax.ShapeDtypeStruct((lat_count, couples, 2 * columns), jnp.float32),
            jax.ShapeDtypeStruct((lat_count, STENCIL, blocks, 1, LANES), jnp.int32),
            jax.ShapeDtypeStruct((weights.size // LANES, LANES), jnp.float32),
            jax.ShapeDtypeStruct((4 * lat_count, LANES), jnp.int32),
            jax.ShapeDtypeStruct((lat_count, blocks + 2, SUB, LANES), jnp.float32),
        ),
        in_specs=[remote] * 5 + [vector],
        out_specs=(vector,) * 7,
        scratch_shapes=[
            pltpu.SMEM(rows_first.shape, jnp.int32),
            pltpu.SMEM(points.shape, jnp.int32),
            pltpu.VMEM(fields.shape, fields.dtype),
            pltpu.VMEM(starts.shape, starts.dtype),
            pltpu.VMEM(weights.shape, weights.dtype),
            pltpu.VMEM((fields.size // LANES, LANES), jnp.float32),
            pltpu.VMEM((fields.size // LANES, LANES), jnp.float32),
            pltpu.VMEM((lat_count, blocks + 2, SUB, LANES), jnp.float32),
            pltpu.SemaphoreType.DMA((5,)),
        ],
        compiler_params=params,
        cost_estimate=pl.CostEstimate(flops=10_000_000, bytes_accessed=4_000_000, transcendentals=0),
        name="near_rows",
    )(*(held(value) for value in (rows_first, points, fields, starts, weights)), sides[0])

    coefficients = pl.pallas_call(
        far_kernel,
        out_shape=jax.ShapeDtypeStruct((owners, 2 * SUB * lat_count, LANES), jnp.bfloat16),
        in_specs=[vector] * 8,
        out_specs=vector,
        scratch_shapes=[
            pltpu.VMEM((fields.size // LANES, LANES), jnp.float32),
            pltpu.VMEM((2 * lat_count, blocks + 2, SUB, LANES), jnp.float32),
            pltpu.VMEM((lat_count, couples, SUB, 2 * LANES), jnp.float32),
            pltpu.VMEM((lat_count, 2 * SUB, columns + LANES), jnp.float32),
        ],
        compiler_params=params,
        name="far_rows",
    )(beside, sides[1], begins, factors, facts, partial, table, twiddle)

    received = lax.all_to_all(coefficients, "lat", split_axis=0, concat_axis=0, tiled=True)
    by_level = received.reshape(lat_total, 2, level_count, field_count, LANES).astype(jnp.float32)
    virtual = by_level[:, :, :, 2] + 0.61 * by_level[:, :, :, 3]
    total = jnp.sum(thickness[None, None, :, None] * virtual, axis=2).transpose(1, 0, 2)
    level_owners = lax.axis_size("lev")
    if level_owners == 2:
        totals = lax.ppermute(total, "lev", [(0, 1), (1, 0)])[None]
    else:
        totals = lax.all_gather(total, "lev")

    out_shape = (level_count, field_count + 1, 2, pair_count, degrees)
    half = level_count * (field_count + 1) * 2 * SUB
    group_count = (pair_count + SUB - 1) // SUB
    left_shape = jax.ShapeDtypeStruct((group_count, 2 * half, SUB * lat_total), jnp.bfloat16)
    wide = pltpu.VMEM((lat_total * 2 * SUB, LANES), jnp.float32)
    left = pl.pallas_call(
        functools.partial(left_kernel, level_count, field_count, pair_count),
        out_shape=left_shape,
        in_specs=[vector],
        out_specs=vector,
        scratch_shapes=[wide],
        compiler_params=params,
        cost_estimate=pl.CostEstimate(flops=50_000_000, bytes_accessed=2_000_000, transcendentals=0),
        name="left_rows",
    )(received)
    return pl.pallas_call(
        functools.partial(legendre_kernel, level_owners, level_count, field_count),
        out_shape=(jax.ShapeDtypeStruct(out_shape, jnp.bfloat16), left_shape),
        in_specs=[scalar, vector, vector, vector, vector],
        out_specs=(pl.BlockSpec(memory_space=pl.ANY), vector),
        input_output_aliases={4: 1},
        scratch_shapes=[
            wide,
            pltpu.VMEM(out_shape, jnp.bfloat16),
            pltpu.SemaphoreType.DMA(((degrees + 255) // 256,)),
        ],
        compiler_params=params,
        name="degree_sums",
    )(thickness, received, totals, legendre, left)[0]


def solution(mesh):
    placed = (
        P("lev", None, "lat", None),
        P("lat"),
        P(),
        P("lat", None, None),
        P("lat", None, None, None),
        P("lev"),
        P("lat", None, None),
    )
    return jax.shard_map(
        local,
        mesh=mesh,
        in_specs=placed,
        out_specs=P("lev", None, None, "lat", None),
        check_vma=False,
    )
```

```python
import functools

import jax
import jax.numpy as jnp
import numpy as np
from jax import lax
from jax.experimental import pallas as pl
from jax.experimental.pallas import tpu as pltpu
from jax.sharding import PartitionSpec as P

LANES = 128
SUB = 8
HALF = 64
STENCIL = 4
LIMIT = 24 * 1024 * 1024


def lane_gather(values, lanes):
    return jnp.take_along_axis(values, lanes, axis=1, mode="promise_in_bounds")


SINE = (-70.99342854244645, 81.34076844400118, -41.337142359536955, 6.283164044230117)
COSINE = (
    56.2423804697887, -85.2403304160897, 64.93459063550272, -19.739171434929204, 0.9999999534680867,
)


def polynomial(terms, square):
    value = np.float32(terms[0])
    for term in terms[1:]:
        value = value * square + np.float32(term)
    return value


def turn_parts(product, total, inverse):
    turns = (product - jnp.floor(product * inverse + 0.5) * total) * inverse
    halves = jnp.floor(2.0 * turns + 0.5)
    sign = 1.0 - 2.0 * jnp.abs(halves)
    part = turns - 0.5 * halves
    square = part * part
    return sign * polynomial(COSINE, square), (sign * part) * polynomial(SINE, square)


def wavenumbers(at, width, pair_count, pair_total):
    column = lax.broadcasted_iota(jnp.int32, (1, width), 1).astype(jnp.float32) + float(at)
    owner = jnp.floor((column + 0.5) * (1.0 / (2 * pair_count)))
    inner = column - owner * (2.0 * pair_count)
    second = inner >= pair_count
    pair = owner * pair_count + jnp.where(second, inner - pair_count, inner)
    return jnp.where(second, 2.0 * pair_total - 1.0 - pair, pair)


def multiplied(one, two):
    return one[0] * two[0] - one[1] * two[1], one[0] * two[1] + one[1] * two[0]


def row_of(pair, row):
    return tuple(part[row : row + 1] for part in pair)


def extend(lines, row, rows_each, missing, ext, slot):
    blocks = ext.shape[1] - 2
    for block in range(blocks):
        ext[slot, block + 1] = lines[
            pl.ds(block * rows_each + row, SUB, stride=blocks * rows_each), :
        ]
    lane = lax.broadcasted_iota(jnp.int32, (SUB, LANES), 1)
    ahead = lane + missing
    behind = lane - missing
    first = lane_gather(ext[slot, 1], ahead & (LANES - 1))
    second = lane_gather(ext[slot, 2], ahead & (LANES - 1))
    last = ext[slot, blocks]
    final = lane_gather(last, behind & (LANES - 1))
    before = lane_gather(ext[slot, blocks - 1], behind & (LANES - 1))
    ext[slot, 0] = jnp.where(behind >= 0, final, before)
    ext[slot, blocks] = jnp.where(ahead < LANES, last, first)
    ext[slot, blocks + 1] = jnp.where(ahead < LANES, first, second)


def spread_rows(starts, begins):
    lat_count, _, blocks = begins.shape[:3]
    for latitude in range(lat_count):
        for block in range(blocks):
            for row in range(STENCIL):
                lanes = slice(block * LANES, (block + 1) * LANES)
                begins[latitude, row, block] = (
                    starts[latitude, row : row + 1, lanes] - (block - 1) * LANES
                )


def spread_lines(source, lines):
    first, second, rows, lon = source.shape
    at = 0
    for one in range(first):
        for two in range(second):
            values = source[one, two].astype(jnp.float32)
            for block in range(lon // LANES):
                lines[at : at + rows, :] = values[:, block * LANES : (block + 1) * LANES]
                at += rows


def gathered(totals, starts, scales, parts):
    for side in range(2):
        for column in range(4):
            place = starts[side] + column
            lane = place & (LANES - 1)
            low, middle, high = [lane_gather(part, lane) for part in parts[side : side + 3]]
            value = jnp.where(place < LANES, low, jnp.where(place < 2 * LANES, middle, high))
            totals[side] = totals[side] + scales[STENCIL * side + column] * value
    return totals


def near_kernel(
    pair_total, pair_count, rows_first_far, points_far, fields_far, starts_far, weights_far,
    partial, table, twiddle, far_starts, far_scales, facts,
    rows_first, points, fields, starts, weights, begins, factors, lines, ext, arrived,
):
    lat_count, couples = partial.shape[:2]
    lon = 2 * couples * LANES
    columns = table.shape[2] // 2
    first_lat = lax.axis_index("lat") * lat_count
    fetches = [
        pltpu.make_async_copy(source, target, arrived.at[place])
        for place, (source, target) in enumerate(
            (
                (points_far, points),
                (rows_first_far, rows_first),
                (starts_far, starts),
                (weights_far, weights),
                (fields_far, fields),
            )
        )
    ]
    for fetch in fetches:
        fetch.start()
    fetches[0].wait()
    width = 256
    scales = []
    for latitude in range(lat_count):
        total = jnp.full((1, 1), points[first_lat + latitude], jnp.int32).astype(jnp.float32)
        inverse = 1.0 / total
        scales.append((total, inverse, jnp.sqrt(2.0 * inverse)))
    few = lax.broadcasted_iota(jnp.int32, (SUB, width), 0).astype(jnp.float32)
    many = lax.broadcasted_iota(jnp.int32, (couples + 3, width), 0)
    many = jnp.where(many < couples, many * (2 * LANES), (many - (couples - 1)) * HALF)
    many = many.astype(jnp.float32)
    for at in range(0, columns, width):
        numbers = wavenumbers(at, width, pair_count, pair_total)
        for latitude, (total, inverse, scaling) in enumerate(scales):
            ones = turn_parts(numbers * few, total, inverse)
            eights = turn_parts(numbers * (few * float(SUB)), total, inverse)
            large = turn_parts(numbers * many, total, inverse)
            here = slice(at, at + width)
            there = slice(columns + at, columns + at + width)
            for couple in range(couples):
                for lanes, part in ((here, large[0]), (there, large[1])):
                    twiddle[latitude, couple, :, lanes] = jnp.broadcast_to(
                        scaling * part[couple : couple + 1], (SUB, width)
                    )
            products = [ones] + [multiplied(row_of(eights, row), ones) for row in range(1, SUB)]
            block = tuple(jnp.concatenate(parts, axis=0) for parts in zip(*products))
            for quarter in range(4):
                turned = block
                if quarter > 0:
                    turned = multiplied(row_of(large, couples + quarter - 1), block)
                rows = slice(HALF * quarter, HALF * (quarter + 1))
                table[latitude, rows, here] = turned[0].astype(jnp.bfloat16)
                table[latitude, rows, there] = turned[1].astype(jnp.bfloat16)
    for fetch in fetches[1:]:
        fetch.wait()
    known = [first_lat - rows_first[latitude] for latitude in range(lat_count)]
    known += [points[first_lat + latitude] for latitude in range(lat_count)]
    for place in range(-lat_count, 2 * lat_count):
        if place < 0 or place >= lat_count:
            place = jnp.clip(first_lat + place, 0, points.shape[0] - 1)
            known.append(lon - points[place])
    facts[...] = jnp.concatenate([jnp.full((1, LANES), one, jnp.int32) for one in known], axis=0)
    spread_rows(starts, begins)
    spread_lines(weights, factors)
    spread_lines(fields, lines)
    for latitude in range(lat_count):
        extend(lines, latitude, lat_count, lon - points[first_lat + latitude], ext, latitude)
    for latitude in range(lat_count):
        mine = first_lat - rows_first[latitude]
        for couple in range(couples):

            def spread_row(row):
                at = ((latitude * STENCIL + row) * couples + couple) * SUB
                tile = factors[pl.ds(pl.multiple_of(at, SUB), SUB), :]
                return (
                    [
                        jnp.broadcast_to(begins[latitude, row, 2 * couple + side], (SUB, LANES))
                        for side in range(2)
                    ],
                    [jnp.broadcast_to(tile[line : line + 1], (SUB, LANES)) for line in range(SUB)],
                )

            totals = [jnp.zeros((SUB, LANES), jnp.float32) for _ in range(2)]
            for slot in range(lat_count):
                begun, scales = spread_row(mine + slot)
                parts = [ext[slot, 2 * couple + piece] for piece in range(4)]
                totals = gathered(totals, begun, scales, parts)
            for side in range(2):
                partial[latitude, couple, :, side * LANES : (side + 1) * LANES] = totals[side]
            others = (jnp.where(mine >= 1, 0, 2), jnp.where(mine <= 1, 3, 1))
            for choice, row in enumerate(others):
                begun, scales = spread_row(row)
                for side in range(2):
                    far_starts[latitude, choice, couple, side] = begun[side]
                for line in range(SUB):
                    far_scales[latitude, choice, couple, line] = scales[line]


def far_kernel(
    near_side, far_side, far_starts, far_scales, facts, partial, table, twiddle,
    out, lines, ext, grid, waves,
):
    lat_count, couples = partial.shape[:2]
    columns = table.shape[2] // 2
    owners = out.shape[0]
    toward = 1 - lax.axis_index("lat") % 2
    spread_lines(near_side, lines.at[toward])
    spread_lines(far_side, lines.at[1 - toward])
    fact = [jnp.broadcast_to(facts[row : row + 1], (SUB, LANES)) for row in range(4 * lat_count)]
    for slot in range(2 * lat_count):
        side, row = divmod(slot, lat_count)
        extend(lines.at[side], row, lat_count, fact[2 * lat_count + slot], ext, slot)
    lane = lax.broadcasted_iota(jnp.int32, (SUB, LANES), 1)
    width = 256
    choices = ((2, 1, 0), (3, 2, 1))
    for latitude in range(lat_count):
        at_zero = fact[latitude] == 0
        at_one = fact[latitude] == 1
        for couple in range(couples):
            sides = [pl.ds(side * LANES, LANES) for side in range(2)]
            totals = [partial[latitude, couple, :, lanes] for lanes in sides]
            for choice, slots in enumerate(choices):
                parts = []
                for piece in range(4):
                    zero, one, two = [ext[slot, 2 * couple + piece] for slot in slots]
                    parts.append(jnp.where(at_zero, zero, jnp.where(at_one, one, two)))
                totals = gathered(
                    totals,
                    [far_starts[latitude, choice, couple, side] for side in range(2)],
                    [far_scales[latitude, choice, couple, line] for line in range(SUB)],
                    parts,
                )
            for side in range(2):
                live = lane + (2 * couple + side) * LANES < fact[lat_count + latitude]
                grid[latitude, couple, :, sides[side]] = jnp.where(live, totals[side], 0.0)
    for latitude in range(lat_count):
        rows = grid[latitude].reshape(couples * SUB, 2 * LANES).astype(jnp.bfloat16)
        for at in range(0, columns, width):
            real = jnp.dot(
                rows, table[latitude, :, at : at + width], preferred_element_type=jnp.float32
            )
            imag = jnp.dot(
                rows,
                table[latitude, :, columns + at : columns + at + width],
                preferred_element_type=jnp.float32,
            )
            cosine = jnp.zeros((SUB, width), jnp.float32)
            sine = jnp.zeros((SUB, width), jnp.float32)
            for couple in range(couples):
                turn_cos = twiddle[latitude, couple, :, at : at + width]
                turn_sin = twiddle[latitude, couple, :, columns + at : columns + at + width]
                here = slice(couple * SUB, (couple + 1) * SUB)
                cosine = cosine + (real[here] * turn_cos - imag[here] * turn_sin)
                sine = sine - (real[here] * turn_sin + imag[here] * turn_cos)
            waves[latitude, 0:SUB, at : at + width] = cosine
            waves[latitude, SUB : 2 * SUB, at : at + width] = sine
        waves[latitude, :, columns:] = jnp.zeros((2 * SUB, waves.shape[2] - columns), jnp.float32)
        used = columns // owners
        for owner in range(owners):
            out[owner, 2 * SUB * latitude : 2 * SUB * (latitude + 1), :] = waves[
                latitude, :, owner * used : owner * used + LANES
            ].astype(jnp.bfloat16)


def row_keys(level_count, field_count):
    return [
        (level, field, part)
        for level in range(level_count)
        for field in range(field_count + 1)
        for part in range(2)
    ]


def place_rows(lines, keys, pair_count, left):
    lat_total = next(iter(lines.values())).shape[0]
    depth = SUB * lat_total
    half = len(keys) * SUB
    spread = (
        lax.broadcasted_iota(jnp.int32, (lat_total, depth), 0)
        == lax.broadcasted_iota(jnp.int32, (lat_total, depth), 1) % lat_total
    ).astype(jnp.bfloat16)
    keep = (
        lax.broadcasted_iota(jnp.int32, (SUB, depth), 0)
        == lax.broadcasted_iota(jnp.int32, (SUB, depth), 1) // lat_total
    )
    for place in range(0, len(keys), 2):
        if keys[place] not in lines:
            continue
        couple = [
            lax.dot_general(
                lines[key].astype(jnp.bfloat16),
                spread,
                (((0,), (0,)), ((), ())),
                preferred_element_type=jnp.float32,
            )
            for key in keys[place : place + 2]
        ]
        for member in range(2):
            for group in range(left.shape[0]):
                begin = member * pair_count + group * SUB
                pieces = [jnp.where(keep, one[begin : begin + SUB], 0.0) for one in couple]
                into = member * half + place * SUB
                left[group, into : into + 2 * SUB, :] = jnp.concatenate(pieces, axis=0).astype(
                    jnp.bfloat16
                )


def received_rows(received, wide, keys, field_count):
    wide[...] = received[...].astype(jnp.float32).reshape(wide.shape)
    lat_total = wide.shape[0] // (2 * SUB)
    return {
        (level, field, part): wide[
            pl.ds(part * SUB + level * field_count + field, lat_total, stride=2 * SUB), :
        ]
        for level, field, part in keys
    }


def left_kernel(level_count, field_count, pair_count, received, left, wide):
    keys = row_keys(level_count, field_count)
    wanted = [key for key in keys if key[1] < field_count]
    place_rows(received_rows(received, wide, wanted, field_count), keys, pair_count, left)


def legendre_kernel(
    level_owners, level_count, field_count, thickness, received, totals, legendre, left_given,
    out, left, wide, planes, sent,
):
    owners = received.shape[0]
    pair_count, lat_total, degrees = legendre.shape
    pair_total = pair_count * owners
    groups = [(at, min(SUB, pair_count - at)) for at in range(0, pair_count, SUB)]
    keys = row_keys(level_count, field_count)
    half = len(keys) * SUB
    level_place = lax.axis_index("lev")
    first_pair = lax.axis_index("lat") * pair_count
    wanted = [(level, field, part) for level in range(level_count) for field in (2, 3) for part in range(2)]
    lines = received_rows(received, wide, wanted, field_count)
    sums = {}
    for part in range(2):
        running = jnp.zeros((lat_total, LANES), jnp.float32)
        for place in range(totals.shape[0]):
            other = 1 - level_place if level_owners == 2 else place
            running = running + jnp.where(other > level_place, totals[place, part], 0.0)
        for level in reversed(range(level_count)):
            running = running + thickness[level] * (
                lines[level, 2, part] + 0.61 * lines[level, 3, part]
            )
            sums[level, field_count, part] = running
    place_rows(sums, keys, pair_count, left)
    copies = []
    for start in range(0, degrees, 256):
        stop = min(start + 256, degrees)
        low = 0 if start < 2 * pair_total else half
        high = 2 * half if stop > pair_total + 1 else half
        parts = []
        for group, (at, size) in enumerate(groups):
            values = legendre[at : at + size, :, start:stop].reshape(size * lat_total, stop - start)
            sums = jnp.dot(
                left[group, low:high, : size * lat_total],
                values,
                preferred_element_type=jnp.float32,
            ).reshape((high - low) // SUB, SUB, stop - start)
            if high - low > half:
                shape = (SUB, stop - start)
                slot = lax.broadcasted_iota(jnp.int32, shape, 1) + start
                pair = lax.broadcasted_iota(jnp.int32, shape, 0) + (first_pair + at)
                sums = jnp.where(
                    slot + pair < 2 * pair_total, sums[: len(keys)], sums[len(keys) :]
                )
            parts.append(sums[:, :size])
        planes[:, :, :, :, start:stop] = (
            jnp.concatenate(parts, axis=1).astype(jnp.bfloat16).reshape(planes.shape[:4] + (stop - start,))
        )
        here = pl.ds(start, stop - start)
        copies.append(
            pltpu.make_async_copy(
                planes.at[:, :, :, :, here], out.at[:, :, :, :, here], sent.at[len(copies)]
            )
        )
        copies[-1].start()
    for copy in copies:
        copy.wait()


def held(value):
    return pltpu.with_memory_space_constraint(value, pltpu.HBM)


def local(fields, rows_first, points, starts, weights, thickness, legendre):
    level_count, field_count, lat_count, lon_count = fields.shape
    pair_count, lat_total, degrees = legendre.shape
    owners = lax.axis_size("lat")
    couples = lon_count // (2 * LANES)
    blocks = 2 * couples
    columns = 2 * owners * pair_count
    sides = []
    for first in range(2):
        edges = [(i, i + 1) for i in range(first, owners - 1, 2)]
        sides.append(lax.ppermute(fields, "lat", edges + [(j, i) for i, j in edges]))

    scalar = pl.BlockSpec(memory_space=pltpu.SMEM)
    vector = pl.BlockSpec(memory_space=pltpu.VMEM)
    params = pltpu.CompilerParams(vmem_limit_bytes=LIMIT)
    remote = pl.BlockSpec(memory_space=pltpu.HBM)
    partial, table, twiddle, far_starts, far_scales, facts = pl.pallas_call(
        functools.partial(near_kernel, pair_count * owners, pair_count),
        out_shape=(
            jax.ShapeDtypeStruct((lat_count, couples, SUB, 2 * LANES), jnp.float32),
            jax.ShapeDtypeStruct((lat_count, 2 * LANES, 2 * columns), jnp.bfloat16),
            jax.ShapeDtypeStruct((lat_count, couples, SUB, 2 * columns), jnp.float32),
            jax.ShapeDtypeStruct((lat_count, 2, couples, 2, SUB, LANES), jnp.int32),
            jax.ShapeDtypeStruct((lat_count, 2, couples, SUB, SUB, LANES), jnp.float32),
            jax.ShapeDtypeStruct((4 * lat_count, LANES), jnp.int32),
        ),
        in_specs=[remote] * 5,
        out_specs=(vector,) * 6,
        scratch_shapes=[
            pltpu.SMEM(rows_first.shape, jnp.int32),
            pltpu.SMEM(points.shape, jnp.int32),
            pltpu.VMEM(fields.shape, fields.dtype),
            pltpu.VMEM(starts.shape, starts.dtype),
            pltpu.VMEM(weights.shape, weights.dtype),
            pltpu.VMEM((lat_count, STENCIL, blocks, 1, LANES), jnp.int32),
            pltpu.VMEM((weights.size // LANES, LANES), jnp.float32),
            pltpu.VMEM((fields.size // LANES, LANES), jnp.float32),
            pltpu.VMEM((lat_count, blocks + 2, SUB, LANES), jnp.float32),
            pltpu.SemaphoreType.DMA((5,)),
        ],
        compiler_params=params,
        cost_estimate=pl.CostEstimate(flops=10_000_000, bytes_accessed=4_000_000, transcendentals=0),
        name="near_rows",
    )(*(held(value) for value in (rows_first, points, fields, starts, weights)))

    coefficients = pl.pallas_call(
        far_kernel,
        out_shape=jax.ShapeDtypeStruct((owners, 2 * SUB * lat_count, LANES), jnp.bfloat16),
        in_specs=[vector] * 8,
        out_specs=vector,
        scratch_shapes=[
            pltpu.VMEM((2, fields.size // LANES, LANES), jnp.float32),
            pltpu.VMEM((2 * lat_count, blocks + 2, SUB, LANES), jnp.float32),
            pltpu.VMEM((lat_count, couples, SUB, 2 * LANES), jnp.float32),
            pltpu.VMEM((lat_count, 2 * SUB, columns + LANES), jnp.float32),
        ],
        compiler_params=params,
        name="far_rows",
    )(*sides, far_starts, far_scales, facts, partial, table, twiddle)

    received = lax.all_to_all(coefficients, "lat", split_axis=0, concat_axis=0, tiled=True)
    by_level = received.reshape(lat_total, 2, level_count, field_count, LANES).astype(jnp.float32)
    virtual = by_level[:, :, :, 2] + 0.61 * by_level[:, :, :, 3]
    total = jnp.sum(thickness[None, None, :, None] * virtual, axis=2).transpose(1, 0, 2)
    level_owners = lax.axis_size("lev")
    if level_owners == 2:
        totals = lax.ppermute(total, "lev", [(0, 1), (1, 0)])[None]
    else:
        totals = lax.all_gather(total, "lev")

    out_shape = (level_count, field_count + 1, 2, pair_count, degrees)
    half = level_count * (field_count + 1) * 2 * SUB
    group_count = (pair_count + SUB - 1) // SUB
    left_shape = jax.ShapeDtypeStruct((group_count, 2 * half, SUB * lat_total), jnp.bfloat16)
    wide = pltpu.VMEM((lat_total * 2 * SUB, LANES), jnp.float32)
    left = pl.pallas_call(
        functools.partial(left_kernel, level_count, field_count, pair_count),
        out_shape=left_shape,
        in_specs=[vector],
        out_specs=vector,
        scratch_shapes=[wide],
        compiler_params=params,
        cost_estimate=pl.CostEstimate(flops=50_000_000, bytes_accessed=2_000_000, transcendentals=0),
        name="left_rows",
    )(received)
    return pl.pallas_call(
        functools.partial(legendre_kernel, level_owners, level_count, field_count),
        out_shape=(jax.ShapeDtypeStruct(out_shape, jnp.bfloat16), left_shape),
        in_specs=[scalar, vector, vector, vector, vector],
        out_specs=(pl.BlockSpec(memory_space=pl.ANY), vector),
        input_output_aliases={4: 1},
        scratch_shapes=[
            wide,
            pltpu.VMEM(out_shape, jnp.bfloat16),
            pltpu.SemaphoreType.DMA(((degrees + 255) // 256,)),
        ],
        compiler_params=params,
        name="degree_sums",
    )(thickness, received, totals, legendre, left)[0]


def solution(mesh):
    placed = (
        P("lev", None, "lat", None),
        P("lat"),
        P(),
        P("lat", None, None),
        P("lat", None, None, None),
        P("lev"),
        P("lat", None, None),
    )
    return jax.shard_map(
        local,
        mesh=mesh,
        in_specs=placed,
        out_specs=P("lev", None, None, "lat", None),
        check_vma=False,
    )
```

```python
import functools

import jax
import jax.numpy as jnp
import numpy as np
from jax import lax
from jax.experimental import pallas as pl
from jax.experimental.pallas import tpu as pltpu
from jax.sharding import PartitionSpec as P

LANES = 128
SUB = 8
HALF = 64
STENCIL = 4
LIMIT = 24 * 1024 * 1024


def lane_gather(values, lanes):
    return jnp.take_along_axis(values, lanes, axis=1, mode="promise_in_bounds")


TAKE = lax.GatherDimensionNumbers(
    offset_dims=(),
    collapsed_slice_dims=(1,),
    start_index_map=(1,),
    operand_batching_dims=(0,),
    start_indices_batching_dims=(0,),
)


def short_gather(values, lanes):
    mode = lax.GatherScatterMode.PROMISE_IN_BOUNDS
    return lax.gather(values, lanes[:, :, None], TAKE, (1, 1), mode=mode)


SINE = (-70.99342854244645, 81.34076844400118, -41.337142359536955, 6.283164044230117)
COSINE = (
    56.2423804697887, -85.2403304160897, 64.93459063550272, -19.739171434929204, 0.9999999534680867,
)


def polynomial(terms, square):
    value = np.float32(terms[0])
    for term in terms[1:]:
        value = value * square + np.float32(term)
    return value


def turn_parts(product, total, inverse):
    turns = (product - jnp.floor(product * inverse + 0.5) * total) * inverse
    halves = jnp.floor(2.0 * turns + 0.5)
    sign = 1.0 - 2.0 * jnp.abs(halves)
    part = turns - 0.5 * halves
    square = part * part
    return sign * polynomial(COSINE, square), (sign * part) * polynomial(SINE, square)


def wavenumbers(at, width, pair_count, pair_total):
    column = lax.broadcasted_iota(jnp.int32, (1, width), 1).astype(jnp.float32) + float(at)
    owner = jnp.floor((column + 0.5) * (1.0 / (2 * pair_count)))
    inner = column - owner * (2.0 * pair_count)
    second = inner >= pair_count
    pair = owner * pair_count + jnp.where(second, inner - pair_count, inner)
    return jnp.where(second, 2.0 * pair_total - 1.0 - pair, pair)


def multiplied(one, two):
    return one[0] * two[0] - one[1] * two[1], one[0] * two[1] + one[1] * two[0]


def row_of(pair, row):
    return tuple(part[row : row + 1] for part in pair)


def extend(lines, row, rows_each, missing, ext, slot):
    blocks = ext.shape[1] - 2

    def block_of(block):
        return lines[pl.ds(block * rows_each + row, SUB, stride=blocks * rows_each), :]

    def place(block, values):
        ext[slot, block] = jnp.concatenate([values, values], axis=0).astype(jnp.bfloat16)

    for block in range(blocks - 1):
        place(block + 1, block_of(block))
    lane = lax.broadcasted_iota(jnp.int32, (SUB, LANES), 1)
    ahead = lane + missing
    behind = lane - missing
    first = lane_gather(block_of(0), ahead & (LANES - 1))
    second = lane_gather(block_of(1), ahead & (LANES - 1))
    last = block_of(blocks - 1)
    final = lane_gather(last, behind & (LANES - 1))
    before = lane_gather(block_of(blocks - 2), behind & (LANES - 1))
    place(0, jnp.where(behind >= 0, final, before))
    place(blocks, jnp.where(ahead < LANES, last, first))
    place(blocks + 1, jnp.where(ahead < LANES, first, second))


def spread_rows(starts, begins):
    lat_count, _, blocks = begins.shape[:3]
    for latitude in range(lat_count):
        for block in range(blocks):
            for row in range(STENCIL):
                lanes = slice(block * LANES, (block + 1) * LANES)
                begins[latitude, row, block] = (
                    starts[latitude, row : row + 1, lanes] - (block - 1) * LANES
                )


def spread_lines(source, lines):
    first, second, rows, lon = source.shape
    at = 0
    for one in range(first):
        for two in range(second):
            values = source[one, two].astype(jnp.float32)
            for block in range(lon // LANES):
                lines[at : at + rows, :] = values[:, block * LANES : (block + 1) * LANES]
                at += rows


def gathered(totals, starts, scales, parts):
    for side in range(2):
        for pair in range(2):
            spot = starts[side] + jnp.int16(2 * pair)
            lane = spot & jnp.int16(LANES - 1)
            low, middle, high = [short_gather(part, lane) for part in parts[side : side + 3]]
            value = jnp.where(
                spot < jnp.int16(LANES),
                low,
                jnp.where(spot < jnp.int16(2 * LANES), middle, high),
            ).astype(jnp.float32)
            line = STENCIL * side + 2 * pair
            totals[side] = (
                totals[side] + scales[line] * value[:SUB] + scales[line + 1] * value[SUB:]
            )
    return totals


def near_kernel(
    pair_total, pair_count, rows_first_far, points_far, fields_far, starts_far, weights_far,
    partial, table, twiddle, far_starts, far_scales, facts,
    rows_first, points, fields, starts, weights, begins, factors, lines, ext, arrived,
):
    lat_count, couples = partial.shape[:2]
    lon = 2 * couples * LANES
    columns = table.shape[2] // 2
    first_lat = lax.axis_index("lat") * lat_count
    fetches = [
        pltpu.make_async_copy(source, target, arrived.at[place])
        for place, (source, target) in enumerate(
            (
                (points_far, points),
                (rows_first_far, rows_first),
                (starts_far, starts),
                (weights_far, weights),
                (fields_far, fields),
            )
        )
    ]
    for fetch in fetches:
        fetch.start()
    fetches[0].wait()
    width = 256
    scales = []
    for latitude in range(lat_count):
        total = jnp.full((1, 1), points[first_lat + latitude], jnp.int32).astype(jnp.float32)
        inverse = 1.0 / total
        scales.append((total, inverse, jnp.sqrt(2.0 * inverse)))
    few = lax.broadcasted_iota(jnp.int32, (SUB, width), 0).astype(jnp.float32)
    many = lax.broadcasted_iota(jnp.int32, (couples + 3, width), 0)
    many = jnp.where(many < couples, many * (2 * LANES), (many - (couples - 1)) * HALF)
    many = many.astype(jnp.float32)
    for at in range(0, columns, width):
        numbers = wavenumbers(at, width, pair_count, pair_total)
        for latitude, (total, inverse, scaling) in enumerate(scales):
            ones = turn_parts(numbers * few, total, inverse)
            eights = turn_parts(numbers * (few * float(SUB)), total, inverse)
            large = turn_parts(numbers * many, total, inverse)
            here = slice(at, at + width)
            there = slice(columns + at, columns + at + width)
            for couple in range(couples):
                for lanes, part in ((here, large[0]), (there, large[1])):
                    twiddle[latitude, couple, :, lanes] = jnp.broadcast_to(
                        scaling * part[couple : couple + 1], (SUB, width)
                    )
            products = [ones] + [multiplied(row_of(eights, row), ones) for row in range(1, SUB)]
            block = tuple(jnp.concatenate(parts, axis=0) for parts in zip(*products))
            for quarter in range(4):
                turned = block
                if quarter > 0:
                    turned = multiplied(row_of(large, couples + quarter - 1), block)
                rows = slice(HALF * quarter, HALF * (quarter + 1))
                table[latitude, rows, here] = turned[0].astype(jnp.bfloat16)
                table[latitude, rows, there] = turned[1].astype(jnp.bfloat16)
    for fetch in fetches[1:]:
        fetch.wait()
    known = [first_lat - rows_first[latitude] for latitude in range(lat_count)]
    known += [points[first_lat + latitude] for latitude in range(lat_count)]
    for place in range(-lat_count, 2 * lat_count):
        if place < 0 or place >= lat_count:
            place = jnp.clip(first_lat + place, 0, points.shape[0] - 1)
            known.append(lon - points[place])
    facts[...] = jnp.concatenate([jnp.full((1, LANES), one, jnp.int32) for one in known], axis=0)
    spread_rows(starts, begins)
    spread_lines(weights, factors)
    spread_lines(fields, lines)
    for latitude in range(lat_count):
        extend(lines, latitude, lat_count, lon - points[first_lat + latitude], ext, latitude)
    lower = (lax.broadcasted_iota(jnp.int32, (2 * SUB, LANES), 0) >= SUB).astype(jnp.int32)
    for latitude in range(lat_count):
        mine = first_lat - rows_first[latitude]
        for couple in range(couples):

            def spread_row(row):
                at = ((latitude * STENCIL + row) * couples + couple) * SUB
                tile = factors[pl.ds(pl.multiple_of(at, SUB), SUB), :]
                begun = []
                for side in range(2):
                    start = jnp.broadcast_to(
                        begins[latitude, row, 2 * couple + side], (2 * SUB, LANES)
                    )
                    begun.append((start + lower).astype(jnp.int16))
                return (
                    begun,
                    [jnp.broadcast_to(tile[line : line + 1], (SUB, LANES)) for line in range(SUB)],
                )

            totals = [jnp.zeros((SUB, LANES), jnp.float32) for _ in range(2)]
            for slot in range(lat_count):
                begun, scales = spread_row(mine + slot)
                parts = [ext[slot, 2 * couple + piece] for piece in range(4)]
                totals = gathered(totals, begun, scales, parts)
            for side in range(2):
                partial[latitude, couple, :, side * LANES : (side + 1) * LANES] = totals[side]
            others = (jnp.where(mine >= 1, 0, 2), jnp.where(mine <= 1, 3, 1))
            for choice, row in enumerate(others):
                begun, scales = spread_row(row)
                for side in range(2):
                    far_starts[latitude, choice, couple, side] = begun[side]
                for line in range(SUB):
                    far_scales[latitude, choice, couple, line] = scales[line]


def far_kernel(
    near_side, far_side, far_starts, far_scales, facts, partial, table, twiddle,
    out, lines, ext, grid, waves,
):
    lat_count, couples = partial.shape[:2]
    columns = table.shape[2] // 2
    owners = out.shape[0]
    toward = 1 - lax.axis_index("lat") % 2
    spread_lines(near_side, lines.at[toward])
    spread_lines(far_side, lines.at[1 - toward])
    fact = [jnp.broadcast_to(facts[row : row + 1], (SUB, LANES)) for row in range(4 * lat_count)]
    for slot in range(2 * lat_count):
        side, row = divmod(slot, lat_count)
        extend(lines.at[side], row, lat_count, fact[2 * lat_count + slot], ext, slot)
    lane = lax.broadcasted_iota(jnp.int32, (SUB, LANES), 1)
    width = 256
    choices = ((2, 1, 0), (3, 2, 1))
    for latitude in range(lat_count):
        own = jnp.broadcast_to(facts[latitude : latitude + 1], (2 * SUB, LANES)).astype(jnp.int16)
        at_zero = own == jnp.int16(0)
        at_one = own == jnp.int16(1)
        for couple in range(couples):
            sides = [pl.ds(side * LANES, LANES) for side in range(2)]
            totals = [partial[latitude, couple, :, lanes] for lanes in sides]
            for choice, slots in enumerate(choices):
                parts = []
                for piece in range(4):
                    zero, one, two = [ext[slot, 2 * couple + piece] for slot in slots]
                    parts.append(jnp.where(at_zero, zero, jnp.where(at_one, one, two)))
                totals = gathered(
                    totals,
                    [far_starts[latitude, choice, couple, side] for side in range(2)],
                    [far_scales[latitude, choice, couple, line] for line in range(SUB)],
                    parts,
                )
            for side in range(2):
                live = lane + (2 * couple + side) * LANES < fact[lat_count + latitude]
                grid[latitude, couple, :, sides[side]] = jnp.where(live, totals[side], 0.0)
    for latitude in range(lat_count):
        rows = grid[latitude].reshape(couples * SUB, 2 * LANES).astype(jnp.bfloat16)
        for at in range(0, columns, width):
            real = jnp.dot(
                rows, table[latitude, :, at : at + width], preferred_element_type=jnp.float32
            )
            imag = jnp.dot(
                rows,
                table[latitude, :, columns + at : columns + at + width],
                preferred_element_type=jnp.float32,
            )
            cosine = jnp.zeros((SUB, width), jnp.float32)
            sine = jnp.zeros((SUB, width), jnp.float32)
            for couple in range(couples):
                turn_cos = twiddle[latitude, couple, :, at : at + width]
                turn_sin = twiddle[latitude, couple, :, columns + at : columns + at + width]
                here = slice(couple * SUB, (couple + 1) * SUB)
                cosine = cosine + (real[here] * turn_cos - imag[here] * turn_sin)
                sine = sine - (real[here] * turn_sin + imag[here] * turn_cos)
            waves[latitude, 0:SUB, at : at + width] = cosine
            waves[latitude, SUB : 2 * SUB, at : at + width] = sine
        waves[latitude, :, columns:] = jnp.zeros((2 * SUB, waves.shape[2] - columns), jnp.float32)
        used = columns // owners
        for owner in range(owners):
            out[owner, 2 * SUB * latitude : 2 * SUB * (latitude + 1), :] = waves[
                latitude, :, owner * used : owner * used + LANES
            ].astype(jnp.bfloat16)


def row_keys(level_count, field_count):
    return [
        (level, field, part)
        for level in range(level_count)
        for field in range(field_count + 1)
        for part in range(2)
    ]


def place_rows(lines, keys, pair_count, left):
    lat_total = next(iter(lines.values())).shape[0]
    depth = SUB * lat_total
    half = len(keys) * SUB
    spread = (
        lax.broadcasted_iota(jnp.int32, (lat_total, depth), 0)
        == lax.broadcasted_iota(jnp.int32, (lat_total, depth), 1) % lat_total
    ).astype(jnp.bfloat16)
    keep = (
        lax.broadcasted_iota(jnp.int32, (SUB, depth), 0)
        == lax.broadcasted_iota(jnp.int32, (SUB, depth), 1) // lat_total
    )
    for place in range(0, len(keys), 2):
        if keys[place] not in lines:
            continue
        couple = [
            lax.dot_general(
                lines[key].astype(jnp.bfloat16),
                spread,
                (((0,), (0,)), ((), ())),
                preferred_element_type=jnp.float32,
            )
            for key in keys[place : place + 2]
        ]
        for member in range(2):
            for group in range(left.shape[0]):
                begin = member * pair_count + group * SUB
                pieces = [jnp.where(keep, one[begin : begin + SUB], 0.0) for one in couple]
                into = member * half + place * SUB
                left[group, into : into + 2 * SUB, :] = jnp.concatenate(pieces, axis=0).astype(
                    jnp.bfloat16
                )


def received_rows(received, wide, keys, field_count):
    wide[...] = received[...].astype(jnp.float32).reshape(wide.shape)
    lat_total = wide.shape[0] // (2 * SUB)
    return {
        (level, field, part): wide[
            pl.ds(part * SUB + level * field_count + field, lat_total, stride=2 * SUB), :
        ]
        for level, field, part in keys
    }


def left_kernel(level_count, field_count, pair_count, received, left, wide):
    keys = row_keys(level_count, field_count)
    wanted = [key for key in keys if key[1] < field_count]
    place_rows(received_rows(received, wide, wanted, field_count), keys, pair_count, left)


def legendre_kernel(
    level_owners, level_count, field_count, thickness, received, totals, legendre, left_given,
    out, left, wide, planes, sent,
):
    owners = received.shape[0]
    pair_count, lat_total, degrees = legendre.shape
    pair_total = pair_count * owners
    groups = [(at, min(SUB, pair_count - at)) for at in range(0, pair_count, SUB)]
    keys = row_keys(level_count, field_count)
    half = len(keys) * SUB
    level_place = lax.axis_index("lev")
    first_pair = lax.axis_index("lat") * pair_count
    wanted = [(level, field, part) for level in range(level_count) for field in (2, 3) for part in range(2)]
    lines = received_rows(received, wide, wanted, field_count)
    sums = {}
    for part in range(2):
        running = jnp.zeros((lat_total, LANES), jnp.float32)
        for place in range(totals.shape[0]):
            other = 1 - level_place if level_owners == 2 else place
            running = running + jnp.where(other > level_place, totals[place, part], 0.0)
        for level in reversed(range(level_count)):
            running = running + thickness[level] * (
                lines[level, 2, part] + 0.61 * lines[level, 3, part]
            )
            sums[level, field_count, part] = running
    place_rows(sums, keys, pair_count, left)
    copies = []
    for start in range(0, degrees, 256):
        stop = min(start + 256, degrees)
        low = 0 if start < 2 * pair_total else half
        high = 2 * half if stop > pair_total + 1 else half
        parts = []
        for group, (at, size) in enumerate(groups):
            values = legendre[at : at + size, :, start:stop].reshape(size * lat_total, stop - start)
            sums = jnp.dot(
                left[group, low:high, : size * lat_total],
                values,
                preferred_element_type=jnp.float32,
            ).reshape((high - low) // SUB, SUB, stop - start)
            if high - low > half:
                shape = (SUB, stop - start)
                slot = lax.broadcasted_iota(jnp.int32, shape, 1) + start
                pair = lax.broadcasted_iota(jnp.int32, shape, 0) + (first_pair + at)
                sums = jnp.where(
                    slot + pair < 2 * pair_total, sums[: len(keys)], sums[len(keys) :]
                )
            parts.append(sums[:, :size])
        planes[:, :, :, :, start:stop] = (
            jnp.concatenate(parts, axis=1).astype(jnp.bfloat16).reshape(planes.shape[:4] + (stop - start,))
        )
        here = pl.ds(start, stop - start)
        copies.append(
            pltpu.make_async_copy(
                planes.at[:, :, :, :, here], out.at[:, :, :, :, here], sent.at[len(copies)]
            )
        )
        copies[-1].start()
    for copy in copies:
        copy.wait()


def held(value):
    return pltpu.with_memory_space_constraint(value, pltpu.HBM)


def local(fields, rows_first, points, starts, weights, thickness, legendre):
    level_count, field_count, lat_count, lon_count = fields.shape
    pair_count, lat_total, degrees = legendre.shape
    owners = lax.axis_size("lat")
    couples = lon_count // (2 * LANES)
    blocks = 2 * couples
    columns = 2 * owners * pair_count
    sides = []
    for first in range(2):
        edges = [(i, i + 1) for i in range(first, owners - 1, 2)]
        sides.append(lax.ppermute(fields, "lat", edges + [(j, i) for i, j in edges]))

    scalar = pl.BlockSpec(memory_space=pltpu.SMEM)
    vector = pl.BlockSpec(memory_space=pltpu.VMEM)
    params = pltpu.CompilerParams(vmem_limit_bytes=LIMIT)
    remote = pl.BlockSpec(memory_space=pltpu.HBM)
    partial, table, twiddle, far_starts, far_scales, facts = pl.pallas_call(
        functools.partial(near_kernel, pair_count * owners, pair_count),
        out_shape=(
            jax.ShapeDtypeStruct((lat_count, couples, SUB, 2 * LANES), jnp.float32),
            jax.ShapeDtypeStruct((lat_count, 2 * LANES, 2 * columns), jnp.bfloat16),
            jax.ShapeDtypeStruct((lat_count, couples, SUB, 2 * columns), jnp.float32),
            jax.ShapeDtypeStruct((lat_count, 2, couples, 2, 2 * SUB, LANES), jnp.int16),
            jax.ShapeDtypeStruct((lat_count, 2, couples, SUB, SUB, LANES), jnp.float32),
            jax.ShapeDtypeStruct((4 * lat_count, LANES), jnp.int32),
        ),
        in_specs=[remote] * 5,
        out_specs=(vector,) * 6,
        scratch_shapes=[
            pltpu.SMEM(rows_first.shape, jnp.int32),
            pltpu.SMEM(points.shape, jnp.int32),
            pltpu.VMEM(fields.shape, fields.dtype),
            pltpu.VMEM(starts.shape, starts.dtype),
            pltpu.VMEM(weights.shape, weights.dtype),
            pltpu.VMEM((lat_count, STENCIL, blocks, 1, LANES), jnp.int32),
            pltpu.VMEM((weights.size // LANES, LANES), jnp.float32),
            pltpu.VMEM((fields.size // LANES, LANES), jnp.float32),
            pltpu.VMEM((lat_count, blocks + 2, 2 * SUB, LANES), jnp.bfloat16),
            pltpu.SemaphoreType.DMA((5,)),
        ],
        compiler_params=params,
        cost_estimate=pl.CostEstimate(flops=10_000_000, bytes_accessed=4_000_000, transcendentals=0),
        name="near_rows",
    )(*(held(value) for value in (rows_first, points, fields, starts, weights)))

    coefficients = pl.pallas_call(
        far_kernel,
        out_shape=jax.ShapeDtypeStruct((owners, 2 * SUB * lat_count, LANES), jnp.bfloat16),
        in_specs=[vector] * 8,
        out_specs=vector,
        scratch_shapes=[
            pltpu.VMEM((2, fields.size // LANES, LANES), jnp.float32),
            pltpu.VMEM((2 * lat_count, blocks + 2, 2 * SUB, LANES), jnp.bfloat16),
            pltpu.VMEM((lat_count, couples, SUB, 2 * LANES), jnp.float32),
            pltpu.VMEM((lat_count, 2 * SUB, columns + LANES), jnp.float32),
        ],
        compiler_params=params,
        name="far_rows",
    )(*sides, far_starts, far_scales, facts, partial, table, twiddle)

    received = lax.all_to_all(coefficients, "lat", split_axis=0, concat_axis=0, tiled=True)
    by_level = received.reshape(lat_total, 2, level_count, field_count, LANES).astype(jnp.float32)
    virtual = by_level[:, :, :, 2] + 0.61 * by_level[:, :, :, 3]
    total = jnp.sum(thickness[None, None, :, None] * virtual, axis=2).transpose(1, 0, 2)
    level_owners = lax.axis_size("lev")
    if level_owners == 2:
        totals = lax.ppermute(total, "lev", [(0, 1), (1, 0)])[None]
    else:
        totals = lax.all_gather(total, "lev")

    out_shape = (level_count, field_count + 1, 2, pair_count, degrees)
    half = level_count * (field_count + 1) * 2 * SUB
    group_count = (pair_count + SUB - 1) // SUB
    left_shape = jax.ShapeDtypeStruct((group_count, 2 * half, SUB * lat_total), jnp.bfloat16)
    wide = pltpu.VMEM((lat_total * 2 * SUB, LANES), jnp.float32)
    left = pl.pallas_call(
        functools.partial(left_kernel, level_count, field_count, pair_count),
        out_shape=left_shape,
        in_specs=[vector],
        out_specs=vector,
        scratch_shapes=[wide],
        compiler_params=params,
        cost_estimate=pl.CostEstimate(flops=50_000_000, bytes_accessed=2_000_000, transcendentals=0),
        name="left_rows",
    )(received)
    return pl.pallas_call(
        functools.partial(legendre_kernel, level_owners, level_count, field_count),
        out_shape=(jax.ShapeDtypeStruct(out_shape, jnp.bfloat16), left_shape),
        in_specs=[scalar, vector, vector, vector, vector],
        out_specs=(pl.BlockSpec(memory_space=pl.ANY), vector),
        input_output_aliases={4: 1},
        scratch_shapes=[
            wide,
            pltpu.VMEM(out_shape, jnp.bfloat16),
            pltpu.SemaphoreType.DMA(((degrees + 255) // 256,)),
        ],
        compiler_params=params,
        name="degree_sums",
    )(thickness, received, totals, legendre, left)[0]


def solution(mesh):
    placed = (
        P("lev", None, "lat", None),
        P("lat"),
        P(),
        P("lat", None, None),
        P("lat", None, None, None),
        P("lev"),
        P("lat", None, None),
    )
    return jax.shard_map(
        local,
        mesh=mesh,
        in_specs=placed,
        out_specs=P("lev", None, None, "lat", None),
        check_vma=False,
    )
```

```python
import functools

import jax
import jax.numpy as jnp
import numpy as np
from jax import lax
from jax.experimental import pallas as pl
from jax.experimental.pallas import tpu as pltpu
from jax.sharding import PartitionSpec as P

LANES = 128
SUB = 8
HALF = 64
STENCIL = 4
LIMIT = 24 * 1024 * 1024


def lane_gather(values, lanes):
    return jnp.take_along_axis(values, lanes, axis=1, mode="promise_in_bounds")


TAKE = lax.GatherDimensionNumbers(
    offset_dims=(),
    collapsed_slice_dims=(1,),
    start_index_map=(1,),
    operand_batching_dims=(0,),
    start_indices_batching_dims=(0,),
)


def short_gather(values, lanes):
    mode = lax.GatherScatterMode.PROMISE_IN_BOUNDS
    return lax.gather(values, lanes[:, :, None], TAKE, (1, 1), mode=mode)


SINE = (-70.99342854244645, 81.34076844400118, -41.337142359536955, 6.283164044230117)
COSINE = (
    56.2423804697887, -85.2403304160897, 64.93459063550272, -19.739171434929204, 0.9999999534680867,
)


def polynomial(terms, square):
    value = np.float32(terms[0])
    for term in terms[1:]:
        value = value * square + np.float32(term)
    return value


def turn_parts(product, total, inverse):
    turns = (product - jnp.floor(product * inverse + 0.5) * total) * inverse
    halves = jnp.floor(2.0 * turns + 0.5)
    sign = 1.0 - 2.0 * jnp.abs(halves)
    part = turns - 0.5 * halves
    square = part * part
    return sign * polynomial(COSINE, square), (sign * part) * polynomial(SINE, square)


def wavenumbers(at, width, pair_count, pair_total):
    column = lax.broadcasted_iota(jnp.int32, (1, width), 1).astype(jnp.float32) + float(at)
    owner = jnp.floor((column + 0.5) * (1.0 / (2 * pair_count)))
    inner = column - owner * (2.0 * pair_count)
    second = inner >= pair_count
    pair = owner * pair_count + jnp.where(second, inner - pair_count, inner)
    return jnp.where(second, 2.0 * pair_total - 1.0 - pair, pair)


def multiplied(one, two):
    return one[0] * two[0] - one[1] * two[1], one[0] * two[1] + one[1] * two[0]


def row_of(pair, row):
    return tuple(part[row : row + 1] for part in pair)


def extend(lines, row, rows_each, missing, ext, slot):
    blocks = ext.shape[1] - 2

    def block_of(block):
        return lines[pl.ds(block * rows_each + row, SUB, stride=blocks * rows_each), :]

    def place(block, values):
        ext[slot, block] = jnp.concatenate([values, values], axis=0).astype(jnp.bfloat16)

    for block in range(blocks - 1):
        place(block + 1, block_of(block))
    lane = lax.broadcasted_iota(jnp.int32, (SUB, LANES), 1)
    ahead = lane + missing
    behind = lane - missing
    first = lane_gather(block_of(0), ahead & (LANES - 1))
    second = lane_gather(block_of(1), ahead & (LANES - 1))
    last = block_of(blocks - 1)
    final = lane_gather(last, behind & (LANES - 1))
    before = lane_gather(block_of(blocks - 2), behind & (LANES - 1))
    place(0, jnp.where(behind >= 0, final, before))
    place(blocks, jnp.where(ahead < LANES, last, first))
    place(blocks + 1, jnp.where(ahead < LANES, first, second))


def spread_rows(starts, begins):
    lat_count, _, blocks = begins.shape[:3]
    for latitude in range(lat_count):
        for block in range(blocks):
            for row in range(STENCIL):
                lanes = slice(block * LANES, (block + 1) * LANES)
                begins[latitude, row, block] = (
                    starts[latitude, row : row + 1, lanes] - (block - 1) * LANES
                )


def spread_lines(source, lines):
    first, second, rows, lon = source.shape
    at = 0
    for one in range(first):
        for two in range(second):
            values = source[one, two].astype(jnp.float32)
            for block in range(lon // LANES):
                lines[at : at + rows, :] = values[:, block * LANES : (block + 1) * LANES]
                at += rows


def gathered(totals, starts, scales, parts):
    for side in range(2):
        for pair in range(2):
            spot = starts[side] + jnp.int16(2 * pair)
            lane = spot & jnp.int16(LANES - 1)
            low, middle, high = [short_gather(part, lane) for part in parts[side : side + 3]]
            value = jnp.where(
                spot < jnp.int16(LANES),
                low,
                jnp.where(spot < jnp.int16(2 * LANES), middle, high),
            ).astype(jnp.float32)
            line = STENCIL * side + 2 * pair
            totals[side] = (
                totals[side] + scales[line] * value[:SUB] + scales[line + 1] * value[SUB:]
            )
    return totals


def add_unit(latitude, choice, slot, far_starts, far_scales, ext, into):
    for couple in range(into.shape[1]):
        sides = [pl.ds(side * LANES, LANES) for side in range(2)]
        totals = gathered(
            [into[latitude, couple, :, lanes] for lanes in sides],
            [far_starts[latitude, choice, couple, side] for side in range(2)],
            [far_scales[latitude, choice, couple, line] for line in range(SUB)],
            [ext[slot, 2 * couple + piece] for piece in range(4)],
        )
        for lanes, total in zip(sides, totals):
            into[latitude, couple, :, lanes] = total


def near_kernel(
    pair_total, pair_count, rows_first_far, points_far, fields_far, starts_far, weights_far, side_rows,
    partial, table, twiddle, far_starts, far_scales, facts,
    rows_first, points, fields, starts, weights, begins, factors, lines, side_lines, ext, arrived,
):
    lat_count, couples = partial.shape[:2]
    lon = 2 * couples * LANES
    columns = table.shape[2] // 2
    first_lat = lax.axis_index("lat") * lat_count
    fetches = [
        pltpu.make_async_copy(source, target, arrived.at[place])
        for place, (source, target) in enumerate(
            (
                (points_far, points),
                (rows_first_far, rows_first),
                (starts_far, starts),
                (weights_far, weights),
                (fields_far, fields),
            )
        )
    ]
    for fetch in fetches:
        fetch.start()
    spread_lines(side_rows, side_lines)
    fetches[0].wait()
    width = 256
    scales = []
    for latitude in range(lat_count):
        total = jnp.full((1, 1), points[first_lat + latitude], jnp.int32).astype(jnp.float32)
        inverse = 1.0 / total
        scales.append((total, inverse, jnp.sqrt(2.0 * inverse)))
    few = lax.broadcasted_iota(jnp.int32, (SUB, width), 0).astype(jnp.float32)
    many = lax.broadcasted_iota(jnp.int32, (couples + 3, width), 0)
    many = jnp.where(many < couples, many * (2 * LANES), (many - (couples - 1)) * HALF)
    many = many.astype(jnp.float32)
    for at in range(0, columns, width):
        numbers = wavenumbers(at, width, pair_count, pair_total)
        for latitude, (total, inverse, scaling) in enumerate(scales):
            ones = turn_parts(numbers * few, total, inverse)
            eights = turn_parts(numbers * (few * float(SUB)), total, inverse)
            large = turn_parts(numbers * many, total, inverse)
            here = slice(at, at + width)
            there = slice(columns + at, columns + at + width)
            for couple in range(couples):
                for lanes, part in ((here, large[0]), (there, large[1])):
                    twiddle[latitude, couple, :, lanes] = jnp.broadcast_to(
                        scaling * part[couple : couple + 1], (SUB, width)
                    )
            products = [ones] + [multiplied(row_of(eights, row), ones) for row in range(1, SUB)]
            block = tuple(jnp.concatenate(parts, axis=0) for parts in zip(*products))
            for quarter in range(4):
                turned = block
                if quarter > 0:
                    turned = multiplied(row_of(large, couples + quarter - 1), block)
                rows = slice(HALF * quarter, HALF * (quarter + 1))
                table[latitude, rows, here] = turned[0].astype(jnp.bfloat16)
                table[latitude, rows, there] = turned[1].astype(jnp.bfloat16)
    for fetch in fetches[1:]:
        fetch.wait()
    upper = lax.axis_index("lat") % 2 == 0

    def missing_of(slot, above):
        place = jnp.where(above, first_lat + lat_count + slot, first_lat - lat_count + slot)
        return lon - points[jnp.clip(place, 0, points.shape[0] - 1)]

    units = {}
    for latitude in range(lat_count):
        for choice in range(2):
            slot = 2 + choice - (first_lat - rows_first[latitude])
            units[latitude, choice] = ((slot >= 2) == upper, slot % 2)
    known = [points[first_lat + latitude] for latitude in range(lat_count)]
    known += [jnp.where(ours, -1, row) for ours, row in units.values()]
    known += [missing_of(row, jnp.logical_not(upper)) for row in range(lat_count)]
    facts[...] = jnp.concatenate([jnp.full((1, LANES), one, jnp.int32) for one in known], axis=0)
    spread_rows(starts, begins)
    spread_lines(weights, factors)
    spread_lines(fields, lines)
    for latitude in range(lat_count):
        extend(lines, latitude, lat_count, lon - points[first_lat + latitude], ext, latitude)
        extend(
            side_lines, latitude, lat_count, missing_of(latitude, upper), ext, lat_count + latitude
        )
    lower = (lax.broadcasted_iota(jnp.int32, (2 * SUB, LANES), 0) >= SUB).astype(jnp.int32)
    for latitude in range(lat_count):
        mine = first_lat - rows_first[latitude]
        for couple in range(couples):

            def spread_row(row):
                at = ((latitude * STENCIL + row) * couples + couple) * SUB
                tile = factors[pl.ds(pl.multiple_of(at, SUB), SUB), :]
                begun = []
                for side in range(2):
                    start = jnp.broadcast_to(
                        begins[latitude, row, 2 * couple + side], (2 * SUB, LANES)
                    )
                    begun.append((start + lower).astype(jnp.int16))
                return (
                    begun,
                    [jnp.broadcast_to(tile[line : line + 1], (SUB, LANES)) for line in range(SUB)],
                )

            totals = [jnp.zeros((SUB, LANES), jnp.float32) for _ in range(2)]
            for slot in range(lat_count):
                begun, scales = spread_row(mine + slot)
                parts = [ext[slot, 2 * couple + piece] for piece in range(4)]
                totals = gathered(totals, begun, scales, parts)
            for side in range(2):
                partial[latitude, couple, :, side * LANES : (side + 1) * LANES] = totals[side]
            others = (jnp.where(mine >= 1, 0, 2), jnp.where(mine <= 1, 3, 1))
            for choice, row in enumerate(others):
                begun, scales = spread_row(row)
                for side in range(2):
                    far_starts[latitude, choice, couple, side] = begun[side]
                for line in range(SUB):
                    far_scales[latitude, choice, couple, line] = scales[line]
        for choice in range(2):
            ours, row = units[latitude, choice]

            @pl.when(ours)
            def add(latitude=latitude, choice=choice, row=row):
                add_unit(latitude, choice, lat_count + row, far_starts, far_scales, ext, partial)


def far_kernel(
    far_side, far_starts, far_scales, facts, partial, table, twiddle,
    out, lines, ext, grid, waves,
):
    lat_count, couples = partial.shape[:2]
    columns = table.shape[2] // 2
    owners = out.shape[0]
    spread_lines(far_side, lines)
    fact = [jnp.broadcast_to(facts[row : row + 1], (SUB, LANES)) for row in range(4 * lat_count)]
    for row in range(lat_count):
        extend(lines, row, lat_count, fact[3 * lat_count + row], ext, row)
    grid[...] = partial[...]
    for latitude in range(lat_count):
        for choice in range(2):
            code = fact[lat_count + 2 * latitude + choice].astype(jnp.float32)
            place = jnp.max(code).astype(jnp.int32)

            @pl.when(place >= 0)
            def add(latitude=latitude, choice=choice, place=place):
                add_unit(latitude, choice, place, far_starts, far_scales, ext, grid)

    lane = lax.broadcasted_iota(jnp.int32, (SUB, LANES), 1)
    width = 256
    for latitude in range(lat_count):
        for couple in range(couples):
            for side in range(2):
                lanes = pl.ds(side * LANES, LANES)
                live = lane + (2 * couple + side) * LANES < fact[latitude]
                grid[latitude, couple, :, lanes] = jnp.where(
                    live, grid[latitude, couple, :, lanes], 0.0
                )
    for latitude in range(lat_count):
        rows = grid[latitude].reshape(couples * SUB, 2 * LANES).astype(jnp.bfloat16)
        for at in range(0, columns, width):
            real = jnp.dot(
                rows, table[latitude, :, at : at + width], preferred_element_type=jnp.float32
            )
            imag = jnp.dot(
                rows,
                table[latitude, :, columns + at : columns + at + width],
                preferred_element_type=jnp.float32,
            )
            cosine = jnp.zeros((SUB, width), jnp.float32)
            sine = jnp.zeros((SUB, width), jnp.float32)
            for couple in range(couples):
                turn_cos = twiddle[latitude, couple, :, at : at + width]
                turn_sin = twiddle[latitude, couple, :, columns + at : columns + at + width]
                here = slice(couple * SUB, (couple + 1) * SUB)
                cosine = cosine + (real[here] * turn_cos - imag[here] * turn_sin)
                sine = sine - (real[here] * turn_sin + imag[here] * turn_cos)
            waves[latitude, 0:SUB, at : at + width] = cosine
            waves[latitude, SUB : 2 * SUB, at : at + width] = sine
        waves[latitude, :, columns:] = jnp.zeros((2 * SUB, waves.shape[2] - columns), jnp.float32)
        used = columns // owners
        for owner in range(owners):
            out[owner, 2 * SUB * latitude : 2 * SUB * (latitude + 1), :] = waves[
                latitude, :, owner * used : owner * used + LANES
            ].astype(jnp.bfloat16)


def row_keys(level_count, field_count):
    return [
        (level, field, part)
        for level in range(level_count)
        for field in range(field_count + 1)
        for part in range(2)
    ]


def place_rows(lines, keys, pair_count, left):
    lat_total = next(iter(lines.values())).shape[0]
    depth = SUB * lat_total
    half = len(keys) * SUB
    spread = (
        lax.broadcasted_iota(jnp.int32, (lat_total, depth), 0)
        == lax.broadcasted_iota(jnp.int32, (lat_total, depth), 1) % lat_total
    ).astype(jnp.bfloat16)
    keep = (
        lax.broadcasted_iota(jnp.int32, (SUB, depth), 0)
        == lax.broadcasted_iota(jnp.int32, (SUB, depth), 1) // lat_total
    )
    for place in range(0, len(keys), 2):
        if keys[place] not in lines:
            continue
        couple = [
            lax.dot_general(
                lines[key].astype(jnp.bfloat16),
                spread,
                (((0,), (0,)), ((), ())),
                preferred_element_type=jnp.float32,
            )
            for key in keys[place : place + 2]
        ]
        for member in range(2):
            for group in range(left.shape[0]):
                begin = member * pair_count + group * SUB
                pieces = [jnp.where(keep, one[begin : begin + SUB], 0.0) for one in couple]
                into = member * half + place * SUB
                left[group, into : into + 2 * SUB, :] = jnp.concatenate(pieces, axis=0).astype(
                    jnp.bfloat16
                )


def received_rows(received, wide, keys, field_count):
    wide[...] = received[...].astype(jnp.float32).reshape(wide.shape)
    lat_total = wide.shape[0] // (2 * SUB)
    return {
        (level, field, part): wide[
            pl.ds(part * SUB + level * field_count + field, lat_total, stride=2 * SUB), :
        ]
        for level, field, part in keys
    }


def left_kernel(level_count, field_count, pair_count, received, left, wide):
    keys = row_keys(level_count, field_count)
    wanted = [key for key in keys if key[1] < field_count]
    place_rows(received_rows(received, wide, wanted, field_count), keys, pair_count, left)


def legendre_kernel(
    level_owners, level_count, field_count, thickness, received, totals, legendre, left_given,
    out, left, wide, planes, sent,
):
    owners = received.shape[0]
    pair_count, lat_total, degrees = legendre.shape
    pair_total = pair_count * owners
    groups = [(at, min(SUB, pair_count - at)) for at in range(0, pair_count, SUB)]
    keys = row_keys(level_count, field_count)
    half = len(keys) * SUB
    level_place = lax.axis_index("lev")
    first_pair = lax.axis_index("lat") * pair_count
    wanted = [(level, field, part) for level in range(level_count) for field in (2, 3) for part in range(2)]
    lines = received_rows(received, wide, wanted, field_count)
    sums = {}
    for part in range(2):
        running = jnp.zeros((lat_total, LANES), jnp.float32)
        for place in range(totals.shape[0]):
            other = 1 - level_place if level_owners == 2 else place
            running = running + jnp.where(other > level_place, totals[place, part], 0.0)
        for level in reversed(range(level_count)):
            running = running + thickness[level] * (
                lines[level, 2, part] + 0.61 * lines[level, 3, part]
            )
            sums[level, field_count, part] = running
    place_rows(sums, keys, pair_count, left)
    copies = []
    for start in range(0, degrees, 256):
        stop = min(start + 256, degrees)
        low = 0 if start < 2 * pair_total else half
        high = 2 * half if stop > pair_total + 1 else half
        parts = []
        for group, (at, size) in enumerate(groups):
            values = legendre[at : at + size, :, start:stop].reshape(size * lat_total, stop - start)
            sums = jnp.dot(
                left[group, low:high, : size * lat_total],
                values,
                preferred_element_type=jnp.float32,
            ).reshape((high - low) // SUB, SUB, stop - start)
            if high - low > half:
                shape = (SUB, stop - start)
                slot = lax.broadcasted_iota(jnp.int32, shape, 1) + start
                pair = lax.broadcasted_iota(jnp.int32, shape, 0) + (first_pair + at)
                sums = jnp.where(
                    slot + pair < 2 * pair_total, sums[: len(keys)], sums[len(keys) :]
                )
            parts.append(sums[:, :size])
        planes[:, :, :, :, start:stop] = (
            jnp.concatenate(parts, axis=1).astype(jnp.bfloat16).reshape(planes.shape[:4] + (stop - start,))
        )
        here = pl.ds(start, stop - start)
        copies.append(
            pltpu.make_async_copy(
                planes.at[:, :, :, :, here], out.at[:, :, :, :, here], sent.at[len(copies)]
            )
        )
        copies[-1].start()
    for copy in copies:
        copy.wait()


def held(value):
    return pltpu.with_memory_space_constraint(value, pltpu.HBM)


def local(fields, rows_first, points, starts, weights, thickness, legendre):
    level_count, field_count, lat_count, lon_count = fields.shape
    pair_count, lat_total, degrees = legendre.shape
    owners = lax.axis_size("lat")
    couples = lon_count // (2 * LANES)
    blocks = 2 * couples
    columns = 2 * owners * pair_count
    sides = []
    for first in range(2):
        edges = [(i, i + 1) for i in range(first, owners - 1, 2)]
        sides.append(lax.ppermute(fields, "lat", edges + [(j, i) for i, j in edges]))

    scalar = pl.BlockSpec(memory_space=pltpu.SMEM)
    vector = pl.BlockSpec(memory_space=pltpu.VMEM)
    params = pltpu.CompilerParams(vmem_limit_bytes=LIMIT)
    remote = pl.BlockSpec(memory_space=pltpu.HBM)
    partial, table, twiddle, far_starts, far_scales, facts = pl.pallas_call(
        functools.partial(near_kernel, pair_count * owners, pair_count),
        out_shape=(
            jax.ShapeDtypeStruct((lat_count, couples, SUB, 2 * LANES), jnp.float32),
            jax.ShapeDtypeStruct((lat_count, 2 * LANES, 2 * columns), jnp.bfloat16),
            jax.ShapeDtypeStruct((lat_count, couples, SUB, 2 * columns), jnp.float32),
            jax.ShapeDtypeStruct((lat_count, 2, couples, 2, 2 * SUB, LANES), jnp.int16),
            jax.ShapeDtypeStruct((lat_count, 2, couples, SUB, SUB, LANES), jnp.float32),
            jax.ShapeDtypeStruct((4 * lat_count, LANES), jnp.int32),
        ),
        in_specs=[remote] * 5 + [vector],
        out_specs=(vector,) * 6,
        scratch_shapes=[
            pltpu.SMEM(rows_first.shape, jnp.int32),
            pltpu.SMEM(points.shape, jnp.int32),
            pltpu.VMEM(fields.shape, fields.dtype),
            pltpu.VMEM(starts.shape, starts.dtype),
            pltpu.VMEM(weights.shape, weights.dtype),
            pltpu.VMEM((lat_count, STENCIL, blocks, 1, LANES), jnp.int32),
            pltpu.VMEM((weights.size // LANES, LANES), jnp.float32),
            pltpu.VMEM((fields.size // LANES, LANES), jnp.float32),
            pltpu.VMEM((fields.size // LANES, LANES), jnp.float32),
            pltpu.VMEM((2 * lat_count, blocks + 2, 2 * SUB, LANES), jnp.bfloat16),
            pltpu.SemaphoreType.DMA((5,)),
        ],
        compiler_params=params,
        cost_estimate=pl.CostEstimate(flops=10_000_000, bytes_accessed=4_000_000, transcendentals=0),
        name="near_rows",
    )(*(held(value) for value in (rows_first, points, fields, starts, weights)), sides[0])

    coefficients = pl.pallas_call(
        far_kernel,
        out_shape=jax.ShapeDtypeStruct((owners, 2 * SUB * lat_count, LANES), jnp.bfloat16),
        in_specs=[vector] * 7,
        out_specs=vector,
        scratch_shapes=[
            pltpu.VMEM((fields.size // LANES, LANES), jnp.float32),
            pltpu.VMEM((lat_count, blocks + 2, 2 * SUB, LANES), jnp.bfloat16),
            pltpu.VMEM((lat_count, couples, SUB, 2 * LANES), jnp.float32),
            pltpu.VMEM((lat_count, 2 * SUB, columns + LANES), jnp.float32),
        ],
        compiler_params=params,
        name="far_rows",
    )(sides[1], far_starts, far_scales, facts, partial, table, twiddle)

    received = lax.all_to_all(coefficients, "lat", split_axis=0, concat_axis=0, tiled=True)
    by_level = received.reshape(lat_total, 2, level_count, field_count, LANES).astype(jnp.float32)
    virtual = by_level[:, :, :, 2] + 0.61 * by_level[:, :, :, 3]
    total = jnp.sum(thickness[None, None, :, None] * virtual, axis=2).transpose(1, 0, 2)
    level_owners = lax.axis_size("lev")
    if level_owners == 2:
        totals = lax.ppermute(total, "lev", [(0, 1), (1, 0)])[None]
    else:
        totals = lax.all_gather(total, "lev")

    out_shape = (level_count, field_count + 1, 2, pair_count, degrees)
    half = level_count * (field_count + 1) * 2 * SUB
    group_count = (pair_count + SUB - 1) // SUB
    left_shape = jax.ShapeDtypeStruct((group_count, 2 * half, SUB * lat_total), jnp.bfloat16)
    wide = pltpu.VMEM((lat_total * 2 * SUB, LANES), jnp.float32)
    left = pl.pallas_call(
        functools.partial(left_kernel, level_count, field_count, pair_count),
        out_shape=left_shape,
        in_specs=[vector],
        out_specs=vector,
        scratch_shapes=[wide],
        compiler_params=params,
        cost_estimate=pl.CostEstimate(flops=50_000_000, bytes_accessed=2_000_000, transcendentals=0),
        name="left_rows",
    )(received)
    return pl.pallas_call(
        functools.partial(legendre_kernel, level_owners, level_count, field_count),
        out_shape=(jax.ShapeDtypeStruct(out_shape, jnp.bfloat16), left_shape),
        in_specs=[scalar, vector, vector, vector, vector],
        out_specs=(pl.BlockSpec(memory_space=pl.ANY), vector),
        input_output_aliases={4: 1},
        scratch_shapes=[
            wide,
            pltpu.VMEM(out_shape, jnp.bfloat16),
            pltpu.SemaphoreType.DMA(((degrees + 255) // 256,)),
        ],
        compiler_params=params,
        name="degree_sums",
    )(thickness, received, totals, legendre, left)[0]


def solution(mesh):
    placed = (
        P("lev", None, "lat", None),
        P("lat"),
        P(),
        P("lat", None, None),
        P("lat", None, None, None),
        P("lev"),
        P("lat", None, None),
    )
    return jax.shard_map(
        local,
        mesh=mesh,
        in_specs=placed,
        out_specs=P("lev", None, None, "lat", None),
        check_vma=False,
    )
```

```python
import functools

import jax
import jax.numpy as jnp
import numpy as np
from jax import lax
from jax.experimental import pallas as pl
from jax.experimental.pallas import tpu as pltpu
from jax.sharding import PartitionSpec as P

LANES = 128
SUB = 8
HALF = 64
STENCIL = 4
LIMIT = 24 * 1024 * 1024


def lane_gather(values, lanes):
    return jnp.take_along_axis(values, lanes, axis=1, mode="promise_in_bounds")


TAKE = lax.GatherDimensionNumbers(
    offset_dims=(),
    collapsed_slice_dims=(1,),
    start_index_map=(1,),
    operand_batching_dims=(0,),
    start_indices_batching_dims=(0,),
)


def short_gather(values, lanes):
    mode = lax.GatherScatterMode.PROMISE_IN_BOUNDS
    return lax.gather(values, lanes[:, :, None], TAKE, (1, 1), mode=mode)


SINE = (-70.99342854244645, 81.34076844400118, -41.337142359536955, 6.283164044230117)
COSINE = (
    56.2423804697887, -85.2403304160897, 64.93459063550272, -19.739171434929204, 0.9999999534680867,
)


def polynomial(terms, square):
    value = np.float32(terms[0])
    for term in terms[1:]:
        value = value * square + np.float32(term)
    return value


def turn_parts(product, total, inverse):
    turns = (product - jnp.floor(product * inverse + 0.5) * total) * inverse
    halves = jnp.floor(2.0 * turns + 0.5)
    sign = 1.0 - 2.0 * jnp.abs(halves)
    part = turns - 0.5 * halves
    square = part * part
    return sign * polynomial(COSINE, square), (sign * part) * polynomial(SINE, square)


def wavenumbers(at, width, pair_count, pair_total):
    column = lax.broadcasted_iota(jnp.int32, (1, width), 1).astype(jnp.float32) + float(at)
    owner = jnp.floor((column + 0.5) * (1.0 / (2 * pair_count)))
    inner = column - owner * (2.0 * pair_count)
    second = inner >= pair_count
    pair = owner * pair_count + jnp.where(second, inner - pair_count, inner)
    return jnp.where(second, 2.0 * pair_total - 1.0 - pair, pair)


def multiplied(one, two):
    return one[0] * two[0] - one[1] * two[1], one[0] * two[1] + one[1] * two[0]


def row_of(pair, row):
    return tuple(part[row : row + 1] for part in pair)


def extend(lines, row, rows_each, missing, ext, slot):
    blocks = ext.shape[1] - 2

    def block_of(block):
        return lines[pl.ds(block * rows_each + row, SUB, stride=blocks * rows_each), :]

    def place(block, values):
        ext[slot, block] = jnp.concatenate([values, values], axis=0).astype(jnp.bfloat16)

    for block in range(blocks - 1):
        place(block + 1, block_of(block))
    lane = lax.broadcasted_iota(jnp.int32, (SUB, LANES), 1)
    ahead = lane + missing
    behind = lane - missing
    first = lane_gather(block_of(0), ahead & (LANES - 1))
    second = lane_gather(block_of(1), ahead & (LANES - 1))
    last = block_of(blocks - 1)
    final = lane_gather(last, behind & (LANES - 1))
    before = lane_gather(block_of(blocks - 2), behind & (LANES - 1))
    place(0, jnp.where(behind >= 0, final, before))
    place(blocks, jnp.where(ahead < LANES, last, first))
    place(blocks + 1, jnp.where(ahead < LANES, first, second))


def spread_rows(starts, begins):
    lat_count, _, blocks = begins.shape[:3]
    for latitude in range(lat_count):
        for block in range(blocks):
            for row in range(STENCIL):
                lanes = slice(block * LANES, (block + 1) * LANES)
                begins[latitude, row, block] = (
                    starts[latitude, row : row + 1, lanes] - (block - 1) * LANES
                )


def spread_lines(source, lines):
    first, second, rows, lon = source.shape
    at = 0
    for one in range(first):
        for two in range(second):
            values = source[one, two].astype(jnp.float32)
            for block in range(lon // LANES):
                lines[at : at + rows, :] = values[:, block * LANES : (block + 1) * LANES]
                at += rows


def gathered(totals, starts, scales, parts):
    for side in range(2):
        for pair in range(2):
            spot = starts[side] + jnp.int16(2 * pair)
            lane = spot & jnp.int16(LANES - 1)
            low, middle, high = [short_gather(part, lane) for part in parts[side : side + 3]]
            value = jnp.where(
                spot < jnp.int16(LANES),
                low,
                jnp.where(spot < jnp.int16(2 * LANES), middle, high),
            ).astype(jnp.float32)
            line = STENCIL * side + 2 * pair
            totals[side] = (
                totals[side] + scales[line] * value[:SUB] + scales[line + 1] * value[SUB:]
            )
    return totals


def near_kernel(
    pair_total, pair_count, rows_first_far, points_far, fields_far, starts_far, weights_far, side,
    partial, table, twiddle, far_starts, far_scales, facts, beside,
    rows_first, points, fields, starts, weights, begins, factors, lines, side_lines, ext, arrived,
):
    lat_count, couples = partial.shape[:2]
    lon = 2 * couples * LANES
    columns = table.shape[2] // 2
    first_lat = lax.axis_index("lat") * lat_count
    fetches = [
        pltpu.make_async_copy(source, target, arrived.at[place])
        for place, (source, target) in enumerate(
            (
                (points_far, points),
                (rows_first_far, rows_first),
                (starts_far, starts),
                (weights_far, weights),
                (fields_far, fields),
            )
        )
    ]
    for fetch in fetches:
        fetch.start()
    spread_lines(side, side_lines)
    fetches[0].wait()
    width = 256
    scales = []
    for latitude in range(lat_count):
        total = jnp.full((1, 1), points[first_lat + latitude], jnp.int32).astype(jnp.float32)
        inverse = 1.0 / total
        scales.append((total, inverse, jnp.sqrt(2.0 * inverse)))
    few = lax.broadcasted_iota(jnp.int32, (SUB, width), 0).astype(jnp.float32)
    many = lax.broadcasted_iota(jnp.int32, (couples + 3, width), 0)
    many = jnp.where(many < couples, many * (2 * LANES), (many - (couples - 1)) * HALF)
    many = many.astype(jnp.float32)
    for at in range(0, columns, width):
        numbers = wavenumbers(at, width, pair_count, pair_total)
        for latitude, (total, inverse, scaling) in enumerate(scales):
            ones = turn_parts(numbers * few, total, inverse)
            eights = turn_parts(numbers * (few * float(SUB)), total, inverse)
            large = turn_parts(numbers * many, total, inverse)
            here = slice(at, at + width)
            there = slice(columns + at, columns + at + width)
            for couple in range(couples):
                for lanes, part in ((here, large[0]), (there, large[1])):
                    twiddle[latitude, couple, :, lanes] = jnp.broadcast_to(
                        scaling * part[couple : couple + 1], (SUB, width)
                    )
            products = [ones] + [multiplied(row_of(eights, row), ones) for row in range(1, SUB)]
            block = tuple(jnp.concatenate(parts, axis=0) for parts in zip(*products))
            for quarter in range(4):
                turned = block
                if quarter > 0:
                    turned = multiplied(row_of(large, couples + quarter - 1), block)
                rows = slice(HALF * quarter, HALF * (quarter + 1))
                table[latitude, rows, here] = turned[0].astype(jnp.bfloat16)
                table[latitude, rows, there] = turned[1].astype(jnp.bfloat16)
    for fetch in fetches[1:]:
        fetch.wait()
    known = [first_lat - rows_first[latitude] for latitude in range(lat_count)]
    known += [points[first_lat + latitude] for latitude in range(lat_count)]
    for place in range(-lat_count, 2 * lat_count):
        if place < 0 or place >= lat_count:
            place = jnp.clip(first_lat + place, 0, points.shape[0] - 1)
            known.append(lon - points[place])
    facts[...] = jnp.concatenate([jnp.full((1, LANES), one, jnp.int32) for one in known], axis=0)
    upper = lax.axis_index("lat") % 2 == 0
    for row in range(lat_count):
        missing = jnp.where(upper, known[3 * lat_count + row], known[2 * lat_count + row])
        extend(side_lines, row, lat_count, missing, beside, row)
    spread_rows(starts, begins)
    spread_lines(weights, factors)
    spread_lines(fields, lines)
    for latitude in range(lat_count):
        extend(lines, latitude, lat_count, lon - points[first_lat + latitude], ext, latitude)
    lower = (lax.broadcasted_iota(jnp.int32, (2 * SUB, LANES), 0) >= SUB).astype(jnp.int32)
    for latitude in range(lat_count):
        mine = first_lat - rows_first[latitude]
        for couple in range(couples):

            def spread_row(row):
                at = ((latitude * STENCIL + row) * couples + couple) * SUB
                tile = factors[pl.ds(pl.multiple_of(at, SUB), SUB), :]
                begun = []
                for side in range(2):
                    start = jnp.broadcast_to(
                        begins[latitude, row, 2 * couple + side], (2 * SUB, LANES)
                    )
                    begun.append((start + lower).astype(jnp.int16))
                return (
                    begun,
                    [jnp.broadcast_to(tile[line : line + 1], (SUB, LANES)) for line in range(SUB)],
                )

            totals = [jnp.zeros((SUB, LANES), jnp.float32) for _ in range(2)]
            for slot in range(lat_count):
                begun, scales = spread_row(mine + slot)
                parts = [ext[slot, 2 * couple + piece] for piece in range(4)]
                totals = gathered(totals, begun, scales, parts)
            for side in range(2):
                partial[latitude, couple, :, side * LANES : (side + 1) * LANES] = totals[side]
            others = (jnp.where(mine >= 1, 0, 2), jnp.where(mine <= 1, 3, 1))
            for choice, row in enumerate(others):
                begun, scales = spread_row(row)
                for side in range(2):
                    far_starts[latitude, choice, couple, side] = begun[side]
                for line in range(SUB):
                    far_scales[latitude, choice, couple, line] = scales[line]


def far_kernel(
    beside, far_side, far_starts, far_scales, facts, partial, table, twiddle,
    out, lines, ext, grid, waves,
):
    lat_count, couples = partial.shape[:2]
    columns = table.shape[2] // 2
    owners = out.shape[0]
    fact = [jnp.broadcast_to(facts[row : row + 1], (SUB, LANES)) for row in range(4 * lat_count)]
    toward = 1 - lax.axis_index("lat") % 2
    ext[pl.ds(toward * lat_count, lat_count)] = beside[...]
    spread_lines(far_side, lines)
    for row in range(lat_count):
        missing = jnp.where(toward == 1, fact[2 * lat_count + row], fact[3 * lat_count + row])
        extend(lines, row, lat_count, missing, ext, (1 - toward) * lat_count + row)
    lane = lax.broadcasted_iota(jnp.int32, (SUB, LANES), 1)
    width = 256
    choices = ((2, 1, 0), (3, 2, 1))
    for latitude in range(lat_count):
        own = jnp.broadcast_to(facts[latitude : latitude + 1], (2 * SUB, LANES)).astype(jnp.int16)
        at_zero = own == jnp.int16(0)
        at_one = own == jnp.int16(1)
        for couple in range(couples):
            sides = [pl.ds(side * LANES, LANES) for side in range(2)]
            totals = [partial[latitude, couple, :, lanes] for lanes in sides]
            for choice, slots in enumerate(choices):
                parts = []
                for piece in range(4):
                    zero, one, two = [ext[slot, 2 * couple + piece] for slot in slots]
                    parts.append(jnp.where(at_zero, zero, jnp.where(at_one, one, two)))
                totals = gathered(
                    totals,
                    [far_starts[latitude, choice, couple, side] for side in range(2)],
                    [far_scales[latitude, choice, couple, line] for line in range(SUB)],
                    parts,
                )
            for side in range(2):
                live = lane + (2 * couple + side) * LANES < fact[lat_count + latitude]
                grid[latitude, couple, :, sides[side]] = jnp.where(live, totals[side], 0.0)
    for latitude in range(lat_count):
        rows = grid[latitude].reshape(couples * SUB, 2 * LANES).astype(jnp.bfloat16)
        for at in range(0, columns, width):
            real = jnp.dot(
                rows, table[latitude, :, at : at + width], preferred_element_type=jnp.float32
            )
            imag = jnp.dot(
                rows,
                table[latitude, :, columns + at : columns + at + width],
                preferred_element_type=jnp.float32,
            )
            cosine = jnp.zeros((SUB, width), jnp.float32)
            sine = jnp.zeros((SUB, width), jnp.float32)
            for couple in range(couples):
                turn_cos = twiddle[latitude, couple, :, at : at + width]
                turn_sin = twiddle[latitude, couple, :, columns + at : columns + at + width]
                here = slice(couple * SUB, (couple + 1) * SUB)
                cosine = cosine + (real[here] * turn_cos - imag[here] * turn_sin)
                sine = sine - (real[here] * turn_sin + imag[here] * turn_cos)
            waves[latitude, 0:SUB, at : at + width] = cosine
            waves[latitude, SUB : 2 * SUB, at : at + width] = sine
        waves[latitude, :, columns:] = jnp.zeros((2 * SUB, waves.shape[2] - columns), jnp.float32)
        used = columns // owners
        for owner in range(owners):
            out[owner, 2 * SUB * latitude : 2 * SUB * (latitude + 1), :] = waves[
                latitude, :, owner * used : owner * used + LANES
            ].astype(jnp.bfloat16)


def row_keys(level_count, field_count):
    return [
        (level, field, part)
        for level in range(level_count)
        for field in range(field_count + 1)
        for part in range(2)
    ]


def place_rows(lines, keys, pair_count, left):
    lat_total = next(iter(lines.values())).shape[0]
    depth = SUB * lat_total
    half = len(keys) * SUB
    spread = (
        lax.broadcasted_iota(jnp.int32, (lat_total, depth), 0)
        == lax.broadcasted_iota(jnp.int32, (lat_total, depth), 1) % lat_total
    ).astype(jnp.bfloat16)
    keep = (
        lax.broadcasted_iota(jnp.int32, (SUB, depth), 0)
        == lax.broadcasted_iota(jnp.int32, (SUB, depth), 1) // lat_total
    )
    for place in range(0, len(keys), 2):
        if keys[place] not in lines:
            continue
        couple = [
            lax.dot_general(
                lines[key].astype(jnp.bfloat16),
                spread,
                (((0,), (0,)), ((), ())),
                preferred_element_type=jnp.float32,
            )
            for key in keys[place : place + 2]
        ]
        for member in range(2):
            for group in range(left.shape[0]):
                begin = member * pair_count + group * SUB
                pieces = [jnp.where(keep, one[begin : begin + SUB], 0.0) for one in couple]
                into = member * half + place * SUB
                left[group, into : into + 2 * SUB, :] = jnp.concatenate(pieces, axis=0).astype(
                    jnp.bfloat16
                )


def received_rows(received, wide, keys, field_count):
    wide[...] = received[...].astype(jnp.float32).reshape(wide.shape)
    lat_total = wide.shape[0] // (2 * SUB)
    return {
        (level, field, part): wide[
            pl.ds(part * SUB + level * field_count + field, lat_total, stride=2 * SUB), :
        ]
        for level, field, part in keys
    }


def left_kernel(level_count, field_count, pair_count, received, left, wide):
    keys = row_keys(level_count, field_count)
    wanted = [key for key in keys if key[1] < field_count]
    place_rows(received_rows(received, wide, wanted, field_count), keys, pair_count, left)


def legendre_kernel(
    level_owners, level_count, field_count, thickness, received, totals, legendre, left_given,
    out, left, wide, planes, sent,
):
    owners = received.shape[0]
    pair_count, lat_total, degrees = legendre.shape
    pair_total = pair_count * owners
    groups = [(at, min(SUB, pair_count - at)) for at in range(0, pair_count, SUB)]
    keys = row_keys(level_count, field_count)
    half = len(keys) * SUB
    level_place = lax.axis_index("lev")
    first_pair = lax.axis_index("lat") * pair_count
    wanted = [(level, field, part) for level in range(level_count) for field in (2, 3) for part in range(2)]
    lines = received_rows(received, wide, wanted, field_count)
    sums = {}
    for part in range(2):
        running = jnp.zeros((lat_total, LANES), jnp.float32)
        for place in range(totals.shape[0]):
            other = 1 - level_place if level_owners == 2 else place
            running = running + jnp.where(other > level_place, totals[place, part], 0.0)
        for level in reversed(range(level_count)):
            running = running + thickness[level] * (
                lines[level, 2, part] + 0.61 * lines[level, 3, part]
            )
            sums[level, field_count, part] = running
    place_rows(sums, keys, pair_count, left)
    copies = []
    starts = list(range(0, degrees, 256))
    starts = starts[-1:] + starts[:-1]
    for start in starts:
        stop = min(start + 256, degrees)
        low = 0 if start < 2 * pair_total else half
        high = 2 * half if stop > pair_total + 1 else half
        parts = []
        for group, (at, size) in enumerate(groups):
            values = legendre[at : at + size, :, start:stop].reshape(size * lat_total, stop - start)
            sums = jnp.dot(
                left[group, low:high, : size * lat_total],
                values,
                preferred_element_type=jnp.float32,
            ).reshape((high - low) // SUB, SUB, stop - start)
            if high - low > half:
                shape = (SUB, stop - start)
                slot = lax.broadcasted_iota(jnp.int32, shape, 1) + start
                pair = lax.broadcasted_iota(jnp.int32, shape, 0) + (first_pair + at)
                sums = jnp.where(
                    slot + pair < 2 * pair_total, sums[: len(keys)], sums[len(keys) :]
                )
            parts.append(sums[:, :size])
        planes[:, :, :, :, start:stop] = (
            jnp.concatenate(parts, axis=1).astype(jnp.bfloat16).reshape(planes.shape[:4] + (stop - start,))
        )
        if start == starts[0]:
            continue
        end = degrees if start == starts[-1] else stop
        here = pl.ds(start, end - start)
        copies.append(
            pltpu.make_async_copy(
                planes.at[:, :, :, :, here], out.at[:, :, :, :, here], sent.at[len(copies)]
            )
        )
        copies[-1].start()
    for copy in copies:
        copy.wait()


def held(value):
    return pltpu.with_memory_space_constraint(value, pltpu.HBM)


def local(fields, rows_first, points, starts, weights, thickness, legendre):
    level_count, field_count, lat_count, lon_count = fields.shape
    pair_count, lat_total, degrees = legendre.shape
    owners = lax.axis_size("lat")
    couples = lon_count // (2 * LANES)
    blocks = 2 * couples
    columns = 2 * owners * pair_count
    sides = []
    for first in range(2):
        edges = [(i, i + 1) for i in range(first, owners - 1, 2)]
        sides.append(lax.ppermute(fields, "lat", edges + [(j, i) for i, j in edges]))

    scalar = pl.BlockSpec(memory_space=pltpu.SMEM)
    vector = pl.BlockSpec(memory_space=pltpu.VMEM)
    params = pltpu.CompilerParams(vmem_limit_bytes=LIMIT)
    remote = pl.BlockSpec(memory_space=pltpu.HBM)
    partial, table, twiddle, far_starts, far_scales, facts, beside = pl.pallas_call(
        functools.partial(near_kernel, pair_count * owners, pair_count),
        out_shape=(
            jax.ShapeDtypeStruct((lat_count, couples, SUB, 2 * LANES), jnp.float32),
            jax.ShapeDtypeStruct((lat_count, 2 * LANES, 2 * columns), jnp.bfloat16),
            jax.ShapeDtypeStruct((lat_count, couples, SUB, 2 * columns), jnp.float32),
            jax.ShapeDtypeStruct((lat_count, 2, couples, 2, 2 * SUB, LANES), jnp.int16),
            jax.ShapeDtypeStruct((lat_count, 2, couples, SUB, SUB, LANES), jnp.float32),
            jax.ShapeDtypeStruct((4 * lat_count, LANES), jnp.int32),
            jax.ShapeDtypeStruct((lat_count, blocks + 2, 2 * SUB, LANES), jnp.bfloat16),
        ),
        in_specs=[remote] * 5 + [vector],
        out_specs=(vector,) * 7,
        scratch_shapes=[
            pltpu.SMEM(rows_first.shape, jnp.int32),
            pltpu.SMEM(points.shape, jnp.int32),
            pltpu.VMEM(fields.shape, fields.dtype),
            pltpu.VMEM(starts.shape, starts.dtype),
            pltpu.VMEM(weights.shape, weights.dtype),
            pltpu.VMEM((lat_count, STENCIL, blocks, 1, LANES), jnp.int32),
            pltpu.VMEM((weights.size // LANES, LANES), jnp.float32),
            pltpu.VMEM((fields.size // LANES, LANES), jnp.float32),
            pltpu.VMEM((fields.size // LANES, LANES), jnp.float32),
            pltpu.VMEM((lat_count, blocks + 2, 2 * SUB, LANES), jnp.bfloat16),
            pltpu.SemaphoreType.DMA((5,)),
        ],
        compiler_params=params,
        cost_estimate=pl.CostEstimate(flops=10_000_000, bytes_accessed=4_000_000, transcendentals=0),
        name="near_rows",
    )(*(held(value) for value in (rows_first, points, fields, starts, weights)), sides[0])

    coefficients = pl.pallas_call(
        far_kernel,
        out_shape=jax.ShapeDtypeStruct((owners, 2 * SUB * lat_count, LANES), jnp.bfloat16),
        in_specs=[vector] * 8,
        out_specs=vector,
        scratch_shapes=[
            pltpu.VMEM((fields.size // LANES, LANES), jnp.float32),
            pltpu.VMEM((2 * lat_count, blocks + 2, 2 * SUB, LANES), jnp.bfloat16),
            pltpu.VMEM((lat_count, couples, SUB, 2 * LANES), jnp.float32),
            pltpu.VMEM((lat_count, 2 * SUB, columns + LANES), jnp.float32),
        ],
        compiler_params=params,
        name="far_rows",
    )(beside, sides[1], far_starts, far_scales, facts, partial, table, twiddle)

    received = lax.all_to_all(coefficients, "lat", split_axis=0, concat_axis=0, tiled=True)
    by_level = received.reshape(lat_total, 2, level_count, field_count, LANES).astype(jnp.float32)
    virtual = by_level[:, :, :, 2] + 0.61 * by_level[:, :, :, 3]
    total = jnp.sum(thickness[None, None, :, None] * virtual, axis=2).transpose(1, 0, 2)
    level_owners = lax.axis_size("lev")
    if level_owners == 2:
        totals = lax.ppermute(total, "lev", [(0, 1), (1, 0)])[None]
    else:
        totals = lax.all_gather(total, "lev")

    out_shape = (level_count, field_count + 1, 2, pair_count, degrees)
    half = level_count * (field_count + 1) * 2 * SUB
    group_count = (pair_count + SUB - 1) // SUB
    left_shape = jax.ShapeDtypeStruct((group_count, 2 * half, SUB * lat_total), jnp.bfloat16)
    wide = pltpu.VMEM((lat_total * 2 * SUB, LANES), jnp.float32)
    left = pl.pallas_call(
        functools.partial(left_kernel, level_count, field_count, pair_count),
        out_shape=left_shape,
        in_specs=[vector],
        out_specs=vector,
        scratch_shapes=[wide],
        compiler_params=params,
        cost_estimate=pl.CostEstimate(flops=50_000_000, bytes_accessed=2_000_000, transcendentals=0),
        name="left_rows",
    )(received)
    return pl.pallas_call(
        functools.partial(legendre_kernel, level_owners, level_count, field_count),
        out_shape=(jax.ShapeDtypeStruct(out_shape, jnp.bfloat16), left_shape),
        in_specs=[scalar, vector, vector, vector, vector],
        out_specs=(pl.BlockSpec(memory_space=pl.ANY), vector),
        input_output_aliases={4: 1},
        scratch_shapes=[
            wide,
            pltpu.VMEM(out_shape, jnp.bfloat16),
            pltpu.SemaphoreType.DMA(((degrees + 255) // 256,)),
        ],
        compiler_params=params,
        name="degree_sums",
    )(thickness, received, totals, legendre, left)[0]


def solution(mesh):
    placed = (
        P("lev", None, "lat", None),
        P("lat"),
        P(),
        P("lat", None, None),
        P("lat", None, None, None),
        P("lev"),
        P("lat", None, None),
    )
    return jax.shard_map(
        local,
        mesh=mesh,
        in_specs=placed,
        out_specs=P("lev", None, None, "lat", None),
        check_vma=False,
    )
```

```python
import functools

import jax
import jax.numpy as jnp
import numpy as np
from jax import lax
from jax.experimental import pallas as pl
from jax.experimental.pallas import tpu as pltpu
from jax.sharding import PartitionSpec as P

LANES = 128
SUB = 8
HALF = 64
STENCIL = 4
LIMIT = 24 * 1024 * 1024


def lane_gather(values, lanes):
    return jnp.take_along_axis(values, lanes, axis=1, mode="promise_in_bounds")


TAKE = lax.GatherDimensionNumbers(
    offset_dims=(),
    collapsed_slice_dims=(1,),
    start_index_map=(1,),
    operand_batching_dims=(0,),
    start_indices_batching_dims=(0,),
)


def short_gather(values, lanes):
    mode = lax.GatherScatterMode.PROMISE_IN_BOUNDS
    return lax.gather(values, lanes[:, :, None], TAKE, (1, 1), mode=mode)


SINE = (-70.99342854244645, 81.34076844400118, -41.337142359536955, 6.283164044230117)
COSINE = (
    56.2423804697887, -85.2403304160897, 64.93459063550272, -19.739171434929204, 0.9999999534680867,
)


def polynomial(terms, square):
    value = np.float32(terms[0])
    for term in terms[1:]:
        value = value * square + np.float32(term)
    return value


def turn_parts(product, total, inverse):
    turns = (product - jnp.floor(product * inverse + 0.5) * total) * inverse
    halves = jnp.floor(2.0 * turns + 0.5)
    sign = 1.0 - 2.0 * jnp.abs(halves)
    part = turns - 0.5 * halves
    square = part * part
    return sign * polynomial(COSINE, square), (sign * part) * polynomial(SINE, square)


def wavenumbers(at, width, pair_count, pair_total):
    column = lax.broadcasted_iota(jnp.int32, (1, width), 1).astype(jnp.float32) + float(at)
    owner = jnp.floor((column + 0.5) * (1.0 / (2 * pair_count)))
    inner = column - owner * (2.0 * pair_count)
    second = inner >= pair_count
    pair = owner * pair_count + jnp.where(second, inner - pair_count, inner)
    return jnp.where(second, 2.0 * pair_total - 1.0 - pair, pair)


def multiplied(one, two):
    return one[0] * two[0] - one[1] * two[1], one[0] * two[1] + one[1] * two[0]


def row_of(pair, row):
    return tuple(part[row : row + 1] for part in pair)


def extend(lines, row, rows_each, missing, ext, slot):
    blocks = ext.shape[1] - 2

    def block_of(block):
        return lines[pl.ds(block * rows_each + row, SUB, stride=blocks * rows_each), :]

    def place(block, values):
        ext[slot, block] = jnp.concatenate([values, values], axis=0).astype(jnp.bfloat16)

    for block in range(blocks - 1):
        place(block + 1, block_of(block))
    lane = lax.broadcasted_iota(jnp.int32, (SUB, LANES), 1)
    ahead = lane + missing
    behind = lane - missing
    first = lane_gather(block_of(0), ahead & (LANES - 1))
    second = lane_gather(block_of(1), ahead & (LANES - 1))
    last = block_of(blocks - 1)
    final = lane_gather(last, behind & (LANES - 1))
    before = lane_gather(block_of(blocks - 2), behind & (LANES - 1))
    place(0, jnp.where(behind >= 0, final, before))
    place(blocks, jnp.where(ahead < LANES, last, first))
    place(blocks + 1, jnp.where(ahead < LANES, first, second))


def spread_rows(starts, begins):
    lat_count, _, blocks = begins.shape[:3]
    for latitude in range(lat_count):
        for block in range(blocks):
            for row in range(STENCIL):
                lanes = slice(block * LANES, (block + 1) * LANES)
                begins[latitude, row, block] = (
                    starts[latitude, row : row + 1, lanes] - (block - 1) * LANES
                )


def spread_lines(source, lines):
    first, second, rows, lon = source.shape
    at = 0
    for one in range(first):
        for two in range(second):
            values = source[one, two].astype(jnp.float32)
            for block in range(lon // LANES):
                lines[at : at + rows, :] = values[:, block * LANES : (block + 1) * LANES]
                at += rows


def gathered(totals, starts, scales, parts):
    for side in range(2):
        for pair in range(2):
            spot = starts[side] + jnp.int16(2 * pair)
            lane = spot & jnp.int16(LANES - 1)
            low, middle, high = [short_gather(part, lane) for part in parts[side : side + 3]]
            value = jnp.where(
                spot < jnp.int16(LANES),
                low,
                jnp.where(spot < jnp.int16(2 * LANES), middle, high),
            ).astype(jnp.float32)
            line = STENCIL * side + 2 * pair
            totals[side] = (
                totals[side] + scales[line] * value[:SUB] + scales[line + 1] * value[SUB:]
            )
    return totals


def near_kernel(
    pair_total, pair_count, rows_first_far, points_far, fields_far, starts_far, weights_far,
    partial, table, twiddle, far_starts, far_scales, facts,
    rows_first, points, fields, starts, weights, begins, factors, lines, ext, arrived,
):
    lat_count, couples = partial.shape[:2]
    lon = 2 * couples * LANES
    columns = table.shape[2] // 2
    first_lat = lax.axis_index("lat") * lat_count
    fetches = [
        pltpu.make_async_copy(source, target, arrived.at[place])
        for place, (source, target) in enumerate(
            (
                (points_far, points),
                (rows_first_far, rows_first),
                (starts_far, starts),
                (weights_far, weights),
                (fields_far, fields),
            )
        )
    ]
    for fetch in fetches:
        fetch.start()
    fetches[0].wait()
    width = 256
    scales = []
    for latitude in range(lat_count):
        total = jnp.full((1, 1), points[first_lat + latitude], jnp.int32).astype(jnp.float32)
        inverse = 1.0 / total
        scales.append((total, inverse, jnp.sqrt(2.0 * inverse)))
    few = lax.broadcasted_iota(jnp.int32, (SUB, width), 0).astype(jnp.float32)
    many = lax.broadcasted_iota(jnp.int32, (couples + 3, width), 0)
    many = jnp.where(many < couples, many * (2 * LANES), (many - (couples - 1)) * HALF)
    many = many.astype(jnp.float32)
    for at in range(0, columns, width):
        numbers = wavenumbers(at, width, pair_count, pair_total)
        for latitude, (total, inverse, scaling) in enumerate(scales):
            ones = turn_parts(numbers * few, total, inverse)
            eights = turn_parts(numbers * (few * float(SUB)), total, inverse)
            large = turn_parts(numbers * many, total, inverse)
            here = slice(at, at + width)
            there = slice(columns + at, columns + at + width)
            for couple in range(couples):
                for lanes, part in ((here, large[0]), (there, large[1])):
                    twiddle[latitude, couple, :, lanes] = jnp.broadcast_to(
                        scaling * part[couple : couple + 1], (SUB, width)
                    )
            products = [ones] + [multiplied(row_of(eights, row), ones) for row in range(1, SUB)]
            block = tuple(jnp.concatenate(parts, axis=0) for parts in zip(*products))
            for quarter in range(4):
                turned = block
                if quarter > 0:
                    turned = multiplied(row_of(large, couples + quarter - 1), block)
                rows = slice(HALF * quarter, HALF * (quarter + 1))
                table[latitude, rows, here] = turned[0].astype(jnp.bfloat16)
                table[latitude, rows, there] = turned[1].astype(jnp.bfloat16)
    for fetch in fetches[1:]:
        fetch.wait()
    known = [first_lat - rows_first[latitude] for latitude in range(lat_count)]
    known += [points[first_lat + latitude] for latitude in range(lat_count)]
    for place in range(-lat_count, 2 * lat_count):
        if place < 0 or place >= lat_count:
            place = jnp.clip(first_lat + place, 0, points.shape[0] - 1)
            known.append(lon - points[place])
    facts[...] = jnp.concatenate([jnp.full((1, LANES), one, jnp.int32) for one in known], axis=0)
    spread_rows(starts, begins)
    spread_lines(weights, factors)
    spread_lines(fields, lines)
    for latitude in range(lat_count):
        extend(lines, latitude, lat_count, lon - points[first_lat + latitude], ext, latitude)
    lower = (lax.broadcasted_iota(jnp.int32, (2 * SUB, LANES), 0) >= SUB).astype(jnp.int32)
    for latitude in range(lat_count):
        mine = first_lat - rows_first[latitude]
        for couple in range(couples):

            def spread_row(row):
                at = ((latitude * STENCIL + row) * couples + couple) * SUB
                tile = factors[pl.ds(pl.multiple_of(at, SUB), SUB), :]
                begun = []
                for side in range(2):
                    start = jnp.broadcast_to(
                        begins[latitude, row, 2 * couple + side], (2 * SUB, LANES)
                    )
                    begun.append((start + lower).astype(jnp.int16))
                return (
                    begun,
                    [jnp.broadcast_to(tile[line : line + 1], (SUB, LANES)) for line in range(SUB)],
                )

            totals = [jnp.zeros((SUB, LANES), jnp.float32) for _ in range(2)]
            for slot in range(lat_count):
                begun, scales = spread_row(mine + slot)
                parts = [ext[slot, 2 * couple + piece] for piece in range(4)]
                totals = gathered(totals, begun, scales, parts)
            for side in range(2):
                partial[latitude, couple, :, side * LANES : (side + 1) * LANES] = totals[side]
            others = (jnp.where(mine >= 1, 0, 2), jnp.where(mine <= 1, 3, 1))
            for choice, row in enumerate(others):
                begun, scales = spread_row(row)
                for side in range(2):
                    far_starts[latitude, choice, couple, side] = begun[side]
                for line in range(SUB):
                    far_scales[latitude, choice, couple, line] = scales[line]


def far_kernel(
    near_side, far_side, far_starts, far_scales, facts, partial, table, twiddle,
    out, lines, ext, grid, waves,
):
    lat_count, couples = partial.shape[:2]
    columns = table.shape[2] // 2
    owners = out.shape[0]
    toward = 1 - (lax.axis_index("lat") + lax.axis_index("lev")) % 2
    spread_lines(near_side, lines.at[toward])
    spread_lines(far_side, lines.at[1 - toward])
    fact = [jnp.broadcast_to(facts[row : row + 1], (SUB, LANES)) for row in range(4 * lat_count)]
    for slot in range(2 * lat_count):
        side, row = divmod(slot, lat_count)
        extend(lines.at[side], row, lat_count, fact[2 * lat_count + slot], ext, slot)
    lane = lax.broadcasted_iota(jnp.int32, (SUB, LANES), 1)
    width = 256
    choices = ((2, 1, 0), (3, 2, 1))
    for latitude in range(lat_count):
        own = jnp.broadcast_to(facts[latitude : latitude + 1], (2 * SUB, LANES)).astype(jnp.int16)
        at_zero = own == jnp.int16(0)
        at_one = own == jnp.int16(1)
        for couple in range(couples):
            sides = [pl.ds(side * LANES, LANES) for side in range(2)]
            totals = [partial[latitude, couple, :, lanes] for lanes in sides]
            for choice, slots in enumerate(choices):
                parts = []
                for piece in range(4):
                    zero, one, two = [ext[slot, 2 * couple + piece] for slot in slots]
                    parts.append(jnp.where(at_zero, zero, jnp.where(at_one, one, two)))
                totals = gathered(
                    totals,
                    [far_starts[latitude, choice, couple, side] for side in range(2)],
                    [far_scales[latitude, choice, couple, line] for line in range(SUB)],
                    parts,
                )
            for side in range(2):
                live = lane + (2 * couple + side) * LANES < fact[lat_count + latitude]
                grid[latitude, couple, :, sides[side]] = jnp.where(live, totals[side], 0.0)
    for latitude in range(lat_count):
        rows = grid[latitude].reshape(couples * SUB, 2 * LANES).astype(jnp.bfloat16)
        for at in range(0, columns, width):
            real = jnp.dot(
                rows, table[latitude, :, at : at + width], preferred_element_type=jnp.float32
            )
            imag = jnp.dot(
                rows,
                table[latitude, :, columns + at : columns + at + width],
                preferred_element_type=jnp.float32,
            )
            cosine = jnp.zeros((SUB, width), jnp.float32)
            sine = jnp.zeros((SUB, width), jnp.float32)
            for couple in range(couples):
                turn_cos = twiddle[latitude, couple, :, at : at + width]
                turn_sin = twiddle[latitude, couple, :, columns + at : columns + at + width]
                here = slice(couple * SUB, (couple + 1) * SUB)
                cosine = cosine + (real[here] * turn_cos - imag[here] * turn_sin)
                sine = sine - (real[here] * turn_sin + imag[here] * turn_cos)
            waves[latitude, 0:SUB, at : at + width] = cosine
            waves[latitude, SUB : 2 * SUB, at : at + width] = sine
        waves[latitude, :, columns:] = jnp.zeros((2 * SUB, waves.shape[2] - columns), jnp.float32)
        used = columns // owners
        for owner in range(owners):
            out[owner, 2 * SUB * latitude : 2 * SUB * (latitude + 1), :] = waves[
                latitude, :, owner * used : owner * used + LANES
            ].astype(jnp.bfloat16)


def row_keys(level_count, field_count):
    return [
        (level, field, part)
        for level in range(level_count)
        for field in range(field_count + 1)
        for part in range(2)
    ]


def place_rows(lines, keys, pair_count, left):
    lat_total = next(iter(lines.values())).shape[0]
    depth = SUB * lat_total
    half = len(keys) * SUB
    spread = (
        lax.broadcasted_iota(jnp.int32, (lat_total, depth), 0)
        == lax.broadcasted_iota(jnp.int32, (lat_total, depth), 1) % lat_total
    ).astype(jnp.bfloat16)
    keep = (
        lax.broadcasted_iota(jnp.int32, (SUB, depth), 0)
        == lax.broadcasted_iota(jnp.int32, (SUB, depth), 1) // lat_total
    )
    for place in range(0, len(keys), 2):
        if keys[place] not in lines:
            continue
        couple = [
            lax.dot_general(
                lines[key].astype(jnp.bfloat16),
                spread,
                (((0,), (0,)), ((), ())),
                preferred_element_type=jnp.float32,
            )
            for key in keys[place : place + 2]
        ]
        for member in range(2):
            for group in range(left.shape[0]):
                begin = member * pair_count + group * SUB
                pieces = [jnp.where(keep, one[begin : begin + SUB], 0.0) for one in couple]
                into = member * half + place * SUB
                left[group, into : into + 2 * SUB, :] = jnp.concatenate(pieces, axis=0).astype(
                    jnp.bfloat16
                )


def received_rows(received, wide, keys, field_count):
    wide[...] = received[...].astype(jnp.float32).reshape(wide.shape)
    lat_total = wide.shape[0] // (2 * SUB)
    return {
        (level, field, part): wide[
            pl.ds(part * SUB + level * field_count + field, lat_total, stride=2 * SUB), :
        ]
        for level, field, part in keys
    }


def left_kernel(level_count, field_count, pair_count, received, left, wide):
    keys = row_keys(level_count, field_count)
    wanted = [key for key in keys if key[1] < field_count]
    place_rows(received_rows(received, wide, wanted, field_count), keys, pair_count, left)


def legendre_kernel(
    level_owners, level_count, field_count, thickness, received, totals, legendre, left_given,
    out, left, wide, planes, sent,
):
    owners = received.shape[0]
    pair_count, lat_total, degrees = legendre.shape
    pair_total = pair_count * owners
    groups = [(at, min(SUB, pair_count - at)) for at in range(0, pair_count, SUB)]
    keys = row_keys(level_count, field_count)
    half = len(keys) * SUB
    level_place = lax.axis_index("lev")
    first_pair = lax.axis_index("lat") * pair_count
    wanted = [(level, field, part) for level in range(level_count) for field in (2, 3) for part in range(2)]
    lines = received_rows(received, wide, wanted, field_count)
    sums = {}
    for part in range(2):
        running = jnp.zeros((lat_total, LANES), jnp.float32)
        for place in range(totals.shape[0]):
            other = 1 - level_place if level_owners == 2 else place
            running = running + jnp.where(other > level_place, totals[place, part], 0.0)
        for level in reversed(range(level_count)):
            running = running + thickness[level] * (
                lines[level, 2, part] + 0.61 * lines[level, 3, part]
            )
            sums[level, field_count, part] = running
    place_rows(sums, keys, pair_count, left)
    copies = []
    for start in range(0, degrees, 256):
        stop = min(start + 256, degrees)
        low = 0 if start < 2 * pair_total else half
        high = 2 * half if stop > pair_total + 1 else half
        parts = []
        for group, (at, size) in enumerate(groups):
            values = legendre[at : at + size, :, start:stop].reshape(size * lat_total, stop - start)
            sums = jnp.dot(
                left[group, low:high, : size * lat_total],
                values,
                preferred_element_type=jnp.float32,
            ).reshape((high - low) // SUB, SUB, stop - start)
            if high - low > half:
                shape = (SUB, stop - start)
                slot = lax.broadcasted_iota(jnp.int32, shape, 1) + start
                pair = lax.broadcasted_iota(jnp.int32, shape, 0) + (first_pair + at)
                sums = jnp.where(
                    slot + pair < 2 * pair_total, sums[: len(keys)], sums[len(keys) :]
                )
            parts.append(sums[:, :size])
        planes[:, :, :, :, start:stop] = (
            jnp.concatenate(parts, axis=1).astype(jnp.bfloat16).reshape(planes.shape[:4] + (stop - start,))
        )
        here = pl.ds(start, stop - start)
        copies.append(
            pltpu.make_async_copy(
                planes.at[:, :, :, :, here], out.at[:, :, :, :, here], sent.at[len(copies)]
            )
        )
        copies[-1].start()
    for copy in copies:
        copy.wait()


def held(value):
    return pltpu.with_memory_space_constraint(value, pltpu.HBM)


def local(fields, rows_first, points, starts, weights, thickness, legendre):
    level_count, field_count, lat_count, lon_count = fields.shape
    pair_count, lat_total, degrees = legendre.shape
    owners = lax.axis_size("lat")
    couples = lon_count // (2 * LANES)
    blocks = 2 * couples
    columns = 2 * owners * pair_count
    level_owners = lax.axis_size("lev")
    sides = []
    for first in range(2):
        edges = [
            (i * level_owners + place, (i + 1) * level_owners + place)
            for place in range(level_owners)
            for i in range((first + place) % 2, owners - 1, 2)
        ]
        sides.append(lax.ppermute(fields, ("lat", "lev"), edges + [(j, i) for i, j in edges]))

    scalar = pl.BlockSpec(memory_space=pltpu.SMEM)
    vector = pl.BlockSpec(memory_space=pltpu.VMEM)
    params = pltpu.CompilerParams(vmem_limit_bytes=LIMIT)
    remote = pl.BlockSpec(memory_space=pltpu.HBM)
    partial, table, twiddle, far_starts, far_scales, facts = pl.pallas_call(
        functools.partial(near_kernel, pair_count * owners, pair_count),
        out_shape=(
            jax.ShapeDtypeStruct((lat_count, couples, SUB, 2 * LANES), jnp.float32),
            jax.ShapeDtypeStruct((lat_count, 2 * LANES, 2 * columns), jnp.bfloat16),
            jax.ShapeDtypeStruct((lat_count, couples, SUB, 2 * columns), jnp.float32),
            jax.ShapeDtypeStruct((lat_count, 2, couples, 2, 2 * SUB, LANES), jnp.int16),
            jax.ShapeDtypeStruct((lat_count, 2, couples, SUB, SUB, LANES), jnp.float32),
            jax.ShapeDtypeStruct((4 * lat_count, LANES), jnp.int32),
        ),
        in_specs=[remote] * 5,
        out_specs=(vector,) * 6,
        scratch_shapes=[
            pltpu.SMEM(rows_first.shape, jnp.int32),
            pltpu.SMEM(points.shape, jnp.int32),
            pltpu.VMEM(fields.shape, fields.dtype),
            pltpu.VMEM(starts.shape, starts.dtype),
            pltpu.VMEM(weights.shape, weights.dtype),
            pltpu.VMEM((lat_count, STENCIL, blocks, 1, LANES), jnp.int32),
            pltpu.VMEM((weights.size // LANES, LANES), jnp.float32),
            pltpu.VMEM((fields.size // LANES, LANES), jnp.float32),
            pltpu.VMEM((lat_count, blocks + 2, 2 * SUB, LANES), jnp.bfloat16),
            pltpu.SemaphoreType.DMA((5,)),
        ],
        compiler_params=params,
        cost_estimate=pl.CostEstimate(flops=10_000_000, bytes_accessed=4_000_000, transcendentals=0),
        name="near_rows",
    )(*(held(value) for value in (rows_first, points, fields, starts, weights)))

    coefficients = pl.pallas_call(
        far_kernel,
        out_shape=jax.ShapeDtypeStruct((owners, 2 * SUB * lat_count, LANES), jnp.bfloat16),
        in_specs=[vector] * 8,
        out_specs=vector,
        scratch_shapes=[
            pltpu.VMEM((2, fields.size // LANES, LANES), jnp.float32),
            pltpu.VMEM((2 * lat_count, blocks + 2, 2 * SUB, LANES), jnp.bfloat16),
            pltpu.VMEM((lat_count, couples, SUB, 2 * LANES), jnp.float32),
            pltpu.VMEM((lat_count, 2 * SUB, columns + LANES), jnp.float32),
        ],
        compiler_params=params,
        name="far_rows",
    )(*sides, far_starts, far_scales, facts, partial, table, twiddle)

    received = lax.all_to_all(coefficients, "lat", split_axis=0, concat_axis=0, tiled=True)
    by_level = received.reshape(lat_total, 2, level_count, field_count, LANES).astype(jnp.float32)
    virtual = by_level[:, :, :, 2] + 0.61 * by_level[:, :, :, 3]
    total = jnp.sum(thickness[None, None, :, None] * virtual, axis=2).transpose(1, 0, 2)
    if level_owners == 2:
        totals = lax.ppermute(total, "lev", [(0, 1), (1, 0)])[None]
    else:
        totals = lax.all_gather(total, "lev")

    out_shape = (level_count, field_count + 1, 2, pair_count, degrees)
    half = level_count * (field_count + 1) * 2 * SUB
    group_count = (pair_count + SUB - 1) // SUB
    left_shape = jax.ShapeDtypeStruct((group_count, 2 * half, SUB * lat_total), jnp.bfloat16)
    wide = pltpu.VMEM((lat_total * 2 * SUB, LANES), jnp.float32)
    left = pl.pallas_call(
        functools.partial(left_kernel, level_count, field_count, pair_count),
        out_shape=left_shape,
        in_specs=[vector],
        out_specs=vector,
        scratch_shapes=[wide],
        compiler_params=params,
        cost_estimate=pl.CostEstimate(flops=50_000_000, bytes_accessed=2_000_000, transcendentals=0),
        name="left_rows",
    )(received)
    return pl.pallas_call(
        functools.partial(legendre_kernel, level_owners, level_count, field_count),
        out_shape=(jax.ShapeDtypeStruct(out_shape, jnp.bfloat16), left_shape),
        in_specs=[scalar, vector, vector, vector, vector],
        out_specs=(pl.BlockSpec(memory_space=pl.ANY), vector),
        input_output_aliases={4: 1},
        scratch_shapes=[
            wide,
            pltpu.VMEM(out_shape, jnp.bfloat16),
            pltpu.SemaphoreType.DMA(((degrees + 255) // 256,)),
        ],
        compiler_params=params,
        name="degree_sums",
    )(thickness, received, totals, legendre, left)[0]


def solution(mesh):
    placed = (
        P("lev", None, "lat", None),
        P("lat"),
        P(),
        P("lat", None, None),
        P("lat", None, None, None),
        P("lev"),
        P("lat", None, None),
    )
    return jax.shard_map(
        local,
        mesh=mesh,
        in_specs=placed,
        out_specs=P("lev", None, None, "lat", None),
        check_vma=False,
    )
```

```python
import functools

import jax
import jax.numpy as jnp
import numpy as np
from jax import lax
from jax.experimental import pallas as pl
from jax.experimental.pallas import tpu as pltpu
from jax.sharding import PartitionSpec as P

LANES = 128
SUB = 8
HALF = 64
STENCIL = 4
LIMIT = 24 * 1024 * 1024


def lane_gather(values, lanes):
    return jnp.take_along_axis(values, lanes, axis=1, mode="promise_in_bounds")


TAKE = lax.GatherDimensionNumbers(
    offset_dims=(),
    collapsed_slice_dims=(1,),
    start_index_map=(1,),
    operand_batching_dims=(0,),
    start_indices_batching_dims=(0,),
)


def short_gather(values, lanes):
    mode = lax.GatherScatterMode.PROMISE_IN_BOUNDS
    return lax.gather(values, lanes[:, :, None], TAKE, (1, 1), mode=mode)


SINE = (-70.99342854244645, 81.34076844400118, -41.337142359536955, 6.283164044230117)
COSINE = (
    56.2423804697887, -85.2403304160897, 64.93459063550272, -19.739171434929204, 0.9999999534680867,
)


def polynomial(terms, square):
    value = np.float32(terms[0])
    for term in terms[1:]:
        value = value * square + np.float32(term)
    return value


def turn_parts(product, total, inverse):
    turns = (product - jnp.floor(product * inverse + 0.5) * total) * inverse
    halves = jnp.floor(2.0 * turns + 0.5)
    sign = 1.0 - 2.0 * jnp.abs(halves)
    part = turns - 0.5 * halves
    square = part * part
    return sign * polynomial(COSINE, square), (sign * part) * polynomial(SINE, square)


def wavenumbers(at, width, pair_count, pair_total):
    column = lax.broadcasted_iota(jnp.int32, (1, width), 1).astype(jnp.float32) + float(at)
    owner = jnp.floor((column + 0.5) * (1.0 / (2 * pair_count)))
    inner = column - owner * (2.0 * pair_count)
    second = inner >= pair_count
    pair = owner * pair_count + jnp.where(second, inner - pair_count, inner)
    return jnp.where(second, 2.0 * pair_total - 1.0 - pair, pair)


def multiplied(one, two):
    return one[0] * two[0] - one[1] * two[1], one[0] * two[1] + one[1] * two[0]


def row_of(pair, row):
    return tuple(part[row : row + 1] for part in pair)


def extend(lines, row, rows_each, missing, ext, slot):
    blocks = ext.shape[1] - 2

    def block_of(block):
        return lines[pl.ds(block * rows_each + row, SUB, stride=blocks * rows_each), :]

    def place(block, values):
        ext[slot, block] = jnp.concatenate([values, values], axis=0).astype(jnp.bfloat16)

    for block in range(blocks - 1):
        place(block + 1, block_of(block))
    lane = lax.broadcasted_iota(jnp.int32, (SUB, LANES), 1)
    ahead = lane + missing
    behind = lane - missing
    first = lane_gather(block_of(0), ahead & (LANES - 1))
    second = lane_gather(block_of(1), ahead & (LANES - 1))
    last = block_of(blocks - 1)
    final = lane_gather(last, behind & (LANES - 1))
    before = lane_gather(block_of(blocks - 2), behind & (LANES - 1))
    place(0, jnp.where(behind >= 0, final, before))
    place(blocks, jnp.where(ahead < LANES, last, first))
    place(blocks + 1, jnp.where(ahead < LANES, first, second))


def spread_rows(starts, begins):
    lat_count, _, blocks = begins.shape[:3]
    for latitude in range(lat_count):
        for block in range(blocks):
            for row in range(STENCIL):
                lanes = slice(block * LANES, (block + 1) * LANES)
                begins[latitude, row, block] = (
                    starts[latitude, row : row + 1, lanes] - (block - 1) * LANES
                )


def spread_lines(source, lines):
    first, second, rows, lon = source.shape
    at = 0
    for one in range(first):
        for two in range(second):
            values = source[one, two].astype(jnp.float32)
            for block in range(lon // LANES):
                lines[at : at + rows, :] = values[:, block * LANES : (block + 1) * LANES]
                at += rows


def gathered(totals, starts, scales, parts):
    for side in range(2):
        for pair in range(2):
            spot = starts[side] + jnp.int16(2 * pair)
            lane = spot & jnp.int16(LANES - 1)
            low, middle, high = [short_gather(part, lane) for part in parts[side : side + 3]]
            value = jnp.where(
                spot < jnp.int16(LANES),
                low,
                jnp.where(spot < jnp.int16(2 * LANES), middle, high),
            ).astype(jnp.float32)
            line = STENCIL * side + 2 * pair
            totals[side] = (
                totals[side] + scales[line] * value[:SUB] + scales[line + 1] * value[SUB:]
            )
    return totals


def near_kernel(
    pair_total, pair_count, rows_first_far, points_far, fields_far, starts_far, weights_far,
    partial, table, twiddle, far_starts, far_scales, facts,
    rows_first, points, fields, starts, weights, begins, factors, lines, ext, arrived,
):
    lat_count, couples = partial.shape[:2]
    lon = 2 * couples * LANES
    columns = table.shape[2] // 2
    first_lat = lax.axis_index("lat") * lat_count
    fetches = [
        pltpu.make_async_copy(source, target, arrived.at[place])
        for place, (source, target) in enumerate(
            (
                (points_far, points),
                (rows_first_far, rows_first),
                (starts_far, starts),
                (weights_far, weights),
                (fields_far, fields),
            )
        )
    ]
    for fetch in fetches:
        fetch.start()
    fetches[0].wait()
    width = 256
    scales = []
    for latitude in range(lat_count):
        total = jnp.full((1, 1), points[first_lat + latitude], jnp.int32).astype(jnp.float32)
        inverse = 1.0 / total
        scales.append((total, inverse, jnp.sqrt(2.0 * inverse)))
    few = lax.broadcasted_iota(jnp.int32, (SUB, width), 0).astype(jnp.float32)
    many = lax.broadcasted_iota(jnp.int32, (couples + 3, width), 0)
    many = jnp.where(many < couples, many * (2 * LANES), (many - (couples - 1)) * HALF)
    many = many.astype(jnp.float32)
    for at in range(0, columns, width):
        numbers = wavenumbers(at, width, pair_count, pair_total)
        for latitude, (total, inverse, scaling) in enumerate(scales):
            ones = turn_parts(numbers * few, total, inverse)
            eights = turn_parts(numbers * (few * float(SUB)), total, inverse)
            large = turn_parts(numbers * many, total, inverse)
            here = slice(at, at + width)
            there = slice(columns + at, columns + at + width)
            for couple in range(couples):
                for lanes, part in ((here, large[0]), (there, large[1])):
                    twiddle[latitude, couple, :, lanes] = jnp.broadcast_to(
                        scaling * part[couple : couple + 1], (SUB, width)
                    )
            products = [ones] + [multiplied(row_of(eights, row), ones) for row in range(1, SUB)]
            block = tuple(jnp.concatenate(parts, axis=0) for parts in zip(*products))
            for quarter in range(4):
                turned = block
                if quarter > 0:
                    turned = multiplied(row_of(large, couples + quarter - 1), block)
                rows = slice(HALF * quarter, HALF * (quarter + 1))
                table[latitude, rows, here] = turned[0].astype(jnp.bfloat16)
                table[latitude, rows, there] = turned[1].astype(jnp.bfloat16)
    for fetch in fetches[1:]:
        fetch.wait()
    known = [first_lat - rows_first[latitude] for latitude in range(lat_count)]
    known += [points[first_lat + latitude] for latitude in range(lat_count)]
    for place in range(-lat_count, 2 * lat_count):
        if place < 0 or place >= lat_count:
            place = jnp.clip(first_lat + place, 0, points.shape[0] - 1)
            known.append(lon - points[place])
    facts[...] = jnp.concatenate([jnp.full((1, LANES), one, jnp.int32) for one in known], axis=0)
    spread_rows(starts, begins)
    spread_lines(weights, factors)
    spread_lines(fields, lines)
    for latitude in range(lat_count):
        extend(lines, latitude, lat_count, lon - points[first_lat + latitude], ext, latitude)
    lower = (lax.broadcasted_iota(jnp.int32, (2 * SUB, LANES), 0) >= SUB).astype(jnp.int32)
    for latitude in range(lat_count):
        mine = first_lat - rows_first[latitude]
        for couple in range(couples):

            def spread_row(row):
                at = ((latitude * STENCIL + row) * couples + couple) * SUB
                tile = factors[pl.ds(pl.multiple_of(at, SUB), SUB), :]
                begun = []
                for side in range(2):
                    start = jnp.broadcast_to(
                        begins[latitude, row, 2 * couple + side], (2 * SUB, LANES)
                    )
                    begun.append((start + lower).astype(jnp.int16))
                return (
                    begun,
                    [jnp.broadcast_to(tile[line : line + 1], (SUB, LANES)) for line in range(SUB)],
                )

            totals = [jnp.zeros((SUB, LANES), jnp.float32) for _ in range(2)]
            for slot in range(lat_count):
                begun, scales = spread_row(mine + slot)
                parts = [ext[slot, 2 * couple + piece] for piece in range(4)]
                totals = gathered(totals, begun, scales, parts)
            for side in range(2):
                partial[latitude, couple, :, side * LANES : (side + 1) * LANES] = totals[side]
            others = (jnp.where(mine >= 1, 0, 2), jnp.where(mine <= 1, 3, 1))
            for choice, row in enumerate(others):
                begun, scales = spread_row(row)
                for side in range(2):
                    far_starts[latitude, choice, couple, side] = begun[side]
                for line in range(SUB):
                    far_scales[latitude, choice, couple, line] = scales[line]


def far_kernel(
    near_side, far_side, far_starts, far_scales, facts, partial, table, twiddle,
    out, lines, ext, grid, waves,
):
    lat_count, couples = partial.shape[:2]
    columns = table.shape[2] // 2
    owners = out.shape[0]
    toward = 1 - lax.axis_index("lat") % 2
    spread_lines(near_side, lines.at[toward])
    spread_lines(far_side, lines.at[1 - toward])
    fact = [jnp.broadcast_to(facts[row : row + 1], (SUB, LANES)) for row in range(4 * lat_count)]
    for slot in range(2 * lat_count):
        side, row = divmod(slot, lat_count)
        extend(lines.at[side], row, lat_count, fact[2 * lat_count + slot], ext, slot)
    lane = lax.broadcasted_iota(jnp.int32, (SUB, LANES), 1)
    width = 256
    choices = ((2, 1, 0), (3, 2, 1))
    for latitude in range(lat_count):
        own = jnp.broadcast_to(facts[latitude : latitude + 1], (2 * SUB, LANES)).astype(jnp.int16)
        at_zero = own == jnp.int16(0)
        at_one = own == jnp.int16(1)
        for couple in range(couples):
            sides = [pl.ds(side * LANES, LANES) for side in range(2)]
            totals = [partial[latitude, couple, :, lanes] for lanes in sides]
            for choice, slots in enumerate(choices):
                parts = []
                for piece in range(4):
                    zero, one, two = [ext[slot, 2 * couple + piece] for slot in slots]
                    parts.append(jnp.where(at_zero, zero, jnp.where(at_one, one, two)))
                totals = gathered(
                    totals,
                    [far_starts[latitude, choice, couple, side] for side in range(2)],
                    [far_scales[latitude, choice, couple, line] for line in range(SUB)],
                    parts,
                )
            for side in range(2):
                live = lane + (2 * couple + side) * LANES < fact[lat_count + latitude]
                grid[latitude, couple, :, sides[side]] = jnp.where(live, totals[side], 0.0)
    for latitude in range(lat_count):
        rows = grid[latitude].reshape(couples * SUB, 2 * LANES).astype(jnp.bfloat16)
        for at in range(0, columns, width):
            real = jnp.dot(
                rows, table[latitude, :, at : at + width], preferred_element_type=jnp.float32
            )
            imag = jnp.dot(
                rows,
                table[latitude, :, columns + at : columns + at + width],
                preferred_element_type=jnp.float32,
            )
            cosine = jnp.zeros((SUB, width), jnp.float32)
            sine = jnp.zeros((SUB, width), jnp.float32)
            for couple in range(couples):
                turn_cos = twiddle[latitude, couple, :, at : at + width]
                turn_sin = twiddle[latitude, couple, :, columns + at : columns + at + width]
                here = slice(couple * SUB, (couple + 1) * SUB)
                cosine = cosine + (real[here] * turn_cos - imag[here] * turn_sin)
                sine = sine - (real[here] * turn_sin + imag[here] * turn_cos)
            waves[latitude, 0:SUB, at : at + width] = cosine
            waves[latitude, SUB : 2 * SUB, at : at + width] = sine
        waves[latitude, :, columns:] = jnp.zeros((2 * SUB, waves.shape[2] - columns), jnp.float32)
        used = columns // owners
        for owner in range(owners):
            out[owner, 2 * SUB * latitude : 2 * SUB * (latitude + 1), :] = waves[
                latitude, :, owner * used : owner * used + LANES
            ].astype(jnp.bfloat16)


def row_keys(level_count, field_count):
    return [
        (level, field, part)
        for level in range(level_count)
        for field in range(field_count + 1)
        for part in range(2)
    ]


def place_rows(lines, keys, pair_count, left):
    lat_total = next(iter(lines.values())).shape[0]
    depth = SUB * lat_total
    half = len(keys) * SUB
    spread = (
        lax.broadcasted_iota(jnp.int32, (lat_total, depth), 0)
        == lax.broadcasted_iota(jnp.int32, (lat_total, depth), 1) % lat_total
    ).astype(jnp.bfloat16)
    keep = (
        lax.broadcasted_iota(jnp.int32, (SUB, depth), 0)
        == lax.broadcasted_iota(jnp.int32, (SUB, depth), 1) // lat_total
    )
    for place in range(0, len(keys), 2):
        if keys[place] not in lines:
            continue
        couple = [
            lax.dot_general(
                lines[key].astype(jnp.bfloat16),
                spread,
                (((0,), (0,)), ((), ())),
                preferred_element_type=jnp.float32,
            )
            for key in keys[place : place + 2]
        ]
        for member in range(2):
            for group in range(left.shape[0]):
                begin = member * pair_count + group * SUB
                pieces = [jnp.where(keep, one[begin : begin + SUB], 0.0) for one in couple]
                into = member * half + place * SUB
                left[group, into : into + 2 * SUB, :] = jnp.concatenate(pieces, axis=0).astype(
                    jnp.bfloat16
                )


def received_rows(received, wide, keys, field_count):
    wide[...] = received[...].astype(jnp.float32).reshape(wide.shape)
    lat_total = wide.shape[0] // (2 * SUB)
    return {
        (level, field, part): wide[
            pl.ds(part * SUB + level * field_count + field, lat_total, stride=2 * SUB), :
        ]
        for level, field, part in keys
    }


def left_kernel(
    level_count, field_count, pair_count, thickness, received, left, base, wide,
):
    keys = row_keys(level_count, field_count)
    wanted = [key for key in keys if key[1] < field_count]
    lines = received_rows(received, wide, wanted, field_count)
    place_rows(lines, keys, pair_count, left)
    for part in range(2):
        running = jnp.zeros(base.shape[1:], jnp.float32)
        for level in reversed(range(level_count)):
            running = running + thickness[level] * (
                lines[level, 2, part] + 0.61 * lines[level, 3, part]
            )
            base[2 * level + part] = running


def legendre_kernel(
    level_owners, level_count, field_count, owners, base, totals, legendre, left_given,
    out, left, planes, sent,
):
    pair_count, lat_total, degrees = legendre.shape
    pair_total = pair_count * owners
    groups = [(at, min(SUB, pair_count - at)) for at in range(0, pair_count, SUB)]
    keys = row_keys(level_count, field_count)
    half = len(keys) * SUB
    level_place = lax.axis_index("lev")
    first_pair = lax.axis_index("lat") * pair_count
    sums = {}
    for part in range(2):
        deeper = jnp.zeros((lat_total, LANES), jnp.float32)
        for place in range(totals.shape[0]):
            other = 1 - level_place if level_owners == 2 else place
            deeper = deeper + jnp.where(other > level_place, totals[place, part], 0.0)
        for level in range(level_count):
            sums[level, field_count, part] = base[2 * level + part] + deeper
    place_rows(sums, keys, pair_count, left)
    copies = []
    for start in range(0, degrees, 256):
        stop = min(start + 256, degrees)
        low = 0 if start < 2 * pair_total else half
        high = 2 * half if stop > pair_total + 1 else half
        parts = []
        for group, (at, size) in enumerate(groups):
            values = legendre[at : at + size, :, start:stop].reshape(size * lat_total, stop - start)
            sums = jnp.dot(
                left[group, low:high, : size * lat_total],
                values,
                preferred_element_type=jnp.float32,
            ).reshape((high - low) // SUB, SUB, stop - start)
            if high - low > half:
                shape = (SUB, stop - start)
                slot = lax.broadcasted_iota(jnp.int32, shape, 1) + start
                pair = lax.broadcasted_iota(jnp.int32, shape, 0) + (first_pair + at)
                sums = jnp.where(
                    slot + pair < 2 * pair_total, sums[: len(keys)], sums[len(keys) :]
                )
            parts.append(sums[:, :size])
        planes[:, :, :, :, start:stop] = (
            jnp.concatenate(parts, axis=1).astype(jnp.bfloat16).reshape(planes.shape[:4] + (stop - start,))
        )
        here = pl.ds(start, stop - start)
        copies.append(
            pltpu.make_async_copy(
                planes.at[:, :, :, :, here], out.at[:, :, :, :, here], sent.at[len(copies)]
            )
        )
        copies[-1].start()
    for copy in copies:
        copy.wait()


def held(value):
    return pltpu.with_memory_space_constraint(value, pltpu.HBM)


def local(fields, rows_first, points, starts, weights, thickness, legendre):
    level_count, field_count, lat_count, lon_count = fields.shape
    pair_count, lat_total, degrees = legendre.shape
    owners = lax.axis_size("lat")
    couples = lon_count // (2 * LANES)
    blocks = 2 * couples
    columns = 2 * owners * pair_count
    sides = []
    for first in range(2):
        edges = [(i, i + 1) for i in range(first, owners - 1, 2)]
        sides.append(lax.ppermute(fields, "lat", edges + [(j, i) for i, j in edges]))

    scalar = pl.BlockSpec(memory_space=pltpu.SMEM)
    vector = pl.BlockSpec(memory_space=pltpu.VMEM)
    params = pltpu.CompilerParams(vmem_limit_bytes=LIMIT)
    remote = pl.BlockSpec(memory_space=pltpu.HBM)
    partial, table, twiddle, far_starts, far_scales, facts = pl.pallas_call(
        functools.partial(near_kernel, pair_count * owners, pair_count),
        out_shape=(
            jax.ShapeDtypeStruct((lat_count, couples, SUB, 2 * LANES), jnp.float32),
            jax.ShapeDtypeStruct((lat_count, 2 * LANES, 2 * columns), jnp.bfloat16),
            jax.ShapeDtypeStruct((lat_count, couples, SUB, 2 * columns), jnp.float32),
            jax.ShapeDtypeStruct((lat_count, 2, couples, 2, 2 * SUB, LANES), jnp.int16),
            jax.ShapeDtypeStruct((lat_count, 2, couples, SUB, SUB, LANES), jnp.float32),
            jax.ShapeDtypeStruct((4 * lat_count, LANES), jnp.int32),
        ),
        in_specs=[remote] * 5,
        out_specs=(vector,) * 6,
        scratch_shapes=[
            pltpu.SMEM(rows_first.shape, jnp.int32),
            pltpu.SMEM(points.shape, jnp.int32),
            pltpu.VMEM(fields.shape, fields.dtype),
            pltpu.VMEM(starts.shape, starts.dtype),
            pltpu.VMEM(weights.shape, weights.dtype),
            pltpu.VMEM((lat_count, STENCIL, blocks, 1, LANES), jnp.int32),
            pltpu.VMEM((weights.size // LANES, LANES), jnp.float32),
            pltpu.VMEM((fields.size // LANES, LANES), jnp.float32),
            pltpu.VMEM((lat_count, blocks + 2, 2 * SUB, LANES), jnp.bfloat16),
            pltpu.SemaphoreType.DMA((5,)),
        ],
        compiler_params=params,
        cost_estimate=pl.CostEstimate(flops=10_000_000, bytes_accessed=4_000_000, transcendentals=0),
        name="near_rows",
    )(*(held(value) for value in (rows_first, points, fields, starts, weights)))

    coefficients = pl.pallas_call(
        far_kernel,
        out_shape=jax.ShapeDtypeStruct((owners, 2 * SUB * lat_count, LANES), jnp.bfloat16),
        in_specs=[vector] * 8,
        out_specs=vector,
        scratch_shapes=[
            pltpu.VMEM((2, fields.size // LANES, LANES), jnp.float32),
            pltpu.VMEM((2 * lat_count, blocks + 2, 2 * SUB, LANES), jnp.bfloat16),
            pltpu.VMEM((lat_count, couples, SUB, 2 * LANES), jnp.float32),
            pltpu.VMEM((lat_count, 2 * SUB, columns + LANES), jnp.float32),
        ],
        compiler_params=params,
        name="far_rows",
    )(*sides, far_starts, far_scales, facts, partial, table, twiddle)

    received = lax.all_to_all(coefficients, "lat", split_axis=0, concat_axis=0, tiled=True)
    by_level = received.reshape(lat_total, 2, level_count, field_count, LANES).astype(jnp.float32)
    virtual = by_level[:, :, :, 2] + 0.61 * by_level[:, :, :, 3]
    total = jnp.sum(thickness[None, None, :, None] * virtual, axis=2).transpose(1, 0, 2)
    level_owners = lax.axis_size("lev")
    if level_owners == 2:
        totals = lax.ppermute(total, "lev", [(0, 1), (1, 0)])[None]
    else:
        totals = lax.all_gather(total, "lev")

    out_shape = (level_count, field_count + 1, 2, pair_count, degrees)
    half = level_count * (field_count + 1) * 2 * SUB
    group_count = (pair_count + SUB - 1) // SUB
    left_shape = jax.ShapeDtypeStruct((group_count, 2 * half, SUB * lat_total), jnp.bfloat16)
    wide = pltpu.VMEM((lat_total * 2 * SUB, LANES), jnp.float32)
    left, base = pl.pallas_call(
        functools.partial(left_kernel, level_count, field_count, pair_count),
        out_shape=(
            left_shape,
            jax.ShapeDtypeStruct((2 * level_count, lat_total, LANES), jnp.float32),
        ),
        in_specs=[scalar, vector],
        out_specs=(vector, vector),
        scratch_shapes=[wide],
        compiler_params=params,
        cost_estimate=pl.CostEstimate(flops=50_000_000, bytes_accessed=2_000_000, transcendentals=0),
        name="left_rows",
    )(thickness, received)
    return pl.pallas_call(
        functools.partial(legendre_kernel, level_owners, level_count, field_count, owners),
        out_shape=(jax.ShapeDtypeStruct(out_shape, jnp.bfloat16), left_shape),
        in_specs=[vector, vector, vector, vector],
        out_specs=(pl.BlockSpec(memory_space=pl.ANY), vector),
        input_output_aliases={3: 1},
        scratch_shapes=[
            pltpu.VMEM(out_shape, jnp.bfloat16),
            pltpu.SemaphoreType.DMA(((degrees + 255) // 256,)),
        ],
        compiler_params=params,
        name="degree_sums",
    )(base, totals, legendre, left)[0]


def solution(mesh):
    placed = (
        P("lev", None, "lat", None),
        P("lat"),
        P(),
        P("lat", None, None),
        P("lat", None, None, None),
        P("lev"),
        P("lat", None, None),
    )
    return jax.shard_map(
        local,
        mesh=mesh,
        in_specs=placed,
        out_specs=P("lev", None, None, "lat", None),
        check_vma=False,
    )
```

```python
import functools

import jax
import jax.numpy as jnp
import numpy as np
from jax import lax
from jax.experimental import pallas as pl
from jax.experimental.pallas import tpu as pltpu
from jax.sharding import PartitionSpec as P

LANES = 128
SUB = 8
HALF = 64
STENCIL = 4
LIMIT = 24 * 1024 * 1024


def lane_gather(values, lanes):
    return jnp.take_along_axis(values, lanes, axis=1, mode="promise_in_bounds")


TAKE = lax.GatherDimensionNumbers(
    offset_dims=(),
    collapsed_slice_dims=(1,),
    start_index_map=(1,),
    operand_batching_dims=(0,),
    start_indices_batching_dims=(0,),
)


def short_gather(values, lanes):
    mode = lax.GatherScatterMode.PROMISE_IN_BOUNDS
    return lax.gather(values, lanes[:, :, None], TAKE, (1, 1), mode=mode)


SINE = (-70.99342854244645, 81.34076844400118, -41.337142359536955, 6.283164044230117)
COSINE = (
    56.2423804697887, -85.2403304160897, 64.93459063550272, -19.739171434929204, 0.9999999534680867,
)


def polynomial(terms, square):
    value = np.float32(terms[0])
    for term in terms[1:]:
        value = value * square + np.float32(term)
    return value


def turn_parts(product, total, inverse):
    turns = (product - jnp.floor(product * inverse + 0.5) * total) * inverse
    halves = jnp.floor(2.0 * turns + 0.5)
    sign = 1.0 - 2.0 * jnp.abs(halves)
    part = turns - 0.5 * halves
    square = part * part
    return sign * polynomial(COSINE, square), (sign * part) * polynomial(SINE, square)


def wavenumbers(at, width, pair_count, pair_total):
    column = lax.broadcasted_iota(jnp.int32, (1, width), 1).astype(jnp.float32) + float(at)
    owner = jnp.floor((column + 0.5) * (1.0 / (2 * pair_count)))
    inner = column - owner * (2.0 * pair_count)
    second = inner >= pair_count
    pair = owner * pair_count + jnp.where(second, inner - pair_count, inner)
    return jnp.where(second, 2.0 * pair_total - 1.0 - pair, pair)


def multiplied(one, two):
    return one[0] * two[0] - one[1] * two[1], one[0] * two[1] + one[1] * two[0]


def row_of(pair, row):
    return tuple(part[row : row + 1] for part in pair)


def extend(lines, row, rows_each, missing, ext, slot):
    blocks = ext.shape[1] - 2

    def block_of(block):
        return lines[pl.ds(block * rows_each + row, SUB, stride=blocks * rows_each), :]

    def place(block, values):
        ext[slot, block] = jnp.concatenate([values, values], axis=0).astype(jnp.bfloat16)

    for block in range(blocks - 1):
        place(block + 1, block_of(block))
    lane = lax.broadcasted_iota(jnp.int32, (SUB, LANES), 1)
    ahead = lane + missing
    behind = lane - missing
    first = lane_gather(block_of(0), ahead & (LANES - 1))
    second = lane_gather(block_of(1), ahead & (LANES - 1))
    last = block_of(blocks - 1)
    final = lane_gather(last, behind & (LANES - 1))
    before = lane_gather(block_of(blocks - 2), behind & (LANES - 1))
    place(0, jnp.where(behind >= 0, final, before))
    place(blocks, jnp.where(ahead < LANES, last, first))
    place(blocks + 1, jnp.where(ahead < LANES, first, second))


def spread_rows(starts, begins):
    lat_count, _, blocks = begins.shape[:3]
    for latitude in range(lat_count):
        for block in range(blocks):
            for row in range(STENCIL):
                lanes = slice(block * LANES, (block + 1) * LANES)
                begins[latitude, row, block] = (
                    starts[latitude, row : row + 1, lanes] - (block - 1) * LANES
                )


def spread_lines(source, lines):
    first, second, rows, lon = source.shape
    at = 0
    for one in range(first):
        for two in range(second):
            values = source[one, two].astype(jnp.float32)
            for block in range(lon // LANES):
                lines[at : at + rows, :] = values[:, block * LANES : (block + 1) * LANES]
                at += rows


def gathered(totals, starts, scales, parts):
    for side in range(2):
        for pair in range(2):
            spot = starts[side] + jnp.int16(2 * pair)
            lane = spot & jnp.int16(LANES - 1)
            low, middle, high = [short_gather(part, lane) for part in parts[side : side + 3]]
            value = jnp.where(
                spot < jnp.int16(LANES),
                low,
                jnp.where(spot < jnp.int16(2 * LANES), middle, high),
            ).astype(jnp.float32)
            line = STENCIL * side + 2 * pair
            totals[side] = (
                totals[side] + scales[line] * value[:SUB] + scales[line + 1] * value[SUB:]
            )
    return totals


def near_kernel(
    pair_total, pair_count, rows_first_far, points_far, fields_far, starts_far, weights_far,
    partial, table, twiddle, far_starts, far_scales, facts,
    rows_first, points, fields, starts, weights, begins, factors, lines, ext, arrived,
):
    lat_count, couples = partial.shape[:2]
    lon = 2 * couples * LANES
    columns = table.shape[2] // 2
    first_lat = lax.axis_index("lat") * lat_count
    fetches = [
        pltpu.make_async_copy(source, target, arrived.at[place])
        for place, (source, target) in enumerate(
            (
                (points_far, points),
                (rows_first_far, rows_first),
                (starts_far, starts),
                (weights_far, weights),
                (fields_far, fields),
            )
        )
    ]
    for fetch in fetches:
        fetch.start()
    fetches[0].wait()
    width = 256
    scales = []
    for latitude in range(lat_count):
        total = jnp.full((1, 1), points[first_lat + latitude], jnp.int32).astype(jnp.float32)
        inverse = 1.0 / total
        scales.append((total, inverse, jnp.sqrt(2.0 * inverse)))
    few = lax.broadcasted_iota(jnp.int32, (SUB, width), 0).astype(jnp.float32)
    many = lax.broadcasted_iota(jnp.int32, (2 * couples + 1, width), 0)
    many = jnp.where(many < 2 * couples, many * LANES, HALF)
    many = many.astype(jnp.float32)
    for at in range(0, columns, width):
        numbers = wavenumbers(at, width, pair_count, pair_total)
        for latitude, (total, inverse, scaling) in enumerate(scales):
            ones = turn_parts(numbers * few, total, inverse)
            eights = turn_parts(numbers * (few * float(SUB)), total, inverse)
            large = turn_parts(numbers * many, total, inverse)
            here = slice(at, at + width)
            there = slice(columns + at, columns + at + width)
            for block in range(2 * couples):
                for lanes, part in ((here, large[0]), (there, large[1])):
                    twiddle[latitude, block, :, lanes] = jnp.broadcast_to(
                        scaling * part[block : block + 1], (SUB, width)
                    )
            products = [ones] + [multiplied(row_of(eights, row), ones) for row in range(1, SUB)]
            products = tuple(jnp.concatenate(parts, axis=0) for parts in zip(*products))
            for upper_half in range(2):
                turned = products
                if upper_half:
                    turned = multiplied(row_of(large, 2 * couples), products)
                rows = slice(HALF * upper_half, HALF * (upper_half + 1))
                table[latitude, rows, here] = turned[0].astype(jnp.bfloat16)
                table[latitude, rows, there] = turned[1].astype(jnp.bfloat16)
    for fetch in fetches[1:]:
        fetch.wait()
    known = [first_lat - rows_first[latitude] for latitude in range(lat_count)]
    known += [points[first_lat + latitude] for latitude in range(lat_count)]
    for place in range(-lat_count, 2 * lat_count):
        if place < 0 or place >= lat_count:
            place = jnp.clip(first_lat + place, 0, points.shape[0] - 1)
            known.append(lon - points[place])
    facts[...] = jnp.concatenate([jnp.full((1, LANES), one, jnp.int32) for one in known], axis=0)
    spread_rows(starts, begins)
    spread_lines(weights, factors)
    spread_lines(fields, lines)
    for latitude in range(lat_count):
        extend(lines, latitude, lat_count, lon - points[first_lat + latitude], ext, latitude)
    lower = (lax.broadcasted_iota(jnp.int32, (2 * SUB, LANES), 0) >= SUB).astype(jnp.int32)
    for latitude in range(lat_count):
        mine = first_lat - rows_first[latitude]
        for couple in range(couples):

            def spread_row(row):
                at = ((latitude * STENCIL + row) * couples + couple) * SUB
                tile = factors[pl.ds(pl.multiple_of(at, SUB), SUB), :]
                begun = []
                for side in range(2):
                    start = jnp.broadcast_to(
                        begins[latitude, row, 2 * couple + side], (2 * SUB, LANES)
                    )
                    begun.append((start + lower).astype(jnp.int16))
                return (
                    begun,
                    [jnp.broadcast_to(tile[line : line + 1], (SUB, LANES)) for line in range(SUB)],
                )

            totals = [jnp.zeros((SUB, LANES), jnp.float32) for _ in range(2)]
            for slot in range(lat_count):
                begun, scales = spread_row(mine + slot)
                parts = [ext[slot, 2 * couple + piece] for piece in range(4)]
                totals = gathered(totals, begun, scales, parts)
            for side in range(2):
                partial[latitude, couple, :, side * LANES : (side + 1) * LANES] = totals[side]
            others = (jnp.where(mine >= 1, 0, 2), jnp.where(mine <= 1, 3, 1))
            for choice, row in enumerate(others):
                begun, scales = spread_row(row)
                for side in range(2):
                    far_starts[latitude, choice, couple, side] = begun[side]
                for line in range(SUB):
                    far_scales[latitude, choice, couple, line] = scales[line]


def far_kernel(
    near_side, far_side, far_starts, far_scales, facts, partial, table, twiddle,
    out, lines, ext, grid, waves,
):
    lat_count, couples = partial.shape[:2]
    columns = table.shape[2] // 2
    owners = out.shape[0]
    toward = 1 - lax.axis_index("lat") % 2
    spread_lines(near_side, lines.at[toward])
    spread_lines(far_side, lines.at[1 - toward])
    fact = [jnp.broadcast_to(facts[row : row + 1], (SUB, LANES)) for row in range(4 * lat_count)]
    for slot in range(2 * lat_count):
        side, row = divmod(slot, lat_count)
        extend(lines.at[side], row, lat_count, fact[2 * lat_count + slot], ext, slot)
    lane = lax.broadcasted_iota(jnp.int32, (SUB, LANES), 1)
    width = 256
    choices = ((2, 1, 0), (3, 2, 1))
    for latitude in range(lat_count):
        own = jnp.broadcast_to(facts[latitude : latitude + 1], (2 * SUB, LANES)).astype(jnp.int16)
        at_zero = own == jnp.int16(0)
        at_one = own == jnp.int16(1)
        for couple in range(couples):
            sides = [pl.ds(side * LANES, LANES) for side in range(2)]
            totals = [partial[latitude, couple, :, lanes] for lanes in sides]
            for choice, slots in enumerate(choices):
                parts = []
                for piece in range(4):
                    zero, one, two = [ext[slot, 2 * couple + piece] for slot in slots]
                    parts.append(jnp.where(at_zero, zero, jnp.where(at_one, one, two)))
                totals = gathered(
                    totals,
                    [far_starts[latitude, choice, couple, side] for side in range(2)],
                    [far_scales[latitude, choice, couple, line] for line in range(SUB)],
                    parts,
                )
            for side in range(2):
                live = lane + (2 * couple + side) * LANES < fact[lat_count + latitude]
                grid[latitude, 2 * couple + side] = jnp.where(live, totals[side], 0.0)
    for latitude in range(lat_count):
        rows = grid[latitude].reshape(2 * couples * SUB, LANES).astype(jnp.bfloat16)
        for at in range(0, columns, width):
            real = jnp.dot(
                rows, table[latitude, :, at : at + width], preferred_element_type=jnp.float32
            )
            imag = jnp.dot(
                rows,
                table[latitude, :, columns + at : columns + at + width],
                preferred_element_type=jnp.float32,
            )
            cosine = jnp.zeros((SUB, width), jnp.float32)
            sine = jnp.zeros((SUB, width), jnp.float32)
            for block in range(2 * couples):
                turn_cos = twiddle[latitude, block, :, at : at + width]
                turn_sin = twiddle[latitude, block, :, columns + at : columns + at + width]
                here = slice(block * SUB, (block + 1) * SUB)
                cosine = cosine + (real[here] * turn_cos - imag[here] * turn_sin)
                sine = sine - (real[here] * turn_sin + imag[here] * turn_cos)
            waves[latitude, 0:SUB, at : at + width] = cosine
            waves[latitude, SUB : 2 * SUB, at : at + width] = sine
        waves[latitude, :, columns:] = jnp.zeros((2 * SUB, waves.shape[2] - columns), jnp.float32)
        used = columns // owners
        for owner in range(owners):
            out[owner, 2 * SUB * latitude : 2 * SUB * (latitude + 1), :] = waves[
                latitude, :, owner * used : owner * used + LANES
            ].astype(jnp.bfloat16)


def row_keys(level_count, field_count):
    return [
        (level, field, part)
        for level in range(level_count)
        for field in range(field_count + 1)
        for part in range(2)
    ]


def place_rows(lines, keys, pair_count, left):
    lat_total = next(iter(lines.values())).shape[0]
    depth = SUB * lat_total
    half = len(keys) * SUB
    spread = (
        lax.broadcasted_iota(jnp.int32, (lat_total, depth), 0)
        == lax.broadcasted_iota(jnp.int32, (lat_total, depth), 1) % lat_total
    ).astype(jnp.bfloat16)
    keep = (
        lax.broadcasted_iota(jnp.int32, (SUB, depth), 0)
        == lax.broadcasted_iota(jnp.int32, (SUB, depth), 1) // lat_total
    )
    for place in range(0, len(keys), 2):
        if keys[place] not in lines:
            continue
        couple = [
            lax.dot_general(
                lines[key].astype(jnp.bfloat16),
                spread,
                (((0,), (0,)), ((), ())),
                preferred_element_type=jnp.float32,
            )
            for key in keys[place : place + 2]
        ]
        for member in range(2):
            for group in range(left.shape[0]):
                begin = member * pair_count + group * SUB
                pieces = [jnp.where(keep, one[begin : begin + SUB], 0.0) for one in couple]
                into = member * half + place * SUB
                left[group, into : into + 2 * SUB, :] = jnp.concatenate(pieces, axis=0).astype(
                    jnp.bfloat16
                )


def received_rows(received, wide, keys, field_count):
    wide[...] = received[...].astype(jnp.float32).reshape(wide.shape)
    lat_total = wide.shape[0] // (2 * SUB)
    return {
        (level, field, part): wide[
            pl.ds(part * SUB + level * field_count + field, lat_total, stride=2 * SUB), :
        ]
        for level, field, part in keys
    }


def left_kernel(
    level_count, field_count, pair_count, thickness, received, left, base, wide,
):
    keys = row_keys(level_count, field_count)
    wanted = [key for key in keys if key[1] < field_count]
    lines = received_rows(received, wide, wanted, field_count)
    place_rows(lines, keys, pair_count, left)
    for part in range(2):
        running = jnp.zeros(base.shape[1:], jnp.float32)
        for level in reversed(range(level_count)):
            running = running + thickness[level] * (
                lines[level, 2, part] + 0.61 * lines[level, 3, part]
            )
            base[2 * level + part] = running


def legendre_kernel(
    level_owners, level_count, field_count, owners, base, totals, legendre, left_given,
    out, left, planes, sent,
):
    pair_count, lat_total, degrees = legendre.shape
    pair_total = pair_count * owners
    groups = [(at, min(SUB, pair_count - at)) for at in range(0, pair_count, SUB)]
    keys = row_keys(level_count, field_count)
    half = len(keys) * SUB
    level_place = lax.axis_index("lev")
    first_pair = lax.axis_index("lat") * pair_count
    sums = {}
    for part in range(2):
        deeper = jnp.zeros((lat_total, LANES), jnp.float32)
        for place in range(totals.shape[0]):
            other = 1 - level_place if level_owners == 2 else place
            deeper = deeper + jnp.where(other > level_place, totals[place, part], 0.0)
        for level in range(level_count):
            sums[level, field_count, part] = base[2 * level + part] + deeper
    place_rows(sums, keys, pair_count, left)
    copies = []
    for start in range(0, degrees, 256):
        stop = min(start + 256, degrees)
        low = 0 if start < 2 * pair_total else half
        high = 2 * half if stop > pair_total + 1 else half
        parts = []
        for group, (at, size) in enumerate(groups):
            values = legendre[at : at + size, :, start:stop].reshape(size * lat_total, stop - start)
            sums = jnp.dot(
                left[group, low:high, : size * lat_total],
                values,
                preferred_element_type=jnp.float32,
            ).reshape((high - low) // SUB, SUB, stop - start)
            if high - low > half:
                shape = (SUB, stop - start)
                slot = lax.broadcasted_iota(jnp.int32, shape, 1) + start
                pair = lax.broadcasted_iota(jnp.int32, shape, 0) + (first_pair + at)
                sums = jnp.where(
                    slot + pair < 2 * pair_total, sums[: len(keys)], sums[len(keys) :]
                )
            parts.append(sums[:, :size])
        planes[:, :, :, :, start:stop] = (
            jnp.concatenate(parts, axis=1).astype(jnp.bfloat16).reshape(planes.shape[:4] + (stop - start,))
        )
        here = pl.ds(start, stop - start)
        copies.append(
            pltpu.make_async_copy(
                planes.at[:, :, :, :, here], out.at[:, :, :, :, here], sent.at[len(copies)]
            )
        )
        copies[-1].start()
    for copy in copies:
        copy.wait()


def held(value):
    return pltpu.with_memory_space_constraint(value, pltpu.HBM)


def local(fields, rows_first, points, starts, weights, thickness, legendre):
    level_count, field_count, lat_count, lon_count = fields.shape
    pair_count, lat_total, degrees = legendre.shape
    owners = lax.axis_size("lat")
    couples = lon_count // (2 * LANES)
    blocks = 2 * couples
    columns = 2 * owners * pair_count
    sides = []
    for first in range(2):
        edges = [(i, i + 1) for i in range(first, owners - 1, 2)]
        sides.append(lax.ppermute(fields, "lat", edges + [(j, i) for i, j in edges]))

    scalar = pl.BlockSpec(memory_space=pltpu.SMEM)
    vector = pl.BlockSpec(memory_space=pltpu.VMEM)
    params = pltpu.CompilerParams(vmem_limit_bytes=LIMIT)
    remote = pl.BlockSpec(memory_space=pltpu.HBM)
    partial, table, twiddle, far_starts, far_scales, facts = pl.pallas_call(
        functools.partial(near_kernel, pair_count * owners, pair_count),
        out_shape=(
            jax.ShapeDtypeStruct((lat_count, couples, SUB, 2 * LANES), jnp.float32),
            jax.ShapeDtypeStruct((lat_count, LANES, 2 * columns), jnp.bfloat16),
            jax.ShapeDtypeStruct((lat_count, blocks, SUB, 2 * columns), jnp.float32),
            jax.ShapeDtypeStruct((lat_count, 2, couples, 2, 2 * SUB, LANES), jnp.int16),
            jax.ShapeDtypeStruct((lat_count, 2, couples, SUB, SUB, LANES), jnp.float32),
            jax.ShapeDtypeStruct((4 * lat_count, LANES), jnp.int32),
        ),
        in_specs=[remote] * 5,
        out_specs=(vector,) * 6,
        scratch_shapes=[
            pltpu.SMEM(rows_first.shape, jnp.int32),
            pltpu.SMEM(points.shape, jnp.int32),
            pltpu.VMEM(fields.shape, fields.dtype),
            pltpu.VMEM(starts.shape, starts.dtype),
            pltpu.VMEM(weights.shape, weights.dtype),
            pltpu.VMEM((lat_count, STENCIL, blocks, 1, LANES), jnp.int32),
            pltpu.VMEM((weights.size // LANES, LANES), jnp.float32),
            pltpu.VMEM((fields.size // LANES, LANES), jnp.float32),
            pltpu.VMEM((lat_count, blocks + 2, 2 * SUB, LANES), jnp.bfloat16),
            pltpu.SemaphoreType.DMA((5,)),
        ],
        compiler_params=params,
        cost_estimate=pl.CostEstimate(flops=10_000_000, bytes_accessed=4_000_000, transcendentals=0),
        name="near_rows",
    )(*(held(value) for value in (rows_first, points, fields, starts, weights)))

    coefficients = pl.pallas_call(
        far_kernel,
        out_shape=jax.ShapeDtypeStruct((owners, 2 * SUB * lat_count, LANES), jnp.bfloat16),
        in_specs=[vector] * 8,
        out_specs=vector,
        scratch_shapes=[
            pltpu.VMEM((2, fields.size // LANES, LANES), jnp.float32),
            pltpu.VMEM((2 * lat_count, blocks + 2, 2 * SUB, LANES), jnp.bfloat16),
            pltpu.VMEM((lat_count, blocks, SUB, LANES), jnp.float32),
            pltpu.VMEM((lat_count, 2 * SUB, columns + LANES), jnp.float32),
        ],
        compiler_params=params,
        name="far_rows",
    )(*sides, far_starts, far_scales, facts, partial, table, twiddle)

    received = lax.all_to_all(coefficients, "lat", split_axis=0, concat_axis=0, tiled=True)
    by_level = received.reshape(lat_total, 2, level_count, field_count, LANES).astype(jnp.float32)
    virtual = by_level[:, :, :, 2] + 0.61 * by_level[:, :, :, 3]
    total = jnp.sum(thickness[None, None, :, None] * virtual, axis=2).transpose(1, 0, 2)
    level_owners = lax.axis_size("lev")
    if level_owners == 2:
        totals = lax.ppermute(total, "lev", [(0, 1), (1, 0)])[None]
    else:
        totals = lax.all_gather(total, "lev")

    out_shape = (level_count, field_count + 1, 2, pair_count, degrees)
    half = level_count * (field_count + 1) * 2 * SUB
    group_count = (pair_count + SUB - 1) // SUB
    left_shape = jax.ShapeDtypeStruct((group_count, 2 * half, SUB * lat_total), jnp.bfloat16)
    wide = pltpu.VMEM((lat_total * 2 * SUB, LANES), jnp.float32)
    left, base = pl.pallas_call(
        functools.partial(left_kernel, level_count, field_count, pair_count),
        out_shape=(
            left_shape,
            jax.ShapeDtypeStruct((2 * level_count, lat_total, LANES), jnp.float32),
        ),
        in_specs=[scalar, vector],
        out_specs=(vector, vector),
        scratch_shapes=[wide],
        compiler_params=params,
        cost_estimate=pl.CostEstimate(flops=50_000_000, bytes_accessed=2_000_000, transcendentals=0),
        name="left_rows",
    )(thickness, received)
    return pl.pallas_call(
        functools.partial(legendre_kernel, level_owners, level_count, field_count, owners),
        out_shape=(jax.ShapeDtypeStruct(out_shape, jnp.bfloat16), left_shape),
        in_specs=[vector, vector, vector, vector],
        out_specs=(pl.BlockSpec(memory_space=pl.ANY), vector),
        input_output_aliases={3: 1},
        scratch_shapes=[
            pltpu.VMEM(out_shape, jnp.bfloat16),
            pltpu.SemaphoreType.DMA(((degrees + 255) // 256,)),
        ],
        compiler_params=params,
        name="degree_sums",
    )(base, totals, legendre, left)[0]


def solution(mesh):
    placed = (
        P("lev", None, "lat", None),
        P("lat"),
        P(),
        P("lat", None, None),
        P("lat", None, None, None),
        P("lev"),
        P("lat", None, None),
    )
    return jax.shard_map(
        local,
        mesh=mesh,
        in_specs=placed,
        out_specs=P("lev", None, None, "lat", None),
        check_vma=False,
    )
```

```python
import functools

import jax
import jax.numpy as jnp
import numpy as np
from jax import lax
from jax.experimental import pallas as pl
from jax.experimental.pallas import tpu as pltpu
from jax.sharding import PartitionSpec as P

LANES = 128
SUB = 8
HALF = 64
STENCIL = 4
LIMIT = 24 * 1024 * 1024


def lane_gather(values, lanes):
    return jnp.take_along_axis(values, lanes, axis=1, mode="promise_in_bounds")


TAKE = lax.GatherDimensionNumbers(
    offset_dims=(),
    collapsed_slice_dims=(1,),
    start_index_map=(1,),
    operand_batching_dims=(0,),
    start_indices_batching_dims=(0,),
)


def short_gather(values, lanes):
    mode = lax.GatherScatterMode.PROMISE_IN_BOUNDS
    return lax.gather(values, lanes[:, :, None], TAKE, (1, 1), mode=mode)


SINE = (-70.99342854244645, 81.34076844400118, -41.337142359536955, 6.283164044230117)
COSINE = (
    56.2423804697887, -85.2403304160897, 64.93459063550272, -19.739171434929204, 0.9999999534680867,
)


def polynomial(terms, square):
    value = np.float32(terms[0])
    for term in terms[1:]:
        value = value * square + np.float32(term)
    return value


def turn_parts(product, total, inverse):
    turns = (product - jnp.floor(product * inverse + 0.5) * total) * inverse
    halves = jnp.floor(2.0 * turns + 0.5)
    sign = 1.0 - 2.0 * jnp.abs(halves)
    part = turns - 0.5 * halves
    square = part * part
    return sign * polynomial(COSINE, square), (sign * part) * polynomial(SINE, square)


def wavenumbers(at, width, pair_count, pair_total):
    column = lax.broadcasted_iota(jnp.int32, (1, width), 1).astype(jnp.float32) + float(at)
    owner = jnp.floor((column + 0.5) * (1.0 / (2 * pair_count)))
    inner = column - owner * (2.0 * pair_count)
    second = inner >= pair_count
    pair = owner * pair_count + jnp.where(second, inner - pair_count, inner)
    return jnp.where(second, 2.0 * pair_total - 1.0 - pair, pair)


def multiplied(one, two):
    return one[0] * two[0] - one[1] * two[1], one[0] * two[1] + one[1] * two[0]


def row_of(pair, row):
    return tuple(part[row : row + 1] for part in pair)


def extend(lines, row, rows_each, missing, ext, slot):
    blocks = ext.shape[1] - 2

    def block_of(block):
        return lines[pl.ds(block * rows_each + row, SUB, stride=blocks * rows_each), :]

    def place(block, values):
        ext[slot, block] = jnp.concatenate([values, values], axis=0).astype(jnp.bfloat16)

    for block in range(blocks - 1):
        place(block + 1, block_of(block))
    lane = lax.broadcasted_iota(jnp.int32, (SUB, LANES), 1)
    ahead = lane + missing
    behind = lane - missing
    first = lane_gather(block_of(0), ahead & (LANES - 1))
    second = lane_gather(block_of(1), ahead & (LANES - 1))
    last = block_of(blocks - 1)
    final = lane_gather(last, behind & (LANES - 1))
    before = lane_gather(block_of(blocks - 2), behind & (LANES - 1))
    place(0, jnp.where(behind >= 0, final, before))
    place(blocks, jnp.where(ahead < LANES, last, first))
    place(blocks + 1, jnp.where(ahead < LANES, first, second))


def spread_rows(starts, begins):
    lat_count, _, blocks = begins.shape[:3]
    for latitude in range(lat_count):
        for block in range(blocks):
            for row in range(STENCIL):
                lanes = slice(block * LANES, (block + 1) * LANES)
                begins[latitude, row, block] = (
                    starts[latitude, row : row + 1, lanes] - (block - 1) * LANES
                )


def spread_lines(source, lines):
    first, second, rows, lon = source.shape
    at = 0
    for one in range(first):
        for two in range(second):
            values = source[one, two].astype(jnp.float32)
            for block in range(lon // LANES):
                lines[at : at + rows, :] = values[:, block * LANES : (block + 1) * LANES]
                at += rows


def gathered(totals, starts, scales, parts):
    for side in range(2):
        for pair in range(2):
            spot = starts[side] + jnp.int16(2 * pair)
            lane = spot & jnp.int16(LANES - 1)
            low, middle, high = [short_gather(part, lane) for part in parts[side : side + 3]]
            value = jnp.where(
                spot < jnp.int16(LANES),
                low,
                jnp.where(spot < jnp.int16(2 * LANES), middle, high),
            ).astype(jnp.float32)
            line = STENCIL * side + 2 * pair
            totals[side] = (
                totals[side] + scales[line] * value[:SUB] + scales[line + 1] * value[SUB:]
            )
    return totals


def near_kernel(
    pair_total, pair_count, rows_first_far, points_far, fields_far, starts_far, weights_far,
    partial, table, twiddle, far_starts, far_scales, facts,
    rows_first, points, fields, starts, weights, begins, factors, lines, ext, arrived,
):
    lat_count, couples = partial.shape[:2]
    lon = 2 * couples * LANES
    columns = table.shape[2] // 2
    first_lat = lax.axis_index("lat") * lat_count
    fetches = [
        pltpu.make_async_copy(source, target, arrived.at[place])
        for place, (source, target) in enumerate(
            (
                (points_far, points),
                (rows_first_far, rows_first),
                (starts_far, starts),
                (weights_far, weights),
                (fields_far, fields),
            )
        )
    ]
    for fetch in fetches:
        fetch.start()
    fetches[0].wait()
    width = 256
    scales = []
    for latitude in range(lat_count):
        total = jnp.full((1, 1), points[first_lat + latitude], jnp.int32).astype(jnp.float32)
        inverse = 1.0 / total
        scales.append((total, inverse, jnp.sqrt(2.0 * inverse)))
    few = lax.broadcasted_iota(jnp.int32, (SUB, width), 0).astype(jnp.float32)
    many = lax.broadcasted_iota(jnp.int32, (couples + 3, width), 0)
    many = jnp.where(many < couples, many * (2 * LANES), (many - (couples - 1)) * HALF)
    many = many.astype(jnp.float32)
    for at in range(0, columns, width):
        numbers = wavenumbers(at, width, pair_count, pair_total)
        for latitude, (total, inverse, scaling) in enumerate(scales):
            ones = turn_parts(numbers * few, total, inverse)
            eights = turn_parts(numbers * (few * float(SUB)), total, inverse)
            large = turn_parts(numbers * many, total, inverse)
            here = slice(at, at + width)
            there = slice(columns + at, columns + at + width)
            for couple in range(couples):
                for lanes, part in ((here, large[0]), (there, large[1])):
                    twiddle[latitude, couple, :, lanes] = jnp.broadcast_to(
                        scaling * part[couple : couple + 1], (SUB, width)
                    )
            products = [ones] + [multiplied(row_of(eights, row), ones) for row in range(1, SUB)]
            block = tuple(jnp.concatenate(parts, axis=0) for parts in zip(*products))
            for quarter in range(4):
                turned = block
                if quarter > 0:
                    turned = multiplied(row_of(large, couples + quarter - 1), block)
                rows = slice(HALF * quarter, HALF * (quarter + 1))
                table[latitude, rows, here] = turned[0].astype(jnp.bfloat16)
                table[latitude, rows, there] = turned[1].astype(jnp.bfloat16)
    for fetch in fetches[1:]:
        fetch.wait()
    known = [first_lat - rows_first[latitude] for latitude in range(lat_count)]
    known += [points[first_lat + latitude] for latitude in range(lat_count)]
    for place in range(-lat_count, 2 * lat_count):
        if place < 0 or place >= lat_count:
            place = jnp.clip(first_lat + place, 0, points.shape[0] - 1)
            known.append(lon - points[place])
    facts[...] = jnp.concatenate([jnp.full((1, LANES), one, jnp.int32) for one in known], axis=0)
    spread_rows(starts, begins)
    spread_lines(weights, factors)
    spread_lines(fields, lines)
    for latitude in range(lat_count):
        extend(lines, latitude, lat_count, lon - points[first_lat + latitude], ext, latitude)
    lower = (lax.broadcasted_iota(jnp.int32, (2 * SUB, LANES), 0) >= SUB).astype(jnp.int32)
    for latitude in range(lat_count):
        mine = first_lat - rows_first[latitude]
        for couple in range(couples):

            def spread_row(row):
                at = ((latitude * STENCIL + row) * couples + couple) * SUB
                tile = factors[pl.ds(pl.multiple_of(at, SUB), SUB), :]
                begun = []
                for side in range(2):
                    start = jnp.broadcast_to(
                        begins[latitude, row, 2 * couple + side], (2 * SUB, LANES)
                    )
                    begun.append((start + lower).astype(jnp.int16))
                return (
                    begun,
                    [jnp.broadcast_to(tile[line : line + 1], (SUB, LANES)) for line in range(SUB)],
                )

            totals = [jnp.zeros((SUB, LANES), jnp.float32) for _ in range(2)]
            for slot in range(lat_count):
                begun, scales = spread_row(mine + slot)
                parts = [ext[slot, 2 * couple + piece] for piece in range(4)]
                totals = gathered(totals, begun, scales, parts)
            for side in range(2):
                partial[latitude, couple, :, side * LANES : (side + 1) * LANES] = totals[side]
            others = (jnp.where(mine >= 1, 0, 2), jnp.where(mine <= 1, 3, 1))
            for choice, row in enumerate(others):
                begun, scales = spread_row(row)
                for side in range(2):
                    far_starts[latitude, choice, couple, side] = begun[side]
                for line in range(SUB):
                    far_scales[latitude, choice, couple, line] = scales[line]


def far_kernel(
    near_side, far_side, far_starts, far_scales, facts, partial, table, twiddle,
    out, lines, ext, grid, waves,
):
    lat_count, couples = partial.shape[:2]
    columns = table.shape[2] // 2
    owners = out.shape[0]
    toward = 1 - lax.axis_index("lat") % 2
    spread_lines(near_side, lines.at[toward])
    spread_lines(far_side, lines.at[1 - toward])
    fact = [jnp.broadcast_to(facts[row : row + 1], (SUB, LANES)) for row in range(4 * lat_count)]
    for slot in range(2 * lat_count):
        side, row = divmod(slot, lat_count)
        extend(lines.at[side], row, lat_count, fact[2 * lat_count + slot], ext, slot)
    lane = lax.broadcasted_iota(jnp.int32, (SUB, LANES), 1)
    width = 256
    choices = ((2, 1, 0), (3, 2, 1))
    for latitude in range(lat_count):
        own = jnp.broadcast_to(facts[latitude : latitude + 1], (2 * SUB, LANES)).astype(jnp.int16)
        at_zero = own == jnp.int16(0)
        at_one = own == jnp.int16(1)
        for couple in range(couples):
            sides = [pl.ds(side * LANES, LANES) for side in range(2)]
            totals = [partial[latitude, couple, :, lanes] for lanes in sides]
            for choice, slots in enumerate(choices):
                parts = []
                for piece in range(4):
                    zero, one, two = [ext[slot, 2 * couple + piece] for slot in slots]
                    parts.append(jnp.where(at_zero, zero, jnp.where(at_one, one, two)))
                totals = gathered(
                    totals,
                    [far_starts[latitude, choice, couple, side] for side in range(2)],
                    [far_scales[latitude, choice, couple, line] for line in range(SUB)],
                    parts,
                )
            for side in range(2):
                live = lane + (2 * couple + side) * LANES < fact[lat_count + latitude]
                grid[latitude, couple, :, sides[side]] = jnp.where(live, totals[side], 0.0)
    for latitude in range(lat_count):
        rows = grid[latitude].reshape(couples * SUB, 2 * LANES).astype(jnp.bfloat16)
        for at in range(0, columns, width):
            real = jnp.dot(
                rows, table[latitude, :, at : at + width], preferred_element_type=jnp.float32
            )
            imag = jnp.dot(
                rows,
                table[latitude, :, columns + at : columns + at + width],
                preferred_element_type=jnp.float32,
            )
            cosine = jnp.zeros((SUB, width), jnp.float32)
            sine = jnp.zeros((SUB, width), jnp.float32)
            for couple in range(couples):
                turn_cos = twiddle[latitude, couple, :, at : at + width]
                turn_sin = twiddle[latitude, couple, :, columns + at : columns + at + width]
                here = slice(couple * SUB, (couple + 1) * SUB)
                cosine = cosine + (real[here] * turn_cos - imag[here] * turn_sin)
                sine = sine - (real[here] * turn_sin + imag[here] * turn_cos)
            waves[latitude, :, at : at + width] = jnp.concatenate([cosine, sine], axis=0).astype(
                jnp.bfloat16
            )
        waves[latitude, :, columns:] = jnp.zeros((2 * SUB, waves.shape[2] - columns), jnp.bfloat16)
        used = columns // owners
        for owner in range(owners):
            out[owner, 2 * SUB * latitude : 2 * SUB * (latitude + 1), :] = waves[
                latitude, :, owner * used : owner * used + LANES
            ]


def row_keys(level_count, field_count):
    return [
        (level, field, part)
        for level in range(level_count)
        for field in range(field_count + 1)
        for part in range(2)
    ]


def place_rows(lines, keys, pair_count, left):
    lat_total = next(iter(lines.values())).shape[0]
    depth = SUB * lat_total
    half = len(keys) * SUB
    spread = (
        lax.broadcasted_iota(jnp.int32, (lat_total, depth), 0)
        == lax.broadcasted_iota(jnp.int32, (lat_total, depth), 1) % lat_total
    ).astype(jnp.bfloat16)
    keep = (
        lax.broadcasted_iota(jnp.int32, (SUB, depth), 0)
        == lax.broadcasted_iota(jnp.int32, (SUB, depth), 1) // lat_total
    )
    for place in range(0, len(keys), 2):
        if keys[place] not in lines:
            continue
        couple = [
            lax.dot_general(
                lines[key].astype(jnp.bfloat16),
                spread,
                (((0,), (0,)), ((), ())),
                preferred_element_type=jnp.float32,
            )
            for key in keys[place : place + 2]
        ]
        for member in range(2):
            for group in range(left.shape[0]):
                begin = member * pair_count + group * SUB
                pieces = [jnp.where(keep, one[begin : begin + SUB], 0.0) for one in couple]
                into = member * half + place * SUB
                left[group, into : into + 2 * SUB, :] = jnp.concatenate(pieces, axis=0).astype(
                    jnp.bfloat16
                )


def received_rows(received, wide, keys, field_count):
    wide[...] = received[...].astype(jnp.float32).reshape(wide.shape)
    lat_total = wide.shape[0] // (2 * SUB)
    return {
        (level, field, part): wide[
            pl.ds(part * SUB + level * field_count + field, lat_total, stride=2 * SUB), :
        ]
        for level, field, part in keys
    }


def left_kernel(
    level_count, field_count, pair_count, thickness, received, left, base, wide,
):
    keys = row_keys(level_count, field_count)
    wanted = [key for key in keys if key[1] < field_count]
    lines = received_rows(received, wide, wanted, field_count)
    place_rows(lines, keys, pair_count, left)
    for part in range(2):
        running = jnp.zeros(base.shape[1:], jnp.float32)
        for level in reversed(range(level_count)):
            running = running + thickness[level] * (
                lines[level, 2, part] + 0.61 * lines[level, 3, part]
            )
            base[2 * level + part] = running


def legendre_kernel(
    level_owners, level_count, field_count, owners, base, totals, legendre, left_given,
    out, left, planes, sent,
):
    pair_count, lat_total, degrees = legendre.shape
    pair_total = pair_count * owners
    groups = [(at, min(SUB, pair_count - at)) for at in range(0, pair_count, SUB)]
    keys = row_keys(level_count, field_count)
    half = len(keys) * SUB
    level_place = lax.axis_index("lev")
    first_pair = lax.axis_index("lat") * pair_count
    sums = {}
    for part in range(2):
        deeper = jnp.zeros((lat_total, LANES), jnp.float32)
        for place in range(totals.shape[0]):
            other = 1 - level_place if level_owners == 2 else place
            deeper = deeper + jnp.where(other > level_place, totals[place, part], 0.0)
        for level in range(level_count):
            sums[level, field_count, part] = base[2 * level + part] + deeper
    place_rows(sums, keys, pair_count, left)
    copies = []
    for start in range(0, degrees, 256):
        stop = min(start + 256, degrees)
        low = 0 if start < 2 * pair_total else half
        high = 2 * half if stop > pair_total + 1 else half
        parts = []
        for group, (at, size) in enumerate(groups):
            values = legendre[at : at + size, :, start:stop].reshape(size * lat_total, stop - start)
            sums = jnp.dot(
                left[group, low:high, : size * lat_total],
                values,
                preferred_element_type=jnp.float32,
            ).reshape((high - low) // SUB, SUB, stop - start)
            if high - low > half:
                shape = (SUB, stop - start)
                slot = lax.broadcasted_iota(jnp.int32, shape, 1) + start
                pair = lax.broadcasted_iota(jnp.int32, shape, 0) + (first_pair + at)
                sums = jnp.where(
                    slot + pair < 2 * pair_total, sums[: len(keys)], sums[len(keys) :]
                )
            parts.append(sums[:, :size])
        planes[:, :, :, :, start:stop] = (
            jnp.concatenate(parts, axis=1).astype(jnp.bfloat16).reshape(planes.shape[:4] + (stop - start,))
        )
        here = pl.ds(start, stop - start)
        copies.append(
            pltpu.make_async_copy(
                planes.at[:, :, :, :, here], out.at[:, :, :, :, here], sent.at[len(copies)]
            )
        )
        copies[-1].start()
    for copy in copies:
        copy.wait()


def held(value):
    return pltpu.with_memory_space_constraint(value, pltpu.HBM)


def local(fields, rows_first, points, starts, weights, thickness, legendre):
    level_count, field_count, lat_count, lon_count = fields.shape
    pair_count, lat_total, degrees = legendre.shape
    owners = lax.axis_size("lat")
    couples = lon_count // (2 * LANES)
    blocks = 2 * couples
    columns = 2 * owners * pair_count
    sides = []
    for first in range(2):
        edges = [(i, i + 1) for i in range(first, owners - 1, 2)]
        sides.append(lax.ppermute(fields, "lat", edges + [(j, i) for i, j in edges]))

    scalar = pl.BlockSpec(memory_space=pltpu.SMEM)
    vector = pl.BlockSpec(memory_space=pltpu.VMEM)
    params = pltpu.CompilerParams(vmem_limit_bytes=LIMIT)
    remote = pl.BlockSpec(memory_space=pltpu.HBM)
    partial, table, twiddle, far_starts, far_scales, facts = pl.pallas_call(
        functools.partial(near_kernel, pair_count * owners, pair_count),
        out_shape=(
            jax.ShapeDtypeStruct((lat_count, couples, SUB, 2 * LANES), jnp.float32),
            jax.ShapeDtypeStruct((lat_count, 2 * LANES, 2 * columns), jnp.bfloat16),
            jax.ShapeDtypeStruct((lat_count, couples, SUB, 2 * columns), jnp.float32),
            jax.ShapeDtypeStruct((lat_count, 2, couples, 2, 2 * SUB, LANES), jnp.int16),
            jax.ShapeDtypeStruct((lat_count, 2, couples, SUB, SUB, LANES), jnp.float32),
            jax.ShapeDtypeStruct((4 * lat_count, LANES), jnp.int32),
        ),
        in_specs=[remote] * 5,
        out_specs=(vector,) * 6,
        scratch_shapes=[
            pltpu.SMEM(rows_first.shape, jnp.int32),
            pltpu.SMEM(points.shape, jnp.int32),
            pltpu.VMEM(fields.shape, fields.dtype),
            pltpu.VMEM(starts.shape, starts.dtype),
            pltpu.VMEM(weights.shape, weights.dtype),
            pltpu.VMEM((lat_count, STENCIL, blocks, 1, LANES), jnp.int32),
            pltpu.VMEM((weights.size // LANES, LANES), jnp.float32),
            pltpu.VMEM((fields.size // LANES, LANES), jnp.float32),
            pltpu.VMEM((lat_count, blocks + 2, 2 * SUB, LANES), jnp.bfloat16),
            pltpu.SemaphoreType.DMA((5,)),
        ],
        compiler_params=params,
        cost_estimate=pl.CostEstimate(flops=10_000_000, bytes_accessed=4_000_000, transcendentals=0),
        name="near_rows",
    )(*(held(value) for value in (rows_first, points, fields, starts, weights)))

    coefficients = pl.pallas_call(
        far_kernel,
        out_shape=jax.ShapeDtypeStruct((owners, 2 * SUB * lat_count, LANES), jnp.bfloat16),
        in_specs=[vector] * 8,
        out_specs=vector,
        scratch_shapes=[
            pltpu.VMEM((2, fields.size // LANES, LANES), jnp.float32),
            pltpu.VMEM((2 * lat_count, blocks + 2, 2 * SUB, LANES), jnp.bfloat16),
            pltpu.VMEM((lat_count, couples, SUB, 2 * LANES), jnp.float32),
            pltpu.VMEM((lat_count, 2 * SUB, columns + LANES), jnp.bfloat16),
        ],
        compiler_params=params,
        name="far_rows",
    )(*sides, far_starts, far_scales, facts, partial, table, twiddle)

    received = lax.all_to_all(coefficients, "lat", split_axis=0, concat_axis=0, tiled=True)
    by_level = received.reshape(lat_total, 2, level_count, field_count, LANES).astype(jnp.float32)
    virtual = by_level[:, :, :, 2] + 0.61 * by_level[:, :, :, 3]
    total = jnp.sum(thickness[None, None, :, None] * virtual, axis=2).transpose(1, 0, 2)
    level_owners = lax.axis_size("lev")
    if level_owners == 2:
        totals = lax.ppermute(total, "lev", [(0, 1), (1, 0)])[None]
    else:
        totals = lax.all_gather(total, "lev")

    out_shape = (level_count, field_count + 1, 2, pair_count, degrees)
    half = level_count * (field_count + 1) * 2 * SUB
    group_count = (pair_count + SUB - 1) // SUB
    left_shape = jax.ShapeDtypeStruct((group_count, 2 * half, SUB * lat_total), jnp.bfloat16)
    wide = pltpu.VMEM((lat_total * 2 * SUB, LANES), jnp.float32)
    left, base = pl.pallas_call(
        functools.partial(left_kernel, level_count, field_count, pair_count),
        out_shape=(
            left_shape,
            jax.ShapeDtypeStruct((2 * level_count, lat_total, LANES), jnp.float32),
        ),
        in_specs=[scalar, vector],
        out_specs=(vector, vector),
        scratch_shapes=[wide],
        compiler_params=params,
        cost_estimate=pl.CostEstimate(flops=50_000_000, bytes_accessed=2_000_000, transcendentals=0),
        name="left_rows",
    )(thickness, received)
    return pl.pallas_call(
        functools.partial(legendre_kernel, level_owners, level_count, field_count, owners),
        out_shape=(jax.ShapeDtypeStruct(out_shape, jnp.bfloat16), left_shape),
        in_specs=[vector, vector, vector, vector],
        out_specs=(pl.BlockSpec(memory_space=pl.ANY), vector),
        input_output_aliases={3: 1},
        scratch_shapes=[
            pltpu.VMEM(out_shape, jnp.bfloat16),
            pltpu.SemaphoreType.DMA(((degrees + 255) // 256,)),
        ],
        compiler_params=params,
        name="degree_sums",
    )(base, totals, legendre, left)[0]


def solution(mesh):
    placed = (
        P("lev", None, "lat", None),
        P("lat"),
        P(),
        P("lat", None, None),
        P("lat", None, None, None),
        P("lev"),
        P("lat", None, None),
    )
    return jax.shard_map(
        local,
        mesh=mesh,
        in_specs=placed,
        out_specs=P("lev", None, None, "lat", None),
        check_vma=False,
    )
```

```python
import functools

import jax
import jax.numpy as jnp
import numpy as np
from jax import lax
from jax.experimental import pallas as pl
from jax.experimental.pallas import tpu as pltpu
from jax.sharding import PartitionSpec as P

LANES = 128
SUB = 8
HALF = 64
STENCIL = 4
LIMIT = 24 * 1024 * 1024


def lane_gather(values, lanes):
    return jnp.take_along_axis(values, lanes, axis=1, mode="promise_in_bounds")


TAKE = lax.GatherDimensionNumbers(
    offset_dims=(),
    collapsed_slice_dims=(1,),
    start_index_map=(1,),
    operand_batching_dims=(0,),
    start_indices_batching_dims=(0,),
)


def short_gather(values, lanes):
    mode = lax.GatherScatterMode.PROMISE_IN_BOUNDS
    return lax.gather(values, lanes[:, :, None], TAKE, (1, 1), mode=mode)


SINE = (-70.99342854244645, 81.34076844400118, -41.337142359536955, 6.283164044230117)
COSINE = (
    56.2423804697887, -85.2403304160897, 64.93459063550272, -19.739171434929204, 0.9999999534680867,
)


def polynomial(terms, square):
    value = np.float32(terms[0])
    for term in terms[1:]:
        value = value * square + np.float32(term)
    return value


def turn_parts(product, total, inverse):
    turns = (product - jnp.floor(product * inverse + 0.5) * total) * inverse
    halves = jnp.floor(2.0 * turns + 0.5)
    sign = 1.0 - 2.0 * jnp.abs(halves)
    part = turns - 0.5 * halves
    square = part * part
    return sign * polynomial(COSINE, square), (sign * part) * polynomial(SINE, square)


def wavenumbers(at, width, pair_count, pair_total):
    column = lax.broadcasted_iota(jnp.int32, (1, width), 1).astype(jnp.float32) + float(at)
    owner = jnp.floor((column + 0.5) * (1.0 / (2 * pair_count)))
    inner = column - owner * (2.0 * pair_count)
    second = inner >= pair_count
    pair = owner * pair_count + jnp.where(second, inner - pair_count, inner)
    return jnp.where(second, 2.0 * pair_total - 1.0 - pair, pair)


def multiplied(one, two):
    return one[0] * two[0] - one[1] * two[1], one[0] * two[1] + one[1] * two[0]


def row_of(pair, row):
    return tuple(part[row : row + 1] for part in pair)


def extend(lines, row, rows_each, missing, ext, slot):
    blocks = ext.shape[1] - 2

    def block_of(block):
        return lines[pl.ds(block * rows_each + row, SUB, stride=blocks * rows_each), :]

    def place(block, values):
        ext[slot, block] = jnp.concatenate([values, values], axis=0).astype(jnp.bfloat16)

    for block in range(blocks - 1):
        place(block + 1, block_of(block))
    lane = lax.broadcasted_iota(jnp.int32, (SUB, LANES), 1)
    ahead = lane + missing
    behind = lane - missing
    first = lane_gather(block_of(0), ahead & (LANES - 1))
    second = lane_gather(block_of(1), ahead & (LANES - 1))
    last = block_of(blocks - 1)
    final = lane_gather(last, behind & (LANES - 1))
    before = lane_gather(block_of(blocks - 2), behind & (LANES - 1))
    place(0, jnp.where(behind >= 0, final, before))
    place(blocks, jnp.where(ahead < LANES, last, first))
    place(blocks + 1, jnp.where(ahead < LANES, first, second))


def spread_rows(starts, begins):
    lat_count, _, blocks = begins.shape[:3]
    for latitude in range(lat_count):
        for block in range(blocks):
            for row in range(STENCIL):
                lanes = slice(block * LANES, (block + 1) * LANES)
                begins[latitude, row, block] = (
                    starts[latitude, row : row + 1, lanes] - (block - 1) * LANES
                )


def spread_lines(source, lines):
    first, second, rows, lon = source.shape
    at = 0
    for one in range(first):
        for two in range(second):
            values = source[one, two].astype(jnp.float32)
            for block in range(lon // LANES):
                lines[at : at + rows, :] = values[:, block * LANES : (block + 1) * LANES]
                at += rows


def gathered(totals, starts, scales, parts):
    for side in range(2):
        for pair in range(2):
            spot = starts[side] + jnp.int16(2 * pair)
            lane = spot & jnp.int16(LANES - 1)
            low, middle, high = [short_gather(part, lane) for part in parts[side : side + 3]]
            value = jnp.where(
                spot < jnp.int16(LANES),
                low,
                jnp.where(spot < jnp.int16(2 * LANES), middle, high),
            ).astype(jnp.float32)
            line = STENCIL * side + 2 * pair
            totals[side] = (
                totals[side] + scales[line] * value[:SUB] + scales[line + 1] * value[SUB:]
            )
    return totals


def near_kernel(
    pair_total, pair_count, rows_first_far, points_far, fields_far, starts_far, weights_far,
    partial, table, twiddle, far_starts, far_scales, facts,
    rows_first, points, fields, starts, weights, begins, factors, lines, ext, arrived,
):
    lat_count, couples = partial.shape[:2]
    lon = 2 * couples * LANES
    columns = table.shape[2] // 2
    first_lat = lax.axis_index("lat") * lat_count
    fetches = [
        pltpu.make_async_copy(source, target, arrived.at[place])
        for place, (source, target) in enumerate(
            (
                (points_far, points),
                (rows_first_far, rows_first),
                (starts_far, starts),
                (weights_far, weights),
                (fields_far, fields),
            )
        )
    ]
    for fetch in fetches:
        fetch.start()
    fetches[0].wait()
    width = 256
    scales = []
    for latitude in range(lat_count):
        total = jnp.full((1, 1), points[first_lat + latitude], jnp.int32).astype(jnp.float32)
        inverse = 1.0 / total
        scales.append((total, inverse, jnp.sqrt(2.0 * inverse)))
    few = lax.broadcasted_iota(jnp.int32, (SUB, width), 0).astype(jnp.float32)
    many = lax.broadcasted_iota(jnp.int32, (couples + 3, width), 0)
    many = jnp.where(many < couples, many * (2 * LANES), (many - (couples - 1)) * HALF)
    many = many.astype(jnp.float32)
    for at in range(0, columns, width):
        numbers = wavenumbers(at, width, pair_count, pair_total)
        for latitude, (total, inverse, scaling) in enumerate(scales):
            ones = turn_parts(numbers * few, total, inverse)
            eights = turn_parts(numbers * (few * float(SUB)), total, inverse)
            large = turn_parts(numbers * many, total, inverse)
            here = slice(at, at + width)
            there = slice(columns + at, columns + at + width)
            for couple in range(couples):
                for lanes, part in ((here, large[0]), (there, large[1])):
                    twiddle[latitude, couple, :, lanes] = jnp.broadcast_to(
                        scaling * part[couple : couple + 1], (SUB, width)
                    )
            products = [ones] + [multiplied(row_of(eights, row), ones) for row in range(1, SUB)]
            block = tuple(jnp.concatenate(parts, axis=0) for parts in zip(*products))
            for quarter in range(4):
                turned = block
                if quarter > 0:
                    turned = multiplied(row_of(large, couples + quarter - 1), block)
                rows = slice(HALF * quarter, HALF * (quarter + 1))
                table[latitude, rows, here] = turned[0].astype(jnp.bfloat16)
                table[latitude, rows, there] = turned[1].astype(jnp.bfloat16)
    for fetch in fetches[1:]:
        fetch.wait()
    known = [first_lat - rows_first[latitude] for latitude in range(lat_count)]
    known += [points[first_lat + latitude] for latitude in range(lat_count)]
    for place in range(-lat_count, 2 * lat_count):
        if place < 0 or place >= lat_count:
            place = jnp.clip(first_lat + place, 0, points.shape[0] - 1)
            known.append(lon - points[place])
    facts[...] = jnp.concatenate([jnp.full((1, LANES), one, jnp.int32) for one in known], axis=0)
    spread_rows(starts, begins)
    spread_lines(weights, factors)
    spread_lines(fields, lines)
    for latitude in range(lat_count):
        extend(lines, latitude, lat_count, lon - points[first_lat + latitude], ext, latitude)
    lower = (lax.broadcasted_iota(jnp.int32, (2 * SUB, LANES), 0) >= SUB).astype(jnp.int32)
    for latitude in range(lat_count):
        mine = first_lat - rows_first[latitude]
        for couple in range(couples):

            def spread_row(row):
                at = ((latitude * STENCIL + row) * couples + couple) * SUB
                tile = factors[pl.ds(pl.multiple_of(at, SUB), SUB), :]
                begun = []
                for side in range(2):
                    start = jnp.broadcast_to(
                        begins[latitude, row, 2 * couple + side], (2 * SUB, LANES)
                    )
                    begun.append((start + lower).astype(jnp.int16))
                return (
                    begun,
                    [jnp.broadcast_to(tile[line : line + 1], (SUB, LANES)) for line in range(SUB)],
                )

            totals = [jnp.zeros((SUB, LANES), jnp.float32) for _ in range(2)]
            for slot in range(lat_count):
                begun, scales = spread_row(mine + slot)
                parts = [ext[slot, 2 * couple + piece] for piece in range(4)]
                totals = gathered(totals, begun, scales, parts)
            for side in range(2):
                partial[latitude, couple, :, side * LANES : (side + 1) * LANES] = totals[side]
            others = (jnp.where(mine >= 1, 0, 2), jnp.where(mine <= 1, 3, 1))
            for choice, row in enumerate(others):
                begun, scales = spread_row(row)
                for side in range(2):
                    far_starts[latitude, choice, couple, side] = begun[side]
                for line in range(SUB):
                    far_scales[latitude, choice, couple, line] = scales[line]


def far_kernel(
    near_side, far_side, far_starts, far_scales, facts, partial, table, twiddle,
    out, lines, ext, grid, waves,
):
    lat_count, couples = partial.shape[:2]
    columns = table.shape[2] // 2
    owners = out.shape[0]
    toward = 1 - lax.axis_index("lat") % 2
    spread_lines(near_side, lines.at[toward])
    spread_lines(far_side, lines.at[1 - toward])
    fact = [jnp.broadcast_to(facts[row : row + 1], (SUB, LANES)) for row in range(4 * lat_count)]
    for slot in range(2 * lat_count):
        side, row = divmod(slot, lat_count)
        extend(lines.at[side], row, lat_count, fact[2 * lat_count + slot], ext, slot)
    lane = lax.broadcasted_iota(jnp.int32, (SUB, LANES), 1)
    width = 256
    choices = ((2, 1, 0), (3, 2, 1))
    for latitude in range(lat_count):
        own = jnp.broadcast_to(facts[latitude : latitude + 1], (2 * SUB, LANES)).astype(jnp.int16)
        at_zero = own == jnp.int16(0)
        at_one = own == jnp.int16(1)
        for couple in range(couples):
            sides = [pl.ds(side * LANES, LANES) for side in range(2)]
            totals = [partial[latitude, couple, :, lanes] for lanes in sides]
            for choice, slots in enumerate(choices):
                parts = []
                for piece in range(4):
                    zero, one, two = [ext[slot, 2 * couple + piece] for slot in slots]
                    parts.append(jnp.where(at_zero, zero, jnp.where(at_one, one, two)))
                totals = gathered(
                    totals,
                    [far_starts[latitude, choice, couple, side] for side in range(2)],
                    [far_scales[latitude, choice, couple, line] for line in range(SUB)],
                    parts,
                )
            for side in range(2):
                live = lane + (2 * couple + side) * LANES < fact[lat_count + latitude]
                grid[latitude, couple, :, sides[side]] = jnp.where(live, totals[side], 0.0)
    for latitude in range(lat_count):
        rows = grid[latitude].reshape(couples * SUB, 2 * LANES).astype(jnp.bfloat16)
        for at in range(0, columns, width):
            real = jnp.dot(
                rows, table[latitude, :, at : at + width], preferred_element_type=jnp.float32
            )
            imag = jnp.dot(
                rows,
                table[latitude, :, columns + at : columns + at + width],
                preferred_element_type=jnp.float32,
            )
            cosine = jnp.zeros((SUB, width), jnp.float32)
            sine = jnp.zeros((SUB, width), jnp.float32)
            for couple in range(couples):
                turn_cos = twiddle[latitude, couple, :, at : at + width]
                turn_sin = twiddle[latitude, couple, :, columns + at : columns + at + width]
                here = slice(couple * SUB, (couple + 1) * SUB)
                cosine = cosine + (real[here] * turn_cos - imag[here] * turn_sin)
                sine = sine - (real[here] * turn_sin + imag[here] * turn_cos)
            waves[latitude, 0:SUB, at : at + width] = cosine
            waves[latitude, SUB : 2 * SUB, at : at + width] = sine
        waves[latitude, :, columns:] = jnp.zeros((2 * SUB, waves.shape[2] - columns), jnp.float32)
        used = columns // owners
        for owner in range(owners):
            out[owner, 2 * SUB * latitude : 2 * SUB * (latitude + 1), :] = waves[
                latitude, :, owner * used : owner * used + LANES
            ].astype(jnp.bfloat16)


def row_keys(level_count, field_count):
    return [
        (level, field, part)
        for level in range(level_count)
        for field in range(field_count + 1)
        for part in range(2)
    ]


def place_rows(lines, keys, pair_count, left):
    lat_total = next(iter(lines.values())).shape[0]
    depth = SUB * lat_total
    half = len(keys) * SUB
    spread = (
        lax.broadcasted_iota(jnp.int32, (lat_total, depth), 0)
        == lax.broadcasted_iota(jnp.int32, (lat_total, depth), 1) % lat_total
    ).astype(jnp.bfloat16)
    keep = (
        lax.broadcasted_iota(jnp.int32, (SUB, depth), 0)
        == lax.broadcasted_iota(jnp.int32, (SUB, depth), 1) // lat_total
    )
    for place in range(0, len(keys), 2):
        if keys[place] not in lines:
            continue
        couple = [
            lax.dot_general(
                lines[key].astype(jnp.bfloat16),
                spread,
                (((0,), (0,)), ((), ())),
                preferred_element_type=jnp.float32,
            )
            for key in keys[place : place + 2]
        ]
        for member in range(2):
            for group in range(left.shape[0]):
                begin = member * pair_count + group * SUB
                pieces = [jnp.where(keep, one[begin : begin + SUB], 0.0) for one in couple]
                into = member * half + place * SUB
                left[group, into : into + 2 * SUB, :] = jnp.concatenate(pieces, axis=0).astype(
                    jnp.bfloat16
                )


def received_rows(received, wide, keys, field_count):
    wide[...] = received[...].astype(jnp.float32).reshape(wide.shape)
    lat_total = wide.shape[0] // (2 * SUB)
    return {
        (level, field, part): wide[
            pl.ds(part * SUB + level * field_count + field, lat_total, stride=2 * SUB), :
        ]
        for level, field, part in keys
    }


def left_kernel(
    level_count, field_count, pair_count, thickness, received, left, base, wide,
):
    keys = row_keys(level_count, field_count)
    wanted = [key for key in keys if key[1] < field_count]
    lines = received_rows(received, wide, wanted, field_count)
    place_rows(lines, keys, pair_count, left)
    for part in range(2):
        running = jnp.zeros(base.shape[1:], jnp.float32)
        for level in reversed(range(level_count)):
            running = running + thickness[level] * (
                lines[level, 2, part] + 0.61 * lines[level, 3, part]
            )
            base[2 * level + part] = running


def legendre_kernel(
    level_owners, level_count, field_count, owners, base, totals, legendre, left_given,
    out, left, planes, sent,
):
    pair_count, lat_total, degrees = legendre.shape
    pair_total = pair_count * owners
    groups = [(at, min(SUB, pair_count - at)) for at in range(0, pair_count, SUB)]
    keys = row_keys(level_count, field_count)
    half = len(keys) * SUB
    level_place = lax.axis_index("lev")
    first_pair = lax.axis_index("lat") * pair_count
    sums = {}
    for part in range(2):
        deeper = jnp.zeros((lat_total, LANES), jnp.float32)
        for place in range(totals.shape[0]):
            other = 1 - level_place if level_owners == 2 else place
            deeper = deeper + jnp.where(other > level_place, totals[place, part], 0.0)
        for level in range(level_count):
            sums[level, field_count, part] = base[2 * level + part] + deeper
    place_rows(sums, keys, pair_count, left)
    copies = []
    for start in range(0, degrees, 512):
        stop = min(start + 512, degrees)
        low = 0 if start < 2 * pair_total else half
        high = 2 * half if stop > pair_total + 1 else half
        parts = []
        for group, (at, size) in enumerate(groups):
            values = legendre[at : at + size, :, start:stop].reshape(size * lat_total, stop - start)
            sums = jnp.dot(
                left[group, low:high, : size * lat_total],
                values,
                preferred_element_type=jnp.float32,
            ).reshape((high - low) // SUB, SUB, stop - start)
            if high - low > half:
                shape = (SUB, stop - start)
                slot = lax.broadcasted_iota(jnp.int32, shape, 1) + start
                pair = lax.broadcasted_iota(jnp.int32, shape, 0) + (first_pair + at)
                sums = jnp.where(
                    slot + pair < 2 * pair_total, sums[: len(keys)], sums[len(keys) :]
                )
            parts.append(sums[:, :size])
        planes[:, :, :, :, start:stop] = (
            jnp.concatenate(parts, axis=1).astype(jnp.bfloat16).reshape(planes.shape[:4] + (stop - start,))
        )
        here = pl.ds(start, stop - start)
        copies.append(
            pltpu.make_async_copy(
                planes.at[:, :, :, :, here], out.at[:, :, :, :, here], sent.at[len(copies)]
            )
        )
        copies[-1].start()
    for copy in copies:
        copy.wait()


def held(value):
    return pltpu.with_memory_space_constraint(value, pltpu.HBM)


def local(fields, rows_first, points, starts, weights, thickness, legendre):
    level_count, field_count, lat_count, lon_count = fields.shape
    pair_count, lat_total, degrees = legendre.shape
    owners = lax.axis_size("lat")
    couples = lon_count // (2 * LANES)
    blocks = 2 * couples
    columns = 2 * owners * pair_count
    sides = []
    for first in range(2):
        edges = [(i, i + 1) for i in range(first, owners - 1, 2)]
        sides.append(lax.ppermute(fields, "lat", edges + [(j, i) for i, j in edges]))

    scalar = pl.BlockSpec(memory_space=pltpu.SMEM)
    vector = pl.BlockSpec(memory_space=pltpu.VMEM)
    params = pltpu.CompilerParams(vmem_limit_bytes=LIMIT)
    remote = pl.BlockSpec(memory_space=pltpu.HBM)
    partial, table, twiddle, far_starts, far_scales, facts = pl.pallas_call(
        functools.partial(near_kernel, pair_count * owners, pair_count),
        out_shape=(
            jax.ShapeDtypeStruct((lat_count, couples, SUB, 2 * LANES), jnp.float32),
            jax.ShapeDtypeStruct((lat_count, 2 * LANES, 2 * columns), jnp.bfloat16),
            jax.ShapeDtypeStruct((lat_count, couples, SUB, 2 * columns), jnp.float32),
            jax.ShapeDtypeStruct((lat_count, 2, couples, 2, 2 * SUB, LANES), jnp.int16),
            jax.ShapeDtypeStruct((lat_count, 2, couples, SUB, SUB, LANES), jnp.float32),
            jax.ShapeDtypeStruct((4 * lat_count, LANES), jnp.int32),
        ),
        in_specs=[remote] * 5,
        out_specs=(vector,) * 6,
        scratch_shapes=[
            pltpu.SMEM(rows_first.shape, jnp.int32),
            pltpu.SMEM(points.shape, jnp.int32),
            pltpu.VMEM(fields.shape, fields.dtype),
            pltpu.VMEM(starts.shape, starts.dtype),
            pltpu.VMEM(weights.shape, weights.dtype),
            pltpu.VMEM((lat_count, STENCIL, blocks, 1, LANES), jnp.int32),
            pltpu.VMEM((weights.size // LANES, LANES), jnp.float32),
            pltpu.VMEM((fields.size // LANES, LANES), jnp.float32),
            pltpu.VMEM((lat_count, blocks + 2, 2 * SUB, LANES), jnp.bfloat16),
            pltpu.SemaphoreType.DMA((5,)),
        ],
        compiler_params=params,
        cost_estimate=pl.CostEstimate(flops=10_000_000, bytes_accessed=4_000_000, transcendentals=0),
        name="near_rows",
    )(*(held(value) for value in (rows_first, points, fields, starts, weights)))

    coefficients = pl.pallas_call(
        far_kernel,
        out_shape=jax.ShapeDtypeStruct((owners, 2 * SUB * lat_count, LANES), jnp.bfloat16),
        in_specs=[vector] * 8,
        out_specs=vector,
        scratch_shapes=[
            pltpu.VMEM((2, fields.size // LANES, LANES), jnp.float32),
            pltpu.VMEM((2 * lat_count, blocks + 2, 2 * SUB, LANES), jnp.bfloat16),
            pltpu.VMEM((lat_count, couples, SUB, 2 * LANES), jnp.float32),
            pltpu.VMEM((lat_count, 2 * SUB, columns + LANES), jnp.float32),
        ],
        compiler_params=params,
        name="far_rows",
    )(*sides, far_starts, far_scales, facts, partial, table, twiddle)

    received = lax.all_to_all(coefficients, "lat", split_axis=0, concat_axis=0, tiled=True)
    by_level = received.reshape(lat_total, 2, level_count, field_count, LANES).astype(jnp.float32)
    virtual = by_level[:, :, :, 2] + 0.61 * by_level[:, :, :, 3]
    total = jnp.sum(thickness[None, None, :, None] * virtual, axis=2).transpose(1, 0, 2)
    level_owners = lax.axis_size("lev")
    if level_owners == 2:
        totals = lax.ppermute(total, "lev", [(0, 1), (1, 0)])[None]
    else:
        totals = lax.all_gather(total, "lev")

    out_shape = (level_count, field_count + 1, 2, pair_count, degrees)
    half = level_count * (field_count + 1) * 2 * SUB
    group_count = (pair_count + SUB - 1) // SUB
    left_shape = jax.ShapeDtypeStruct((group_count, 2 * half, SUB * lat_total), jnp.bfloat16)
    wide = pltpu.VMEM((lat_total * 2 * SUB, LANES), jnp.float32)
    left, base = pl.pallas_call(
        functools.partial(left_kernel, level_count, field_count, pair_count),
        out_shape=(
            left_shape,
            jax.ShapeDtypeStruct((2 * level_count, lat_total, LANES), jnp.float32),
        ),
        in_specs=[scalar, vector],
        out_specs=(vector, vector),
        scratch_shapes=[wide],
        compiler_params=params,
        cost_estimate=pl.CostEstimate(flops=50_000_000, bytes_accessed=2_000_000, transcendentals=0),
        name="left_rows",
    )(thickness, received)
    return pl.pallas_call(
        functools.partial(legendre_kernel, level_owners, level_count, field_count, owners),
        out_shape=(jax.ShapeDtypeStruct(out_shape, jnp.bfloat16), left_shape),
        in_specs=[vector, vector, vector, vector],
        out_specs=(pl.BlockSpec(memory_space=pl.ANY), vector),
        input_output_aliases={3: 1},
        scratch_shapes=[
            pltpu.VMEM(out_shape, jnp.bfloat16),
            pltpu.SemaphoreType.DMA(((degrees + 511) // 512,)),
        ],
        compiler_params=params,
        name="degree_sums",
    )(base, totals, legendre, left)[0]


def solution(mesh):
    placed = (
        P("lev", None, "lat", None),
        P("lat"),
        P(),
        P("lat", None, None),
        P("lat", None, None, None),
        P("lev"),
        P("lat", None, None),
    )
    return jax.shard_map(
        local,
        mesh=mesh,
        in_specs=placed,
        out_specs=P("lev", None, None, "lat", None),
        check_vma=False,
    )
```
